32 devices in a mesh: dp: 8 (over z, x), head: 4 (over y, core).
Axes of the slice: x: 2, y: 2, z: 4, core: 2. Of those that a mesh axis runs over, the one named last changes fastest.
Arguments:
- tokens: bfloat16 [8, 2048, 1024], P('dp', 'head'), may hold values from -6 to 6
- doc_starts: int32 [8, 4], P('dp'), may hold values from 0 to 2047, as said below
- grad_out: bfloat16 [8, 2048, 1024], P('dp', 'head'), may hold values from -6 to 6
- norm_one: float32 [2, 1024], replicated, may hold values from 0.1 to 1.9
- w_query: bfloat16 [2, 1024, 512], P(None, None, 'head'), may hold values from -0.1875 to 0.1875
- w_key: bfloat16 [2, 1024, 512], P(None, None, 'head'), may hold values from -0.1875 to 0.1875
- w_value: bfloat16 [2, 1024, 1024], P(None, None, 'head'), may hold values from -0.1875 to 0.1875
- w_outgate: bfloat16 [2, 1024, 1024], P(None, None, 'head'), may hold values from -0.1875 to 0.1875
- w_rank: bfloat16 [2, 1024, 16], replicated, may hold values from -0.1875 to 0.1875
- w_decay: bfloat16 [2, 16, 512], P(None, None, 'head'), may hold values from -1.5 to 1.5
- decay_bias: float32 [2, 512], P(None, 'head'), may hold values from 0 to 6
- group_gain: float32 [2, 256], replicated, may hold values from 0.1 to 1.9
- w_out: bfloat16 [2, 1024, 1024], P(None, 'head'), may hold values from -0.1875 to 0.1875
- norm_two: float32 [2, 1024], replicated, may hold values from 0.1 to 1.9
- w_gate: bfloat16 [2, 1024, 2816], P(None, None, 'head'), may hold values from -0.1875 to 0.1875
- w_up: bfloat16 [2, 1024, 2816], P(None, None, 'head'), may hold values from -0.1875 to 0.1875
- w_down: bfloat16 [2, 2816, 1024], P(None, 'head'), may hold values from -0.109375 to 0.109375
Outputs:
- result: bfloat16 [8, 2048, 1024], P('dp', 'head')
- grad_tokens: float32 [8, 2048, 1024], P('dp', 'head')
- grad_norm_one: float32 [2, 1024], replicated
- grad_w_query: float32 [2, 1024, 512], P(None, None, 'head')
- grad_w_key: float32 [2, 1024, 512], P(None, None, 'head')
- grad_w_value: float32 [2, 1024, 1024], P(None, None, 'head')
- grad_w_outgate: float32 [2, 1024, 1024], P(None, None, 'head')
- grad_w_rank: float32 [2, 1024, 16], replicated
- grad_w_decay: float32 [2, 16, 512], P(None, None, 'head')
- grad_decay_bias: float32 [2, 512], P(None, 'head')
- grad_group_gain: float32 [2, 256], replicated
- grad_w_out: float32 [2, 1024, 1024], P(None, 'head')
- grad_norm_two: float32 [2, 1024], replicated
- grad_w_gate: float32 [2, 1024, 2816], P(None, None, 'head')
- grad_w_up: float32 [2, 1024, 2816], P(None, None, 'head')
- grad_w_down: float32 [2, 2816, 1024], P(None, 'head')
The draws below stay inside these ranges and needn't reach their ends.
Inputs may be any that keep to these rules, and one draw needn't show every extreme that they name: `doc_starts`: each row's entries rise strictly and the first is 0; in the first row the last entry is 2047.
All inputs are finite; a program needn't handle non-finite values.
Results may differ from the reference program's by a relative error of at most 0.024.
Values may be sent and summed in bfloat16 or wider, within the bound.
A program may use at most 256 MiB of HBM per device.

```python
import jax
import jax.numpy as jnp
from jax import lax

D = 1024
KD = 512
VD = 1024
HEADS = 4
RANK = 16
FF = 2816
SPAN = 64
LAYERS = 2
SEQ = 2048
NDOC = 4
ROWS = 8
HK = 128
HV = 256
N_HEAD = 4


def draw_doc_starts(key, part):
    row_keys = jax.random.split(key, ROWS)
    row_index = jnp.arange(ROWS, dtype=jnp.int32)

    def one_row(row_key, which_row):
        order = jax.random.permutation(row_key, SEQ - 1) + 1
        chosen = jnp.sort(order[:NDOC - 1].astype(jnp.int32))
        last_value = jnp.where(which_row == 0, jnp.int32(SEQ - 1), chosen[-1])
        chosen = chosen.at[-1].set(last_value)
        return jnp.concatenate([jnp.zeros((1,), jnp.int32), chosen])
    return jax.vmap(one_row)(row_keys, row_index)


def block_levels(own_key, extent, cuts, least, top_value):
    factor_of = 1.0
    for dim, shards_of in cuts:
        draws = jax.random.uniform(jax.random.fold_in(jax.random.fold_in(own_key, 6), dim), (shards_of,), jnp.float32, least / len(cuts), top_value / len(cuts))
        factor_of = factor_of * jnp.repeat(jnp.exp(draws), extent[dim] // shards_of).reshape((-1,) + (1,) * (len(extent) - 1 - dim))
    return factor_of


def normal_values(rng, dims, deviation, reach, cuts=(), held_as=jnp.bfloat16):
    level = block_levels(rng, dims, cuts, -0.22, 0.18) if cuts else 1.0
    drawn = jax.random.normal(rng, dims, jnp.float32) * deviation * level
    return jnp.minimum(jnp.maximum(drawn, -reach), reach).astype(held_as)


def setup_inputs(seed: int = 0) -> dict:
    seeds = jax.random.split(jax.random.key(seed), 18)
    tokens = normal_values(seeds[0], (ROWS, SEQ, D), 1.0, 6.0, ((0, 8), (1, 4)))
    doc_starts = draw_doc_starts(jax.random.fold_in(seeds[17], 71), 0)
    grad_out = normal_values(seeds[2], (ROWS, SEQ, D), 1.0, 6.0, ((0, 8), (1, 4)))
    norm_one = jnp.clip(1.0 + 0.18 * jax.random.normal(seeds[3], (LAYERS, D), jnp.float32), 0.1, 1.9)
    w_query = normal_values(seeds[4], (LAYERS, D, KD), D ** -0.5, 0.1875, ((2, 4),))
    w_key = normal_values(seeds[5], (LAYERS, D, KD), D ** -0.5, 0.1875, ((2, 4),))
    w_value = normal_values(seeds[6], (LAYERS, D, VD), D ** -0.5, 0.1875, ((2, 4),))
    w_outgate = normal_values(seeds[7], (LAYERS, D, VD), D ** -0.5, 0.1875, ((2, 4),))
    w_rank = normal_values(seeds[8], (LAYERS, D, RANK), D ** -0.5, 0.1875)
    w_decay = normal_values(seeds[9], (LAYERS, RANK, KD), RANK ** -0.5, 1.5, ((2, 4),))
    decay_bias = jnp.clip(6.0 * jax.random.uniform(seeds[10], (LAYERS, KD), jnp.float32) ** block_levels(seeds[10], (LAYERS, KD), ((1, 4),), -0.2, 0.2), 0.0, 6.0)
    group_gain = jnp.clip(1.0 + 0.18 * jax.random.normal(seeds[11], (LAYERS, HV), jnp.float32), 0.1, 1.9)
    w_out = normal_values(seeds[12], (LAYERS, VD, D), VD ** -0.5, 0.1875, ((1, 4),))
    norm_two = jnp.clip(1.0 + 0.18 * jax.random.normal(seeds[13], (LAYERS, D), jnp.float32), 0.1, 1.9)
    w_gate = normal_values(seeds[14], (LAYERS, D, FF), D ** -0.5, 0.1875, ((2, 4),))
    w_up = normal_values(seeds[15], (LAYERS, D, FF), D ** -0.5, 0.1875, ((2, 4),))
    w_down = normal_values(seeds[16], (LAYERS, FF, D), FF ** -0.5, 0.109375, ((1, 4),))
    return {"tokens": tokens, "doc_starts": doc_starts, "grad_out": grad_out, "norm_one": norm_one, "w_query": w_query, "w_key": w_key, "w_value": w_value, "w_outgate": w_outgate, "w_rank": w_rank, "w_decay": w_decay, "decay_bias": decay_bias, "group_gain": group_gain, "w_out": w_out, "norm_two": norm_two, "w_gate": w_gate, "w_up": w_up, "w_down": w_down}


epsilon = 1e-06
highest = lax.Precision.HIGHEST

@jax.custom_vjp
def low(v):
    return lax.optimization_barrier(v.astype(jnp.bfloat16)).astype(jnp.float32)

@jax.custom_vjp
def low_back(v):
    return v

def low_keep(v):
    return (low(v), None)

def low_pass(kept, grad):
    return (grad,)

def back_keep(v):
    return (v, None)

def back_low(kept, grad):
    return (low(grad),)
low.defvjp(low_keep, low_pass)
low_back.defvjp(back_keep, back_low)

def product_of(left, right):
    return jnp.dot(left, right, precision=highest, preferred_element_type=jnp.float32)

def rms_norm(hidden, gain):
    return hidden * lax.rsqrt(lax.optimization_barrier(jnp.mean(hidden * hidden, axis=-1, keepdims=True)) + epsilon) * gain

def span_step(state, inputs):
    queries, keys_in, values_in, decays, doc_ids, doc_before = inputs
    doc_ids = doc_ids.astype(jnp.int32)
    doc_before = doc_before.astype(jnp.int32)
    running = jnp.cumsum(decays, axis=0)
    scaled_query = queries * jnp.exp(running)
    scaled_key = keys_in * jnp.exp(-running)
    scores = jnp.dot(scaled_query, scaled_key.T, precision=highest)
    places = lax.iota(jnp.int32, queries.shape[0])
    allowed = (places[:, None] >= places[None, :]) & (doc_ids[:, None] == doc_ids[None, :])
    scores = jnp.where(allowed, scores, jnp.zeros_like(scores))
    carried = (doc_ids == doc_before).astype(jnp.float32)
    output = jnp.dot(scores, values_in, precision=highest) + carried[:, None] * jnp.dot(scaled_query, state, precision=highest)
    ending = running[-1]
    same_doc = (doc_ids == doc_ids[-1]).astype(jnp.float32)
    moved_key = keys_in * jnp.exp(ending[None, :] - running) * same_doc[:, None]
    new_state = state * (jnp.exp(ending)[:, None] * carried[-1]) + jnp.dot(moved_key.T, values_in, precision=highest)
    return (new_state, output)

def mix_head(queries, keys_in, values_in, decays, doc_ids):
    total = queries.shape[0]
    blocks = total // SPAN
    queries = queries * queries.shape[-1] ** (-0.5)
    block_q = queries.reshape(blocks, SPAN, -1)
    block_k = keys_in.reshape(blocks, SPAN, -1)
    block_v = values_in.reshape(blocks, SPAN, -1)
    block_d = decays.reshape(blocks, SPAN, -1)
    block_ids = doc_ids.astype(jnp.int32).reshape(blocks, SPAN)
    doc_before = jnp.concatenate([jnp.full((1,), -1, jnp.int32), block_ids[:-1, -1].astype(jnp.int32)])
    start_state = jnp.zeros((queries.shape[-1], values_in.shape[-1]), jnp.float32)
    final_state, outputs = lax.scan(jax.checkpoint(span_step), start_state, (block_q, block_k, block_v, block_d, block_ids, doc_before))
    return outputs.reshape(total, -1)

def head_norm(mixed, gain):
    return mixed * lax.rsqrt(jnp.maximum(lax.optimization_barrier(jnp.mean(mixed * mixed, axis=-1, keepdims=True)), 1.0)) * gain

def row_forward(params, hidden, doc_ids):
    norm_one, w_query, w_key, w_value, w_outgate, w_rank, w_decay, decay_bias, group_gain, w_out, norm_two, w_gate, w_up, w_down = params
    per_head = jax.vmap(mix_head, in_axes=(1, 1, 1, 1, None), out_axes=1)
    group_cols = KD // N_HEAD
    for which_layer in range(LAYERS):
        normed_in = low(rms_norm(hidden, norm_one[which_layer]))
        queries = low_back(product_of(normed_in, w_query[which_layer]))
        keys_in = low_back(product_of(normed_in, w_key[which_layer]))
        values_in = low_back(product_of(normed_in, w_value[which_layer]))
        outgate = low_back(product_of(normed_in, w_outgate[which_layer]))
        ranked = product_of(normed_in, w_rank[which_layer])
        pieces = []
        for member in range(N_HEAD):
            cols = w_decay[which_layer][:, member * group_cols:(member + 1) * group_cols]
            pieces.append(product_of(low_back(ranked), cols))
        before = jnp.concatenate(pieces, axis=1) + decay_bias[which_layer]
        decays = jax.nn.log_sigmoid(before) / 16.0
        mixed = per_head(queries.reshape(SEQ, HEADS, HK), keys_in.reshape(SEQ, HEADS, HK), values_in.reshape(SEQ, HEADS, HV), decays.reshape(SEQ, HEADS, HK), doc_ids)
        normed_heads = head_norm(mixed, group_gain[which_layer])
        gated = low((normed_heads * jax.nn.silu(outgate.reshape(SEQ, HEADS, HV))).reshape(SEQ, VD))
        hidden = hidden + low_back(product_of(gated, w_out[which_layer]))
        normed_mid = low(rms_norm(hidden, norm_two[which_layer]))
        gate_pre = low_back(product_of(normed_mid, w_gate[which_layer]))
        up_pre = low_back(product_of(normed_mid, w_up[which_layer]))
        product = low(jax.nn.silu(gate_pre) * up_pre)
        hidden = hidden + low_back(product_of(product, w_down[which_layer]))
    return hidden

def reference(tokens, doc_starts, grad_out, norm_one, w_query, w_key, w_value, w_outgate, w_rank, w_decay, decay_bias, group_gain, w_out, norm_two, w_gate, w_up, w_down):
    params = tuple((p.astype(jnp.float32) for p in (norm_one, w_query, w_key, w_value, w_outgate, w_rank, w_decay, decay_bias, group_gain, w_out, norm_two, w_gate, w_up, w_down)))
    inputs = tokens.astype(jnp.float32)
    cotangent = grad_out.astype(jnp.float32)
    places = lax.iota(jnp.int32, SEQ)
    doc_ids = (lax.optimization_barrier(jnp.sum((doc_starts.astype(jnp.int32)[:, :, None] <= places[None, None, :]).astype(jnp.int32), axis=1)) - 1).astype(jnp.int32)

    def forward(weights, rows_in):
        stepped = jax.checkpoint(row_forward)

        def one_row(row_data):
            return stepped(weights, row_data[0], row_data[1])
        return lax.map(one_row, (rows_in, doc_ids))
    outcome, pullback = jax.vjp(forward, params, inputs)
    grads, grad_inputs = pullback(cotangent)
    return (outcome.astype(jnp.bfloat16), grad_inputs, grads[0], grads[1], grads[2], grads[3], grads[4], grads[5], grads[6], grads[7], grads[8], grads[9], grads[10], grads[11], grads[12], grads[13])
```

```python
import jax
import jax.numpy as jnp
from jax import lax
from jax.experimental import pallas as pl
from jax.experimental.pallas import tpu as pltpu
from jax.sharding import PartitionSpec as P

LAYERS = 2
HK = 128
HV = 256
HEAD_COLS = 2 * HK + 2 * HV
BLK = 128
MID = BLK // 2 - 1
epsilon = 1e-06
highest = lax.Precision.HIGHEST
VMEM_LIMIT = 48 * 1024 * 1024

f32 = jnp.float32
bf16 = jnp.bfloat16


def nn(left, right):
    return lax.dot_general(left, right, (((1,), (0,)), ((), ())), preferred_element_type=f32)


def nt(left, right):
    return lax.dot_general(left, right, (((1,), (1,)), ((), ())), preferred_element_type=f32)


def tn(left, right):
    return lax.dot_general(left, right, (((0,), (0,)), ((), ())), preferred_element_type=f32)


def doc_count(meta, ndoc, place):
    total = (meta[0] <= place).astype(jnp.int32)
    for which in range(1, ndoc):
        total = total + (meta[which] <= place).astype(jnp.int32)
    return total


def block_masks(meta, ndoc, start):
    rows = lax.broadcasted_iota(jnp.int32, (BLK, BLK), 0) + start
    cols = lax.broadcasted_iota(jnp.int32, (BLK, BLK), 1) + start
    row_ids = doc_count(meta, ndoc, rows)
    col_ids = doc_count(meta, ndoc, cols)
    id_prev = doc_count(meta, ndoc, start - 1)
    id_last = doc_count(meta, ndoc, start + BLK - 1)
    allowed = (rows >= cols) & (row_ids == col_ids)
    carried = jnp.where(row_ids == id_prev, 1.0, 0.0)
    same = jnp.where(row_ids == id_last, 1.0, 0.0)
    keep = jnp.where(id_last == id_prev, 1.0, 0.0)
    return allowed, carried, same, keep


def split_dot(ones_mat, value, dot):
    high = value.astype(bf16)
    low = (value - high.astype(f32)).astype(bf16)
    return dot(ones_mat, high) + dot(ones_mat, low)


def tri_ones():
    rows = lax.broadcasted_iota(jnp.int32, (BLK, BLK), 0)
    cols = lax.broadcasted_iota(jnp.int32, (BLK, BLK), 1)
    return jnp.where(rows >= cols, 1.0, 0.0).astype(bf16)


def head_parts(x_ref, slot):
    at = slot * HEAD_COLS
    query = x_ref[:, at : at + HK] * (HK**-0.5)
    key = x_ref[:, at + HK : at + 2 * HK]
    value = x_ref[:, at + 2 * HK : at + 2 * HK + HV]
    outgate = x_ref[:, at + 2 * HK + HV : at + HEAD_COLS]
    return query, key, value, outgate


def decay_before(x_ref, wdec_ref, bias_ref):
    ranked = x_ref[:, 2 * HEAD_COLS :]
    return jnp.dot(ranked, wdec_ref[...], precision=highest, preferred_element_type=f32) + bias_ref[...]


def states_kernel(ndoc, meta, x_ref, wdec_ref, bias_ref, run_ref, state_ref, cum_ref, final_ref, state, cum):
    block = pl.program_id(0)

    @pl.when(block == 0)
    def _():
        state[...] = jnp.zeros_like(state)
        cum[...] = jnp.ones_like(cum)

    start = meta[ndoc] + block * BLK
    _, _, same, keep = block_masks(meta, ndoc, start)
    before = decay_before(x_ref, wdec_ref, bias_ref)
    decays = (jnp.minimum(before, 0.0) - jnp.log1p(jnp.exp(-jnp.abs(before)))) * (1.0 / 16.0)
    running = split_dot(tri_ones(), decays, nn)
    run_ref[...] = running
    ending = running[BLK - 1 :, :]
    factor = jnp.exp(ending) * keep
    cum_ref[0] = cum[...]
    cum[...] = cum[...] * factor
    for slot in range(2):
        lanes = slice(slot * HK, slot * HK + HK)
        _, key, value, _ = head_parts(x_ref, slot)
        moved = (key * jnp.exp(ending[:, lanes] - running[:, lanes]) * same).astype(bf16)
        old = state[slot]
        state_ref[0, slot] = old.astype(bf16)
        new = old * factor[:, lanes] + tn(value.astype(bf16), moved)
        state[slot] = new
        final_ref[slot] = new.astype(bf16)


def mix_kernel(ndoc, meta, x_ref, run_ref, state_ref, cum_ref, first_ref, gain_ref, gated_ref, mixed_ref):
    block = pl.program_id(0)
    start = meta[ndoc] + block * BLK
    allowed, carried, _, _ = block_masks(meta, ndoc, start)
    gain = gain_ref[...]
    for slot in range(2):
        lanes = slice(slot * HK, slot * HK + HK)
        cols = slice(slot * HV, slot * HV + HV)
        query, key, value, outgate = head_parts(x_ref, slot)
        running = run_ref[:, lanes]
        middle = running[MID : MID + 1, :]
        rel_query = (query * jnp.exp(running - middle)).astype(bf16)
        rel_key = (key * jnp.exp(middle - running)).astype(bf16)
        scores = jnp.where(allowed, nt(rel_query, rel_key), 0.0).astype(bf16)
        far_query = (query * jnp.exp(running) * carried).astype(bf16)
        state = (state_ref[0, slot].astype(f32) + first_ref[slot].astype(f32) * cum_ref[0][:, lanes]).astype(bf16)
        mixed = nn(scores, value.astype(bf16)) + nt(far_query, state)
        scale = lax.rsqrt(jnp.maximum(jnp.mean(mixed * mixed, axis=-1, keepdims=True), 1.0))
        gated_ref[:, cols] = (mixed * scale * gain * outgate * jax.nn.sigmoid(outgate)).astype(bf16)
        mixed_ref[:, cols] = mixed.astype(bf16)


def back_states_kernel(
    ndoc, nblk, meta, x_ref, run_ref, mixed_ref, dgated_ref, gain_ref,
    dmixed_ref, doutgate_ref, dstate_ref, cum_ref, final_ref, dgain_ref, state, cum,
):
    step = pl.program_id(0)

    @pl.when(step == 0)
    def _():
        state[...] = jnp.zeros_like(state)
        cum[...] = jnp.ones_like(cum)
        dgain_ref[...] = jnp.zeros_like(dgain_ref)

    start = meta[ndoc] + (nblk - 1 - step) * BLK
    _, carried, _, keep = block_masks(meta, ndoc, start)
    gain = gain_ref[...]
    running = run_ref[...]
    factor = jnp.exp(running[BLK - 1 :, :]) * keep
    cum_ref[0] = cum[...]
    cum[...] = cum[...] * factor
    for slot in range(2):
        lanes = slice(slot * HK, slot * HK + HK)
        cols = slice(slot * HV, slot * HV + HV)
        query, _, _, outgate = head_parts(x_ref, slot)
        mixed = mixed_ref[:, cols].astype(f32)
        dgated = dgated_ref[:, cols].astype(f32)
        mean = jnp.mean(mixed * mixed, axis=-1, keepdims=True)
        scale = lax.rsqrt(jnp.maximum(mean, 1.0))
        sig = jax.nn.sigmoid(outgate)
        silu = outgate * sig
        dnormed = dgated * silu
        plain = mixed * scale
        doutgate_ref[:, cols] = (dgated * plain * gain * (sig + silu * (1.0 - sig))).astype(bf16)
        dgain_ref[...] += jnp.sum(dnormed * plain, axis=0, keepdims=True)
        weighted = dnormed * gain
        inner = jnp.where(mean > 1.0, jnp.mean(weighted * plain, axis=-1, keepdims=True), 0.0)
        dmixed = (scale * (weighted - plain * inner)).astype(bf16)
        dmixed_ref[:, cols] = dmixed
        far_query = (query * jnp.exp(running[:, lanes]) * carried).astype(bf16)
        old = state[slot]
        dstate_ref[0, slot] = old.astype(bf16)
        new = old * factor[:, lanes] + tn(dmixed, far_query)
        state[slot] = new
        final_ref[slot] = new.astype(bf16)


def back_kernel(
    ndoc, meta, x_ref, run_ref, state_ref, cum_ref, first_ref, dmixed_ref, doutgate_ref,
    dstate_ref, dcum_ref, dlast_ref, wdec_ref, bias_ref, dx_ref, dwdec_ref, dbias_ref,
):
    block = pl.program_id(0)

    @pl.when(block == 0)
    def _():
        dwdec_ref[...] = jnp.zeros_like(dwdec_ref)
        dbias_ref[...] = jnp.zeros_like(dbias_ref)

    start = meta[ndoc] + block * BLK
    allowed, carried, same, keep = block_masks(meta, ndoc, start)
    last_row = lax.broadcasted_iota(jnp.int32, (BLK, HK), 0) == BLK - 1
    drunning = []
    for slot in range(2):
        lanes = slice(slot * HK, slot * HK + HK)
        cols = slice(slot * HV, slot * HV + HV)
        at = slot * HEAD_COLS
        query, key, value, _ = head_parts(x_ref, slot)
        running = run_ref[:, lanes]
        middle = running[MID : MID + 1, :]
        ending = running[BLK - 1 :, :]
        up = jnp.exp(running - middle)
        down = jnp.exp(middle - running)
        far = jnp.exp(running) * carried
        near = jnp.exp(ending - running) * same
        rel_query = (query * up).astype(bf16)
        rel_key = (key * down).astype(bf16)
        far_query = (query * far).astype(bf16)
        moved = (key * near).astype(bf16)
        value = value.astype(bf16)
        scores = jnp.where(allowed, nt(rel_query, rel_key), 0.0).astype(bf16)
        state = state_ref[0, slot].astype(f32) + first_ref[slot].astype(f32) * cum_ref[0][:, lanes]
        dstate = dstate_ref[0, slot].astype(f32) + dlast_ref[slot].astype(f32) * dcum_ref[0][:, lanes]
        state_low = state.astype(bf16)
        dstate_low = dstate.astype(bf16)
        dmixed = dmixed_ref[:, cols]
        dvalue = tn(scores, dmixed) + nt(moved, dstate_low)
        dscores = jnp.where(allowed, nt(dmixed, value), 0.0).astype(bf16)
        drel_query = nn(dscores, rel_key)
        drel_key = tn(dscores, rel_query)
        dfar = nn(dmixed, state_low)
        dmoved = nn(value, dstate_low)
        dquery = drel_query * up + dfar * far
        dkey = drel_key * down + dmoved * near
        moved_grad = dmoved * moved.astype(f32)
        dending = jnp.sum(moved_grad, axis=0, keepdims=True) + jnp.sum(
            state * dstate, axis=0, keepdims=True
        ) * (jnp.exp(ending) * keep)
        drun = (
            drel_query * rel_query.astype(f32)
            - drel_key * rel_key.astype(f32)
            + dfar * far_query.astype(f32)
            - moved_grad
        )
        drunning.append(drun + jnp.where(last_row, dending, 0.0))
        dx_ref[:, at : at + HK] = (dquery * (HK**-0.5)).astype(bf16)
        dx_ref[:, at + HK : at + 2 * HK] = dkey.astype(bf16)
        dx_ref[:, at + 2 * HK : at + 2 * HK + HV] = dvalue.astype(bf16)
        dx_ref[:, at + 2 * HK + HV : at + HEAD_COLS] = doutgate_ref[:, cols]
    drun_both = jnp.concatenate(drunning, axis=1)
    ddecay = split_dot(tri_ones(), drun_both, tn)
    before = decay_before(x_ref, wdec_ref, bias_ref)
    dbefore = ddecay * (1.0 / 16.0) * jax.nn.sigmoid(-before)
    dbias_ref[...] += jnp.sum(dbefore, axis=0, keepdims=True)
    ranked = x_ref[:, 2 * HEAD_COLS :]
    dlow = dbefore.astype(bf16)
    dwdec_ref[...] += tn(ranked.astype(bf16), dlow)
    dx_ref[:, 2 * HEAD_COLS :] = nt(dlow, wdec_ref[...].astype(bf16)).astype(bf16)


def kernel_params():
    return pltpu.CompilerParams(dimension_semantics=("arbitrary",), vmem_limit_bytes=VMEM_LIMIT)


class Mixer:
    def __init__(self, meta, ndoc, tokens):
        self.meta = meta
        self.ndoc = ndoc
        self.tokens = tokens
        self.nblk = tokens // BLK
        self.half = self.nblk // 2

    def rows(self, width, reverse=False):
        nblk, half, core = self.nblk, self.half, self.ndoc + 1

        def place(step, meta):
            time = nblk - 1 - step if reverse else step
            return (lax.rem(time + meta[core] * half, nblk), 0)

        return pl.BlockSpec((BLK, width), place)

    def per_block(self, shape, reverse=False):
        nblk = self.nblk
        zeros = (0,) * len(shape)
        return pl.BlockSpec(
            (1,) + shape, lambda step, meta: ((nblk - 1 - step if reverse else step),) + zeros
        )

    def whole(self, shape):
        zeros = (0,) * len(shape)
        return pl.BlockSpec(shape, lambda step, meta: zeros)

    def call(self, body, in_specs, out_specs, out_shape, scratch, *args):
        return pl.pallas_call(
            body,
            grid_spec=pltpu.PrefetchScalarGridSpec(
                num_scalar_prefetch=1,
                grid=(self.nblk,),
                in_specs=in_specs,
                out_specs=out_specs,
                scratch_shapes=scratch,
            ),
            out_shape=[jax.ShapeDtypeStruct(s, d) for s, d in out_shape],
            compiler_params=kernel_params(),
        )(self.meta, *args)

    def state_scratch(self):
        return [pltpu.VMEM((2, HV, HK), f32), pltpu.VMEM((1, 2 * HK), f32)]

    def states(self, x, wdec, bias):
        ndoc, n = self.ndoc, self.nblk

        def body(*refs):
            states_kernel(ndoc, *refs)

        return self.call(
            body,
            [self.rows(x.shape[1]), self.whole(wdec.shape), self.whole(bias.shape)],
            [
                self.rows(2 * HK),
                self.per_block((2, HV, HK)),
                self.per_block((1, 2 * HK)),
                self.whole((2, HV, HK)),
            ],
            [
                ((self.tokens, 2 * HK), f32),
                ((n, 2, HV, HK), bf16),
                ((n, 1, 2 * HK), f32),
                ((2, HV, HK), bf16),
            ],
            self.state_scratch(),
            x, wdec, bias,
        )

    def mix(self, x, run, states, cum, first, gain):
        ndoc = self.ndoc

        def body(*refs):
            mix_kernel(ndoc, *refs)

        return self.call(
            body,
            [
                self.rows(x.shape[1]),
                self.rows(2 * HK),
                self.per_block((2, HV, HK)),
                self.per_block((1, 2 * HK)),
                self.whole((2, HV, HK)),
                self.whole(gain.shape),
            ],
            [self.rows(2 * HV), self.rows(2 * HV)],
            [((self.tokens, 2 * HV), bf16), ((self.tokens, 2 * HV), bf16)],
            [],
            x, run, states, cum, first, gain,
        )

    def back_states(self, x, run, mixed, dgated, gain):
        ndoc, n = self.ndoc, self.nblk

        def body(*refs):
            back_states_kernel(ndoc, n, *refs)

        return self.call(
            body,
            [
                self.rows(x.shape[1], True),
                self.rows(2 * HK, True),
                self.rows(2 * HV, True),
                self.rows(2 * HV, True),
                self.whole(gain.shape),
            ],
            [
                self.rows(2 * HV, True),
                self.rows(2 * HV, True),
                self.per_block((2, HV, HK), True),
                self.per_block((1, 2 * HK), True),
                self.whole((2, HV, HK)),
                self.whole((1, HV)),
            ],
            [
                ((self.tokens, 2 * HV), bf16),
                ((self.tokens, 2 * HV), bf16),
                ((n, 2, HV, HK), bf16),
                ((n, 1, 2 * HK), f32),
                ((2, HV, HK), bf16),
                ((1, HV), f32),
            ],
            self.state_scratch(),
            x, run, mixed, dgated, gain,
        )

    def back(self, x, run, states, cum, first, dmixed, doutgate, dstates, dcum, dlast, wdec, bias):
        ndoc = self.ndoc
        rank = wdec.shape[0]

        def body(*refs):
            back_kernel(ndoc, *refs)

        return self.call(
            body,
            [
                self.rows(x.shape[1]),
                self.rows(2 * HK),
                self.per_block((2, HV, HK)),
                self.per_block((1, 2 * HK)),
                self.whole((2, HV, HK)),
                self.rows(2 * HV),
                self.rows(2 * HV),
                self.per_block((2, HV, HK)),
                self.per_block((1, 2 * HK)),
                self.whole((2, HV, HK)),
                self.whole(wdec.shape),
                self.whole(bias.shape),
            ],
            [self.rows(x.shape[1]), self.whole((rank, 2 * HK)), self.whole((1, 2 * HK))],
            [
                ((self.tokens, x.shape[1]), bf16),
                ((rank, 2 * HK), f32),
                ((1, 2 * HK), f32),
            ],
            [],
            x, run, states, cum, first, dmixed, doutgate, dstates, dcum, dlast, wdec, bias,
        )


def norm_scale(hidden):
    return lax.rsqrt(jnp.mean(hidden * hidden, axis=-1, keepdims=True) + epsilon)


def norm_low(hidden, gain):
    return (hidden * norm_scale(hidden) * gain).astype(bf16)


def norm_back(hidden, gain, grad_normed):
    scale = norm_scale(hidden)
    weighted = grad_normed * gain
    grad_hidden = scale * weighted - hidden * (scale * scale * scale) * jnp.mean(
        weighted * hidden, axis=-1, keepdims=True
    )
    return grad_hidden, jnp.sum(grad_normed * hidden * scale, axis=0)


def core_swap(value):
    return lax.ppermute(value, "head", [(i, i ^ 1) for i in range(4)])


def chip_swap(value):
    return lax.ppermute(value, "head", [(i, i ^ 2) for i in range(4)])


def pad_cols(value, width):
    return jnp.pad(value, ((0, 0), (0, width - value.shape[1])))


def pad_rows(value, height):
    return jnp.pad(value, ((0, height - value.shape[0]), (0, 0)))


def per_device(
    tokens, doc_starts, grad_out, norm_one, w_query, w_key, w_value, w_outgate, w_rank, w_decay,
    decay_bias, group_gain, w_out, norm_two, w_gate, w_up, w_down,
):
    shard_len, width = tokens.shape[1:]
    ndoc = doc_starts.shape[1]
    ff = w_gate.shape[2]
    ffp = -(-ff // 128) * 128
    member = lax.axis_index("head")
    core = member % 2
    chip = member // 2
    meta = jnp.concatenate(
        [doc_starts[0], jnp.stack([chip * (2 * shard_len), core]).astype(jnp.int32)]
    )
    mixer = Mixer(meta, ndoc, 2 * shard_len)

    small = jnp.concatenate([w_decay.astype(f32), decay_bias[:, None, :]], axis=1)
    small = jnp.concatenate([small, chip_swap(small)], axis=2)
    rank = w_decay.shape[1]

    mix_w, out_w, in_w, down_w = [], [], [], []
    for layer in range(LAYERS):
        own = jnp.concatenate([w_query[layer], w_key[layer], w_value[layer], w_outgate[layer]], axis=1)
        mix_w.append(jnp.concatenate([own, chip_swap(own), w_rank[layer]], axis=1))
        out_w.append(jnp.concatenate([w_out[layer], chip_swap(w_out[layer])], axis=0))
        own = jnp.concatenate([w_gate[layer], w_up[layer]], axis=1)
        far = chip_swap(own)
        in_w.append(
            jnp.concatenate(
                [
                    pad_cols(part, ffp)
                    for part in (own[:, :ff], far[:, :ff], own[:, ff:], far[:, ff:])
                ],
                axis=1,
            )
        )
        far = chip_swap(w_down[layer])
        down_w.append(jnp.concatenate([pad_rows(w_down[layer], ffp), pad_rows(far, ffp)], axis=0))

    def with_partner(local):
        return jnp.concatenate([local, core_swap(local)], axis=0)

    def settle(dot, branch, weight):
        sent = core_swap(dot(branch[shard_len:], weight).astype(bf16))
        return dot(branch[:shard_len], weight) + sent.astype(f32)

    hidden = tokens[0].astype(f32)
    saved = []
    for layer in range(LAYERS):
        hidden_in = hidden
        a = with_partner(norm_low(hidden, norm_one[layer]))
        x = nn(a, mix_w[layer])
        wdec, bias = small[layer, :rank], small[layer, rank:]
        run, states, cum, final = mixer.states(x, wdec, bias)
        first = chip_swap(final)[::-1] * chip.astype(bf16)
        gain = group_gain[layer][None]
        gated, mixed = mixer.mix(x, run, states, cum, first, gain)
        hidden_mid = hidden + settle(nn, gated, out_w[layer])
        m = with_partner(norm_low(hidden_mid, norm_two[layer]))
        both = nn(m, in_w[layer])
        gate, up = both[:, : 2 * ffp], both[:, 2 * ffp :]
        product = (jax.nn.silu(gate) * up).astype(bf16)
        gate, up = gate.astype(bf16), up.astype(bf16)
        hidden = hidden_mid + settle(nn, product, down_w[layer])
        saved.append(
            (hidden_in, hidden_mid, a, m, x, run, states, cum, first, mixed, gated, gate, up, product)
        )
    result = hidden.astype(bf16)[None]

    grad = grad_out[0].astype(f32)
    split_grads = [None] * LAYERS
    shared_grads = [None] * LAYERS

    def gather_grad(own, far):
        total = own.astype(f32) + chip_swap(far.astype(bf16)).astype(f32)
        return lax.psum(total.astype(bf16), "dp")

    for layer in reversed(range(LAYERS)):
        (
            hidden_in, hidden_mid, a, m, x, run, states, cum, first, mixed, gated, gate, up, product,
        ) = saved[layer]
        gain = group_gain[layer][None]
        wdec, bias = small[layer, :rank], small[layer, rank:]
        g_out = with_partner(grad.astype(bf16))
        dproduct = nt(g_out, down_w[layer])
        gate, up = gate.astype(f32), up.astype(f32)
        sig = jax.nn.sigmoid(gate)
        dgate = (dproduct * up * sig * (1.0 + gate * (1.0 - sig))).astype(bf16)
        dup = (dproduct * gate * sig).astype(bf16)
        dboth = jnp.concatenate([dgate, dup], axis=1)
        g_down = tn(product, g_out).astype(bf16)
        down_grad = gather_grad(g_down[:ff], g_down[ffp : ffp + ff])
        g_in = tn(m, dboth).astype(bf16)
        in_grad = gather_grad(
            jnp.concatenate([g_in[:, :ff], g_in[:, 2 * ffp : 2 * ffp + ff]], axis=1),
            jnp.concatenate([g_in[:, ffp : ffp + ff], g_in[:, 3 * ffp : 3 * ffp + ff]], axis=1),
        )
        back_mid, gain_two = norm_back(hidden_mid, norm_two[layer], settle(nt, dboth, in_w[layer]))
        grad = grad + back_mid
        g_mix = with_partner(grad.astype(bf16))
        dgated = nt(g_mix, out_w[layer])
        g_wout = tn(gated, g_mix).astype(bf16)
        out_grad = gather_grad(g_wout[:HV], g_wout[HV:])
        dmixed, doutgate, dstates, dcum, dfinal, dgain = mixer.back_states(x, run, mixed, dgated, gain)
        dlast = chip_swap(dfinal)[::-1] * (1 - chip).astype(bf16)
        dx, dwdec, dbias = mixer.back(
            x, run, states, cum, first, dmixed, doutgate, dstates, dcum, dlast, wdec, bias
        )
        g_wmix = tn(a, dx)
        mix_grad = gather_grad(g_wmix[:, :HEAD_COLS], g_wmix[:, HEAD_COLS : 2 * HEAD_COLS])
        back_in, gain_one = norm_back(hidden_in, norm_one[layer], settle(nt, dx, mix_w[layer]))
        grad = grad + back_in
        split_grads[layer] = (mix_grad, out_grad, in_grad, down_grad)
        shared_grads[layer] = (
            gain_one,
            g_wmix[:, 2 * HEAD_COLS :],
            dgain[0],
            gain_two,
            jnp.concatenate([dwdec, dbias], axis=0),
        )

    def stacked(group, pick=lambda v: v):
        return jnp.stack([pick(split_grads[layer][group]).astype(f32) for layer in range(LAYERS)])

    shared = [jnp.stack([shared_grads[layer][i] for layer in range(LAYERS)]) for i in range(5)]
    far_small = chip_swap(shared[4][:, :, HK:])
    own_small = lax.psum(shared[4][:, :, :HK] + far_small, "dp")
    shared = lax.psum(tuple(shared[:4]), ("dp", "head"))
    return (
        result,
        grad[None],
        shared[0],
        stacked(0, lambda v: v[:, :HK]),
        stacked(0, lambda v: v[:, HK : 2 * HK]),
        stacked(0, lambda v: v[:, 2 * HK : 2 * HK + HV]),
        stacked(0, lambda v: v[:, 2 * HK + HV :]),
        shared[1],
        own_small[:, :rank],
        own_small[:, rank],
        shared[2],
        stacked(1),
        shared[3],
        stacked(2, lambda v: v[:, :ff]),
        stacked(2, lambda v: v[:, ff:]),
        stacked(3),
    )


def solution(mesh):
    cols = P(None, None, "head")
    rows = P(None, "head", None)
    place = P("dp", "head", None)
    return jax.shard_map(
        per_device,
        mesh=mesh,
        in_specs=(
            place, P("dp", None), place, P(), cols, cols, cols, cols, P(), cols,
            P(None, "head"), P(), rows, P(), cols, cols, rows,
        ),
        out_specs=(
            place, place, P(), cols, cols, cols, cols, P(), cols, P(None, "head"), P(), rows,
            P(), cols, cols, rows,
        ),
        check_vma=False,
    )
```

```python
import jax
import jax.numpy as jnp
from jax import lax
from jax.experimental import pallas as pl
from jax.experimental.pallas import tpu as pltpu
from jax.sharding import PartitionSpec as P

LAYERS = 2
HK = 128
HV = 256
HEAD_COLS = 2 * HK + 2 * HV
BLK = 128
MID = BLK // 2 - 1
epsilon = 1e-06
highest = lax.Precision.HIGHEST
VMEM_LIMIT = 48 * 1024 * 1024

f32 = jnp.float32
bf16 = jnp.bfloat16


def nn(left, right):
    return lax.dot_general(left, right, (((1,), (0,)), ((), ())), preferred_element_type=f32)


def nt(left, right):
    return lax.dot_general(left, right, (((1,), (1,)), ((), ())), preferred_element_type=f32)


def tn(left, right):
    return lax.dot_general(left, right, (((0,), (0,)), ((), ())), preferred_element_type=f32)


def doc_count(meta, ndoc, place):
    total = (meta[0] <= place).astype(jnp.int32)
    for which in range(1, ndoc):
        total = total + (meta[which] <= place).astype(jnp.int32)
    return total


def block_masks(meta, ndoc, start):
    rows = lax.broadcasted_iota(jnp.int32, (BLK, BLK), 0) + start
    cols = lax.broadcasted_iota(jnp.int32, (BLK, BLK), 1) + start
    row_ids = doc_count(meta, ndoc, rows)
    col_ids = doc_count(meta, ndoc, cols)
    id_prev = doc_count(meta, ndoc, start - 1)
    id_last = doc_count(meta, ndoc, start + BLK - 1)
    allowed = (rows >= cols) & (row_ids == col_ids)
    carried = jnp.where(row_ids == id_prev, 1.0, 0.0)
    same = jnp.where(row_ids == id_last, 1.0, 0.0)
    keep = jnp.where(id_last == id_prev, 1.0, 0.0)
    return allowed, carried, same, keep


def split_dot(ones_mat, value, dot):
    high = value.astype(bf16)
    low = (value - high.astype(f32)).astype(bf16)
    return dot(ones_mat, high) + dot(ones_mat, low)


def tri_ones():
    rows = lax.broadcasted_iota(jnp.int32, (BLK, BLK), 0)
    cols = lax.broadcasted_iota(jnp.int32, (BLK, BLK), 1)
    return jnp.where(rows >= cols, 1.0, 0.0).astype(bf16)


def head_parts(x_ref, slot):
    at = slot * HEAD_COLS
    query = x_ref[:, at : at + HK] * (HK**-0.5)
    key = x_ref[:, at + HK : at + 2 * HK]
    value = x_ref[:, at + 2 * HK : at + 2 * HK + HV]
    outgate = x_ref[:, at + 2 * HK + HV : at + HEAD_COLS]
    return query, key, value, outgate


def decay_before(x_ref, wdec_ref, bias_ref):
    ranked = x_ref[:, 2 * HEAD_COLS :]
    return jnp.dot(ranked, wdec_ref[...], precision=highest, preferred_element_type=f32) + bias_ref[...]


def states_kernel(ndoc, meta, x_ref, wdec_ref, bias_ref, run_ref, state_ref, cum_ref, final_ref, state, cum):
    block = pl.program_id(0)

    @pl.when(block == 0)
    def _():
        state[...] = jnp.zeros_like(state)
        cum[...] = jnp.ones_like(cum)

    start = meta[ndoc] + block * BLK
    _, _, same, keep = block_masks(meta, ndoc, start)
    before = decay_before(x_ref, wdec_ref, bias_ref)
    decays = (jnp.minimum(before, 0.0) - jnp.log1p(jnp.exp(-jnp.abs(before)))) * (1.0 / 16.0)
    running = split_dot(tri_ones(), decays, nn)
    run_ref[...] = running
    ending = running[BLK - 1 :, :]
    factor = jnp.exp(ending) * keep
    cum_ref[0] = cum[...]
    cum[...] = cum[...] * factor
    for slot in range(2):
        lanes = slice(slot * HK, slot * HK + HK)
        _, key, value, _ = head_parts(x_ref, slot)
        moved = (key * jnp.exp(ending[:, lanes] - running[:, lanes]) * same).astype(bf16)
        old = state[slot]
        state_ref[0, slot] = old.astype(bf16)
        new = old * factor[:, lanes] + tn(value.astype(bf16), moved)
        state[slot] = new
        final_ref[slot] = new.astype(bf16)


def mix_kernel(ndoc, meta, x_ref, run_ref, state_ref, cum_ref, first_ref, gain_ref, gated_ref, mixed_ref):
    block = pl.program_id(0)
    start = meta[ndoc] + block * BLK
    allowed, carried, _, _ = block_masks(meta, ndoc, start)
    gain = gain_ref[...]
    for slot in range(2):
        lanes = slice(slot * HK, slot * HK + HK)
        cols = slice(slot * HV, slot * HV + HV)
        query, key, value, outgate = head_parts(x_ref, slot)
        running = run_ref[:, lanes]
        middle = running[MID : MID + 1, :]
        rel_query = (query * jnp.exp(running - middle)).astype(bf16)
        rel_key = (key * jnp.exp(middle - running)).astype(bf16)
        scores = jnp.where(allowed, nt(rel_query, rel_key), 0.0).astype(bf16)
        far_query = (query * jnp.exp(running) * carried).astype(bf16)
        state = (state_ref[0, slot].astype(f32) + first_ref[slot].astype(f32) * cum_ref[0][:, lanes]).astype(bf16)
        mixed = nn(scores, value.astype(bf16)) + nt(far_query, state)
        scale = lax.rsqrt(jnp.maximum(jnp.mean(mixed * mixed, axis=-1, keepdims=True), 1.0))
        gated_ref[:, cols] = (mixed * scale * gain * outgate * jax.nn.sigmoid(outgate)).astype(bf16)
        mixed_ref[:, cols] = mixed.astype(bf16)


def back_states_kernel(
    ndoc, nblk, meta, x_ref, run_ref, mixed_ref, grad_ref, own_out_ref, far_out_ref, gain_ref,
    dmixed_ref, doutgate_ref, dstate_ref, cum_ref, final_ref, dgain_ref, state, cum,
):
    step = pl.program_id(0)

    @pl.when(step == 0)
    def _():
        state[...] = jnp.zeros_like(state)
        cum[...] = jnp.ones_like(cum)
        dgain_ref[...] = jnp.zeros_like(dgain_ref)

    start = meta[ndoc] + (nblk - 1 - step) * BLK
    _, carried, _, keep = block_masks(meta, ndoc, start)
    gain = gain_ref[...]
    running = run_ref[...]
    factor = jnp.exp(running[BLK - 1 :, :]) * keep
    cum_ref[0] = cum[...]
    cum[...] = cum[...] * factor
    for slot in range(2):
        lanes = slice(slot * HK, slot * HK + HK)
        cols = slice(slot * HV, slot * HV + HV)
        query, _, _, outgate = head_parts(x_ref, slot)
        mixed = mixed_ref[:, cols].astype(f32)
        dgated = nt(grad_ref[...], (own_out_ref, far_out_ref)[slot][...])
        mean = jnp.mean(mixed * mixed, axis=-1, keepdims=True)
        scale = lax.rsqrt(jnp.maximum(mean, 1.0))
        sig = jax.nn.sigmoid(outgate)
        silu = outgate * sig
        dnormed = dgated * silu
        plain = mixed * scale
        doutgate_ref[:, cols] = (dgated * plain * gain * (sig + silu * (1.0 - sig))).astype(bf16)
        dgain_ref[...] += jnp.sum(dnormed * plain, axis=0, keepdims=True)
        weighted = dnormed * gain
        inner = jnp.where(mean > 1.0, jnp.mean(weighted * plain, axis=-1, keepdims=True), 0.0)
        dmixed = (scale * (weighted - plain * inner)).astype(bf16)
        dmixed_ref[:, cols] = dmixed
        far_query = (query * jnp.exp(running[:, lanes]) * carried).astype(bf16)
        old = state[slot]
        dstate_ref[0, slot] = old.astype(bf16)
        new = old * factor[:, lanes] + tn(dmixed, far_query)
        state[slot] = new
        final_ref[slot] = new.astype(bf16)


def back_kernel(
    ndoc, meta, x_ref, run_ref, state_ref, cum_ref, first_ref, dmixed_ref, doutgate_ref,
    dstate_ref, dcum_ref, dlast_ref, wdec_ref, bias_ref, dx_ref, dwdec_ref, dbias_ref,
):
    block = pl.program_id(0)

    @pl.when(block == 0)
    def _():
        dwdec_ref[...] = jnp.zeros_like(dwdec_ref)
        dbias_ref[...] = jnp.zeros_like(dbias_ref)

    start = meta[ndoc] + block * BLK
    allowed, carried, same, keep = block_masks(meta, ndoc, start)
    last_row = lax.broadcasted_iota(jnp.int32, (BLK, HK), 0) == BLK - 1
    drunning = []
    for slot in range(2):
        lanes = slice(slot * HK, slot * HK + HK)
        cols = slice(slot * HV, slot * HV + HV)
        at = slot * HEAD_COLS
        query, key, value, _ = head_parts(x_ref, slot)
        running = run_ref[:, lanes]
        middle = running[MID : MID + 1, :]
        ending = running[BLK - 1 :, :]
        up = jnp.exp(running - middle)
        down = jnp.exp(middle - running)
        far = jnp.exp(running) * carried
        near = jnp.exp(ending - running) * same
        rel_query = (query * up).astype(bf16)
        rel_key = (key * down).astype(bf16)
        far_query = (query * far).astype(bf16)
        moved = (key * near).astype(bf16)
        value = value.astype(bf16)
        scores = jnp.where(allowed, nt(rel_query, rel_key), 0.0).astype(bf16)
        state = state_ref[0, slot].astype(f32) + first_ref[slot].astype(f32) * cum_ref[0][:, lanes]
        dstate = dstate_ref[0, slot].astype(f32) + dlast_ref[slot].astype(f32) * dcum_ref[0][:, lanes]
        state_low = state.astype(bf16)
        dstate_low = dstate.astype(bf16)
        dmixed = dmixed_ref[:, cols]
        dvalue = tn(scores, dmixed) + nt(moved, dstate_low)
        dscores = jnp.where(allowed, nt(dmixed, value), 0.0).astype(bf16)
        drel_query = nn(dscores, rel_key)
        drel_key = tn(dscores, rel_query)
        dfar = nn(dmixed, state_low)
        dmoved = nn(value, dstate_low)
        dquery = drel_query * up + dfar * far
        dkey = drel_key * down + dmoved * near
        moved_grad = dmoved * moved.astype(f32)
        dending = jnp.sum(moved_grad, axis=0, keepdims=True) + jnp.sum(
            state * dstate, axis=0, keepdims=True
        ) * (jnp.exp(ending) * keep)
        drun = (
            drel_query * rel_query.astype(f32)
            - drel_key * rel_key.astype(f32)
            + dfar * far_query.astype(f32)
            - moved_grad
        )
        drunning.append(drun + jnp.where(last_row, dending, 0.0))
        dx_ref[:, at : at + HK] = (dquery * (HK**-0.5)).astype(bf16)
        dx_ref[:, at + HK : at + 2 * HK] = dkey.astype(bf16)
        dx_ref[:, at + 2 * HK : at + 2 * HK + HV] = dvalue.astype(bf16)
        dx_ref[:, at + 2 * HK + HV : at + HEAD_COLS] = doutgate_ref[:, cols]
    drun_both = jnp.concatenate(drunning, axis=1)
    ddecay = split_dot(tri_ones(), drun_both, tn)
    before = decay_before(x_ref, wdec_ref, bias_ref)
    dbefore = ddecay * (1.0 / 16.0) * jax.nn.sigmoid(-before)
    dbias_ref[...] += jnp.sum(dbefore, axis=0, keepdims=True)
    ranked = x_ref[:, 2 * HEAD_COLS :]
    dlow = dbefore.astype(bf16)
    dwdec_ref[...] += tn(ranked.astype(bf16), dlow)
    dx_ref[:, 2 * HEAD_COLS :] = nt(dlow, wdec_ref[...].astype(bf16)).astype(bf16)


def kernel_params():
    return pltpu.CompilerParams(dimension_semantics=("arbitrary",), vmem_limit_bytes=VMEM_LIMIT)


class Mixer:
    def __init__(self, meta, ndoc, tokens):
        self.meta = meta
        self.ndoc = ndoc
        self.tokens = tokens
        self.nblk = tokens // BLK
        self.half = self.nblk // 2

    def rows(self, width, reverse=False):
        nblk, half, core = self.nblk, self.half, self.ndoc + 1

        def place(step, meta):
            time = nblk - 1 - step if reverse else step
            return (lax.rem(time + meta[core] * half, nblk), 0)

        return pl.BlockSpec((BLK, width), place)

    def per_block(self, shape, reverse=False):
        nblk = self.nblk
        zeros = (0,) * len(shape)
        return pl.BlockSpec(
            (1,) + shape, lambda step, meta: ((nblk - 1 - step if reverse else step),) + zeros
        )

    def whole(self, shape):
        zeros = (0,) * len(shape)
        return pl.BlockSpec(shape, lambda step, meta: zeros)

    def call(self, body, in_specs, out_specs, out_shape, scratch, *args):
        return pl.pallas_call(
            body,
            grid_spec=pltpu.PrefetchScalarGridSpec(
                num_scalar_prefetch=1,
                grid=(self.nblk,),
                in_specs=in_specs,
                out_specs=out_specs,
                scratch_shapes=scratch,
            ),
            out_shape=[jax.ShapeDtypeStruct(s, d) for s, d in out_shape],
            compiler_params=kernel_params(),
        )(self.meta, *args)

    def state_scratch(self):
        return [pltpu.VMEM((2, HV, HK), f32), pltpu.VMEM((1, 2 * HK), f32)]

    def states(self, x, wdec, bias):
        ndoc, n = self.ndoc, self.nblk

        def body(*refs):
            states_kernel(ndoc, *refs)

        return self.call(
            body,
            [self.rows(x.shape[1]), self.whole(wdec.shape), self.whole(bias.shape)],
            [
                self.rows(2 * HK),
                self.per_block((2, HV, HK)),
                self.per_block((1, 2 * HK)),
                self.whole((2, HV, HK)),
            ],
            [
                ((self.tokens, 2 * HK), f32),
                ((n, 2, HV, HK), bf16),
                ((n, 1, 2 * HK), f32),
                ((2, HV, HK), bf16),
            ],
            self.state_scratch(),
            x, wdec, bias,
        )

    def mix(self, x, run, states, cum, first, gain):
        ndoc = self.ndoc

        def body(*refs):
            mix_kernel(ndoc, *refs)

        return self.call(
            body,
            [
                self.rows(x.shape[1]),
                self.rows(2 * HK),
                self.per_block((2, HV, HK)),
                self.per_block((1, 2 * HK)),
                self.whole((2, HV, HK)),
                self.whole(gain.shape),
            ],
            [self.rows(2 * HV), self.rows(2 * HV)],
            [((self.tokens, 2 * HV), bf16), ((self.tokens, 2 * HV), bf16)],
            [],
            x, run, states, cum, first, gain,
        )

    def back_states(self, x, run, mixed, grad, own_out, far_out, gain):
        ndoc, n = self.ndoc, self.nblk

        def body(*refs):
            back_states_kernel(ndoc, n, *refs)

        return self.call(
            body,
            [
                self.rows(x.shape[1], True),
                self.rows(2 * HK, True),
                self.rows(2 * HV, True),
                self.rows(grad.shape[1], True),
                self.whole(own_out.shape),
                self.whole(far_out.shape),
                self.whole(gain.shape),
            ],
            [
                self.rows(2 * HV, True),
                self.rows(2 * HV, True),
                self.per_block((2, HV, HK), True),
                self.per_block((1, 2 * HK), True),
                self.whole((2, HV, HK)),
                self.whole((1, HV)),
            ],
            [
                ((self.tokens, 2 * HV), bf16),
                ((self.tokens, 2 * HV), bf16),
                ((n, 2, HV, HK), bf16),
                ((n, 1, 2 * HK), f32),
                ((2, HV, HK), bf16),
                ((1, HV), f32),
            ],
            self.state_scratch(),
            x, run, mixed, grad, own_out, far_out, gain,
        )

    def back(self, x, run, states, cum, first, dmixed, doutgate, dstates, dcum, dlast, wdec, bias):
        ndoc = self.ndoc
        rank = wdec.shape[0]

        def body(*refs):
            back_kernel(ndoc, *refs)

        return self.call(
            body,
            [
                self.rows(x.shape[1]),
                self.rows(2 * HK),
                self.per_block((2, HV, HK)),
                self.per_block((1, 2 * HK)),
                self.whole((2, HV, HK)),
                self.rows(2 * HV),
                self.rows(2 * HV),
                self.per_block((2, HV, HK)),
                self.per_block((1, 2 * HK)),
                self.whole((2, HV, HK)),
                self.whole(wdec.shape),
                self.whole(bias.shape),
            ],
            [self.rows(x.shape[1]), self.whole((rank, 2 * HK)), self.whole((1, 2 * HK))],
            [
                ((self.tokens, x.shape[1]), bf16),
                ((rank, 2 * HK), f32),
                ((1, 2 * HK), f32),
            ],
            [],
            x, run, states, cum, first, dmixed, doutgate, dstates, dcum, dlast, wdec, bias,
        )


ROWS_BLK = 256


def layer_spec(array, layer):
    if array.ndim == 3:
        return pl.BlockSpec((None,) + array.shape[1:], lambda i: (layer, 0, 0))
    return pl.BlockSpec(array.shape, lambda i: (0, 0))


def row_spec(array, first=0, last=None):
    def place(i):
        at = i + first
        return (at if last is None else jnp.minimum(at, last), 0)

    return pl.BlockSpec((ROWS_BLK, array.shape[1]), place)


def grid_params():
    return pltpu.CompilerParams(dimension_semantics=("arbitrary",), vmem_limit_bytes=VMEM_LIMIT)


def sum_of_dots(terms, layer, first_row, rows, out_type):
    lefts = []
    for left, _, _, _ in terms:
        if not any(left is seen for seen in lefts):
            lefts.append(left)
    which = [next(i for i, seen in enumerate(lefts) if seen is left) for left, _, _, _ in terms]
    rights = [right for _, _, right, _ in terms]
    width = rights[0].shape[-2] if terms[0][3] else rights[0].shape[-1]

    def body(*refs):
        left_refs, right_refs, out = refs[: len(lefts)], refs[len(lefts) : -1], refs[-1]
        total = None
        for (_, at, _, turned), index, right in zip(terms, which, right_refs):
            depth = right.shape[1] if turned else right.shape[0]
            part = (nt if turned else nn)(left_refs[index][:, at : at + depth], right[...])
            total = part if total is None else total + part
        out[...] = total.astype(out_type)

    return pl.pallas_call(
        body,
        grid=(rows // ROWS_BLK,),
        in_specs=[row_spec(v, first_row // ROWS_BLK) for v in lefts] + [layer_spec(v, layer) for v in rights],
        out_specs=pl.BlockSpec((ROWS_BLK, width), lambda i: (i, 0)),
        out_shape=jax.ShapeDtypeStruct((rows, width), out_type),
        compiler_params=grid_params(),
    )(*lefts, *rights)


def project(a, parts, layer):
    widths = [v.shape[-1] for v in parts]

    def body(left, *refs):
        out = refs[-1]
        at = 0
        for right, width in zip(refs[:-1], widths):
            out[:, at : at + width] = nn(left[...], right[...])
            at += width

    return pl.pallas_call(
        body,
        grid=(a.shape[0] // ROWS_BLK,),
        in_specs=[row_spec(a)] + [layer_spec(v, layer) for v in parts],
        out_specs=pl.BlockSpec((ROWS_BLK, sum(widths)), lambda i: (i, 0)),
        out_shape=jax.ShapeDtypeStruct((a.shape[0], sum(widths)), f32),
        compiler_params=grid_params(),
    )(a, *parts)


def ff_forward(m, w_gate, w_up, far, layer, ffp):
    ff = w_gate.shape[-1]

    def body(m_ref, gate_w, up_w, far_w, gate_ref, up_ref, product_ref):
        m = m_ref[...]
        both = nn(m, far_w[...])
        values = ((nn(m, gate_w[...]), nn(m, up_w[...])), (both[:, :ff], both[:, ff:]))
        for slot, (gate, up) in enumerate(values):
            at = slot * ffp
            gate_ref[:, at : at + ff] = gate.astype(bf16)
            up_ref[:, at : at + ff] = up.astype(bf16)
            product_ref[:, at : at + ff] = (gate * jax.nn.sigmoid(gate) * up).astype(bf16)

    shape = (m.shape[0], 2 * ffp)
    return pl.pallas_call(
        body,
        grid=(m.shape[0] // ROWS_BLK,),
        in_specs=[row_spec(m), layer_spec(w_gate, layer), layer_spec(w_up, layer), layer_spec(far, layer)],
        out_specs=[pl.BlockSpec((ROWS_BLK, 2 * ffp), lambda i: (i, 0))] * 3,
        out_shape=[jax.ShapeDtypeStruct(shape, bf16)] * 3,
        compiler_params=grid_params(),
    )(m, w_gate, w_up, far)


def ff_backward(m_all, g_all, gate, up, product, w_gate, w_up, w_down, down_far, layer, ffp):
    ff = w_gate.shape[-1]
    near = gate.shape[0] // ROWS_BLK

    def pair(gate, up, dproduct):
        sig = jax.nn.sigmoid(gate)
        silu = gate * sig
        dgate = dproduct * up * (sig + silu * (1.0 - sig))
        return jnp.concatenate([dgate.astype(bf16), (dproduct * silu).astype(bf16)], axis=1), silu

    def body(m_ref, g_ref, gate_ref, up_ref, product_ref, gate_w, up_w, down_w, far_w, own_ref, far_ref, all_ref):
        step = pl.program_id(0)
        g = g_ref[...]
        dproduct = nt(g, down_w[...])

        @pl.when(step < near)
        def _():
            own_ref[...] = pair(gate_ref[:, :ff].astype(f32), up_ref[:, :ff].astype(f32), dproduct)[0]
            all_ref[...] = product_ref[:, :ff]
            cols = slice(ffp, ffp + ff)
            far_ref[...] = pair(
                gate_ref[:, cols].astype(f32), up_ref[:, cols].astype(f32), nt(g, far_w[...])
            )[0]

        @pl.when(step >= near)
        def _():
            gate, up = nn(m_ref[...], gate_w[...]), nn(m_ref[...], up_w[...])
            value, silu = pair(gate, up, dproduct)
            own_ref[...] = value
            all_ref[...] = (silu * up).astype(bf16)

    rows = m_all.shape[0]
    far_rows = gate.shape[0]
    return pl.pallas_call(
        body,
        grid=(rows // ROWS_BLK,),
        in_specs=[
            pl.BlockSpec((ROWS_BLK, m_all.shape[1]), lambda i: (jnp.maximum(i, near), 0)),
            row_spec(g_all),
            row_spec(gate, 0, near - 1),
            row_spec(up, 0, near - 1),
            row_spec(product, 0, near - 1),
            layer_spec(w_gate, layer),
            layer_spec(w_up, layer),
            layer_spec(w_down, layer),
            layer_spec(down_far, layer),
        ],
        out_specs=[
            pl.BlockSpec((ROWS_BLK, 2 * ff), lambda i: (i, 0)),
            pl.BlockSpec((ROWS_BLK, 2 * ff), lambda i: (jnp.minimum(i, near - 1), 0)),
            pl.BlockSpec((ROWS_BLK, ff), lambda i: (i, 0)),
        ],
        out_shape=[
            jax.ShapeDtypeStruct((rows, 2 * ff), bf16),
            jax.ShapeDtypeStruct((far_rows, 2 * ff), bf16),
            jax.ShapeDtypeStruct((rows, ff), bf16),
        ],
        compiler_params=grid_params(),
    )(m_all, g_all, gate, up, product, w_gate, w_up, w_down, down_far)


def ring_place(index, n):
    return jnp.where(index % 2 == 0, index // 2, n - 1 - index // 2)


def ring_index(place, n):
    return jnp.where(place < n // 2, 2 * place, 2 * (n - 1 - place) + 1)


def ring_sum(n, data, out, slots, send, recv, out_send, out_recv):
    me = ring_place(lax.axis_index("dp"), n)
    peers = [ring_index(lax.rem(me + 1, n), n), ring_index(lax.rem(me + n - 1, n), n)]
    rows = data.shape[0] // (2 * n)
    signs = (1, -1)

    def chunk(ref, way, back):
        which = lax.rem(me + 2 * n - signs[way] * back, n)
        return ref.at[pl.ds(pl.multiple_of((2 * which + way) * rows, 16), rows)]

    def partial(way, source, step):
        return pltpu.make_async_remote_copy(
            src_ref=source, dst_ref=slots.at[way, step],
            send_sem=send.at[way, step], recv_sem=recv.at[way, step],
            device_id={"dp": peers[way]}, device_id_type=pl.DeviceIdType.MESH,
        )

    def final(way, step):
        part = chunk(out, way, step - 1)
        return pltpu.make_async_remote_copy(
            src_ref=part, dst_ref=part,
            send_sem=out_send.at[way, step], recv_sem=out_recv.at[way, step],
            device_id={"dp": peers[way]}, device_id_type=pl.DeviceIdType.MESH,
        )

    def arrived(way, step):
        part = chunk(out, way, step)
        return pltpu.make_async_remote_copy(
            src_ref=part, dst_ref=part,
            send_sem=out_send.at[way, step], recv_sem=out_recv.at[way, step],
            device_id={"dp": peers[way]}, device_id_type=pl.DeviceIdType.MESH,
        )

    for way in range(2):
        partial(way, chunk(data, way, 0), 0).start()

    def reduce_step(step, carry):
        for way in range(2):
            slot = slots.at[way, step]
            partial(way, slot, step).wait_recv()
            slot[...] = (slot[...].astype(f32) + chunk(data, way, step + 1)[...].astype(f32)).astype(bf16)

            @pl.when(step < n - 2)
            def _():
                partial(way, slot, step + 1).start()

        return carry

    lax.fori_loop(0, n - 1, reduce_step, 0)
    for way in range(2):
        chunk(out, way, -1)[...] = slots[way, n - 2]
        final(way, 0).start()

    def gather_step(step, carry):
        for way in range(2):
            arrived(way, step).wait_recv()

            @pl.when(step < n - 2)
            def _():
                final(way, step + 1).start()

        return carry

    lax.fori_loop(0, n - 1, gather_step, 0)

    def sent_step(step, carry):
        for way in range(2):
            partial(way, slots.at[way, step], step).wait_send()
            final(way, step).wait_send()
        return carry

    lax.fori_loop(0, n - 1, sent_step, 0)


def mix_sum_kernel(n, done, own, far, out_done, out_own, came, total, slots, send, recv, out_send, out_recv, chip_send, chip_recv):
    me = ring_place(lax.axis_index("dp"), n)
    barrier = pltpu.get_barrier_semaphore()
    for place in (lax.rem(me + 1, n), lax.rem(me + n - 1, n)):
        pl.semaphore_signal(
            barrier, inc=1, device_id={"dp": ring_index(place, n)}, device_id_type=pl.DeviceIdType.MESH
        )
    other = lax.axis_index("head") ^ 2
    pl.semaphore_signal(barrier, inc=1, device_id={"head": other}, device_id_type=pl.DeviceIdType.MESH)
    pl.semaphore_wait(barrier, 3)
    swap = pltpu.make_async_remote_copy(
        src_ref=far, dst_ref=came, send_sem=chip_send, recv_sem=chip_recv,
        device_id={"head": other}, device_id_type=pl.DeviceIdType.MESH,
    )
    swap.start()
    ring_sum(n, done, out_done, slots.at[0], send.at[0], recv.at[0], out_send.at[0], out_recv.at[0])
    swap.wait()
    total[...] = (own[...].astype(f32) + came[...].astype(f32)).astype(bf16)
    ring_sum(n, total, out_own, slots.at[1], send.at[1], recv.at[1], out_send.at[1], out_recv.at[1])


def mix_sum(done, own, far, n):
    if n == 1:
        return done, (own.astype(f32) + chip_swap(far).astype(f32)).astype(bf16)
    rows, cols = own.shape

    def body(*refs):
        mix_sum_kernel(n, *refs)

    vmem = pl.BlockSpec(memory_space=pltpu.VMEM)
    return pl.pallas_call(
        body,
        in_specs=[vmem] * 3,
        out_specs=[vmem] * 2,
        out_shape=[jax.ShapeDtypeStruct((rows, cols), bf16)] * 2,
        scratch_shapes=[
            pltpu.VMEM((rows, cols), bf16),
            pltpu.VMEM((rows, cols), bf16),
            pltpu.VMEM((2, 2, n - 1, rows // (2 * n), cols), bf16),
        ]
        + [pltpu.SemaphoreType.DMA((2, 2, n - 1))] * 4
        + [pltpu.SemaphoreType.DMA] * 2,
        compiler_params=pltpu.CompilerParams(
            collective_id=0, has_side_effects=True, vmem_limit_bytes=VMEM_LIMIT
        ),
    )(done, own, far)


def norm_scale(hidden):
    return lax.rsqrt(jnp.mean(hidden * hidden, axis=-1, keepdims=True) + epsilon)


def norm_low(hidden, gain):
    return (hidden * norm_scale(hidden) * gain).astype(bf16)


def norm_back(hidden, gain, grad_normed):
    scale = norm_scale(hidden)
    weighted = grad_normed * gain
    grad_hidden = scale * weighted - hidden * (scale * scale * scale) * jnp.mean(
        weighted * hidden, axis=-1, keepdims=True
    )
    return grad_hidden, jnp.sum(grad_normed * hidden * scale, axis=0)


def core_swap(value):
    return lax.ppermute(value, "head", [(i, i ^ 1) for i in range(4)])


def chip_swap(value):
    return lax.ppermute(value, "head", [(i, i ^ 2) for i in range(4)])


def dp_swap(value, bit):
    return lax.ppermute(value, "dp", [(i, i ^ (1 << bit)) for i in range(lax.axis_size("dp"))])


def dp_bits():
    return lax.axis_size("dp").bit_length() - 1


def small_sum(value):
    value = value + core_swap(value)
    value = value + chip_swap(value)
    for bit in range(dp_bits()):
        value = value + dp_swap(value, bit)
    return value


def dp_slice(own):
    rows = own.shape[0] // lax.axis_size("dp")
    return lax.dynamic_slice_in_dim(own, lax.axis_index("dp") * rows, rows, 0)


def dp_gather(part):
    return lax.all_gather(part, "dp", axis=0, tiled=True)


def after(value, *others):
    return lax.optimization_barrier((value,) + others)[0]


def per_device(
    tokens, doc_starts, grad_out, norm_one, w_query, w_key, w_value, w_outgate, w_rank, w_decay,
    decay_bias, group_gain, w_out, norm_two, w_gate, w_up, w_down,
):
    shard_len, width = tokens.shape[1:]
    ndoc = doc_starts.shape[1]
    ff = w_gate.shape[2]
    ffp = -(-ff // 128) * 128
    rank = w_decay.shape[1]
    member = lax.axis_index("head")
    core = member % 2
    chip = member // 2
    meta = jnp.concatenate(
        [doc_starts[0], jnp.stack([chip * (2 * shard_len), core]).astype(jnp.int32)]
    )
    mixer = Mixer(meta, ndoc, 2 * shard_len)

    def mix_pack(layer):
        return jnp.concatenate(
            [w_query[layer], w_key[layer], w_value[layer], w_outgate[layer]], axis=1
        )

    def ff_parts(layer, wait):
        part = jnp.concatenate([dp_slice(w_gate[layer]), dp_slice(w_up[layer])], axis=1)
        return chip_swap(after(part, wait)), chip_swap(after(dp_slice(w_down[layer]), wait))

    def with_partner(local):
        return jnp.concatenate([local, core_swap(local)], axis=0)

    def settle(terms, layer):
        sent = core_swap(sum_of_dots(terms, layer, shard_len, shard_len, bf16))
        return sum_of_dots(terms, layer, 0, shard_len, f32) + sent.astype(f32)

    small = jnp.concatenate([w_decay.astype(f32), decay_bias[:, None, :]], axis=1)
    small = jnp.concatenate([small, chip_swap(small)], axis=2)
    in_part, down_part = ff_parts(0, meta)
    in_far = dp_gather(in_part)
    down_far = dp_gather(after(down_part, in_far))
    mix_own = mix_pack(0)
    mix_far = chip_swap(after(mix_own, in_part, down_part))
    out_far = chip_swap(after(w_out[0], in_part, down_part))

    grad = grad_out[0].astype(f32)
    hidden = tokens[0].astype(f32)
    saved = []
    for layer in range(LAYERS):
        hidden_in = hidden
        a = with_partner(norm_low(hidden, norm_one[layer]))
        x = project(a, (mix_own, mix_far, w_rank), layer)
        wdec, bias = small[layer, :rank], small[layer, rank:]
        run, states, cum, final = mixer.states(x, wdec, bias)
        got = chip_swap(final)
        first = got[::-1] * chip.astype(bf16)
        gain = group_gain[layer][None]
        gated, mixed = mixer.mix(x, run, states, cum, first, gain)
        hidden_mid = hidden + settle([(gated, 0, w_out, False), (gated, HV, out_far, False)], layer)
        if layer + 1 < LAYERS:
            next_own = mix_pack(layer + 1)
            next_mix = chip_swap(after(next_own, gated))
            next_out = chip_swap(after(w_out[layer + 1], gated))
            in_part, down_part = ff_parts(layer + 1, down_far)
            next_in = dp_gather(in_part)
            next_down = dp_gather(after(down_part, next_in))
        m_own = norm_low(hidden_mid, norm_two[layer])
        m = with_partner(m_own)
        gate, up, product = ff_forward(m, w_gate, w_up, in_far, layer, ffp)
        hidden = hidden_mid + settle([(product, 0, w_down, False), (product, ffp, down_far, False)], layer)
        m_y = chip_swap(m_own)
        m_all = jnp.concatenate([m, m_y, core_swap(m_y)], axis=0)
        saved.append(
            (hidden_in, hidden_mid, a, m_all, x, run, states, cum, first, mixed, gated, gate, up, product,
             mix_own, mix_far, out_far, in_far, down_far)
        )
        if layer + 1 < LAYERS:
            mix_own, mix_far, out_far, in_far, down_far = next_own, next_mix, next_out, next_in, next_down
    result = hidden.astype(bf16)[None]

    ff_grads, misc_grads = [None] * LAYERS, [None] * LAYERS
    for layer in reversed(range(LAYERS)):
        (
            hidden_in, hidden_mid, a, m_all, x, run, states, cum, first, mixed, gated, gate, up, product,
            mix_own, mix_far, out_far, in_far, down_far,
        ) = saved[layer]
        gain = group_gain[layer][None]
        wdec, bias = small[layer, :rank], small[layer, rank:]
        g_own = grad.astype(bf16)
        g_y = chip_swap(g_own)
        if layer + 1 < LAYERS:
            far_came = chip_swap(after(far, g_y))
        g_all = jnp.concatenate([g_own, core_swap(g_own), g_y, core_swap(g_y)], axis=0)
        dboth, dfar, product_all = ff_backward(
            m_all, g_all, gate, up, product, w_gate, w_up, w_down, down_far, layer, ffp
        )
        in_grad = tn(dboth, m_all).astype(bf16)
        down_grad = tn(product_all, g_all).astype(bf16)
        back_mid, gain_two = norm_back(
            hidden_mid,
            norm_two[layer],
            settle([(dboth, 0, w_gate, True), (dboth, ff, w_up, True), (dfar, 0, in_far, True)], layer),
        )
        grad = grad + back_mid
        g_mix = with_partner(grad.astype(bf16))
        g_wout = tn(gated, g_mix).astype(bf16)
        dmixed, doutgate, dstates, dcum, dfinal, dgain = mixer.back_states(
            x, run, mixed, g_mix, w_out[layer], out_far, gain
        )
        got = chip_swap(dfinal)
        dlast = got[::-1] * (1 - chip).astype(bf16)
        dx, dwdec, dbias = mixer.back(
            x, run, states, cum, first, dmixed, doutgate, dstates, dcum, dlast, wdec, bias
        )
        g_wmix = tn(dx, a)
        if layer + 1 < LAYERS:
            done = (own.astype(f32) + after(far_came, dx).astype(f32)).astype(bf16)
        far = jnp.concatenate([g_wmix[HEAD_COLS : 2 * HEAD_COLS].astype(bf16), g_wout[HV:]], axis=0)
        own = jnp.concatenate([g_wmix[:HEAD_COLS].astype(bf16), g_wout[:HV]], axis=0)
        back_first, gain_one = norm_back(hidden_in, norm_one[layer], settle(
            [(dx, 0, mix_own, True), (dx, HEAD_COLS, mix_far, True), (dx, 2 * HEAD_COLS, w_rank, True)], layer
        ))
        grad = grad + back_first
        if layer > 0:
            ff_grads[layer] = lax.psum((in_grad, down_grad), "dp")
        else:
            in_grad, down_grad, _ = lax.optimization_barrier((in_grad, down_grad, ff_grads[1]))
            ff_grads[layer] = lax.psum((in_grad, down_grad), "dp")
            mix_grads = mix_sum(done, own, far, lax.axis_size("dp"))
            mix_grads = [mix_grads[1], mix_grads[0]]
        heads = jnp.concatenate([dwdec, dbias], axis=0)
        places = lax.iota(jnp.int32, 4)[:, None, None]
        heads = jnp.where(places == member, heads[None, :, :HK], 0.0) + jnp.where(
            places == member ^ 2, heads[None, :, HK:], 0.0
        )
        misc_grads[layer] = jnp.concatenate(
            [g_wmix[2 * HEAD_COLS :].reshape(-1), gain_one, gain_two, dgain[0], heads.reshape(-1)]
        )

    misc = jnp.stack(misc_grads)
    misc = small_sum(misc.reshape(-1, 128)).reshape(LAYERS, -1)
    sizes = (rank * width, width, width, HV, 4 * (rank + 1) * HK)
    pieces, at = [], 0
    for size in sizes:
        pieces.append(misc[:, at : at + size])
        at += size
    heads = lax.dynamic_index_in_dim(
        pieces[4].reshape(LAYERS, 4, rank + 1, HK), member, axis=1, keepdims=False
    )

    def rows_of(grads, start, stop):
        return jnp.stack([g[start:stop].astype(f32) for g in grads])

    def cols_of(grads, start, stop):
        return jnp.stack([g[start:stop].T.astype(f32) for g in grads])

    return (
        result,
        grad[None],
        pieces[1],
        cols_of(mix_grads, 0, HK),
        cols_of(mix_grads, HK, 2 * HK),
        cols_of(mix_grads, 2 * HK, 2 * HK + HV),
        cols_of(mix_grads, 2 * HK + HV, HEAD_COLS),
        jnp.swapaxes(pieces[0].reshape(LAYERS, rank, width), 1, 2),
        heads[:, :rank],
        heads[:, rank],
        pieces[3],
        rows_of(mix_grads, HEAD_COLS, HEAD_COLS + HV),
        pieces[2],
        cols_of([g[0] for g in ff_grads], 0, ff),
        cols_of([g[0] for g in ff_grads], ff, 2 * ff),
        rows_of([g[1] for g in ff_grads], 0, ff),
    )


def solution(mesh):
    cols = P(None, None, "head")
    rows = P(None, "head", None)
    place = P("dp", "head", None)
    return jax.shard_map(
        per_device,
        mesh=mesh,
        in_specs=(
            place, P("dp", None), place, P(), cols, cols, cols, cols, P(), cols,
            P(None, "head"), P(), rows, P(), cols, cols, rows,
        ),
        out_specs=(
            place, place, P(), cols, cols, cols, cols, P(), cols, P(None, "head"), P(), rows,
            P(), cols, cols, rows,
        ),
        check_vma=False,
    )
```

```python
import jax
import jax.numpy as jnp
from jax import lax
from jax.experimental import pallas as pl
from jax.experimental.pallas import tpu as pltpu
from jax.sharding import PartitionSpec as P

LAYERS = 2
HK = 128
HV = 256
HEAD_COLS = 2 * HK + 2 * HV
BLK = 128
MID = BLK // 2 - 1
epsilon = 1e-06
highest = lax.Precision.HIGHEST
VMEM_LIMIT = 48 * 1024 * 1024

f32 = jnp.float32
bf16 = jnp.bfloat16


def nn(left, right):
    return lax.dot_general(left, right, (((1,), (0,)), ((), ())), preferred_element_type=f32)


def nt(left, right):
    return lax.dot_general(left, right, (((1,), (1,)), ((), ())), preferred_element_type=f32)


def tn(left, right):
    return lax.dot_general(left, right, (((0,), (0,)), ((), ())), preferred_element_type=f32)


def doc_count(meta, ndoc, place):
    total = (meta[0] <= place).astype(jnp.int32)
    for which in range(1, ndoc):
        total = total + (meta[which] <= place).astype(jnp.int32)
    return total


def block_masks(meta, ndoc, start):
    rows = lax.broadcasted_iota(jnp.int32, (BLK, BLK), 0) + start
    cols = lax.broadcasted_iota(jnp.int32, (BLK, BLK), 1) + start
    row_ids = doc_count(meta, ndoc, rows)
    col_ids = doc_count(meta, ndoc, cols)
    id_prev = doc_count(meta, ndoc, start - 1)
    id_last = doc_count(meta, ndoc, start + BLK - 1)
    allowed = (rows >= cols) & (row_ids == col_ids)
    carried = jnp.where(row_ids == id_prev, 1.0, 0.0)
    same = jnp.where(row_ids == id_last, 1.0, 0.0)
    keep = jnp.where(id_last == id_prev, 1.0, 0.0)
    return allowed, carried, same, keep


def split_dot(ones_mat, value, dot):
    high = value.astype(bf16)
    low = (value - high.astype(f32)).astype(bf16)
    return dot(ones_mat, high) + dot(ones_mat, low)


def tri_ones():
    rows = lax.broadcasted_iota(jnp.int32, (BLK, BLK), 0)
    cols = lax.broadcasted_iota(jnp.int32, (BLK, BLK), 1)
    return jnp.where(rows >= cols, 1.0, 0.0).astype(bf16)


def head_parts(x_ref, slot):
    at = slot * HEAD_COLS
    query = x_ref[:, at : at + HK] * (HK**-0.5)
    key = x_ref[:, at + HK : at + 2 * HK]
    value = x_ref[:, at + 2 * HK : at + 2 * HK + HV]
    outgate = x_ref[:, at + 2 * HK + HV : at + HEAD_COLS]
    return query, key, value, outgate


def decay_before(x_ref, wdec_ref, bias_ref):
    ranked = x_ref[:, 2 * HEAD_COLS :]
    return jnp.dot(ranked, wdec_ref[...], precision=highest, preferred_element_type=f32) + bias_ref[...]


def states_kernel(ndoc, meta, x_ref, wdec_ref, bias_ref, run_ref, state_ref, cum_ref, final_ref, state, cum):
    block = pl.program_id(0)

    @pl.when(block == 0)
    def _():
        state[...] = jnp.zeros_like(state)
        cum[...] = jnp.ones_like(cum)

    start = meta[ndoc] + block * BLK
    _, _, same, keep = block_masks(meta, ndoc, start)
    before = decay_before(x_ref, wdec_ref, bias_ref)
    decays = (jnp.minimum(before, 0.0) - jnp.log1p(jnp.exp(-jnp.abs(before)))) * (1.0 / 16.0)
    running = split_dot(tri_ones(), decays, nn)
    run_ref[...] = running
    ending = running[BLK - 1 :, :]
    factor = jnp.exp(ending) * keep
    cum_ref[0] = cum[...]
    cum[...] = cum[...] * factor
    for slot in range(2):
        lanes = slice(slot * HK, slot * HK + HK)
        _, key, value, _ = head_parts(x_ref, slot)
        moved = (key * jnp.exp(ending[:, lanes] - running[:, lanes]) * same).astype(bf16)
        old = state[slot]
        state_ref[0, slot] = old.astype(bf16)
        new = old * factor[:, lanes] + tn(value.astype(bf16), moved)
        state[slot] = new
        final_ref[slot] = new.astype(bf16)


def mix_kernel(ndoc, meta, x_ref, run_ref, state_ref, cum_ref, first_ref, gain_ref, gated_ref, mixed_ref):
    block = pl.program_id(0)
    start = meta[ndoc] + block * BLK
    allowed, carried, _, _ = block_masks(meta, ndoc, start)
    gain = gain_ref[...]
    for slot in range(2):
        lanes = slice(slot * HK, slot * HK + HK)
        cols = slice(slot * HV, slot * HV + HV)
        query, key, value, outgate = head_parts(x_ref, slot)
        running = run_ref[:, lanes]
        middle = running[MID : MID + 1, :]
        rel_query = (query * jnp.exp(running - middle)).astype(bf16)
        rel_key = (key * jnp.exp(middle - running)).astype(bf16)
        scores = jnp.where(allowed, nt(rel_query, rel_key), 0.0).astype(bf16)
        far_query = (query * jnp.exp(running) * carried).astype(bf16)
        state = (state_ref[0, slot].astype(f32) + first_ref[slot].astype(f32) * cum_ref[0][:, lanes]).astype(bf16)
        mixed = nn(scores, value.astype(bf16)) + nt(far_query, state)
        scale = lax.rsqrt(jnp.maximum(jnp.mean(mixed * mixed, axis=-1, keepdims=True), 1.0))
        gated_ref[:, cols] = (mixed * scale * gain * outgate * jax.nn.sigmoid(outgate)).astype(bf16)
        mixed_ref[:, cols] = mixed.astype(bf16)


def back_states_kernel(
    ndoc, nblk, meta, x_ref, run_ref, mixed_ref, grad_ref, own_out_ref, far_out_ref, gain_ref,
    dmixed_ref, doutgate_ref, dstate_ref, cum_ref, final_ref, dgain_ref, state, cum,
):
    step = pl.program_id(0)

    @pl.when(step == 0)
    def _():
        state[...] = jnp.zeros_like(state)
        cum[...] = jnp.ones_like(cum)
        dgain_ref[...] = jnp.zeros_like(dgain_ref)

    start = meta[ndoc] + (nblk - 1 - step) * BLK
    _, carried, _, keep = block_masks(meta, ndoc, start)
    gain = gain_ref[...]
    running = run_ref[...]
    factor = jnp.exp(running[BLK - 1 :, :]) * keep
    cum_ref[0] = cum[...]
    cum[...] = cum[...] * factor
    for slot in range(2):
        lanes = slice(slot * HK, slot * HK + HK)
        cols = slice(slot * HV, slot * HV + HV)
        query, _, _, outgate = head_parts(x_ref, slot)
        mixed = mixed_ref[:, cols].astype(f32)
        dgated = nt(grad_ref[...], (own_out_ref, far_out_ref)[slot][...])
        mean = jnp.mean(mixed * mixed, axis=-1, keepdims=True)
        scale = lax.rsqrt(jnp.maximum(mean, 1.0))
        sig = jax.nn.sigmoid(outgate)
        silu = outgate * sig
        dnormed = dgated * silu
        plain = mixed * scale
        doutgate_ref[:, cols] = (dgated * plain * gain * (sig + silu * (1.0 - sig))).astype(bf16)
        dgain_ref[...] += jnp.sum(dnormed * plain, axis=0, keepdims=True)
        weighted = dnormed * gain
        inner = jnp.where(mean > 1.0, jnp.mean(weighted * plain, axis=-1, keepdims=True), 0.0)
        dmixed = (scale * (weighted - plain * inner)).astype(bf16)
        dmixed_ref[:, cols] = dmixed
        far_query = (query * jnp.exp(running[:, lanes]) * carried).astype(bf16)
        old = state[slot]
        dstate_ref[0, slot] = old.astype(bf16)
        new = old * factor[:, lanes] + tn(dmixed, far_query)
        state[slot] = new
        final_ref[slot] = new.astype(bf16)


def back_kernel(
    ndoc, meta, x_ref, run_ref, state_ref, cum_ref, first_ref, dmixed_ref, doutgate_ref,
    dstate_ref, dcum_ref, dlast_ref, wdec_ref, bias_ref, dx_ref, dwdec_ref, dbias_ref,
):
    block = pl.program_id(0)

    @pl.when(block == 0)
    def _():
        dwdec_ref[...] = jnp.zeros_like(dwdec_ref)
        dbias_ref[...] = jnp.zeros_like(dbias_ref)

    start = meta[ndoc] + block * BLK
    allowed, carried, same, keep = block_masks(meta, ndoc, start)
    last_row = lax.broadcasted_iota(jnp.int32, (BLK, HK), 0) == BLK - 1
    drunning = []
    for slot in range(2):
        lanes = slice(slot * HK, slot * HK + HK)
        cols = slice(slot * HV, slot * HV + HV)
        at = slot * HEAD_COLS
        query, key, value, _ = head_parts(x_ref, slot)
        running = run_ref[:, lanes]
        middle = running[MID : MID + 1, :]
        ending = running[BLK - 1 :, :]
        up = jnp.exp(running - middle)
        down = jnp.exp(middle - running)
        far = jnp.exp(running) * carried
        near = jnp.exp(ending - running) * same
        rel_query = (query * up).astype(bf16)
        rel_key = (key * down).astype(bf16)
        far_query = (query * far).astype(bf16)
        moved = (key * near).astype(bf16)
        value = value.astype(bf16)
        scores = jnp.where(allowed, nt(rel_query, rel_key), 0.0).astype(bf16)
        state = state_ref[0, slot].astype(f32) + first_ref[slot].astype(f32) * cum_ref[0][:, lanes]
        dstate = dstate_ref[0, slot].astype(f32) + dlast_ref[slot].astype(f32) * dcum_ref[0][:, lanes]
        state_low = state.astype(bf16)
        dstate_low = dstate.astype(bf16)
        dmixed = dmixed_ref[:, cols]
        dvalue = tn(scores, dmixed) + nt(moved, dstate_low)
        dscores = jnp.where(allowed, nt(dmixed, value), 0.0).astype(bf16)
        drel_query = nn(dscores, rel_key)
        drel_key = tn(dscores, rel_query)
        dfar = nn(dmixed, state_low)
        dmoved = nn(value, dstate_low)
        dquery = drel_query * up + dfar * far
        dkey = drel_key * down + dmoved * near
        moved_grad = dmoved * moved.astype(f32)
        dending = jnp.sum(moved_grad, axis=0, keepdims=True) + jnp.sum(
            state * dstate, axis=0, keepdims=True
        ) * (jnp.exp(ending) * keep)
        drun = (
            drel_query * rel_query.astype(f32)
            - drel_key * rel_key.astype(f32)
            + dfar * far_query.astype(f32)
            - moved_grad
        )
        drunning.append(drun + jnp.where(last_row, dending, 0.0))
        dx_ref[:, at : at + HK] = (dquery * (HK**-0.5)).astype(bf16)
        dx_ref[:, at + HK : at + 2 * HK] = dkey.astype(bf16)
        dx_ref[:, at + 2 * HK : at + 2 * HK + HV] = dvalue.astype(bf16)
        dx_ref[:, at + 2 * HK + HV : at + HEAD_COLS] = doutgate_ref[:, cols]
    drun_both = jnp.concatenate(drunning, axis=1)
    ddecay = split_dot(tri_ones(), drun_both, tn)
    before = decay_before(x_ref, wdec_ref, bias_ref)
    dbefore = ddecay * (1.0 / 16.0) * jax.nn.sigmoid(-before)
    dbias_ref[...] += jnp.sum(dbefore, axis=0, keepdims=True)
    ranked = x_ref[:, 2 * HEAD_COLS :]
    dlow = dbefore.astype(bf16)
    dwdec_ref[...] += tn(ranked.astype(bf16), dlow)
    dx_ref[:, 2 * HEAD_COLS :] = nt(dlow, wdec_ref[...].astype(bf16)).astype(bf16)


def kernel_params():
    return pltpu.CompilerParams(dimension_semantics=("arbitrary",), vmem_limit_bytes=VMEM_LIMIT)


class Mixer:
    def __init__(self, meta, ndoc, tokens):
        self.meta = meta
        self.ndoc = ndoc
        self.tokens = tokens
        self.nblk = tokens // BLK
        self.half = self.nblk // 2

    def rows(self, width, reverse=False):
        nblk, half, core = self.nblk, self.half, self.ndoc + 1

        def place(step, meta):
            time = nblk - 1 - step if reverse else step
            return (lax.rem(time + meta[core] * half, nblk), 0)

        return pl.BlockSpec((BLK, width), place)

    def per_block(self, shape, reverse=False):
        nblk = self.nblk
        zeros = (0,) * len(shape)
        return pl.BlockSpec(
            (1,) + shape, lambda step, meta: ((nblk - 1 - step if reverse else step),) + zeros
        )

    def whole(self, shape):
        zeros = (0,) * len(shape)
        return pl.BlockSpec(shape, lambda step, meta: zeros)

    def call(self, body, in_specs, out_specs, out_shape, scratch, *args):
        return pl.pallas_call(
            body,
            grid_spec=pltpu.PrefetchScalarGridSpec(
                num_scalar_prefetch=1,
                grid=(self.nblk,),
                in_specs=in_specs,
                out_specs=out_specs,
                scratch_shapes=scratch,
            ),
            out_shape=[jax.ShapeDtypeStruct(s, d) for s, d in out_shape],
            cost_estimate=NO_COST,
            compiler_params=kernel_params(),
        )(self.meta, *args)

    def state_scratch(self):
        return [pltpu.VMEM((2, HV, HK), f32), pltpu.VMEM((1, 2 * HK), f32)]

    def states(self, x, wdec, bias):
        ndoc, n = self.ndoc, self.nblk

        def body(*refs):
            states_kernel(ndoc, *refs)

        return self.call(
            body,
            [self.rows(x.shape[1]), self.whole(wdec.shape), self.whole(bias.shape)],
            [
                self.rows(2 * HK),
                self.per_block((2, HV, HK)),
                self.per_block((1, 2 * HK)),
                self.whole((2, HV, HK)),
            ],
            [
                ((self.tokens, 2 * HK), f32),
                ((n, 2, HV, HK), bf16),
                ((n, 1, 2 * HK), f32),
                ((2, HV, HK), bf16),
            ],
            self.state_scratch(),
            x, wdec, bias,
        )

    def mix(self, x, run, states, cum, first, gain):
        ndoc = self.ndoc

        def body(*refs):
            mix_kernel(ndoc, *refs)

        return self.call(
            body,
            [
                self.rows(x.shape[1]),
                self.rows(2 * HK),
                self.per_block((2, HV, HK)),
                self.per_block((1, 2 * HK)),
                self.whole((2, HV, HK)),
                self.whole(gain.shape),
            ],
            [self.rows(2 * HV), self.rows(2 * HV)],
            [((self.tokens, 2 * HV), bf16), ((self.tokens, 2 * HV), bf16)],
            [],
            x, run, states, cum, first, gain,
        )

    def back_states(self, x, run, mixed, grad, own_out, far_out, gain):
        ndoc, n = self.ndoc, self.nblk

        def body(*refs):
            back_states_kernel(ndoc, n, *refs)

        return self.call(
            body,
            [
                self.rows(x.shape[1], True),
                self.rows(2 * HK, True),
                self.rows(2 * HV, True),
                self.rows(grad.shape[1], True),
                self.whole(own_out.shape),
                self.whole(far_out.shape),
                self.whole(gain.shape),
            ],
            [
                self.rows(2 * HV, True),
                self.rows(2 * HV, True),
                self.per_block((2, HV, HK), True),
                self.per_block((1, 2 * HK), True),
                self.whole((2, HV, HK)),
                self.whole((1, HV)),
            ],
            [
                ((self.tokens, 2 * HV), bf16),
                ((self.tokens, 2 * HV), bf16),
                ((n, 2, HV, HK), bf16),
                ((n, 1, 2 * HK), f32),
                ((2, HV, HK), bf16),
                ((1, HV), f32),
            ],
            self.state_scratch(),
            x, run, mixed, grad, own_out, far_out, gain,
        )

    def back(self, x, run, states, cum, first, dmixed, doutgate, dstates, dcum, dlast, wdec, bias):
        ndoc = self.ndoc
        rank = wdec.shape[0]

        def body(*refs):
            back_kernel(ndoc, *refs)

        return self.call(
            body,
            [
                self.rows(x.shape[1]),
                self.rows(2 * HK),
                self.per_block((2, HV, HK)),
                self.per_block((1, 2 * HK)),
                self.whole((2, HV, HK)),
                self.rows(2 * HV),
                self.rows(2 * HV),
                self.per_block((2, HV, HK)),
                self.per_block((1, 2 * HK)),
                self.whole((2, HV, HK)),
                self.whole(wdec.shape),
                self.whole(bias.shape),
            ],
            [self.rows(x.shape[1]), self.whole((rank, 2 * HK)), self.whole((1, 2 * HK))],
            [
                ((self.tokens, x.shape[1]), bf16),
                ((rank, 2 * HK), f32),
                ((1, 2 * HK), f32),
            ],
            [],
            x, run, states, cum, first, dmixed, doutgate, dstates, dcum, dlast, wdec, bias,
        )


ROWS_BLK = 256


def matrix_spec(part):
    array, which = part
    if array.ndim == 3:
        return pl.BlockSpec((None,) + array.shape[1:], lambda i: (which, 0, 0))
    if which is None:
        return pl.BlockSpec(array.shape, lambda i: (0, 0))
    at, rows = which
    return pl.BlockSpec((rows, array.shape[1]), lambda i: (at, 0))


def matrix_shape(part):
    array, which = part
    if array.ndim == 3 or which is None:
        return array.shape[-2:]
    return which[1], array.shape[1]


def row_spec(array, first=0):
    return pl.BlockSpec((ROWS_BLK, array.shape[1]), lambda i: (i + first, 0))


NO_COST = pl.CostEstimate(flops=0, bytes_accessed=0, transcendentals=0)


def local_call(body, grid, in_specs, out_specs, out_shape, args, aliases=None):
    return pl.pallas_call(
        body,
        grid=(grid,),
        in_specs=in_specs,
        out_specs=out_specs,
        out_shape=out_shape,
        input_output_aliases=aliases or {},
        cost_estimate=NO_COST,
        compiler_params=pltpu.CompilerParams(
            dimension_semantics=("arbitrary",), vmem_limit_bytes=VMEM_LIMIT
        ),
    )(*args)


def sum_of_dots(terms, first_row, rows, out_type):
    lefts = []
    for left, _, _, _ in terms:
        if not any(left is seen for seen in lefts):
            lefts.append(left)
    which = [next(i for i, seen in enumerate(lefts) if seen is left) for left, _, _, _ in terms]
    rights = [right for _, _, right, _ in terms]
    width = matrix_shape(rights[0])[0 if terms[0][3] else 1]

    def body(*refs):
        left_refs, right_refs, out = refs[: len(lefts)], refs[len(lefts) : -1], refs[-1]
        total = None
        for (_, at, _, turned), index, right in zip(terms, which, right_refs):
            depth = right.shape[1] if turned else right.shape[0]
            part = (nt if turned else nn)(left_refs[index][:, at : at + depth], right[...])
            total = part if total is None else total + part
        out[...] = total.astype(out_type)

    return local_call(
        body,
        rows // ROWS_BLK,
        [row_spec(v, first_row // ROWS_BLK) for v in lefts] + [matrix_spec(v) for v in rights],
        pl.BlockSpec((ROWS_BLK, width), lambda i: (i, 0)),
        jax.ShapeDtypeStruct((rows, width), out_type),
        lefts + [v[0] for v in rights],
    )


def project(a, parts):
    widths = [matrix_shape(v)[1] for v in parts[:-1]] + [matrix_shape(parts[-1])[0]]

    def body(left, *refs):
        out = refs[-1]
        at = 0
        for right, width in zip(refs[:-1], widths):
            turned = at + width == out.shape[1]
            out[:, at : at + width] = (nt if turned else nn)(left[...], right[...])
            at += width

    return local_call(
        body,
        a.shape[0] // ROWS_BLK,
        [row_spec(a)] + [matrix_spec(v) for v in parts],
        pl.BlockSpec((ROWS_BLK, sum(widths)), lambda i: (i, 0)),
        jax.ShapeDtypeStruct((a.shape[0], sum(widths)), f32),
        [a] + [v[0] for v in parts],
    )


def ff_forward(m, gate_w, up_w, far, ffp):
    ff = matrix_shape(gate_w)[0]

    def body(m_ref, gate_w, up_w, far_gate, far_up, gate_ref, up_ref, product_ref):
        m = m_ref[...]
        for slot, (gate_t, up_t) in enumerate(((gate_w, up_w), (far_gate, far_up))):
            gate, up = nt(m, gate_t[...]), nt(m, up_t[...])
            at = slot * ffp
            gate_ref[:, at : at + ff] = gate.astype(bf16)
            up_ref[:, at : at + ff] = up.astype(bf16)
            product_ref[:, at : at + ff] = (gate * jax.nn.sigmoid(gate) * up).astype(bf16)

    shape = (m.shape[0], 2 * ffp)
    parts = [gate_w, up_w, (far, (0, ff)), (far, (1, ff))]
    return local_call(
        body,
        m.shape[0] // ROWS_BLK,
        [row_spec(m)] + [matrix_spec(v) for v in parts],
        [pl.BlockSpec((ROWS_BLK, 2 * ffp), lambda i: (i, 0))] * 3,
        [jax.ShapeDtypeStruct(shape, bf16)] * 3,
        [m] + [v[0] for v in parts],
    )


def gate_pair(gate, up, dproduct):
    sig = jax.nn.sigmoid(gate)
    silu = gate * sig
    dgate = dproduct * up * (sig + silu * (1.0 - sig))
    return jnp.concatenate([dgate.astype(bf16), (dproduct * silu).astype(bf16)], axis=1), silu


def ff_backward(g, gate, up, product, down_w, far, ffp):
    ff = matrix_shape(down_w)[0]

    def body(g_ref, gate_ref, up_ref, product_ref, down_ref, far_ref, own_out, far_out, product_out):
        g = g_ref[...]
        for slot, (weight, out) in enumerate(((down_ref, own_out), (far_ref, far_out))):
            cols = slice(slot * ffp, slot * ffp + ff)
            out[...] = gate_pair(
                gate_ref[:, cols].astype(f32), up_ref[:, cols].astype(f32), nt(g, weight[...])
            )[0]
        product_out[...] = product_ref[:, :ff]

    rows = g.shape[0]
    parts = [down_w, (far, (2, ff))]
    return local_call(
        body,
        rows // ROWS_BLK,
        [row_spec(v) for v in (g, gate, up, product)] + [matrix_spec(v) for v in parts],
        [
            pl.BlockSpec((ROWS_BLK, 2 * ff), lambda i: (i, 0)),
            pl.BlockSpec((ROWS_BLK, 2 * ff), lambda i: (i, 0)),
            pl.BlockSpec((ROWS_BLK, ff), lambda i: (i, 0)),
        ],
        [
            jax.ShapeDtypeStruct((2 * rows, 2 * ff), bf16),
            jax.ShapeDtypeStruct((rows, 2 * ff), bf16),
            jax.ShapeDtypeStruct((2 * rows, ff), bf16),
        ],
        [g, gate, up, product] + [v[0] for v in parts],
    )


def ff_backward_far(m_all, g_all, dboth, product_all, gate_w, up_w, down_w):
    def body(m_ref, g_ref, gate_t, up_t, down_ref, _, __, own_out, product_out):
        gate, up = nt(m_ref[...], gate_t[...]), nt(m_ref[...], up_t[...])
        value, silu = gate_pair(gate, up, nt(g_ref[...], down_ref[...]))
        own_out[...] = value
        product_out[...] = (silu * up).astype(bf16)

    near = m_all.shape[0] // ROWS_BLK // 2
    parts = [gate_w, up_w, down_w]
    return local_call(
        body,
        near,
        [row_spec(m_all, near), row_spec(g_all, near)]
        + [matrix_spec(v) for v in parts]
        + [pl.BlockSpec(memory_space=pl.ANY)] * 2,
        [row_spec(dboth, near), row_spec(product_all, near)],
        [jax.ShapeDtypeStruct(v.shape, bf16) for v in (dboth, product_all)],
        [m_all, g_all] + [v[0] for v in parts] + [dboth, product_all],
        {5: 0, 6: 1},
    )


def ring_place(index, n):
    return jnp.where(index % 2 == 0, index // 2, n - 1 - index // 2)


def ring_index(place, n):
    return jnp.where(place < n // 2, 2 * place, 2 * (n - 1 - place) + 1)


MESH = pl.DeviceIdType.MESH


class Ring:
    def __init__(self, n, data, out, slots, sems):
        self.n, self.data, self.out, self.slots = n, data, out, slots
        self.send, self.recv, self.out_send, self.out_recv = sems
        self.me = ring_place(lax.axis_index("dp"), n)
        self.peers = [
            ring_index(lax.rem(self.me + 1, n), n),
            ring_index(lax.rem(self.me + n - 1, n), n),
        ]
        self.rows = data.shape[0] // (2 * n)

    def chunk(self, ref, way, back):
        which = lax.rem(self.me + 2 * self.n - (1, -1)[way] * back, self.n)
        return ref.at[pl.ds(pl.multiple_of((2 * which + way) * self.rows, 16), self.rows)]

    def partial(self, way, source, step):
        return pltpu.make_async_remote_copy(
            src_ref=source, dst_ref=self.slots.at[way, step],
            send_sem=self.send.at[way, step], recv_sem=self.recv.at[way, step],
            device_id={"dp": self.peers[way]}, device_id_type=MESH,
        )

    def final(self, way, step, back):
        part = self.chunk(self.out, way, back)
        return pltpu.make_async_remote_copy(
            src_ref=part, dst_ref=part,
            send_sem=self.out_send.at[way, step], recv_sem=self.out_recv.at[way, step],
            device_id={"dp": self.peers[way]}, device_id_type=MESH,
        )

    def start(self):
        for way in range(2):
            self.partial(way, self.chunk(self.data, way, 0), 0).start()

    def reduce(self, step):
        for way in range(2):
            slot = self.slots.at[way, step]
            self.partial(way, slot, step).wait_recv()
            part = self.chunk(self.data, way, step + 1)
            slot[...] = (slot[...].astype(f32) + part[...].astype(f32)).astype(bf16)

            @pl.when(step < self.n - 2)
            def _():
                self.partial(way, slot, step + 1).start()

    def turn(self):
        for way in range(2):
            self.chunk(self.out, way, -1)[...] = self.slots[way, self.n - 2]
            self.final(way, 0, -1).start()

    def gather(self, step):
        for way in range(2):
            self.final(way, step, step).wait_recv()

            @pl.when(step < self.n - 2)
            def _():
                self.final(way, step + 1, step).start()

    def sent(self, step):
        for way in range(2):
            self.partial(way, self.slots.at[way, step], step).wait_send()
            self.final(way, step, step - 1).wait_send()


def steps_of(lo, hi, *bodies):
    def body(step, carry):
        for each in bodies:
            each(step)
        return carry

    lax.fori_loop(lo, hi, body, 0)


def mix_sum_kernel(
    n, done, own, far, misc, out_done, out_own, out_misc, came, total, slots,
    send, recv, out_send, out_recv, chip_send, chip_recv, sums, misc_came, misc_send, misc_recv,
):
    me = ring_place(lax.axis_index("dp"), n)
    member, row = lax.axis_index("head"), lax.axis_index("dp")
    swaps = [{"head": member ^ 1}, {"head": member ^ 2}]
    swaps += [{"dp": row ^ (1 << bit)} for bit in range(n.bit_length() - 1)]
    peers = swaps + [
        {"dp": ring_index(lax.rem(me + 1, n), n)},
        {"dp": ring_index(lax.rem(me + n - 1, n), n)},
    ]
    barrier = pltpu.get_barrier_semaphore()
    for peer in peers:
        pl.semaphore_signal(barrier, inc=1, device_id=peer, device_id_type=MESH)
    pl.semaphore_wait(barrier, len(peers))

    def small(step):
        return pltpu.make_async_remote_copy(
            src_ref=sums.at[step], dst_ref=misc_came.at[step],
            send_sem=misc_send.at[step], recv_sem=misc_recv.at[step],
            device_id=swaps[step], device_id_type=MESH,
        )

    taken = [0]

    def small_step():
        step = taken[0]
        if step == len(swaps):
            return
        small(step).wait()
        sums[step + 1] = sums[step] + misc_came[step]
        taken[0] += 1
        if step + 1 < len(swaps):
            small(step + 1).start()

    swap = pltpu.make_async_remote_copy(
        src_ref=far, dst_ref=came, send_sem=chip_send, recv_sem=chip_recv,
        device_id={"head": member ^ 2}, device_id_type=MESH,
    )
    first = Ring(n, done, out_done, slots.at[0], [v.at[0] for v in (send, recv, out_send, out_recv)])
    second = Ring(n, total, out_own, slots.at[1], [v.at[1] for v in (send, recv, out_send, out_recv)])
    middle, last = (n - 1) // 2, n - 1
    sums[0] = misc[...]
    small(0).start()
    swap.start()
    first.start()
    steps_of(0, middle, first.reduce)
    small_step()
    steps_of(middle, last, first.reduce)
    first.turn()
    small_step()
    swap.wait()
    total[...] = (own[...].astype(f32) + came[...].astype(f32)).astype(bf16)
    second.start()
    steps_of(0, middle, first.gather, second.reduce)
    small_step()
    steps_of(middle, last, first.gather, second.reduce)
    second.turn()
    small_step()
    steps_of(0, middle, second.gather)
    small_step()
    steps_of(middle, last, second.gather)
    for _ in swaps:
        small_step()
    out_misc[...] = sums[len(swaps)]
    steps_of(0, last, first.sent, second.sent)


def mix_sum(done, own, far, misc, n):
    if n == 1:
        misc = misc + core_swap(misc)
        return done, (own.astype(f32) + chip_swap(far).astype(f32)).astype(bf16), misc + chip_swap(misc)
    rows, cols = own.shape
    swaps = 2 + n.bit_length() - 1

    def body(*refs):
        mix_sum_kernel(n, *refs)

    vmem = pl.BlockSpec(memory_space=pltpu.VMEM)
    return pl.pallas_call(
        body,
        in_specs=[vmem] * 4,
        out_specs=[vmem] * 3,
        out_shape=[jax.ShapeDtypeStruct((rows, cols), bf16)] * 2 + [jax.ShapeDtypeStruct(misc.shape, f32)],
        scratch_shapes=[
            pltpu.VMEM((rows, cols), bf16),
            pltpu.VMEM((rows, cols), bf16),
            pltpu.VMEM((2, 2, n - 1, rows // (2 * n), cols), bf16),
        ]
        + [pltpu.SemaphoreType.DMA((2, 2, n - 1))] * 4
        + [pltpu.SemaphoreType.DMA] * 2
        + [
            pltpu.VMEM((swaps + 1,) + misc.shape, f32),
            pltpu.VMEM((swaps,) + misc.shape, f32),
            pltpu.SemaphoreType.DMA((swaps,)),
            pltpu.SemaphoreType.DMA((swaps,)),
        ],
        compiler_params=pltpu.CompilerParams(
            collective_id=0, has_side_effects=True, vmem_limit_bytes=VMEM_LIMIT
        ),
    )(done, own, far, misc)


def norm_scale(hidden):
    return lax.rsqrt(jnp.mean(hidden * hidden, axis=-1, keepdims=True) + epsilon)


def norm_low(hidden, gain):
    return (hidden * norm_scale(hidden) * gain).astype(bf16)


def norm_back(hidden, gain, grad_normed):
    scale = norm_scale(hidden)
    weighted = grad_normed * gain
    grad_hidden = scale * weighted - hidden * (scale * scale * scale) * jnp.mean(
        weighted * hidden, axis=-1, keepdims=True
    )
    return grad_hidden, jnp.sum(grad_normed * hidden * scale, axis=0)


def core_swap(value):
    return lax.ppermute(value, "head", [(i, i ^ 1) for i in range(4)])


def chip_swap(value):
    return lax.ppermute(value, "head", [(i, i ^ 2) for i in range(4)])


def dp_slice(own):
    rows = own.shape[0] // lax.axis_size("dp")
    return lax.dynamic_slice_in_dim(own, lax.axis_index("dp") * rows, rows, 0)


def dp_ring():
    n = lax.axis_size("dp")
    return list(range(0, n, 2)) + list(range(n - 1, 0, -2)) if n > 1 else [0]


def after(value, *others):
    return lax.optimization_barrier((value,) + others)[0]


def per_device(
    tokens, doc_starts, grad_out, norm_one, w_query, w_key, w_value, w_outgate, w_rank, w_decay,
    decay_bias, group_gain, w_out, norm_two, w_gate, w_up, w_down,
):
    shard_len, width = tokens.shape[1:]
    ndoc = doc_starts.shape[1]
    ff = w_gate.shape[2]
    ffp = -(-ff // 128) * 128
    rank = w_decay.shape[1]
    member = lax.axis_index("head")
    core = member % 2
    chip = member // 2
    meta = jnp.concatenate(
        [doc_starts[0], jnp.stack([chip * (2 * shard_len), core]).astype(jnp.int32)]
    )
    mixer = Mixer(meta, ndoc, 2 * shard_len)

    def mix_pack(layer):
        return jnp.concatenate(
            [w_query[layer], w_key[layer], w_value[layer], w_outgate[layer]], axis=1
        )

    gate_t, up_t, rank_t = (jnp.swapaxes(v, 1, 2) for v in (w_gate, w_up, w_rank))

    def ff_slice(layer, wait):
        part = jnp.concatenate([dp_slice(v[layer]) for v in (gate_t, up_t, w_down)], axis=0)
        return chip_swap(after(part, wait))

    def ff_gather(part):
        dp = lax.axis_size("dp")
        whole = lax.all_gather(part, "dp", axis=0, tiled=True)
        return jnp.swapaxes(whole.reshape(dp, 3, ff // dp, width), 0, 1).reshape(3 * ff, width)

    def with_partner(local):
        return jnp.concatenate([local, core_swap(local)], axis=0)

    def settle(terms):
        sent = core_swap(sum_of_dots(terms, shard_len, shard_len, bf16))
        return sum_of_dots(terms, 0, shard_len, f32) + sent.astype(f32)

    small = jnp.concatenate([w_decay.astype(f32), decay_bias[:, None, :]], axis=1)
    small = jnp.concatenate([small, chip_swap(small)], axis=2)
    ff_part = ff_slice(0, meta)
    ff_far = ff_gather(ff_part)
    mix_own = mix_pack(0)
    mix_far = chip_swap(after(mix_own, ff_part))
    out_far = chip_swap(after(w_out[0], ff_part))
    next_part = ff_slice(1, mix_far)

    grad = grad_out[0].astype(f32)
    hidden = tokens[0].astype(f32)
    saved = []
    for layer in range(LAYERS):
        hidden_in = hidden
        a = with_partner(norm_low(hidden, norm_one[layer]))
        x = project(a if layer == 0 else after(a, g_y), ((mix_own, None), (mix_far, None), (rank_t, layer)))
        wdec, bias = small[layer, :rank], small[layer, rank:]
        run, states, cum, final = mixer.states(x, wdec, bias)
        got = chip_swap(final)
        first = got[::-1] * chip.astype(bf16)
        gain = group_gain[layer][None]
        gated, mixed = mixer.mix(x, run, states, cum, first, gain)
        if layer + 1 < LAYERS:
            next_own = mix_pack(layer + 1)
            next_mix = chip_swap(after(next_own, got))
            next_out = chip_swap(after(w_out[layer + 1], got))
            next_far = ff_gather(next_part)
        hidden_mid = hidden + settle(
            [(gated, 0, (w_out, layer), False), (gated, HV, (out_far, None), False)]
        )
        m_own = norm_low(hidden_mid, norm_two[layer])
        m = with_partner(m_own)
        gate, up, product = ff_forward(m, (gate_t, layer), (up_t, layer), ff_far, ffp)
        if layer + 1 < LAYERS:
            product = after(product, next_mix, next_out)
        hidden = hidden_mid + settle(
            [(product, 0, (w_down, layer), False), (product, ffp, (ff_far, (2, ff)), False)]
        )
        m_y = chip_swap(m_own)
        m_all = jnp.concatenate([m, m_y, core_swap(m_y)], axis=0)
        saved.append(
            (hidden_in, hidden_mid, a, m_all, x, run, states, cum, first, mixed, gated, gate, up, product,
             mix_own, mix_far, out_far, ff_far)
        )
        if layer + 1 < LAYERS:
            mix_own, mix_far, out_far, ff_far = next_own, next_mix, next_out, next_far
            g_own = grad_out[0]
            g_y = chip_swap(after(g_own, next_mix))
    result = hidden.astype(bf16)[None]

    ff_grads, misc_grads = [None] * LAYERS, [None] * LAYERS
    for layer in reversed(range(LAYERS)):
        (
            hidden_in, hidden_mid, a, m_all, x, run, states, cum, first, mixed, gated, gate, up, product,
            mix_own, mix_far, out_far, ff_far,
        ) = saved[layer]
        gain = group_gain[layer][None]
        wdec, bias = small[layer, :rank], small[layer, rank:]
        if layer + 1 < LAYERS:
            g_own = grad.astype(bf16)
            g_y = chip_swap(g_own)
            far_came = chip_swap(after(far, g_y))
        g = with_partner(g_own)
        g_all = jnp.concatenate([g, g_y, core_swap(g_y)], axis=0)
        dboth, dfar, product_all = ff_backward(g, gate, up, product, (w_down, layer), ff_far, ffp)
        back_mid, gain_two = norm_back(
            hidden_mid,
            norm_two[layer],
            settle(
                [
                    (dboth, 0, (gate_t, layer), False),
                    (dboth, ff, (up_t, layer), False),
                    (dfar, 0, (ff_far, (0, 2 * ff)), False),
                ]
            ),
        )
        dboth, product_all = ff_backward_far(
            m_all, g_all, dboth, product_all, (gate_t, layer), (up_t, layer), (w_down, layer)
        )
        in_grad = tn(dboth, m_all).astype(bf16)
        down_grad = tn(product_all, g_all).astype(bf16)
        grad = grad + back_mid
        g_mix = with_partner(grad.astype(bf16))
        g_wout = tn(g_mix, gated).astype(bf16)
        dmixed, doutgate, dstates, dcum, dfinal, dgain = mixer.back_states(
            x, run, mixed, g_mix, w_out[layer], out_far, gain
        )
        got = chip_swap(dfinal)
        dlast = got[::-1] * (1 - chip).astype(bf16)
        dx, dwdec, dbias = mixer.back(
            x, run, states, cum, first, dmixed, doutgate, dstates, dcum, dlast, wdec, bias
        )
        g_wmix = tn(a, dx[:, : 2 * HEAD_COLS]).astype(bf16)
        g_rank = tn(dx[:, 2 * HEAD_COLS :], a)
        if layer + 1 < LAYERS:
            done = (own.astype(f32) + after(far_came, dx).astype(f32)).astype(bf16)
        far = jnp.concatenate([g_wmix[:, HEAD_COLS:], g_wout[:, HV:]], axis=1)
        own = jnp.concatenate([g_wmix[:, :HEAD_COLS], g_wout[:, :HV]], axis=1)
        back_first, gain_one = norm_back(hidden_in, norm_one[layer], settle(
            [
                (dx, 0, (mix_own, None), True),
                (dx, HEAD_COLS, (mix_far, None), True),
                (dx, 2 * HEAD_COLS, (rank_t, layer), False),
            ]
        ))
        grad = grad + back_first
        if layer > 0:
            ff_grads[layer] = lax.psum((in_grad, down_grad), "dp")
        else:
            ff_grads[layer] = [lax.psum(v, "dp", axis_index_groups=[dp_ring()]) for v in (in_grad, down_grad)]
            ff_grads[1] = after(ff_grads[1], grad)
        heads = jnp.concatenate([dwdec, dbias], axis=0)
        places = lax.iota(jnp.int32, 4)[:, None, None]
        heads = jnp.where(places == member, heads[None, :, :HK], 0.0) + jnp.where(
            places == member ^ 2, heads[None, :, HK:], 0.0
        )
        misc_grads[layer] = jnp.concatenate(
            [g_rank.reshape(-1), gain_one, gain_two, dgain[0], heads.reshape(-1)]
        )

    misc = jnp.stack(misc_grads)
    length = misc.shape[1]
    misc = jnp.pad(misc.reshape(-1), (0, -misc.size % 1024)).reshape(-1, 128)
    later_mix, first_mix, misc = mix_sum(done, own, far, misc, lax.axis_size("dp"))
    mix_grads = [first_mix, later_mix]
    misc = misc.reshape(-1)[: LAYERS * length].reshape(LAYERS, length)
    sizes = (rank * width, width, width, HV, 4 * (rank + 1) * HK)
    pieces, at = [], 0
    for size in sizes:
        pieces.append(misc[:, at : at + size])
        at += size
    heads = lax.dynamic_index_in_dim(
        pieces[4].reshape(LAYERS, 4, rank + 1, HK), member, axis=1, keepdims=False
    )

    def rows_of(grads, start, stop):
        return jnp.stack([g[start:stop].astype(f32) for g in grads])

    def turned(grads, start, stop):
        return jnp.stack([g[start:stop].T.astype(f32) for g in grads])

    def cols_of(grads, start, stop):
        return jnp.stack([g[:, start:stop].astype(f32) for g in grads])

    return (
        result,
        grad[None],
        pieces[1],
        cols_of(mix_grads, 0, HK),
        cols_of(mix_grads, HK, 2 * HK),
        cols_of(mix_grads, 2 * HK, 2 * HK + HV),
        cols_of(mix_grads, 2 * HK + HV, HEAD_COLS),
        jnp.swapaxes(pieces[0].reshape(LAYERS, rank, width), 1, 2),
        heads[:, :rank],
        heads[:, rank],
        pieces[3],
        jnp.stack([g[:, HEAD_COLS:].T.astype(f32) for g in mix_grads]),
        pieces[2],
        turned([g[0] for g in ff_grads], 0, ff),
        turned([g[0] for g in ff_grads], ff, 2 * ff),
        rows_of([g[1] for g in ff_grads], 0, ff),
    )


def solution(mesh):
    cols = P(None, None, "head")
    rows = P(None, "head", None)
    place = P("dp", "head", None)
    return jax.shard_map(
        per_device,
        mesh=mesh,
        in_specs=(
            place, P("dp", None), place, P(), cols, cols, cols, cols, P(), cols,
            P(None, "head"), P(), rows, P(), cols, cols, rows,
        ),
        out_specs=(
            place, place, P(), cols, cols, cols, cols, P(), cols, P(None, "head"), P(), rows,
            P(), cols, cols, rows,
        ),
        check_vma=False,
    )
```

```python
import jax
import jax.numpy as jnp
from jax import lax
from jax.experimental import pallas as pl
from jax.experimental.pallas import tpu as pltpu
from jax.sharding import PartitionSpec as P

LAYERS = 2
HK = 128
HV = 256
HEAD_COLS = 2 * HK + 2 * HV
BLK = 128
MID = BLK // 2 - 1
SUB = 2
epsilon = 1e-06
highest = lax.Precision.HIGHEST
VMEM_LIMIT = 48 * 1024 * 1024

f32 = jnp.float32
bf16 = jnp.bfloat16


def nn(left, right):
    return lax.dot_general(left, right, (((1,), (0,)), ((), ())), preferred_element_type=f32)


def nt(left, right):
    return lax.dot_general(left, right, (((1,), (1,)), ((), ())), preferred_element_type=f32)


def tn(left, right):
    return lax.dot_general(left, right, (((0,), (0,)), ((), ())), preferred_element_type=f32)


def doc_count(meta, ndoc, place):
    total = (meta[0] <= place).astype(jnp.int32)
    for which in range(1, ndoc):
        total = total + (meta[which] <= place).astype(jnp.int32)
    return total


def block_masks(meta, ndoc, start):
    rows = lax.broadcasted_iota(jnp.int32, (BLK, BLK), 0) + start
    cols = lax.broadcasted_iota(jnp.int32, (BLK, BLK), 1) + start
    row_ids = doc_count(meta, ndoc, rows)
    col_ids = doc_count(meta, ndoc, cols)
    id_prev = doc_count(meta, ndoc, start - 1)
    id_last = doc_count(meta, ndoc, start + BLK - 1)
    allowed = (rows >= cols) & (row_ids == col_ids)
    carried = jnp.where(row_ids == id_prev, 1.0, 0.0)
    same = jnp.where(row_ids == id_last, 1.0, 0.0)
    keep = jnp.where(id_last == id_prev, 1.0, 0.0)
    return allowed, carried, same, keep


def split_dot(ones_mat, value, dot):
    high = value.astype(bf16)
    low = (value - high.astype(f32)).astype(bf16)
    return dot(ones_mat, high) + dot(ones_mat, low)


def tri_ones():
    rows = lax.broadcasted_iota(jnp.int32, (BLK, BLK), 0)
    cols = lax.broadcasted_iota(jnp.int32, (BLK, BLK), 1)
    return jnp.where(rows >= cols, 1.0, 0.0).astype(bf16)


def head_parts(x_ref, slot):
    at = slot * HEAD_COLS
    query = x_ref[:, at : at + HK] * (HK**-0.5)
    key = x_ref[:, at + HK : at + 2 * HK]
    value = x_ref[:, at + 2 * HK : at + 2 * HK + HV]
    outgate = x_ref[:, at + 2 * HK + HV : at + HEAD_COLS]
    return query, key, value, outgate


def decay_before(x_ref, wdec_ref, bias_ref):
    ranked = x_ref[:, 2 * HEAD_COLS :]
    return jnp.dot(ranked, wdec_ref[...], precision=highest, preferred_element_type=f32) + bias_ref[...]


def states_kernel(ndoc, block, meta, x_ref, wdec_ref, bias_ref, run_ref, state_ref, cum_ref, final_ref, state, cum):
    start = meta[ndoc] + block * BLK
    _, _, same, keep = block_masks(meta, ndoc, start)
    before = decay_before(x_ref, wdec_ref, bias_ref)
    decays = (jnp.minimum(before, 0.0) - jnp.log1p(jnp.exp(-jnp.abs(before)))) * (1.0 / 16.0)
    running = split_dot(tri_ones(), decays, nn)
    run_ref[...] = running
    ending = running[BLK - 1 :, :]
    factor = jnp.exp(ending) * keep
    cum_ref[0] = cum[...]
    cum[...] = cum[...] * factor
    for slot in range(2):
        lanes = slice(slot * HK, slot * HK + HK)
        _, key, value, _ = head_parts(x_ref, slot)
        moved = (key * jnp.exp(ending[:, lanes] - running[:, lanes]) * same).astype(bf16)
        old = state[slot]
        state_ref[0, slot] = old.astype(bf16)
        new = old * factor[:, lanes] + tn(value.astype(bf16), moved)
        state[slot] = new
        final_ref[slot] = new.astype(bf16)


def mix_kernel(ndoc, block, meta, x_ref, run_ref, state_ref, cum_ref, first_ref, gain_ref, gated_ref, mixed_ref):
    start = meta[ndoc] + block * BLK
    allowed, carried, _, _ = block_masks(meta, ndoc, start)
    gain = gain_ref[...]
    for slot in range(2):
        lanes = slice(slot * HK, slot * HK + HK)
        cols = slice(slot * HV, slot * HV + HV)
        query, key, value, outgate = head_parts(x_ref, slot)
        running = run_ref[:, lanes]
        middle = running[MID : MID + 1, :]
        rel_query = (query * jnp.exp(running - middle)).astype(bf16)
        rel_key = (key * jnp.exp(middle - running)).astype(bf16)
        scores = jnp.where(allowed, nt(rel_query, rel_key), 0.0).astype(bf16)
        far_query = (query * jnp.exp(running) * carried).astype(bf16)
        state = (state_ref[0, slot].astype(f32) + first_ref[slot].astype(f32) * cum_ref[0][:, lanes]).astype(bf16)
        mixed = nn(scores, value.astype(bf16)) + nt(far_query, state)
        scale = lax.rsqrt(jnp.maximum(jnp.mean(mixed * mixed, axis=-1, keepdims=True), 1.0))
        gated_ref[:, cols] = (mixed * scale * gain * outgate * jax.nn.sigmoid(outgate)).astype(bf16)
        mixed_ref[:, cols] = mixed.astype(bf16)


def back_states_kernel(
    ndoc, block, meta, x_ref, run_ref, mixed_ref, grad_ref, own_out_ref, far_out_ref, gain_ref,
    dmixed_ref, doutgate_ref, dstate_ref, cum_ref, final_ref, dgain_ref, state, cum,
):
    start = meta[ndoc] + block * BLK
    _, carried, _, keep = block_masks(meta, ndoc, start)
    gain = gain_ref[...]
    running = run_ref[...]
    factor = jnp.exp(running[BLK - 1 :, :]) * keep
    cum_ref[0] = cum[...]
    cum[...] = cum[...] * factor
    for slot in range(2):
        lanes = slice(slot * HK, slot * HK + HK)
        cols = slice(slot * HV, slot * HV + HV)
        query, _, _, outgate = head_parts(x_ref, slot)
        mixed = mixed_ref[:, cols].astype(f32)
        dgated = nt(grad_ref[...], (own_out_ref, far_out_ref)[slot][...])
        mean = jnp.mean(mixed * mixed, axis=-1, keepdims=True)
        scale = lax.rsqrt(jnp.maximum(mean, 1.0))
        sig = jax.nn.sigmoid(outgate)
        silu = outgate * sig
        dnormed = dgated * silu
        plain = mixed * scale
        doutgate_ref[:, cols] = (dgated * plain * gain * (sig + silu * (1.0 - sig))).astype(bf16)
        dgain_ref[...] += jnp.sum(dnormed * plain, axis=0, keepdims=True)
        weighted = dnormed * gain
        inner = jnp.where(mean > 1.0, jnp.mean(weighted * plain, axis=-1, keepdims=True), 0.0)
        dmixed = (scale * (weighted - plain * inner)).astype(bf16)
        dmixed_ref[:, cols] = dmixed
        far_query = (query * jnp.exp(running[:, lanes]) * carried).astype(bf16)
        old = state[slot]
        dstate_ref[0, slot] = old.astype(bf16)
        new = old * factor[:, lanes] + tn(dmixed, far_query)
        state[slot] = new
        final_ref[slot] = new.astype(bf16)


def back_kernel(
    ndoc, block, meta, x_ref, run_ref, state_ref, cum_ref, first_ref, dmixed_ref, doutgate_ref,
    dstate_ref, dcum_ref, dlast_ref, wdec_ref, bias_ref, dx_ref, dwdec_ref, dbias_ref,
):
    start = meta[ndoc] + block * BLK
    allowed, carried, same, keep = block_masks(meta, ndoc, start)
    last_row = lax.broadcasted_iota(jnp.int32, (BLK, HK), 0) == BLK - 1
    drunning = []
    for slot in range(2):
        lanes = slice(slot * HK, slot * HK + HK)
        cols = slice(slot * HV, slot * HV + HV)
        at = slot * HEAD_COLS
        query, key, value, _ = head_parts(x_ref, slot)
        running = run_ref[:, lanes]
        middle = running[MID : MID + 1, :]
        ending = running[BLK - 1 :, :]
        up = jnp.exp(running - middle)
        down = jnp.exp(middle - running)
        far = jnp.exp(running) * carried
        near = jnp.exp(ending - running) * same
        rel_query = (query * up).astype(bf16)
        rel_key = (key * down).astype(bf16)
        far_query = (query * far).astype(bf16)
        moved = (key * near).astype(bf16)
        value = value.astype(bf16)
        scores = jnp.where(allowed, nt(rel_query, rel_key), 0.0).astype(bf16)
        state = state_ref[0, slot].astype(f32) + first_ref[slot].astype(f32) * cum_ref[0][:, lanes]
        dstate = dstate_ref[0, slot].astype(f32) + dlast_ref[slot].astype(f32) * dcum_ref[0][:, lanes]
        state_low = state.astype(bf16)
        dstate_low = dstate.astype(bf16)
        dmixed = dmixed_ref[:, cols]
        dvalue = tn(scores, dmixed) + nt(moved, dstate_low)
        dscores = jnp.where(allowed, nt(dmixed, value), 0.0).astype(bf16)
        drel_query = nn(dscores, rel_key)
        drel_key = tn(dscores, rel_query)
        dfar = nn(dmixed, state_low)
        dmoved = nn(value, dstate_low)
        dquery = drel_query * up + dfar * far
        dkey = drel_key * down + dmoved * near
        moved_grad = dmoved * moved.astype(f32)
        dending = jnp.sum(moved_grad, axis=0, keepdims=True) + jnp.sum(
            state * dstate, axis=0, keepdims=True
        ) * (jnp.exp(ending) * keep)
        drun = (
            drel_query * rel_query.astype(f32)
            - drel_key * rel_key.astype(f32)
            + dfar * far_query.astype(f32)
            - moved_grad
        )
        drunning.append(drun + jnp.where(last_row, dending, 0.0))
        dx_ref[:, at : at + HK] = (dquery * (HK**-0.5)).astype(bf16)
        dx_ref[:, at + HK : at + 2 * HK] = dkey.astype(bf16)
        dx_ref[:, at + 2 * HK : at + 2 * HK + HV] = dvalue.astype(bf16)
        dx_ref[:, at + 2 * HK + HV : at + HEAD_COLS] = doutgate_ref[:, cols]
    drun_both = jnp.concatenate(drunning, axis=1)
    ddecay = split_dot(tri_ones(), drun_both, tn)
    before = decay_before(x_ref, wdec_ref, bias_ref)
    dbefore = ddecay * (1.0 / 16.0) * jax.nn.sigmoid(-before)
    dbias_ref[...] += jnp.sum(dbefore, axis=0, keepdims=True)
    ranked = x_ref[:, 2 * HEAD_COLS :]
    dlow = dbefore.astype(bf16)
    dwdec_ref[...] += tn(ranked.astype(bf16), dlow)
    dx_ref[:, 2 * HEAD_COLS :] = nt(dlow, wdec_ref[...].astype(bf16)).astype(bf16)


def kernel_params():
    return pltpu.CompilerParams(dimension_semantics=("arbitrary",), vmem_limit_bytes=VMEM_LIMIT)


def sub_blocks(kernel, ndoc, tokens, rows, blocks, reverse, starts):
    steps = tokens // (BLK * SUB)

    def body(meta, *refs):
        step = pl.program_id(0)

        @pl.when(step == 0)
        def _():
            for which, value in starts:
                refs[which][...] = jnp.full_like(refs[which], value)

        first = (steps - 1 - step if reverse else step) * SUB
        for sub in reversed(range(SUB)) if reverse else range(SUB):
            views = [
                ref.at[sub * BLK : (sub + 1) * BLK] if i in rows
                else ref.at[sub : sub + 1] if i in blocks
                else ref
                for i, ref in enumerate(refs)
            ]
            kernel(ndoc, first + sub, meta, *views)

    return body


class Mixer:
    def __init__(self, meta, ndoc, tokens):
        self.meta = meta
        self.ndoc = ndoc
        self.tokens = tokens
        self.nblk = tokens // BLK
        self.steps = self.nblk // SUB

    def rows(self, width, reverse=False):
        steps, core = self.steps, self.ndoc + 1

        def place(step, meta):
            time = steps - 1 - step if reverse else step
            return (lax.rem(time + meta[core] * (steps // 2), steps), 0)

        return pl.BlockSpec((BLK * SUB, width), place)

    def per_block(self, shape, reverse=False):
        steps = self.steps
        zeros = (0,) * len(shape)
        return pl.BlockSpec(
            (SUB,) + shape, lambda step, meta: ((steps - 1 - step if reverse else step),) + zeros
        )

    def whole(self, shape):
        zeros = (0,) * len(shape)
        return pl.BlockSpec(shape, lambda step, meta: zeros)

    def call(self, kernel, layout, in_specs, out_specs, out_shape, scratch, *args):
        return pl.pallas_call(
            sub_blocks(kernel, self.ndoc, self.tokens, *layout),
            grid_spec=pltpu.PrefetchScalarGridSpec(
                num_scalar_prefetch=1,
                grid=(self.steps,),
                in_specs=in_specs,
                out_specs=out_specs,
                scratch_shapes=scratch,
            ),
            out_shape=[jax.ShapeDtypeStruct(s, d) for s, d in out_shape],
            cost_estimate=NO_COST,
            compiler_params=kernel_params(),
        )(self.meta, *args)

    def state_scratch(self):
        return [pltpu.VMEM((2, HV, HK), f32), pltpu.VMEM((1, 2 * HK), f32)]

    def states(self, x, wdec, bias):
        n = self.nblk
        return self.call(
            states_kernel,
            ((0, 3), (4, 5), False, ((7, 0.0), (8, 1.0))),
            [self.rows(x.shape[1]), self.whole(wdec.shape), self.whole(bias.shape)],
            [
                self.rows(2 * HK),
                self.per_block((2, HV, HK)),
                self.per_block((1, 2 * HK)),
                self.whole((2, HV, HK)),
            ],
            [
                ((self.tokens, 2 * HK), f32),
                ((n, 2, HV, HK), bf16),
                ((n, 1, 2 * HK), f32),
                ((2, HV, HK), bf16),
            ],
            self.state_scratch(),
            x, wdec, bias,
        )

    def mix(self, x, run, states, cum, first, gain):
        return self.call(
            mix_kernel,
            ((0, 1, 6, 7), (2, 3), False, ()),
            [
                self.rows(x.shape[1]),
                self.rows(2 * HK),
                self.per_block((2, HV, HK)),
                self.per_block((1, 2 * HK)),
                self.whole((2, HV, HK)),
                self.whole(gain.shape),
            ],
            [self.rows(2 * HV), self.rows(2 * HV)],
            [((self.tokens, 2 * HV), bf16), ((self.tokens, 2 * HV), bf16)],
            [],
            x, run, states, cum, first, gain,
        )

    def back_states(self, x, run, mixed, grad, own_out, far_out, gain):
        n = self.nblk
        return self.call(
            back_states_kernel,
            ((0, 1, 2, 3, 7, 8), (9, 10), True, ((12, 0.0), (13, 0.0), (14, 1.0))),
            [
                self.rows(x.shape[1], True),
                self.rows(2 * HK, True),
                self.rows(2 * HV, True),
                self.rows(grad.shape[1], True),
                self.whole(own_out.shape),
                self.whole(far_out.shape),
                self.whole(gain.shape),
            ],
            [
                self.rows(2 * HV, True),
                self.rows(2 * HV, True),
                self.per_block((2, HV, HK), True),
                self.per_block((1, 2 * HK), True),
                self.whole((2, HV, HK)),
                self.whole((1, HV)),
            ],
            [
                ((self.tokens, 2 * HV), bf16),
                ((self.tokens, 2 * HV), bf16),
                ((n, 2, HV, HK), bf16),
                ((n, 1, 2 * HK), f32),
                ((2, HV, HK), bf16),
                ((1, HV), f32),
            ],
            self.state_scratch(),
            x, run, mixed, grad, own_out, far_out, gain,
        )

    def back(self, x, run, states, cum, first, dmixed, doutgate, dstates, dcum, dlast, wdec, bias):
        rank = wdec.shape[0]
        return self.call(
            back_kernel,
            ((0, 1, 5, 6, 12), (2, 3, 7, 8), False, ((13, 0.0), (14, 0.0))),
            [
                self.rows(x.shape[1]),
                self.rows(2 * HK),
                self.per_block((2, HV, HK)),
                self.per_block((1, 2 * HK)),
                self.whole((2, HV, HK)),
                self.rows(2 * HV),
                self.rows(2 * HV),
                self.per_block((2, HV, HK)),
                self.per_block((1, 2 * HK)),
                self.whole((2, HV, HK)),
                self.whole(wdec.shape),
                self.whole(bias.shape),
            ],
            [self.rows(x.shape[1]), self.whole((rank, 2 * HK)), self.whole((1, 2 * HK))],
            [
                ((self.tokens, x.shape[1]), bf16),
                ((rank, 2 * HK), f32),
                ((1, 2 * HK), f32),
            ],
            [],
            x, run, states, cum, first, dmixed, doutgate, dstates, dcum, dlast, wdec, bias,
        )


ROWS_BLK = 256


def matrix_spec(part):
    array, which = part
    if array.ndim == 3:
        return pl.BlockSpec((None,) + array.shape[1:], lambda i: (which, 0, 0))
    if which is None:
        return pl.BlockSpec(array.shape, lambda i: (0, 0))
    at, rows = which
    return pl.BlockSpec((rows, array.shape[1]), lambda i: (at, 0))


def matrix_shape(part):
    array, which = part
    if array.ndim == 3 or which is None:
        return array.shape[-2:]
    return which[1], array.shape[1]


def row_spec(array, first=0):
    return pl.BlockSpec((ROWS_BLK, array.shape[1]), lambda i: (i + first, 0))


NO_COST = pl.CostEstimate(flops=0, bytes_accessed=0, transcendentals=0)


def local_call(body, grid, in_specs, out_specs, out_shape, args, aliases=None):
    return pl.pallas_call(
        body,
        grid=(grid,),
        in_specs=in_specs,
        out_specs=out_specs,
        out_shape=out_shape,
        input_output_aliases=aliases or {},
        cost_estimate=NO_COST,
        compiler_params=pltpu.CompilerParams(
            dimension_semantics=("arbitrary",), vmem_limit_bytes=VMEM_LIMIT
        ),
    )(*args)


def sum_of_dots(terms, first_row, rows, out_type):
    lefts = []
    for left, _, _, _ in terms:
        if not any(left is seen for seen in lefts):
            lefts.append(left)
    which = [next(i for i, seen in enumerate(lefts) if seen is left) for left, _, _, _ in terms]
    rights = [right for _, _, right, _ in terms]
    width = matrix_shape(rights[0])[0 if terms[0][3] else 1]

    def body(*refs):
        left_refs, right_refs, out = refs[: len(lefts)], refs[len(lefts) : -1], refs[-1]
        total = None
        for (_, at, _, turned), index, right in zip(terms, which, right_refs):
            depth = right.shape[1] if turned else right.shape[0]
            part = (nt if turned else nn)(left_refs[index][:, at : at + depth], right[...])
            total = part if total is None else total + part
        out[...] = total.astype(out_type)

    return local_call(
        body,
        rows // ROWS_BLK,
        [row_spec(v, first_row // ROWS_BLK) for v in lefts] + [matrix_spec(v) for v in rights],
        pl.BlockSpec((ROWS_BLK, width), lambda i: (i, 0)),
        jax.ShapeDtypeStruct((rows, width), out_type),
        lefts + [v[0] for v in rights],
    )


def project(a, parts):
    widths = [matrix_shape(v)[1] for v in parts[:-1]] + [matrix_shape(parts[-1])[0]]

    def body(left, *refs):
        out = refs[-1]
        at = 0
        for right, width in zip(refs[:-1], widths):
            turned = at + width == out.shape[1]
            out[:, at : at + width] = (nt if turned else nn)(left[...], right[...])
            at += width

    return local_call(
        body,
        a.shape[0] // ROWS_BLK,
        [row_spec(a)] + [matrix_spec(v) for v in parts],
        pl.BlockSpec((ROWS_BLK, sum(widths)), lambda i: (i, 0)),
        jax.ShapeDtypeStruct((a.shape[0], sum(widths)), f32),
        [a] + [v[0] for v in parts],
    )


def ff_forward(m, gate_w, up_w, far, ffp):
    ff = matrix_shape(gate_w)[0]

    def body(m_ref, gate_w, up_w, far_gate, far_up, gate_ref, up_ref, product_ref):
        m = m_ref[...]
        for slot, (gate_t, up_t) in enumerate(((gate_w, up_w), (far_gate, far_up))):
            gate, up = nt(m, gate_t[...]), nt(m, up_t[...])
            at = slot * ffp
            gate_ref[:, at : at + ff] = gate.astype(bf16)
            up_ref[:, at : at + ff] = up.astype(bf16)
            product_ref[:, at : at + ff] = (gate * jax.nn.sigmoid(gate) * up).astype(bf16)

    shape = (m.shape[0], 2 * ffp)
    parts = [gate_w, up_w, (far, (0, ff)), (far, (1, ff))]
    return local_call(
        body,
        m.shape[0] // ROWS_BLK,
        [row_spec(m)] + [matrix_spec(v) for v in parts],
        [pl.BlockSpec((ROWS_BLK, 2 * ffp), lambda i: (i, 0))] * 3,
        [jax.ShapeDtypeStruct(shape, bf16)] * 3,
        [m] + [v[0] for v in parts],
    )


def gate_pair(gate, up, dproduct):
    sig = jax.nn.sigmoid(gate)
    silu = gate * sig
    dgate = dproduct * up * (sig + silu * (1.0 - sig))
    return jnp.concatenate([dgate.astype(bf16), (dproduct * silu).astype(bf16)], axis=1), silu


def ff_backward(g, gate, up, product, down_w, far, ffp):
    ff = matrix_shape(down_w)[0]

    def body(g_ref, gate_ref, up_ref, product_ref, down_ref, far_ref, own_out, far_out, product_out):
        g = g_ref[...]
        for slot, (weight, out) in enumerate(((down_ref, own_out), (far_ref, far_out))):
            cols = slice(slot * ffp, slot * ffp + ff)
            out[...] = gate_pair(
                gate_ref[:, cols].astype(f32), up_ref[:, cols].astype(f32), nt(g, weight[...])
            )[0]
        product_out[...] = product_ref[:, :ff]

    rows = g.shape[0]
    parts = [down_w, (far, (2, ff))]
    return local_call(
        body,
        rows // ROWS_BLK,
        [row_spec(v) for v in (g, gate, up, product)] + [matrix_spec(v) for v in parts],
        [
            pl.BlockSpec((ROWS_BLK, 2 * ff), lambda i: (i, 0)),
            pl.BlockSpec((ROWS_BLK, 2 * ff), lambda i: (i, 0)),
            pl.BlockSpec((ROWS_BLK, ff), lambda i: (i, 0)),
        ],
        [
            jax.ShapeDtypeStruct((2 * rows, 2 * ff), bf16),
            jax.ShapeDtypeStruct((rows, 2 * ff), bf16),
            jax.ShapeDtypeStruct((2 * rows, ff), bf16),
        ],
        [g, gate, up, product] + [v[0] for v in parts],
    )


def ff_backward_far(m_all, g_all, dboth, product_all, gate_w, up_w, down_w):
    def body(m_ref, g_ref, gate_t, up_t, down_ref, _, __, own_out, product_out):
        gate, up = nt(m_ref[...], gate_t[...]), nt(m_ref[...], up_t[...])
        value, silu = gate_pair(gate, up, nt(g_ref[...], down_ref[...]))
        own_out[...] = value
        product_out[...] = (silu * up).astype(bf16)

    near = m_all.shape[0] // ROWS_BLK // 2
    parts = [gate_w, up_w, down_w]
    return local_call(
        body,
        near,
        [row_spec(m_all, near), row_spec(g_all, near)]
        + [matrix_spec(v) for v in parts]
        + [pl.BlockSpec(memory_space=pl.ANY)] * 2,
        [row_spec(dboth, near), row_spec(product_all, near)],
        [jax.ShapeDtypeStruct(v.shape, bf16) for v in (dboth, product_all)],
        [m_all, g_all] + [v[0] for v in parts] + [dboth, product_all],
        {5: 0, 6: 1},
    )


def ring_place(index, n):
    return jnp.where(index % 2 == 0, index // 2, n - 1 - index // 2)


def ring_index(place, n):
    return jnp.where(place < n // 2, 2 * place, 2 * (n - 1 - place) + 1)


MESH = pl.DeviceIdType.MESH


class Ring:
    def __init__(self, n, data, out, slots, sems):
        self.n, self.data, self.out, self.slots = n, data, out, slots
        self.send, self.recv, self.out_send, self.out_recv = sems
        self.me = ring_place(lax.axis_index("dp"), n)
        self.peers = [
            ring_index(lax.rem(self.me + 1, n), n),
            ring_index(lax.rem(self.me + n - 1, n), n),
        ]
        self.rows = data.shape[0] // (2 * n)

    def chunk(self, ref, way, back):
        which = lax.rem(self.me + 2 * self.n - (1, -1)[way] * back, self.n)
        return ref.at[pl.ds(pl.multiple_of((2 * which + way) * self.rows, 16), self.rows)]

    def partial(self, way, source, step):
        return pltpu.make_async_remote_copy(
            src_ref=source, dst_ref=self.slots.at[way, step],
            send_sem=self.send.at[way, step], recv_sem=self.recv.at[way, step],
            device_id={"dp": self.peers[way]}, device_id_type=MESH,
        )

    def final(self, way, step, back):
        part = self.chunk(self.out, way, back)
        return pltpu.make_async_remote_copy(
            src_ref=part, dst_ref=part,
            send_sem=self.out_send.at[way, step], recv_sem=self.out_recv.at[way, step],
            device_id={"dp": self.peers[way]}, device_id_type=MESH,
        )

    def start(self):
        for way in range(2):
            self.partial(way, self.chunk(self.data, way, 0), 0).start()

    def reduce(self, step):
        for way in range(2):
            slot = self.slots.at[way, step]
            self.partial(way, slot, step).wait_recv()
            part = self.chunk(self.data, way, step + 1)
            slot[...] = (slot[...].astype(f32) + part[...].astype(f32)).astype(bf16)

            @pl.when(step < self.n - 2)
            def _():
                self.partial(way, slot, step + 1).start()

    def turn(self):
        for way in range(2):
            self.chunk(self.out, way, -1)[...] = self.slots[way, self.n - 2]
            self.final(way, 0, -1).start()

    def gather(self, step):
        for way in range(2):
            self.final(way, step, step).wait_recv()

            @pl.when(step < self.n - 2)
            def _():
                self.final(way, step + 1, step).start()

    def sent(self, step):
        for way in range(2):
            self.partial(way, self.slots.at[way, step], step).wait_send()
            self.final(way, step, step - 1).wait_send()


def steps_of(lo, hi, *bodies):
    def body(step, carry):
        for each in bodies:
            each(step)
        return carry

    lax.fori_loop(lo, hi, body, 0)


def mix_sum_kernel(
    n, done, own, far, misc, out_done, out_own, out_misc, came, total, done_slots, slots,
    send, recv, out_send, out_recv, chip_send, chip_recv, sums, misc_came, misc_send, misc_recv,
):
    me = ring_place(lax.axis_index("dp"), n)
    member, row = lax.axis_index("head"), lax.axis_index("dp")
    swaps = [{"head": member ^ 1}, {"head": member ^ 2}]
    swaps += [{"dp": row ^ (1 << bit)} for bit in range(n.bit_length() - 1)]
    peers = swaps + [
        {"dp": ring_index(lax.rem(me + 1, n), n)},
        {"dp": ring_index(lax.rem(me + n - 1, n), n)},
    ]
    barrier = pltpu.get_barrier_semaphore()
    for peer in peers:
        pl.semaphore_signal(barrier, inc=1, device_id=peer, device_id_type=MESH)
    pl.semaphore_wait(barrier, len(peers))

    def small(step):
        return pltpu.make_async_remote_copy(
            src_ref=sums.at[step], dst_ref=misc_came.at[step],
            send_sem=misc_send.at[step], recv_sem=misc_recv.at[step],
            device_id=swaps[step], device_id_type=MESH,
        )

    taken = [0]

    def small_step():
        step = taken[0]
        if step == len(swaps):
            return
        small(step).wait()
        sums[step + 1] = sums[step] + misc_came[step]
        taken[0] += 1
        if step + 1 < len(swaps):
            small(step + 1).start()

    swap = pltpu.make_async_remote_copy(
        src_ref=far, dst_ref=came, send_sem=chip_send, recv_sem=chip_recv,
        device_id={"head": member ^ 2}, device_id_type=MESH,
    )
    first = Ring(n, done, out_done, done_slots, [v.at[0] for v in (send, recv, out_send, out_recv)])
    second = Ring(n, total, out_own, slots, [v.at[1] for v in (send, recv, out_send, out_recv)])
    middle, last = (n - 1) // 2, n - 1
    sums[0] = misc[...]
    small(0).start()
    swap.start()
    first.start()
    steps_of(0, middle, first.reduce)
    small_step()
    steps_of(middle, last, first.reduce)
    first.turn()
    small_step()
    swap.wait()
    total[...] = (own[...].astype(f32) + came[...].astype(f32)).astype(bf16)
    second.start()
    steps_of(0, middle, first.gather, second.reduce)
    small_step()
    steps_of(middle, last, first.gather, second.reduce)
    second.turn()
    small_step()
    steps_of(0, middle, second.gather)
    small_step()
    steps_of(middle, last, second.gather)
    for _ in swaps:
        small_step()
    out_misc[...] = sums[len(swaps)]
    steps_of(0, last, first.sent, second.sent)


def mix_sum(parts, own, far, misc, n):
    if n == 1:
        misc = misc + core_swap(misc)
        own = (own.astype(f32) + chip_swap(far).astype(f32)).astype(bf16)
        return jnp.concatenate(parts, axis=0), own, misc + chip_swap(misc)
    rows, cols = own.shape
    done_rows = sum(v.shape[0] for v in parts)
    spare = -done_rows % (32 * n)
    done_rows += spare
    done = jnp.concatenate(list(parts) + ([jnp.zeros((spare, cols), bf16)] if spare else []), axis=0)
    swaps = 2 + n.bit_length() - 1

    def body(*refs):
        mix_sum_kernel(n, *refs)

    vmem = pl.BlockSpec(memory_space=pltpu.VMEM)
    return pl.pallas_call(
        body,
        in_specs=[vmem] * 4,
        out_specs=[vmem] * 3,
        out_shape=[
            jax.ShapeDtypeStruct((done_rows, cols), bf16),
            jax.ShapeDtypeStruct((rows, cols), bf16),
        ]
        + [jax.ShapeDtypeStruct(misc.shape, f32)],
        scratch_shapes=[
            pltpu.VMEM((rows, cols), bf16),
            pltpu.VMEM((rows, cols), bf16),
            pltpu.VMEM((2, n - 1, done_rows // (2 * n), cols), bf16),
            pltpu.VMEM((2, n - 1, rows // (2 * n), cols), bf16),
        ]
        + [pltpu.SemaphoreType.DMA((2, 2, n - 1))] * 4
        + [pltpu.SemaphoreType.DMA] * 2
        + [
            pltpu.VMEM((swaps + 1,) + misc.shape, f32),
            pltpu.VMEM((swaps,) + misc.shape, f32),
            pltpu.SemaphoreType.DMA((swaps,)),
            pltpu.SemaphoreType.DMA((swaps,)),
        ],
        compiler_params=pltpu.CompilerParams(
            collective_id=0, has_side_effects=True, vmem_limit_bytes=VMEM_LIMIT
        ),
    )(done, own, far, misc)


def norm_scale(hidden):
    return lax.rsqrt(jnp.mean(hidden * hidden, axis=-1, keepdims=True) + epsilon)


def norm_low(hidden, gain):
    return (hidden * norm_scale(hidden) * gain).astype(bf16)


def norm_back(hidden, gain, grad_normed):
    scale = norm_scale(hidden)
    weighted = grad_normed * gain
    grad_hidden = scale * weighted - hidden * (scale * scale * scale) * jnp.mean(
        weighted * hidden, axis=-1, keepdims=True
    )
    return grad_hidden, jnp.sum(grad_normed * hidden * scale, axis=0)


def core_swap(value):
    return lax.ppermute(value, "head", [(i, i ^ 1) for i in range(4)])


def chip_swap(value):
    return lax.ppermute(value, "head", [(i, i ^ 2) for i in range(4)])


def dp_slice(own):
    rows = own.shape[0] // lax.axis_size("dp")
    return lax.dynamic_slice_in_dim(own, lax.axis_index("dp") * rows, rows, 0)


def dp_ring():
    n = lax.axis_size("dp")
    return list(range(0, n, 2)) + list(range(n - 1, 0, -2)) if n > 1 else [0]


def after(value, *others):
    return lax.optimization_barrier((value,) + others)[0]


def per_device(
    tokens, doc_starts, grad_out, norm_one, w_query, w_key, w_value, w_outgate, w_rank, w_decay,
    decay_bias, group_gain, w_out, norm_two, w_gate, w_up, w_down,
):
    shard_len, width = tokens.shape[1:]
    ndoc = doc_starts.shape[1]
    ff = w_gate.shape[2]
    ffp = -(-ff // 128) * 128
    rank = w_decay.shape[1]
    member = lax.axis_index("head")
    core = member % 2
    chip = member // 2
    meta = jnp.concatenate(
        [doc_starts[0], jnp.stack([chip * (2 * shard_len), core]).astype(jnp.int32)]
    )
    mixer = Mixer(meta, ndoc, 2 * shard_len)

    def mix_pack(layer):
        return jnp.concatenate(
            [w_query[layer], w_key[layer], w_value[layer], w_outgate[layer]], axis=1
        )

    gate_t, up_t, rank_t = (jnp.swapaxes(v, 1, 2) for v in (w_gate, w_up, w_rank))

    def ff_slice(layer, wait):
        part = jnp.concatenate([dp_slice(v[layer]) for v in (gate_t, up_t, w_down)], axis=0)
        return chip_swap(after(part, wait))

    def ff_gather(part):
        dp = lax.axis_size("dp")
        whole = lax.all_gather(part, "dp", axis=0, tiled=True)
        return jnp.swapaxes(whole.reshape(dp, 3, ff // dp, width), 0, 1).reshape(3 * ff, width)

    def with_partner(local):
        return jnp.concatenate([local, core_swap(local)], axis=0)

    def settle(terms):
        sent = core_swap(sum_of_dots(terms, shard_len, shard_len, bf16))
        return sum_of_dots(terms, 0, shard_len, f32) + sent.astype(f32)

    small = jnp.concatenate([w_decay.astype(f32), decay_bias[:, None, :]], axis=1)
    small = jnp.concatenate([small, chip_swap(small)], axis=2)
    ff_part = ff_slice(0, meta)
    ff_far = ff_gather(ff_part)
    mix_own = mix_pack(0)
    mix_far = chip_swap(after(mix_own, ff_part))
    out_far = chip_swap(after(w_out[0], ff_part))
    next_part = ff_slice(1, mix_far)

    grad = grad_out[0].astype(f32)
    hidden = tokens[0].astype(f32)
    saved = []
    for layer in range(LAYERS):
        hidden_in = hidden
        a = with_partner(norm_low(hidden, norm_one[layer]))
        x = project(a, ((mix_own, None), (mix_far, None), (rank_t, layer)))
        wdec, bias = small[layer, :rank], small[layer, rank:]
        run, states, cum, final = mixer.states(x, wdec, bias)
        got = chip_swap(after(final, next_part) if layer == 0 else after(final, g_y))
        first = got[::-1] * chip.astype(bf16)
        gain = group_gain[layer][None]
        gated, mixed = mixer.mix(x, run, states, cum, first, gain)
        if layer + 1 < LAYERS:
            next_own = mix_pack(layer + 1)
            next_mix = chip_swap(after(next_own, got))
            next_out = chip_swap(after(w_out[layer + 1], got))
            next_far = ff_gather(next_part)
        hidden_mid = hidden + settle(
            [(gated, 0, (w_out, layer), False), (gated, HV, (out_far, None), False)]
        )
        m_own = norm_low(hidden_mid, norm_two[layer])
        m = with_partner(m_own)
        if layer + 1 < LAYERS:
            m = after(m, next_mix)
        gate, up, product = ff_forward(m, (gate_t, layer), (up_t, layer), ff_far, ffp)
        if layer + 1 < LAYERS:
            product = after(product, next_out)
        hidden = hidden_mid + settle(
            [(product, 0, (w_down, layer), False), (product, ffp, (ff_far, (2, ff)), False)]
        )
        m_y = chip_swap(m_own)
        m_all = jnp.concatenate([m, m_y, core_swap(m_y)], axis=0)
        saved.append(
            (hidden_in, hidden_mid, a, m_all, x, run, states, cum, first, mixed, gated, gate, up, product,
             mix_own, mix_far, out_far, ff_far)
        )
        if layer + 1 < LAYERS:
            mix_own, mix_far, out_far, ff_far = next_own, next_mix, next_out, next_far
            g_own = grad_out[0]
            g_y = chip_swap(after(g_own, next_mix))
    result = hidden.astype(bf16)[None]

    ff_grads, misc_grads = [None] * LAYERS, [None] * LAYERS
    for layer in reversed(range(LAYERS)):
        (
            hidden_in, hidden_mid, a, m_all, x, run, states, cum, first, mixed, gated, gate, up, product,
            mix_own, mix_far, out_far, ff_far,
        ) = saved[layer]
        gain = group_gain[layer][None]
        wdec, bias = small[layer, :rank], small[layer, rank:]
        if layer + 1 < LAYERS:
            g_own = grad.astype(bf16)
            g_y = chip_swap(g_own)
            mix_done = (own.astype(f32) + chip_swap(after(far, g_y)).astype(f32)).astype(bf16)
            mix_done = lax.psum(mix_done, "dp", axis_index_groups=[dp_ring()])
        g = with_partner(g_own)
        g_all = jnp.concatenate([g, g_y, core_swap(g_y)], axis=0)
        dboth, dfar, product_all = ff_backward(g, gate, up, product, (w_down, layer), ff_far, ffp)
        back_mid, gain_two = norm_back(
            hidden_mid,
            norm_two[layer],
            settle(
                [
                    (dboth, 0, (gate_t, layer), False),
                    (dboth, ff, (up_t, layer), False),
                    (dfar, 0, (ff_far, (0, 2 * ff)), False),
                ]
            ),
        )
        dboth, product_all = ff_backward_far(
            m_all, g_all, dboth, product_all, (gate_t, layer), (up_t, layer), (w_down, layer)
        )
        in_grad = tn(dboth, m_all).astype(bf16)
        down_grad = tn(product_all, g_all).astype(bf16)
        grad = grad + back_mid
        g_mix = with_partner(grad.astype(bf16))
        g_wout = tn(g_mix, gated).astype(bf16)
        dmixed, doutgate, dstates, dcum, dfinal, dgain = mixer.back_states(
            x, run, mixed, g_mix, w_out[layer], out_far, gain
        )
        got = chip_swap(dfinal)
        dlast = got[::-1] * (1 - chip).astype(bf16)
        dx, dwdec, dbias = mixer.back(
            x, run, states, cum, first, dmixed, doutgate, dstates, dcum, dlast, wdec, bias
        )
        g_wmix = tn(a, dx[:, : 2 * HEAD_COLS]).astype(bf16)
        g_rank = tn(dx[:, 2 * HEAD_COLS :], a)
        far = jnp.concatenate([g_wmix[:, HEAD_COLS:], g_wout[:, HV:]], axis=1)
        own = jnp.concatenate([g_wmix[:, :HEAD_COLS], g_wout[:, :HV]], axis=1)
        back_first, gain_one = norm_back(hidden_in, norm_one[layer], settle(
            [
                (dx, 0, (mix_own, None), True),
                (dx, HEAD_COLS, (mix_far, None), True),
                (dx, 2 * HEAD_COLS, (rank_t, layer), False),
            ]
        ))
        grad = grad + back_first
        if layer > 0:
            ff_grads[layer] = lax.psum((in_grad, down_grad), "dp")
        else:
            ff_parts = (in_grad, down_grad)
            ff_grads[1] = after(ff_grads[1], grad)
        heads = jnp.concatenate([dwdec, dbias], axis=0)
        places = lax.iota(jnp.int32, 4)[:, None, None]
        heads = jnp.where(places == member, heads[None, :, :HK], 0.0) + jnp.where(
            places == member ^ 2, heads[None, :, HK:], 0.0
        )
        misc_grads[layer] = jnp.concatenate(
            [g_rank.reshape(-1), gain_one, gain_two, dgain[0], heads.reshape(-1)]
        )

    misc = jnp.stack(misc_grads)
    length = misc.shape[1]
    misc = jnp.pad(misc.reshape(-1), (0, -misc.size % 1024)).reshape(-1, 128)
    ff_done, first_mix, misc = mix_sum(ff_parts, own, far, misc, lax.axis_size("dp"))
    mix_grads = [first_mix, after(mix_done, grad)]
    ff_grads[0] = (ff_done[: 2 * ff], ff_done[2 * ff : 3 * ff])
    misc = misc.reshape(-1)[: LAYERS * length].reshape(LAYERS, length)
    sizes = (rank * width, width, width, HV, 4 * (rank + 1) * HK)
    pieces, at = [], 0
    for size in sizes:
        pieces.append(misc[:, at : at + size])
        at += size
    heads = lax.dynamic_index_in_dim(
        pieces[4].reshape(LAYERS, 4, rank + 1, HK), member, axis=1, keepdims=False
    )

    def rows_of(grads, start, stop):
        return jnp.stack([g[start:stop].astype(f32) for g in grads])

    def turned(grads, start, stop):
        return jnp.stack([g[start:stop].T.astype(f32) for g in grads])

    def cols_of(grads, start, stop):
        return jnp.stack([g[:, start:stop].astype(f32) for g in grads])

    return (
        result,
        grad[None],
        pieces[1],
        cols_of(mix_grads, 0, HK),
        cols_of(mix_grads, HK, 2 * HK),
        cols_of(mix_grads, 2 * HK, 2 * HK + HV),
        cols_of(mix_grads, 2 * HK + HV, HEAD_COLS),
        jnp.swapaxes(pieces[0].reshape(LAYERS, rank, width), 1, 2),
        heads[:, :rank],
        heads[:, rank],
        pieces[3],
        jnp.stack([g[:, HEAD_COLS:].T.astype(f32) for g in mix_grads]),
        pieces[2],
        turned([g[0] for g in ff_grads], 0, ff),
        turned([g[0] for g in ff_grads], ff, 2 * ff),
        rows_of([g[1] for g in ff_grads], 0, ff),
    )


def solution(mesh):
    cols = P(None, None, "head")
    rows = P(None, "head", None)
    place = P("dp", "head", None)
    return jax.shard_map(
        per_device,
        mesh=mesh,
        in_specs=(
            place, P("dp", None), place, P(), cols, cols, cols, cols, P(), cols,
            P(None, "head"), P(), rows, P(), cols, cols, rows,
        ),
        out_specs=(
            place, place, P(), cols, cols, cols, cols, P(), cols, P(None, "head"), P(), rows,
            P(), cols, cols, rows,
        ),
        check_vma=False,
    )
```

```python
import jax
import jax.numpy as jnp
from jax import lax
from jax.experimental import pallas as pl
from jax.experimental.pallas import tpu as pltpu
from jax.sharding import PartitionSpec as P

LAYERS = 2
HK = 128
HV = 256
HEAD_COLS = 2 * HK + 2 * HV
BLK = 128
MID = BLK // 2 - 1
SUB = 2
epsilon = 1e-06
highest = lax.Precision.HIGHEST
VMEM_LIMIT = 48 * 1024 * 1024

f32 = jnp.float32
bf16 = jnp.bfloat16


def nn(left, right):
    return lax.dot_general(left, right, (((1,), (0,)), ((), ())), preferred_element_type=f32)


def nt(left, right):
    return lax.dot_general(left, right, (((1,), (1,)), ((), ())), preferred_element_type=f32)


def tn(left, right):
    return lax.dot_general(left, right, (((0,), (0,)), ((), ())), preferred_element_type=f32)


def doc_count(meta, ndoc, place):
    total = (meta[0] <= place).astype(jnp.int32)
    for which in range(1, ndoc):
        total = total + (meta[which] <= place).astype(jnp.int32)
    return total


def block_masks(meta, ndoc, start):
    rows = lax.broadcasted_iota(jnp.int32, (BLK, BLK), 0) + start
    cols = lax.broadcasted_iota(jnp.int32, (BLK, BLK), 1) + start
    row_ids = doc_count(meta, ndoc, rows)
    col_ids = doc_count(meta, ndoc, cols)
    id_prev = doc_count(meta, ndoc, start - 1)
    id_last = doc_count(meta, ndoc, start + BLK - 1)
    allowed = (rows >= cols) & (row_ids == col_ids)
    carried = jnp.where(row_ids == id_prev, 1.0, 0.0)
    same = jnp.where(row_ids == id_last, 1.0, 0.0)
    keep = jnp.where(id_last == id_prev, 1.0, 0.0)
    return allowed, carried, same, keep


def split_dot(ones_mat, value, dot):
    high = value.astype(bf16)
    low = (value - high.astype(f32)).astype(bf16)
    return dot(ones_mat, high) + dot(ones_mat, low)


def tri_ones():
    rows = lax.broadcasted_iota(jnp.int32, (BLK, BLK), 0)
    cols = lax.broadcasted_iota(jnp.int32, (BLK, BLK), 1)
    return jnp.where(rows >= cols, 1.0, 0.0).astype(bf16)


def head_parts(x_ref, slot):
    at = slot * HEAD_COLS
    query = x_ref[:, at : at + HK] * (HK**-0.5)
    key = x_ref[:, at + HK : at + 2 * HK]
    value = x_ref[:, at + 2 * HK : at + 2 * HK + HV]
    outgate = x_ref[:, at + 2 * HK + HV : at + HEAD_COLS]
    return query, key, value, outgate


def decay_before(x_ref, wdec_ref, bias_ref):
    ranked = x_ref[:, 2 * HEAD_COLS :]
    return jnp.dot(ranked, wdec_ref[...], precision=highest, preferred_element_type=f32) + bias_ref[...]


def states_kernel(ndoc, block, meta, x_ref, wdec_ref, bias_ref, run_ref, state_ref, cum_ref, final_ref, state, cum):
    start = meta[ndoc] + block * BLK
    _, _, same, keep = block_masks(meta, ndoc, start)
    before = decay_before(x_ref, wdec_ref, bias_ref)
    decays = (jnp.minimum(before, 0.0) - jnp.log1p(jnp.exp(-jnp.abs(before)))) * (1.0 / 16.0)
    running = split_dot(tri_ones(), decays, nn)
    run_ref[...] = running
    ending = running[BLK - 1 :, :]
    factor = jnp.exp(ending) * keep
    cum_ref[0] = cum[...]
    cum[...] = cum[...] * factor
    for slot in range(2):
        lanes = slice(slot * HK, slot * HK + HK)
        _, key, value, _ = head_parts(x_ref, slot)
        moved = (key * jnp.exp(ending[:, lanes] - running[:, lanes]) * same).astype(bf16)
        old = state[slot]
        state_ref[0, slot] = old.astype(bf16)
        new = old * factor[:, lanes] + tn(value.astype(bf16), moved)
        state[slot] = new
        final_ref[slot] = new.astype(bf16)


def mix_kernel(ndoc, block, meta, x_ref, run_ref, state_ref, cum_ref, first_ref, gain_ref, gated_ref, mixed_ref):
    start = meta[ndoc] + block * BLK
    allowed, carried, _, _ = block_masks(meta, ndoc, start)
    gain = gain_ref[...]
    for slot in range(2):
        lanes = slice(slot * HK, slot * HK + HK)
        cols = slice(slot * HV, slot * HV + HV)
        query, key, value, outgate = head_parts(x_ref, slot)
        running = run_ref[:, lanes]
        middle = running[MID : MID + 1, :]
        rel_query = (query * jnp.exp(running - middle)).astype(bf16)
        rel_key = (key * jnp.exp(middle - running)).astype(bf16)
        scores = jnp.where(allowed, nt(rel_query, rel_key), 0.0).astype(bf16)
        far_query = (query * jnp.exp(running) * carried).astype(bf16)
        state = (state_ref[0, slot].astype(f32) + first_ref[slot].astype(f32) * cum_ref[0][:, lanes]).astype(bf16)
        mixed = nn(scores, value.astype(bf16)) + nt(far_query, state)
        scale = lax.rsqrt(jnp.maximum(jnp.mean(mixed * mixed, axis=-1, keepdims=True), 1.0))
        gated_ref[:, cols] = (mixed * scale * gain * outgate * jax.nn.sigmoid(outgate)).astype(bf16)
        mixed_ref[:, cols] = mixed.astype(bf16)


def back_states_kernel(
    ndoc, block, meta, x_ref, run_ref, mixed_ref, grad_ref, own_out_ref, far_out_ref, gain_ref,
    dmixed_ref, doutgate_ref, dstate_ref, cum_ref, final_ref, dgain_ref, state, cum,
):
    start = meta[ndoc] + block * BLK
    _, carried, _, keep = block_masks(meta, ndoc, start)
    gain = gain_ref[...]
    running = run_ref[...]
    factor = jnp.exp(running[BLK - 1 :, :]) * keep
    cum_ref[0] = cum[...]
    cum[...] = cum[...] * factor
    for slot in range(2):
        lanes = slice(slot * HK, slot * HK + HK)
        cols = slice(slot * HV, slot * HV + HV)
        query, _, _, outgate = head_parts(x_ref, slot)
        mixed = mixed_ref[:, cols].astype(f32)
        dgated = nt(grad_ref[...], (own_out_ref, far_out_ref)[slot][...])
        mean = jnp.mean(mixed * mixed, axis=-1, keepdims=True)
        scale = lax.rsqrt(jnp.maximum(mean, 1.0))
        sig = jax.nn.sigmoid(outgate)
        silu = outgate * sig
        dnormed = dgated * silu
        plain = mixed * scale
        doutgate_ref[:, cols] = (dgated * plain * gain * (sig + silu * (1.0 - sig))).astype(bf16)
        dgain_ref[...] += jnp.sum(dnormed * plain, axis=0, keepdims=True)
        weighted = dnormed * gain
        inner = jnp.where(mean > 1.0, jnp.mean(weighted * plain, axis=-1, keepdims=True), 0.0)
        dmixed = (scale * (weighted - plain * inner)).astype(bf16)
        dmixed_ref[:, cols] = dmixed
        far_query = (query * jnp.exp(running[:, lanes]) * carried).astype(bf16)
        old = state[slot]
        dstate_ref[0, slot] = old.astype(bf16)
        new = old * factor[:, lanes] + tn(dmixed, far_query)
        state[slot] = new
        final_ref[slot] = new.astype(bf16)


def back_kernel(
    ndoc, block, meta, x_ref, run_ref, state_ref, cum_ref, first_ref, dmixed_ref, doutgate_ref,
    dstate_ref, dcum_ref, dlast_ref, wdec_ref, bias_ref, dx_ref, dwdec_ref, dbias_ref,
):
    start = meta[ndoc] + block * BLK
    allowed, carried, same, keep = block_masks(meta, ndoc, start)
    last_row = lax.broadcasted_iota(jnp.int32, (BLK, HK), 0) == BLK - 1
    drunning = []
    for slot in range(2):
        lanes = slice(slot * HK, slot * HK + HK)
        cols = slice(slot * HV, slot * HV + HV)
        at = slot * HEAD_COLS
        query, key, value, _ = head_parts(x_ref, slot)
        running = run_ref[:, lanes]
        middle = running[MID : MID + 1, :]
        ending = running[BLK - 1 :, :]
        up = jnp.exp(running - middle)
        down = jnp.exp(middle - running)
        far = jnp.exp(running) * carried
        near = jnp.exp(ending - running) * same
        rel_query = (query * up).astype(bf16)
        rel_key = (key * down).astype(bf16)
        far_query = (query * far).astype(bf16)
        moved = (key * near).astype(bf16)
        value = value.astype(bf16)
        scores = jnp.where(allowed, nt(rel_query, rel_key), 0.0).astype(bf16)
        state = state_ref[0, slot].astype(f32) + first_ref[slot].astype(f32) * cum_ref[0][:, lanes]
        dstate = dstate_ref[0, slot].astype(f32) + dlast_ref[slot].astype(f32) * dcum_ref[0][:, lanes]
        state_low = state.astype(bf16)
        dstate_low = dstate.astype(bf16)
        dmixed = dmixed_ref[:, cols]
        dvalue = tn(scores, dmixed) + nt(moved, dstate_low)
        dscores = jnp.where(allowed, nt(dmixed, value), 0.0).astype(bf16)
        drel_query = nn(dscores, rel_key)
        drel_key = tn(dscores, rel_query)
        dfar = nn(dmixed, state_low)
        dmoved = nn(value, dstate_low)
        dquery = drel_query * up + dfar * far
        dkey = drel_key * down + dmoved * near
        moved_grad = dmoved * moved.astype(f32)
        dending = jnp.sum(moved_grad, axis=0, keepdims=True) + jnp.sum(
            state * dstate, axis=0, keepdims=True
        ) * (jnp.exp(ending) * keep)
        drun = (
            drel_query * rel_query.astype(f32)
            - drel_key * rel_key.astype(f32)
            + dfar * far_query.astype(f32)
            - moved_grad
        )
        drunning.append(drun + jnp.where(last_row, dending, 0.0))
        dx_ref[:, at : at + HK] = (dquery * (HK**-0.5)).astype(bf16)
        dx_ref[:, at + HK : at + 2 * HK] = dkey.astype(bf16)
        dx_ref[:, at + 2 * HK : at + 2 * HK + HV] = dvalue.astype(bf16)
        dx_ref[:, at + 2 * HK + HV : at + HEAD_COLS] = doutgate_ref[:, cols]
    drun_both = jnp.concatenate(drunning, axis=1)
    ddecay = split_dot(tri_ones(), drun_both, tn)
    before = decay_before(x_ref, wdec_ref, bias_ref)
    dbefore = ddecay * (1.0 / 16.0) * jax.nn.sigmoid(-before)
    dbias_ref[...] += jnp.sum(dbefore, axis=0, keepdims=True)
    ranked = x_ref[:, 2 * HEAD_COLS :]
    dlow = dbefore.astype(bf16)
    dwdec_ref[...] += tn(ranked.astype(bf16), dlow)
    dx_ref[:, 2 * HEAD_COLS :] = nt(dlow, wdec_ref[...].astype(bf16)).astype(bf16)


def kernel_params():
    return pltpu.CompilerParams(dimension_semantics=("arbitrary",), vmem_limit_bytes=VMEM_LIMIT)


def sub_blocks(kernel, ndoc, tokens, rows, blocks, reverse, starts):
    steps = tokens // (BLK * SUB)

    def body(meta, *refs):
        step = pl.program_id(0)

        @pl.when(step == 0)
        def _():
            for which, value in starts:
                refs[which][...] = jnp.full_like(refs[which], value)

        first = (steps - 1 - step if reverse else step) * SUB
        for sub in reversed(range(SUB)) if reverse else range(SUB):
            views = [
                ref.at[sub * BLK : (sub + 1) * BLK] if i in rows
                else ref.at[sub : sub + 1] if i in blocks
                else ref
                for i, ref in enumerate(refs)
            ]
            kernel(ndoc, first + sub, meta, *views)

    return body


class Mixer:
    def __init__(self, meta, ndoc, tokens):
        self.meta = meta
        self.ndoc = ndoc
        self.tokens = tokens
        self.nblk = tokens // BLK
        self.steps = self.nblk // SUB

    def rows(self, width, reverse=False):
        steps, core = self.steps, self.ndoc + 1

        def place(step, meta):
            time = steps - 1 - step if reverse else step
            return (lax.rem(time + meta[core] * (steps // 2), steps), 0)

        return pl.BlockSpec((BLK * SUB, width), place)

    def per_block(self, shape, reverse=False):
        steps = self.steps
        zeros = (0,) * len(shape)
        return pl.BlockSpec(
            (SUB,) + shape, lambda step, meta: ((steps - 1 - step if reverse else step),) + zeros
        )

    def whole(self, shape):
        zeros = (0,) * len(shape)
        return pl.BlockSpec(shape, lambda step, meta: zeros)

    def call(self, kernel, layout, in_specs, out_specs, out_shape, scratch, *args):
        return pl.pallas_call(
            sub_blocks(kernel, self.ndoc, self.tokens, *layout),
            grid_spec=pltpu.PrefetchScalarGridSpec(
                num_scalar_prefetch=1,
                grid=(self.steps,),
                in_specs=in_specs,
                out_specs=out_specs,
                scratch_shapes=scratch,
            ),
            out_shape=[jax.ShapeDtypeStruct(s, d) for s, d in out_shape],
            cost_estimate=NO_COST,
            compiler_params=kernel_params(),
        )(self.meta, *args)

    def state_scratch(self):
        return [pltpu.VMEM((2, HV, HK), f32), pltpu.VMEM((1, 2 * HK), f32)]

    def states(self, x, wdec, bias):
        n = self.nblk
        return self.call(
            states_kernel,
            ((0, 3), (4, 5), False, ((7, 0.0), (8, 1.0))),
            [self.rows(x.shape[1]), self.whole(wdec.shape), self.whole(bias.shape)],
            [
                self.rows(2 * HK),
                self.per_block((2, HV, HK)),
                self.per_block((1, 2 * HK)),
                self.whole((2, HV, HK)),
            ],
            [
                ((self.tokens, 2 * HK), f32),
                ((n, 2, HV, HK), bf16),
                ((n, 1, 2 * HK), f32),
                ((2, HV, HK), bf16),
            ],
            self.state_scratch(),
            x, wdec, bias,
        )

    def mix(self, x, run, states, cum, first, gain):
        return self.call(
            mix_kernel,
            ((0, 1, 6, 7), (2, 3), False, ()),
            [
                self.rows(x.shape[1]),
                self.rows(2 * HK),
                self.per_block((2, HV, HK)),
                self.per_block((1, 2 * HK)),
                self.whole((2, HV, HK)),
                self.whole(gain.shape),
            ],
            [self.rows(2 * HV), self.rows(2 * HV)],
            [((self.tokens, 2 * HV), bf16), ((self.tokens, 2 * HV), bf16)],
            [],
            x, run, states, cum, first, gain,
        )

    def back_states(self, x, run, mixed, grad, own_out, far_out, gain):
        n = self.nblk
        return self.call(
            back_states_kernel,
            ((0, 1, 2, 3, 7, 8), (9, 10), True, ((12, 0.0), (13, 0.0), (14, 1.0))),
            [
                self.rows(x.shape[1], True),
                self.rows(2 * HK, True),
                self.rows(2 * HV, True),
                self.rows(grad.shape[1], True),
                self.whole(own_out.shape),
                self.whole(far_out.shape),
                self.whole(gain.shape),
            ],
            [
                self.rows(2 * HV, True),
                self.rows(2 * HV, True),
                self.per_block((2, HV, HK), True),
                self.per_block((1, 2 * HK), True),
                self.whole((2, HV, HK)),
                self.whole((1, HV)),
            ],
            [
                ((self.tokens, 2 * HV), bf16),
                ((self.tokens, 2 * HV), bf16),
                ((n, 2, HV, HK), bf16),
                ((n, 1, 2 * HK), f32),
                ((2, HV, HK), bf16),
                ((1, HV), f32),
            ],
            self.state_scratch(),
            x, run, mixed, grad, own_out, far_out, gain,
        )

    def back(self, x, run, states, cum, first, dmixed, doutgate, dstates, dcum, dlast, wdec, bias):
        rank = wdec.shape[0]
        return self.call(
            back_kernel,
            ((0, 1, 5, 6, 12), (2, 3, 7, 8), False, ((13, 0.0), (14, 0.0))),
            [
                self.rows(x.shape[1]),
                self.rows(2 * HK),
                self.per_block((2, HV, HK)),
                self.per_block((1, 2 * HK)),
                self.whole((2, HV, HK)),
                self.rows(2 * HV),
                self.rows(2 * HV),
                self.per_block((2, HV, HK)),
                self.per_block((1, 2 * HK)),
                self.whole((2, HV, HK)),
                self.whole(wdec.shape),
                self.whole(bias.shape),
            ],
            [self.rows(x.shape[1]), self.whole((rank, 2 * HK)), self.whole((1, 2 * HK))],
            [
                ((self.tokens, x.shape[1]), bf16),
                ((rank, 2 * HK), f32),
                ((1, 2 * HK), f32),
            ],
            [],
            x, run, states, cum, first, dmixed, doutgate, dstates, dcum, dlast, wdec, bias,
        )


ROWS_BLK = 256


def matrix_spec(part):
    array, which = part
    if array.ndim == 3:
        return pl.BlockSpec((None,) + array.shape[1:], lambda i: (which, 0, 0))
    if which is None:
        return pl.BlockSpec(array.shape, lambda i: (0, 0))
    at, rows = which
    return pl.BlockSpec((rows, array.shape[1]), lambda i: (at, 0))


def matrix_shape(part):
    array, which = part
    if array.ndim == 3 or which is None:
        return array.shape[-2:]
    return which[1], array.shape[1]


def row_spec(array, first=0):
    return pl.BlockSpec((ROWS_BLK, array.shape[1]), lambda i: (i + first, 0))


NO_COST = pl.CostEstimate(flops=0, bytes_accessed=0, transcendentals=0)


def local_call(body, grid, in_specs, out_specs, out_shape, args, aliases=None):
    return pl.pallas_call(
        body,
        grid=(grid,),
        in_specs=in_specs,
        out_specs=out_specs,
        out_shape=out_shape,
        input_output_aliases=aliases or {},
        cost_estimate=NO_COST,
        compiler_params=pltpu.CompilerParams(
            dimension_semantics=("arbitrary",), vmem_limit_bytes=VMEM_LIMIT
        ),
    )(*args)


def sum_of_dots(terms, first_row, rows, out_type):
    lefts = []
    for left, _, _, _ in terms:
        if not any(left is seen for seen in lefts):
            lefts.append(left)
    which = [next(i for i, seen in enumerate(lefts) if seen is left) for left, _, _, _ in terms]
    rights = [right for _, _, right, _ in terms]
    width = matrix_shape(rights[0])[0 if terms[0][3] else 1]

    def body(*refs):
        left_refs, right_refs, out = refs[: len(lefts)], refs[len(lefts) : -1], refs[-1]
        total = None
        for (_, at, _, turned), index, right in zip(terms, which, right_refs):
            depth = right.shape[1] if turned else right.shape[0]
            part = (nt if turned else nn)(left_refs[index][:, at : at + depth], right[...])
            total = part if total is None else total + part
        out[...] = total.astype(out_type)

    return local_call(
        body,
        rows // ROWS_BLK,
        [row_spec(v, first_row // ROWS_BLK) for v in lefts] + [matrix_spec(v) for v in rights],
        pl.BlockSpec((ROWS_BLK, width), lambda i: (i, 0)),
        jax.ShapeDtypeStruct((rows, width), out_type),
        lefts + [v[0] for v in rights],
    )


def project(a, parts):
    widths = [matrix_shape(v)[1] for v in parts[:-1]] + [matrix_shape(parts[-1])[0]]

    def body(left, *refs):
        out = refs[-1]
        at = 0
        for right, width in zip(refs[:-1], widths):
            turned = at + width == out.shape[1]
            out[:, at : at + width] = (nt if turned else nn)(left[...], right[...])
            at += width

    return local_call(
        body,
        a.shape[0] // ROWS_BLK,
        [row_spec(a)] + [matrix_spec(v) for v in parts],
        pl.BlockSpec((ROWS_BLK, sum(widths)), lambda i: (i, 0)),
        jax.ShapeDtypeStruct((a.shape[0], sum(widths)), f32),
        [a] + [v[0] for v in parts],
    )


def ff_forward(m, gate_w, up_w, far, ffp):
    ff = matrix_shape(gate_w)[0]

    def body(m_ref, gate_w, up_w, far_gate, far_up, gate_ref, up_ref, product_ref):
        m = m_ref[...]
        for slot, (gate_t, up_t) in enumerate(((gate_w, up_w), (far_gate, far_up))):
            gate, up = nt(m, gate_t[...]), nt(m, up_t[...])
            at = slot * ffp
            gate_ref[:, at : at + ff] = gate.astype(bf16)
            up_ref[:, at : at + ff] = up.astype(bf16)
            product_ref[:, at : at + ff] = (gate * jax.nn.sigmoid(gate) * up).astype(bf16)

    shape = (m.shape[0], 2 * ffp)
    parts = [gate_w, up_w, (far, (0, ff)), (far, (1, ff))]
    return local_call(
        body,
        m.shape[0] // ROWS_BLK,
        [row_spec(m)] + [matrix_spec(v) for v in parts],
        [pl.BlockSpec((ROWS_BLK, 2 * ffp), lambda i: (i, 0))] * 3,
        [jax.ShapeDtypeStruct(shape, bf16)] * 3,
        [m] + [v[0] for v in parts],
    )


def gate_pair(gate, up, dproduct):
    sig = jax.nn.sigmoid(gate)
    silu = gate * sig
    dgate = dproduct * up * (sig + silu * (1.0 - sig))
    return jnp.concatenate([dgate.astype(bf16), (dproduct * silu).astype(bf16)], axis=1), silu


def ff_backward(g, gate, up, product, down_w, far, ffp):
    ff = matrix_shape(down_w)[0]

    def body(g_ref, gate_ref, up_ref, product_ref, down_ref, far_ref, own_out, far_out, product_out):
        g = g_ref[...]
        for slot, (weight, out) in enumerate(((down_ref, own_out), (far_ref, far_out))):
            cols = slice(slot * ffp, slot * ffp + ff)
            out[...] = gate_pair(
                gate_ref[:, cols].astype(f32), up_ref[:, cols].astype(f32), nt(g, weight[...])
            )[0]
        product_out[...] = product_ref[:, :ff]

    rows = g.shape[0]
    parts = [down_w, (far, (2, ff))]
    return local_call(
        body,
        rows // ROWS_BLK,
        [row_spec(v) for v in (g, gate, up, product)] + [matrix_spec(v) for v in parts],
        [
            pl.BlockSpec((ROWS_BLK, 2 * ff), lambda i: (i, 0)),
            pl.BlockSpec((ROWS_BLK, 2 * ff), lambda i: (i, 0)),
            pl.BlockSpec((ROWS_BLK, ff), lambda i: (i, 0)),
        ],
        [
            jax.ShapeDtypeStruct((2 * rows, 2 * ff), bf16),
            jax.ShapeDtypeStruct((rows, 2 * ff), bf16),
            jax.ShapeDtypeStruct((2 * rows, ff), bf16),
        ],
        [g, gate, up, product] + [v[0] for v in parts],
    )


def ff_backward_far(m_all, g_all, dboth, product_all, gate_w, up_w, down_w):
    def body(m_ref, g_ref, gate_t, up_t, down_ref, _, __, own_out, product_out):
        gate, up = nt(m_ref[...], gate_t[...]), nt(m_ref[...], up_t[...])
        value, silu = gate_pair(gate, up, nt(g_ref[...], down_ref[...]))
        own_out[...] = value
        product_out[...] = (silu * up).astype(bf16)

    near = m_all.shape[0] // ROWS_BLK // 2
    parts = [gate_w, up_w, down_w]
    return local_call(
        body,
        near,
        [row_spec(m_all, near), row_spec(g_all, near)]
        + [matrix_spec(v) for v in parts]
        + [pl.BlockSpec(memory_space=pl.ANY)] * 2,
        [row_spec(dboth, near), row_spec(product_all, near)],
        [jax.ShapeDtypeStruct(v.shape, bf16) for v in (dboth, product_all)],
        [m_all, g_all] + [v[0] for v in parts] + [dboth, product_all],
        {5: 0, 6: 1},
    )


def ring_place(index, n):
    return jnp.where(index % 2 == 0, index // 2, n - 1 - index // 2)


def ring_index(place, n):
    return jnp.where(place < n // 2, 2 * place, 2 * (n - 1 - place) + 1)


MESH = pl.DeviceIdType.MESH


class Ring:
    def __init__(self, n, data, out, slots, sems):
        self.n, self.data, self.out, self.slots = n, data, out, slots
        self.send, self.recv, self.out_send, self.out_recv = sems
        self.me = ring_place(lax.axis_index("dp"), n)
        self.peers = [
            ring_index(lax.rem(self.me + 1, n), n),
            ring_index(lax.rem(self.me + n - 1, n), n),
        ]
        self.rows = data.shape[0] // (2 * n)

    def chunk(self, ref, way, back):
        which = lax.rem(self.me + 2 * self.n - (1, -1)[way] * back, self.n)
        return ref.at[pl.ds(pl.multiple_of((2 * which + way) * self.rows, 16), self.rows)]

    def partial(self, way, source, step):
        return pltpu.make_async_remote_copy(
            src_ref=source, dst_ref=self.slots.at[way, step],
            send_sem=self.send.at[way, step], recv_sem=self.recv.at[way, step],
            device_id={"dp": self.peers[way]}, device_id_type=MESH,
        )

    def final(self, way, step, back):
        part = self.chunk(self.out, way, back)
        return pltpu.make_async_remote_copy(
            src_ref=part, dst_ref=part,
            send_sem=self.out_send.at[way, step], recv_sem=self.out_recv.at[way, step],
            device_id={"dp": self.peers[way]}, device_id_type=MESH,
        )

    def start(self):
        for way in range(2):
            self.partial(way, self.chunk(self.data, way, 0), 0).start()

    def reduce(self, step):
        for way in range(2):
            slot = self.slots.at[way, step]
            self.partial(way, slot, step).wait_recv()
            part = self.chunk(self.data, way, step + 1)
            slot[...] = (slot[...].astype(f32) + part[...].astype(f32)).astype(bf16)

            @pl.when(step < self.n - 2)
            def _():
                self.partial(way, slot, step + 1).start()

    def turn(self):
        for way in range(2):
            self.chunk(self.out, way, -1)[...] = self.slots[way, self.n - 2]
            self.final(way, 0, -1).start()

    def gather(self, step):
        for way in range(2):
            self.final(way, step, step).wait_recv()

            @pl.when(step < self.n - 2)
            def _():
                self.final(way, step + 1, step).start()

    def sent(self, step):
        for way in range(2):
            self.partial(way, self.slots.at[way, step], step).wait_send()
            self.final(way, step, step - 1).wait_send()


def steps_of(lo, hi, *bodies):
    def body(step, carry):
        for each in bodies:
            each(step)
        return carry

    lax.fori_loop(lo, hi, body, 0)


def mix_sum_kernel(
    n, cuts, done, own, far, misc, out_done, out_own, out_misc, came, total, slot_a, slot_b, slot_c, slot_d,
    send, recv, out_send, out_recv, chip_send, chip_recv, sums, misc_came, misc_send, misc_recv,
):
    me = ring_place(lax.axis_index("dp"), n)
    member, row = lax.axis_index("head"), lax.axis_index("dp")
    swaps = [{"head": member ^ 1}, {"head": member ^ 2}]
    swaps += [{"dp": row ^ (1 << bit)} for bit in range(n.bit_length() - 1)]
    peers = swaps + [
        {"dp": ring_index(lax.rem(me + 1, n), n)},
        {"dp": ring_index(lax.rem(me + n - 1, n), n)},
    ]
    barrier = pltpu.get_barrier_semaphore()
    for peer in peers:
        pl.semaphore_signal(barrier, inc=1, device_id=peer, device_id_type=MESH)
    pl.semaphore_wait(barrier, len(peers))

    def small(step):
        return pltpu.make_async_remote_copy(
            src_ref=sums.at[step], dst_ref=misc_came.at[step],
            send_sem=misc_send.at[step], recv_sem=misc_recv.at[step],
            device_id=swaps[step], device_id_type=MESH,
        )

    taken = [0]

    def small_step():
        step = taken[0]
        if step == len(swaps):
            return
        small(step).wait()
        sums[step + 1] = sums[step] + misc_came[step]
        taken[0] += 1
        if step + 1 < len(swaps):
            small(step + 1).start()

    swap = pltpu.make_async_remote_copy(
        src_ref=far, dst_ref=came, send_sem=chip_send, recv_sem=chip_recv,
        device_id={"head": member ^ 2}, device_id_type=MESH,
    )
    def ring(which, data, out, cut, slots):
        rows = slice(*cut)
        sems = [v.at[which] for v in (send, recv, out_send, out_recv)]
        return Ring(n, data.at[rows], out.at[rows], slots, sems)

    rings = (
        (0, done, out_done, cuts[0], slot_a),
        (1, done, out_done, cuts[1], slot_b),
        (2, total, out_own, cuts[2], slot_c),
        (3, total, out_own, cuts[3], slot_d),
    )
    first, second = ([ring(*v) for v in pair if v[3][1] > v[3][0]] for pair in (rings[:2], rings[2:]))

    def each(rings, name):
        return [getattr(v, name) for v in rings]

    def now(steps):
        for step in steps:
            step()

    middle, last = (n - 1) // 2, n - 1
    sums[0] = misc[...]
    small(0).start()
    swap.start()
    now(each(first, "start"))
    steps_of(0, middle, *each(first, "reduce"))
    small_step()
    steps_of(middle, last, *each(first, "reduce"))
    now(each(first, "turn"))
    small_step()
    swap.wait()
    total[...] = (own[...].astype(f32) + came[...].astype(f32)).astype(bf16)
    now(each(second, "start"))
    together = each(first, "gather") + each(second, "reduce")
    steps_of(0, middle, *together)
    small_step()
    steps_of(middle, last, *together)
    now(each(second, "turn"))
    small_step()
    steps_of(0, middle, *each(second, "gather"))
    small_step()
    steps_of(middle, last, *each(second, "gather"))
    for _ in swaps:
        small_step()
    out_misc[...] = sums[len(swaps)]
    steps_of(0, last, *each(first + second, "sent"))


def mix_sum(parts, own, far, misc, n):
    if n == 1:
        misc = misc + core_swap(misc)
        own = (own.astype(f32) + chip_swap(far).astype(f32)).astype(bf16)
        return jnp.concatenate(parts, axis=0), own, misc + chip_swap(misc)
    rows, cols = own.shape
    done_rows = sum(v.shape[0] for v in parts)
    spare = -done_rows % (32 * n)
    done_rows += spare
    done = jnp.concatenate(list(parts) + ([jnp.zeros((spare, cols), bf16)] if spare else []), axis=0)
    swaps = 2 + n.bit_length() - 1

    def two(total):
        lines = total // (32 * n)
        cut = (lines + 1) // 2 * 32 * n
        return (0, cut), (cut, total)

    cuts = two(done_rows) + two(rows)

    def body(*refs):
        mix_sum_kernel(n, cuts, *refs)

    vmem = pl.BlockSpec(memory_space=pltpu.VMEM)
    return pl.pallas_call(
        body,
        in_specs=[vmem] * 4,
        out_specs=[vmem] * 3,
        out_shape=[
            jax.ShapeDtypeStruct((done_rows, cols), bf16),
            jax.ShapeDtypeStruct((rows, cols), bf16),
        ]
        + [jax.ShapeDtypeStruct(misc.shape, f32)],
        scratch_shapes=[
            pltpu.VMEM((rows, cols), bf16),
            pltpu.VMEM((rows, cols), bf16),
        ]
        + [
            pltpu.VMEM((2, n - 1, max(16, (stop - at) // (2 * n)), cols), bf16) for at, stop in cuts
        ]
        + [pltpu.SemaphoreType.DMA((4, 2, n - 1))] * 4
        + [pltpu.SemaphoreType.DMA] * 2
        + [
            pltpu.VMEM((swaps + 1,) + misc.shape, f32),
            pltpu.VMEM((swaps,) + misc.shape, f32),
            pltpu.SemaphoreType.DMA((swaps,)),
            pltpu.SemaphoreType.DMA((swaps,)),
        ],
        compiler_params=pltpu.CompilerParams(
            collective_id=0, has_side_effects=True, vmem_limit_bytes=VMEM_LIMIT
        ),
    )(done, own, far, misc)


def norm_scale(hidden):
    return lax.rsqrt(jnp.mean(hidden * hidden, axis=-1, keepdims=True) + epsilon)


def norm_low(hidden, gain):
    return (hidden * norm_scale(hidden) * gain).astype(bf16)


def norm_back(hidden, gain, grad_normed):
    scale = norm_scale(hidden)
    weighted = grad_normed * gain
    grad_hidden = scale * weighted - hidden * (scale * scale * scale) * jnp.mean(
        weighted * hidden, axis=-1, keepdims=True
    )
    return grad_hidden, jnp.sum(grad_normed * hidden * scale, axis=0)


def core_swap(value):
    return lax.ppermute(value, "head", [(i, i ^ 1) for i in range(4)])


def chip_swap(value):
    return lax.ppermute(value, "head", [(i, i ^ 2) for i in range(4)])


def dp_slice(own):
    parts = own.reshape((lax.axis_size("dp"), -1) + own.shape[1:])
    return lax.dynamic_index_in_dim(parts, lax.axis_index("dp"), 0, keepdims=False)


def dp_ring():
    n = lax.axis_size("dp")
    return list(range(0, n, 2)) + list(range(n - 1, 0, -2)) if n > 1 else [0]


def after(value, *others):
    return lax.optimization_barrier((value,) + others)[0]


def per_device(
    tokens, doc_starts, grad_out, norm_one, w_query, w_key, w_value, w_outgate, w_rank, w_decay,
    decay_bias, group_gain, w_out, norm_two, w_gate, w_up, w_down,
):
    shard_len, width = tokens.shape[1:]
    ndoc = doc_starts.shape[1]
    ff = w_gate.shape[2]
    ffp = -(-ff // 128) * 128
    rank = w_decay.shape[1]
    member = lax.axis_index("head")
    core = member % 2
    chip = member // 2
    meta = jnp.concatenate(
        [doc_starts[0], jnp.stack([chip * (2 * shard_len), core]).astype(jnp.int32)]
    )
    mixer = Mixer(meta, ndoc, 2 * shard_len)

    def mix_pack(layer):
        return jnp.concatenate(
            [w_query[layer], w_key[layer], w_value[layer], w_outgate[layer]], axis=1
        )

    gate_t, up_t, rank_t = (jnp.swapaxes(v, 1, 2) for v in (w_gate, w_up, w_rank))

    def ff_slice(layer, wait):
        part = jnp.concatenate([dp_slice(v[layer]) for v in (gate_t, up_t, w_down)], axis=0)
        return chip_swap(after(part, wait))

    def ff_gather(part):
        dp = lax.axis_size("dp")
        whole = lax.all_gather(part, "dp", axis=0, tiled=True)
        return jnp.swapaxes(whole.reshape(dp, 3, ff // dp, width), 0, 1).reshape(3 * ff, width)

    def with_partner(local):
        return jnp.concatenate([local, core_swap(local)], axis=0)

    def settle(terms):
        sent = core_swap(sum_of_dots(terms, shard_len, shard_len, bf16))
        return sum_of_dots(terms, 0, shard_len, f32) + sent.astype(f32)

    small = jnp.concatenate([w_decay.astype(f32), decay_bias[:, None, :]], axis=1)
    small = jnp.concatenate([small, chip_swap(small)], axis=2)
    ff_part = ff_slice(0, meta)
    ff_far = ff_gather(ff_part)
    mix_own = mix_pack(0)
    mix_far = chip_swap(after(mix_own, ff_part))
    out_far = chip_swap(after(w_out[0], ff_part))
    next_part = ff_slice(1, mix_far)

    grad = grad_out[0].astype(f32)
    hidden = tokens[0].astype(f32)
    saved = []
    for layer in range(LAYERS):
        hidden_in = hidden
        a = with_partner(norm_low(hidden, norm_one[layer]))
        x = project(a, ((mix_own, None), (mix_far, None), (rank_t, layer)))
        wdec, bias = small[layer, :rank], small[layer, rank:]
        run, states, cum, final = mixer.states(x, wdec, bias)
        got = chip_swap(after(final, next_part) if layer == 0 else after(final, g_y, out_far))
        first = got[::-1] * chip.astype(bf16)
        gain = group_gain[layer][None]
        gated, mixed = mixer.mix(x, run, states, cum, first, gain)
        if layer + 1 < LAYERS:
            next_own = mix_pack(layer + 1)
            next_mix = chip_swap(after(next_own, got))
            next_out = chip_swap(after(w_out[layer + 1], got))
            next_far = ff_gather(next_part)
        hidden_mid = hidden + settle(
            [(gated, 0, (w_out, layer), False), (gated, HV, (out_far, None), False)]
        )
        m_own = norm_low(hidden_mid, norm_two[layer])
        m = with_partner(m_own)
        gate, up, product = ff_forward(m, (gate_t, layer), (up_t, layer), ff_far, ffp)
        if layer + 1 < LAYERS:
            product = after(product, next_mix)
        hidden = hidden_mid + settle(
            [(product, 0, (w_down, layer), False), (product, ffp, (ff_far, (2, ff)), False)]
        )
        saved.append(
            (hidden_in, hidden_mid, a, m_own, m, x, run, states, cum, first, mixed, gated, gate, up, product,
             mix_own, mix_far, out_far, ff_far)
        )
        if layer + 1 < LAYERS:
            mix_own, mix_far, out_far, ff_far = next_own, next_mix, next_out, next_far
            g_own = grad_out[0]
            g_y = chip_swap(after(g_own, next_mix))
    result = hidden.astype(bf16)[None]

    ff_grads, misc_grads = [None] * LAYERS, [None] * LAYERS
    for layer in reversed(range(LAYERS)):
        (
            hidden_in, hidden_mid, a, m_own, m, x, run, states, cum, first, mixed, gated, gate, up, product,
            mix_own, mix_far, out_far, ff_far,
        ) = saved[layer]
        gain = group_gain[layer][None]
        wdec, bias = small[layer, :rank], small[layer, rank:]
        if layer + 1 < LAYERS:
            g_own = grad.astype(bf16)
            g_y = chip_swap(g_own)
            mix_done = (own.astype(f32) + chip_swap(after(far, g_y)).astype(f32)).astype(bf16)
            mix_done = lax.psum(mix_done, "dp", axis_index_groups=[dp_ring()])
        m_y = chip_swap(m_own if layer + 1 == LAYERS else after(m_own, dfar))
        m_all = jnp.concatenate([m, m_y, core_swap(m_y)], axis=0)
        g = with_partner(g_own)
        g_all = jnp.concatenate([g, g_y, core_swap(g_y)], axis=0)
        dboth, dfar, product_all = ff_backward(g, gate, up, product, (w_down, layer), ff_far, ffp)
        back_mid, gain_two = norm_back(
            hidden_mid,
            norm_two[layer],
            settle(
                [
                    (dboth, 0, (gate_t, layer), False),
                    (dboth, ff, (up_t, layer), False),
                    (dfar, 0, (ff_far, (0, 2 * ff)), False),
                ]
            ),
        )
        dboth, product_all = ff_backward_far(
            m_all, g_all, dboth, product_all, (gate_t, layer), (up_t, layer), (w_down, layer)
        )
        in_grad = tn(dboth, m_all).astype(bf16)
        down_grad = tn(product_all, g_all).astype(bf16)
        grad = grad + back_mid
        g_mix = with_partner(grad.astype(bf16))
        if layer + 1 == LAYERS:
            g_mix = after(g_mix, in_grad, down_grad)
        g_wout = tn(g_mix, gated).astype(bf16)
        dmixed, doutgate, dstates, dcum, dfinal, dgain = mixer.back_states(
            x, run, mixed, g_mix, w_out[layer], out_far, gain
        )
        got = chip_swap(dfinal)
        dlast = got[::-1] * (1 - chip).astype(bf16)
        dx, dwdec, dbias = mixer.back(
            x, run, states, cum, first, dmixed, doutgate, dstates, dcum, dlast, wdec, bias
        )
        g_wmix = tn(a, dx[:, : 2 * HEAD_COLS]).astype(bf16)
        g_rank = tn(dx[:, 2 * HEAD_COLS :], a)
        far = jnp.concatenate([g_wmix[:, HEAD_COLS:], g_wout[:, HV:]], axis=1)
        own = jnp.concatenate([g_wmix[:, :HEAD_COLS], g_wout[:, :HV]], axis=1)
        back_first, gain_one = norm_back(hidden_in, norm_one[layer], settle(
            [
                (dx, 0, (mix_own, None), True),
                (dx, HEAD_COLS, (mix_far, None), True),
                (dx, 2 * HEAD_COLS, (rank_t, layer), False),
            ]
        ))
        grad = grad + back_first
        if layer > 0:
            ff_grads[layer] = lax.psum((in_grad, down_grad), "dp")
        else:
            ff_parts = (in_grad, down_grad)
            ff_grads[1] = after(ff_grads[1], grad)
        heads = jnp.concatenate([dwdec, dbias], axis=0)
        places = lax.iota(jnp.int32, 4)[:, None, None]
        heads = jnp.where(places == member, heads[None, :, :HK], 0.0) + jnp.where(
            places == member ^ 2, heads[None, :, HK:], 0.0
        )
        misc_grads[layer] = jnp.concatenate(
            [g_rank.reshape(-1), gain_one, gain_two, dgain[0], heads.reshape(-1)]
        )

    misc = jnp.stack(misc_grads)
    length = misc.shape[1]
    misc = jnp.pad(misc.reshape(-1), (0, -misc.size % 1024)).reshape(-1, 128)
    ff_done, first_mix, misc = mix_sum(ff_parts, own, far, misc, lax.axis_size("dp"))
    mix_grads = [first_mix, after(mix_done, grad)]
    ff_grads[0] = (ff_done[: 2 * ff], ff_done[2 * ff : 3 * ff])
    misc = misc.reshape(-1)[: LAYERS * length].reshape(LAYERS, length)
    sizes = (rank * width, width, width, HV, 4 * (rank + 1) * HK)
    pieces, at = [], 0
    for size in sizes:
        pieces.append(misc[:, at : at + size])
        at += size
    heads = lax.dynamic_index_in_dim(
        pieces[4].reshape(LAYERS, 4, rank + 1, HK), member, axis=1, keepdims=False
    )

    def rows_of(grads, start, stop):
        return jnp.stack([g[start:stop].astype(f32) for g in grads])

    def turned(grads, start, stop):
        return jnp.stack([g[start:stop].T.astype(f32) for g in grads])

    def cols_of(grads, start, stop):
        return jnp.stack([g[:, start:stop].astype(f32) for g in grads])

    return (
        result,
        grad[None],
        pieces[1],
        cols_of(mix_grads, 0, HK),
        cols_of(mix_grads, HK, 2 * HK),
        cols_of(mix_grads, 2 * HK, 2 * HK + HV),
        cols_of(mix_grads, 2 * HK + HV, HEAD_COLS),
        jnp.swapaxes(pieces[0].reshape(LAYERS, rank, width), 1, 2),
        heads[:, :rank],
        heads[:, rank],
        pieces[3],
        jnp.stack([g[:, HEAD_COLS:].T.astype(f32) for g in mix_grads]),
        pieces[2],
        turned([g[0] for g in ff_grads], 0, ff),
        turned([g[0] for g in ff_grads], ff, 2 * ff),
        rows_of([g[1] for g in ff_grads], 0, ff),
    )


def solution(mesh):
    cols = P(None, None, "head")
    rows = P(None, "head", None)
    place = P("dp", "head", None)
    return jax.shard_map(
        per_device,
        mesh=mesh,
        in_specs=(
            place, P("dp", None), place, P(), cols, cols, cols, cols, P(), cols,
            P(None, "head"), P(), rows, P(), cols, cols, rows,
        ),
        out_specs=(
            place, place, P(), cols, cols, cols, cols, P(), cols, P(None, "head"), P(), rows,
            P(), cols, cols, rows,
        ),
        check_vma=False,
    )
```

```python
import jax
import jax.numpy as jnp
from jax import lax
from jax.experimental import pallas as pl
from jax.experimental.pallas import tpu as pltpu
from jax.sharding import PartitionSpec as P

LAYERS = 2
HK = 128
HV = 256
HEAD_COLS = 2 * HK + 2 * HV
BLK = 128
MID = BLK // 2 - 1
SUB = 2
epsilon = 1e-06
highest = lax.Precision.HIGHEST
VMEM_LIMIT = 48 * 1024 * 1024

f32 = jnp.float32
bf16 = jnp.bfloat16


def nn(left, right):
    return lax.dot_general(left, right, (((1,), (0,)), ((), ())), preferred_element_type=f32)


def nt(left, right):
    return lax.dot_general(left, right, (((1,), (1,)), ((), ())), preferred_element_type=f32)


def tn(left, right):
    return lax.dot_general(left, right, (((0,), (0,)), ((), ())), preferred_element_type=f32)


def doc_count(meta, ndoc, place):
    total = (meta[0] <= place).astype(jnp.int32)
    for which in range(1, ndoc):
        total = total + (meta[which] <= place).astype(jnp.int32)
    return total


def block_masks(meta, ndoc, start):
    rows = lax.broadcasted_iota(jnp.int32, (BLK, BLK), 0) + start
    cols = lax.broadcasted_iota(jnp.int32, (BLK, BLK), 1) + start
    row_ids = doc_count(meta, ndoc, rows)
    col_ids = doc_count(meta, ndoc, cols)
    id_prev = doc_count(meta, ndoc, start - 1)
    id_last = doc_count(meta, ndoc, start + BLK - 1)
    allowed = (rows >= cols) & (row_ids == col_ids)
    carried = jnp.where(row_ids == id_prev, 1.0, 0.0)
    same = jnp.where(row_ids == id_last, 1.0, 0.0)
    keep = jnp.where(id_last == id_prev, 1.0, 0.0)
    return allowed, carried, same, keep


def split_dot(ones_mat, value, dot):
    high = value.astype(bf16)
    low = (value - high.astype(f32)).astype(bf16)
    return dot(ones_mat, high) + dot(ones_mat, low)


def tri_ones():
    rows = lax.broadcasted_iota(jnp.int32, (BLK, BLK), 0)
    cols = lax.broadcasted_iota(jnp.int32, (BLK, BLK), 1)
    return jnp.where(rows >= cols, 1.0, 0.0).astype(bf16)


def head_parts(x_ref, slot):
    at = slot * HEAD_COLS
    query = x_ref[:, at : at + HK] * (HK**-0.5)
    key = x_ref[:, at + HK : at + 2 * HK]
    value = x_ref[:, at + 2 * HK : at + 2 * HK + HV]
    outgate = x_ref[:, at + 2 * HK + HV : at + HEAD_COLS]
    return query, key, value, outgate


def decay_before(x_ref, wdec_ref, bias_ref):
    ranked = x_ref[:, 2 * HEAD_COLS :]
    return jnp.dot(ranked, wdec_ref[...], precision=highest, preferred_element_type=f32) + bias_ref[...]


def states_kernel(ndoc, block, meta, x_ref, wdec_ref, bias_ref, run_ref, state_ref, cum_ref, final_ref, state, cum):
    start = meta[ndoc] + block * BLK
    _, _, same, keep = block_masks(meta, ndoc, start)
    before = decay_before(x_ref, wdec_ref, bias_ref)
    decays = (jnp.minimum(before, 0.0) - jnp.log1p(jnp.exp(-jnp.abs(before)))) * (1.0 / 16.0)
    running = split_dot(tri_ones(), decays, nn)
    run_ref[...] = running
    ending = running[BLK - 1 :, :]
    factor = jnp.exp(ending) * keep
    cum_ref[0] = cum[...]
    cum[...] = cum[...] * factor
    for slot in range(2):
        lanes = slice(slot * HK, slot * HK + HK)
        _, key, value, _ = head_parts(x_ref, slot)
        moved = (key * jnp.exp(ending[:, lanes] - running[:, lanes]) * same).astype(bf16)
        old = state[slot]
        state_ref[0, slot] = old.astype(bf16)
        new = old * factor[:, lanes] + tn(value.astype(bf16), moved)
        state[slot] = new
        final_ref[slot] = new.astype(bf16)


def mix_kernel(ndoc, block, meta, x_ref, run_ref, state_ref, cum_ref, first_ref, gain_ref, gated_ref, mixed_ref):
    start = meta[ndoc] + block * BLK
    allowed, carried, _, _ = block_masks(meta, ndoc, start)
    gain = gain_ref[...]
    for slot in range(2):
        lanes = slice(slot * HK, slot * HK + HK)
        cols = slice(slot * HV, slot * HV + HV)
        query, key, value, outgate = head_parts(x_ref, slot)
        running = run_ref[:, lanes]
        middle = running[MID : MID + 1, :]
        rel_query = (query * jnp.exp(running - middle)).astype(bf16)
        rel_key = (key * jnp.exp(middle - running)).astype(bf16)
        scores = jnp.where(allowed, nt(rel_query, rel_key), 0.0).astype(bf16)
        far_query = (query * jnp.exp(running) * carried).astype(bf16)
        state = (state_ref[0, slot].astype(f32) + first_ref[slot].astype(f32) * cum_ref[0][:, lanes]).astype(bf16)
        mixed = nn(scores, value.astype(bf16)) + nt(far_query, state)
        scale = lax.rsqrt(jnp.maximum(jnp.mean(mixed * mixed, axis=-1, keepdims=True), 1.0))
        gated_ref[:, cols] = (mixed * scale * gain * outgate * jax.nn.sigmoid(outgate)).astype(bf16)
        mixed_ref[:, cols] = mixed.astype(bf16)


def back_states_kernel(
    ndoc, block, meta, x_ref, run_ref, mixed_ref, grad_ref, own_out_ref, far_out_ref, gain_ref,
    dmixed_ref, doutgate_ref, dstate_ref, cum_ref, final_ref, dgain_ref, state, cum,
):
    start = meta[ndoc] + block * BLK
    _, carried, _, keep = block_masks(meta, ndoc, start)
    gain = gain_ref[...]
    running = run_ref[...]
    factor = jnp.exp(running[BLK - 1 :, :]) * keep
    cum_ref[0] = cum[...]
    cum[...] = cum[...] * factor
    for slot in range(2):
        lanes = slice(slot * HK, slot * HK + HK)
        cols = slice(slot * HV, slot * HV + HV)
        query, _, _, outgate = head_parts(x_ref, slot)
        mixed = mixed_ref[:, cols].astype(f32)
        dgated = nt(grad_ref[...], (own_out_ref, far_out_ref)[slot][...])
        mean = jnp.mean(mixed * mixed, axis=-1, keepdims=True)
        scale = lax.rsqrt(jnp.maximum(mean, 1.0))
        sig = jax.nn.sigmoid(outgate)
        silu = outgate * sig
        dnormed = dgated * silu
        plain = mixed * scale
        doutgate_ref[:, cols] = (dgated * plain * gain * (sig + silu * (1.0 - sig))).astype(bf16)
        dgain_ref[...] += jnp.sum(dnormed * plain, axis=0, keepdims=True)
        weighted = dnormed * gain
        inner = jnp.where(mean > 1.0, jnp.mean(weighted * plain, axis=-1, keepdims=True), 0.0)
        dmixed = (scale * (weighted - plain * inner)).astype(bf16)
        dmixed_ref[:, cols] = dmixed
        far_query = (query * jnp.exp(running[:, lanes]) * carried).astype(bf16)
        old = state[slot]
        dstate_ref[0, slot] = old.astype(bf16)
        new = old * factor[:, lanes] + tn(dmixed, far_query)
        state[slot] = new
        final_ref[slot] = new.astype(bf16)


def back_kernel(
    ndoc, block, meta, x_ref, run_ref, state_ref, cum_ref, first_ref, dmixed_ref, doutgate_ref,
    dstate_ref, dcum_ref, dlast_ref, wdec_ref, bias_ref, dx_ref, dwdec_ref, dbias_ref,
):
    start = meta[ndoc] + block * BLK
    allowed, carried, same, keep = block_masks(meta, ndoc, start)
    last_row = lax.broadcasted_iota(jnp.int32, (BLK, HK), 0) == BLK - 1
    drunning = []
    for slot in range(2):
        lanes = slice(slot * HK, slot * HK + HK)
        cols = slice(slot * HV, slot * HV + HV)
        at = slot * HEAD_COLS
        query, key, value, _ = head_parts(x_ref, slot)
        running = run_ref[:, lanes]
        middle = running[MID : MID + 1, :]
        ending = running[BLK - 1 :, :]
        up = jnp.exp(running - middle)
        down = jnp.exp(middle - running)
        far = jnp.exp(running) * carried
        near = jnp.exp(ending - running) * same
        rel_query = (query * up).astype(bf16)
        rel_key = (key * down).astype(bf16)
        far_query = (query * far).astype(bf16)
        moved = (key * near).astype(bf16)
        value = value.astype(bf16)
        scores = jnp.where(allowed, nt(rel_query, rel_key), 0.0).astype(bf16)
        state = state_ref[0, slot].astype(f32) + first_ref[slot].astype(f32) * cum_ref[0][:, lanes]
        dstate = dstate_ref[0, slot].astype(f32) + dlast_ref[slot].astype(f32) * dcum_ref[0][:, lanes]
        state_low = state.astype(bf16)
        dstate_low = dstate.astype(bf16)
        dmixed = dmixed_ref[:, cols]
        dvalue = tn(scores, dmixed) + nt(moved, dstate_low)
        dscores = jnp.where(allowed, nt(dmixed, value), 0.0).astype(bf16)
        drel_query = nn(dscores, rel_key)
        drel_key = tn(dscores, rel_query)
        dfar = nn(dmixed, state_low)
        dmoved = nn(value, dstate_low)
        dquery = drel_query * up + dfar * far
        dkey = drel_key * down + dmoved * near
        moved_grad = dmoved * moved.astype(f32)
        dending = jnp.sum(moved_grad, axis=0, keepdims=True) + jnp.sum(
            state * dstate, axis=0, keepdims=True
        ) * (jnp.exp(ending) * keep)
        drun = (
            drel_query * rel_query.astype(f32)
            - drel_key * rel_key.astype(f32)
            + dfar * far_query.astype(f32)
            - moved_grad
        )
        drunning.append(drun + jnp.where(last_row, dending, 0.0))
        dx_ref[:, at : at + HK] = (dquery * (HK**-0.5)).astype(bf16)
        dx_ref[:, at + HK : at + 2 * HK] = dkey.astype(bf16)
        dx_ref[:, at + 2 * HK : at + 2 * HK + HV] = dvalue.astype(bf16)
        dx_ref[:, at + 2 * HK + HV : at + HEAD_COLS] = doutgate_ref[:, cols]
    drun_both = jnp.concatenate(drunning, axis=1)
    ddecay = split_dot(tri_ones(), drun_both, tn)
    before = decay_before(x_ref, wdec_ref, bias_ref)
    dbefore = ddecay * (1.0 / 16.0) * jax.nn.sigmoid(-before)
    dbias_ref[...] += jnp.sum(dbefore, axis=0, keepdims=True)
    ranked = x_ref[:, 2 * HEAD_COLS :]
    dlow = dbefore.astype(bf16)
    dwdec_ref[...] += tn(ranked.astype(bf16), dlow)
    dx_ref[:, 2 * HEAD_COLS :] = nt(dlow, wdec_ref[...].astype(bf16)).astype(bf16)


def kernel_params():
    return pltpu.CompilerParams(dimension_semantics=("arbitrary",), vmem_limit_bytes=VMEM_LIMIT)


def sub_blocks(kernel, ndoc, tokens, rows, blocks, reverse, starts):
    steps = tokens // (BLK * SUB)

    def body(meta, *refs):
        step = pl.program_id(0)

        @pl.when(step == 0)
        def _():
            for which, value in starts:
                refs[which][...] = jnp.full_like(refs[which], value)

        first = (steps - 1 - step if reverse else step) * SUB
        for sub in reversed(range(SUB)) if reverse else range(SUB):
            views = [
                ref.at[sub * BLK : (sub + 1) * BLK] if i in rows
                else ref.at[sub : sub + 1] if i in blocks
                else ref
                for i, ref in enumerate(refs)
            ]
            kernel(ndoc, first + sub, meta, *views)

    return body


class Mixer:
    def __init__(self, meta, ndoc, tokens):
        self.meta = meta
        self.ndoc = ndoc
        self.tokens = tokens
        self.nblk = tokens // BLK
        self.steps = self.nblk // SUB

    def rows(self, width, reverse=False):
        steps, core = self.steps, self.ndoc + 1

        def place(step, meta):
            time = steps - 1 - step if reverse else step
            return (lax.rem(time + meta[core] * (steps // 2), steps), 0)

        return pl.BlockSpec((BLK * SUB, width), place)

    def per_block(self, shape, reverse=False):
        steps = self.steps
        zeros = (0,) * len(shape)
        return pl.BlockSpec(
            (SUB,) + shape, lambda step, meta: ((steps - 1 - step if reverse else step),) + zeros
        )

    def whole(self, shape):
        zeros = (0,) * len(shape)
        return pl.BlockSpec(shape, lambda step, meta: zeros)

    def call(self, kernel, layout, in_specs, out_specs, out_shape, scratch, *args):
        return pl.pallas_call(
            sub_blocks(kernel, self.ndoc, self.tokens, *layout),
            grid_spec=pltpu.PrefetchScalarGridSpec(
                num_scalar_prefetch=1,
                grid=(self.steps,),
                in_specs=in_specs,
                out_specs=out_specs,
                scratch_shapes=scratch,
            ),
            out_shape=[jax.ShapeDtypeStruct(s, d) for s, d in out_shape],
            cost_estimate=NO_COST,
            compiler_params=kernel_params(),
        )(self.meta, *args)

    def state_scratch(self):
        return [pltpu.VMEM((2, HV, HK), f32), pltpu.VMEM((1, 2 * HK), f32)]

    def states(self, x, wdec, bias):
        n = self.nblk
        return self.call(
            states_kernel,
            ((0, 3), (4, 5), False, ((7, 0.0), (8, 1.0))),
            [self.rows(x.shape[1]), self.whole(wdec.shape), self.whole(bias.shape)],
            [
                self.rows(2 * HK),
                self.per_block((2, HV, HK)),
                self.per_block((1, 2 * HK)),
                self.whole((2, HV, HK)),
            ],
            [
                ((self.tokens, 2 * HK), f32),
                ((n, 2, HV, HK), bf16),
                ((n, 1, 2 * HK), f32),
                ((2, HV, HK), bf16),
            ],
            self.state_scratch(),
            x, wdec, bias,
        )

    def mix(self, x, run, states, cum, first, gain):
        return self.call(
            mix_kernel,
            ((0, 1, 6, 7), (2, 3), False, ()),
            [
                self.rows(x.shape[1]),
                self.rows(2 * HK),
                self.per_block((2, HV, HK)),
                self.per_block((1, 2 * HK)),
                self.whole((2, HV, HK)),
                self.whole(gain.shape),
            ],
            [self.rows(2 * HV), self.rows(2 * HV)],
            [((self.tokens, 2 * HV), bf16), ((self.tokens, 2 * HV), bf16)],
            [],
            x, run, states, cum, first, gain,
        )

    def back_states(self, x, run, mixed, grad, own_out, far_out, gain):
        n = self.nblk
        return self.call(
            back_states_kernel,
            ((0, 1, 2, 3, 7, 8), (9, 10), True, ((12, 0.0), (13, 0.0), (14, 1.0))),
            [
                self.rows(x.shape[1], True),
                self.rows(2 * HK, True),
                self.rows(2 * HV, True),
                self.rows(grad.shape[1], True),
                self.whole(own_out.shape),
                self.whole(far_out.shape),
                self.whole(gain.shape),
            ],
            [
                self.rows(2 * HV, True),
                self.rows(2 * HV, True),
                self.per_block((2, HV, HK), True),
                self.per_block((1, 2 * HK), True),
                self.whole((2, HV, HK)),
                self.whole((1, HV)),
            ],
            [
                ((self.tokens, 2 * HV), bf16),
                ((self.tokens, 2 * HV), bf16),
                ((n, 2, HV, HK), bf16),
                ((n, 1, 2 * HK), f32),
                ((2, HV, HK), bf16),
                ((1, HV), f32),
            ],
            self.state_scratch(),
            x, run, mixed, grad, own_out, far_out, gain,
        )

    def back(self, x, run, states, cum, first, dmixed, doutgate, dstates, dcum, dlast, wdec, bias):
        rank = wdec.shape[0]
        return self.call(
            back_kernel,
            ((0, 1, 5, 6, 12), (2, 3, 7, 8), False, ((13, 0.0), (14, 0.0))),
            [
                self.rows(x.shape[1]),
                self.rows(2 * HK),
                self.per_block((2, HV, HK)),
                self.per_block((1, 2 * HK)),
                self.whole((2, HV, HK)),
                self.rows(2 * HV),
                self.rows(2 * HV),
                self.per_block((2, HV, HK)),
                self.per_block((1, 2 * HK)),
                self.whole((2, HV, HK)),
                self.whole(wdec.shape),
                self.whole(bias.shape),
            ],
            [self.rows(x.shape[1]), self.whole((rank, 2 * HK)), self.whole((1, 2 * HK))],
            [
                ((self.tokens, x.shape[1]), bf16),
                ((rank, 2 * HK), f32),
                ((1, 2 * HK), f32),
            ],
            [],
            x, run, states, cum, first, dmixed, doutgate, dstates, dcum, dlast, wdec, bias,
        )


ROWS_BLK = 256


def matrix_spec(part):
    array, which = part
    if array.ndim == 3:
        return pl.BlockSpec((None,) + array.shape[1:], lambda i: (which, 0, 0))
    if which is None:
        return pl.BlockSpec(array.shape, lambda i: (0, 0))
    at, rows = which
    return pl.BlockSpec((rows, array.shape[1]), lambda i: (at, 0))


def matrix_shape(part):
    array, which = part
    if array.ndim == 3 or which is None:
        return array.shape[-2:]
    return which[1], array.shape[1]


def row_spec(array, first=0):
    return pl.BlockSpec((ROWS_BLK, array.shape[1]), lambda i: (i + first, 0))


NO_COST = pl.CostEstimate(flops=0, bytes_accessed=0, transcendentals=0)


def local_call(body, grid, in_specs, out_specs, out_shape, args, scratch=()):
    return pl.pallas_call(
        body,
        grid=(grid,),
        in_specs=in_specs,
        out_specs=out_specs,
        out_shape=out_shape,
        scratch_shapes=list(scratch),
        cost_estimate=NO_COST,
        compiler_params=pltpu.CompilerParams(
            dimension_semantics=("arbitrary",), vmem_limit_bytes=VMEM_LIMIT
        ),
    )(*args)


def sum_of_dots(terms, first_row, rows, out_type):
    lefts = []
    for left, _, _, _ in terms:
        if not any(left is seen for seen in lefts):
            lefts.append(left)
    which = [next(i for i, seen in enumerate(lefts) if seen is left) for left, _, _, _ in terms]
    rights = [right for _, _, right, _ in terms]
    width = matrix_shape(rights[0])[0 if terms[0][3] else 1]

    def body(*refs):
        left_refs, right_refs, out = refs[: len(lefts)], refs[len(lefts) : -1], refs[-1]
        total = None
        for (_, at, _, turned), index, right in zip(terms, which, right_refs):
            depth = right.shape[1] if turned else right.shape[0]
            part = (nt if turned else nn)(left_refs[index][:, at : at + depth], right[...])
            total = part if total is None else total + part
        out[...] = total.astype(out_type)

    return local_call(
        body,
        rows // ROWS_BLK,
        [row_spec(v, first_row // ROWS_BLK) for v in lefts] + [matrix_spec(v) for v in rights],
        pl.BlockSpec((ROWS_BLK, width), lambda i: (i, 0)),
        jax.ShapeDtypeStruct((rows, width), out_type),
        lefts + [v[0] for v in rights],
    )


def project(a, parts):
    widths = [matrix_shape(v)[1] for v in parts[:-1]] + [matrix_shape(parts[-1])[0]]

    def body(left, *refs):
        out = refs[-1]
        at = 0
        for right, width in zip(refs[:-1], widths):
            turned = at + width == out.shape[1]
            out[:, at : at + width] = (nt if turned else nn)(left[...], right[...])
            at += width

    return local_call(
        body,
        a.shape[0] // ROWS_BLK,
        [row_spec(a)] + [matrix_spec(v) for v in parts],
        pl.BlockSpec((ROWS_BLK, sum(widths)), lambda i: (i, 0)),
        jax.ShapeDtypeStruct((a.shape[0], sum(widths)), f32),
        [a] + [v[0] for v in parts],
    )


def piece_specs(pieces):
    per = pieces[0].shape[0] // ROWS_BLK

    def spec(which, piece):
        return pl.BlockSpec(
            (ROWS_BLK, piece.shape[1]), lambda i: (jnp.clip(i - which * per, 0, per - 1), 0)
        )

    return [spec(which, piece) for which, piece in enumerate(pieces)]


def two_pieces(body, near, far):
    step = pl.program_id(0)
    half = pl.num_programs(0) // 2
    pl.when(step < half)(lambda: body(near))
    pl.when(step >= half)(lambda: body(far))


def ff_forward(pieces, gate_w, up_w, far, ffp):
    ff = matrix_shape(gate_w)[0]
    rows = sum(v.shape[0] for v in pieces)

    def body(near_ref, part_ref, gate_w, up_w, far_gate, far_up, gate_ref, up_ref, product_ref):
        def work(m_ref):
            m = m_ref[...]
            for slot, (gate_t, up_t) in enumerate(((gate_w, up_w), (far_gate, far_up))):
                gate, up = nt(m, gate_t[...]), nt(m, up_t[...])
                at = slot * ffp
                gate_ref[:, at : at + ff] = gate.astype(bf16)
                up_ref[:, at : at + ff] = up.astype(bf16)
                product_ref[:, at : at + ff] = (gate * jax.nn.sigmoid(gate) * up).astype(bf16)

        two_pieces(work, near_ref, part_ref)

    parts = [gate_w, up_w, (far, (0, ff)), (far, (1, ff))]
    return local_call(
        body,
        rows // ROWS_BLK,
        piece_specs(pieces) + [matrix_spec(v) for v in parts],
        [pl.BlockSpec((ROWS_BLK, 2 * ffp), lambda i: (i, 0))] * 3,
        [jax.ShapeDtypeStruct((rows, 2 * ffp), bf16)] * 3,
        list(pieces) + [v[0] for v in parts],
    )


def gate_pair(gate, up, dproduct):
    sig = jax.nn.sigmoid(gate)
    silu = gate * sig
    dgate = dproduct * up * (sig + silu * (1.0 - sig))
    return jnp.concatenate([dgate.astype(bf16), (dproduct * silu).astype(bf16)], axis=1), silu


def ff_backward(pieces, gate, up, down_w, far, ffp):
    ff = matrix_shape(down_w)[0]

    def body(near_ref, part_ref, gate_ref, up_ref, down_ref, far_ref, own_out, far_out):
        def work(g_ref):
            g = g_ref[...]
            for slot, (weight, out) in enumerate(((down_ref, own_out), (far_ref, far_out))):
                cols = slice(slot * ffp, slot * ffp + ff)
                out[...] = gate_pair(
                    gate_ref[:, cols].astype(f32), up_ref[:, cols].astype(f32), nt(g, weight[...])
                )[0]

        two_pieces(work, near_ref, part_ref)

    rows = gate.shape[0]
    parts = [down_w, (far, (2, ff))]
    return local_call(
        body,
        rows // ROWS_BLK,
        piece_specs(pieces) + [row_spec(gate), row_spec(up)] + [matrix_spec(v) for v in parts],
        [pl.BlockSpec((ROWS_BLK, 2 * ff), lambda i: (i, 0))] * 2,
        [jax.ShapeDtypeStruct((rows, 2 * ff), bf16)] * 2,
        list(pieces) + [gate, up] + [v[0] for v in parts],
    )


def ff_weight_grads(m_pieces, g_pieces, dboth, product, gate_w, up_w, down_w, spare):
    ff = matrix_shape(down_w)[0]
    rows, width = m_pieces[0].shape

    def body(m0, m1, m2, m3, g0, g1, g2, g3, both_ref, product_ref, gate_t, up_t, down_ref, out, total):
        step = pl.program_id(0)

        def add(both, product, m, g):
            for at, left, right in ((0, both, m), (2 * ff, product, g)):
                part = tn(left, right)
                place = slice(at, at + left.shape[1])

                @pl.when(step == 0)
                def _():
                    total[place] = part

                @pl.when(step > 0)
                def _():
                    total[place] += part

        def near(m_ref, g_ref):
            add(both_ref[...], product_ref[:, :ff], m_ref[...], g_ref[...])

        def far(m_ref, g_ref):
            m, g = m_ref[...], g_ref[...]
            gate, up = nt(m, gate_t[...]), nt(m, up_t[...])
            both, silu = gate_pair(gate, up, nt(g, down_ref[...]))
            add(both, (silu * up).astype(bf16), m, g)

        for which, (work, m_ref, g_ref) in enumerate(
            ((near, m0, g0), (near, m1, g1), (far, m2, g2), (far, m3, g3))
        ):
            pl.when(step == which)(lambda work=work, m_ref=m_ref, g_ref=g_ref: work(m_ref, g_ref))

        @pl.when(step == 3)
        def _():
            out[: 3 * ff] = total[...].astype(bf16)
            if spare:
                out[3 * ff :] = jnp.zeros((spare, width), bf16)

    parts = [gate_w, up_w, down_w]
    once = pl.Buffered(1)

    def alone(spec):
        return pl.BlockSpec(spec.block_shape, spec.index_map, pipeline_mode=once)

    piece = pl.BlockSpec((rows, width), lambda i: (0, 0), pipeline_mode=once)
    return local_call(
        body,
        4,
        [piece] * 8
        + [pl.BlockSpec((rows, v.shape[1]), lambda i: (jnp.minimum(i, 1), 0)) for v in (dboth, product)]
        + [alone(matrix_spec(v)) for v in parts],
        pl.BlockSpec((3 * ff + spare, width), lambda i: (0, 0), pipeline_mode=once),
        jax.ShapeDtypeStruct((3 * ff + spare, width), bf16),
        list(m_pieces) + list(g_pieces) + [dboth, product] + [v[0] for v in parts],
        scratch=[pltpu.VMEM((3 * ff, width), f32)],
    )


def ring_place(index, n):
    return jnp.where(index % 2 == 0, index // 2, n - 1 - index // 2)


def ring_index(place, n):
    return jnp.where(place < n // 2, 2 * place, 2 * (n - 1 - place) + 1)


MESH = pl.DeviceIdType.MESH


class Ring:
    def __init__(self, n, data, out, slots, sems):
        self.n, self.data, self.out, self.slots = n, data, out, slots
        self.send, self.recv, self.out_send, self.out_recv = sems
        self.me = ring_place(lax.axis_index("dp"), n)
        self.peers = [
            ring_index(lax.rem(self.me + 1, n), n),
            ring_index(lax.rem(self.me + n - 1, n), n),
        ]
        self.rows = data.shape[0] // (2 * n)

    def chunk(self, ref, way, back):
        which = lax.rem(self.me + 2 * self.n - (1, -1)[way] * back, self.n)
        return ref.at[pl.ds(pl.multiple_of((2 * which + way) * self.rows, 16), self.rows)]

    def partial(self, way, source, step):
        return pltpu.make_async_remote_copy(
            src_ref=source, dst_ref=self.slots.at[way, step],
            send_sem=self.send.at[way, step], recv_sem=self.recv.at[way, step],
            device_id={"dp": self.peers[way]}, device_id_type=MESH,
        )

    def final(self, way, step, back):
        part = self.chunk(self.out, way, back)
        return pltpu.make_async_remote_copy(
            src_ref=part, dst_ref=part,
            send_sem=self.out_send.at[way, step], recv_sem=self.out_recv.at[way, step],
            device_id={"dp": self.peers[way]}, device_id_type=MESH,
        )

    def start(self):
        for way in range(2):
            self.partial(way, self.chunk(self.data, way, 0), 0).start()

    def reduce(self, step):
        for way in range(2):
            slot = self.slots.at[way, step]
            self.partial(way, slot, step).wait_recv()
            part = self.chunk(self.data, way, step + 1)
            slot[...] = (slot[...].astype(f32) + part[...].astype(f32)).astype(bf16)

            @pl.when(step < self.n - 2)
            def _():
                self.partial(way, slot, step + 1).start()

    def turn(self):
        for way in range(2):
            self.chunk(self.out, way, -1)[...] = self.slots[way, self.n - 2]
            self.final(way, 0, -1).start()

    def gather(self, step):
        for way in range(2):
            self.final(way, step, step).wait_recv()

            @pl.when(step < self.n - 2)
            def _():
                self.final(way, step + 1, step).start()

    def sent(self, step):
        for way in range(2):
            self.partial(way, self.slots.at[way, step], step).wait_send()
            self.final(way, step, step - 1).wait_send()


def steps_of(lo, hi, *bodies):
    def body(step, carry):
        for each in bodies:
            each(step)
        return carry

    lax.fori_loop(lo, hi, body, 0)


def mix_sum_kernel(
    n, cuts, done, own, far, misc, out_done, out_own, out_misc, came, total, slot_a, slot_b, slot_c, slot_d,
    send, recv, out_send, out_recv, chip_send, chip_recv, sums, misc_came, misc_send, misc_recv,
):
    me = ring_place(lax.axis_index("dp"), n)
    member, row = lax.axis_index("head"), lax.axis_index("dp")
    swaps = [{"head": member ^ 1}, {"head": member ^ 2}]
    swaps += [{"dp": row ^ (1 << bit)} for bit in range(n.bit_length() - 1)]
    peers = swaps + [
        {"dp": ring_index(lax.rem(me + 1, n), n)},
        {"dp": ring_index(lax.rem(me + n - 1, n), n)},
    ]
    barrier = pltpu.get_barrier_semaphore()
    for peer in peers:
        pl.semaphore_signal(barrier, inc=1, device_id=peer, device_id_type=MESH)
    pl.semaphore_wait(barrier, len(peers))

    def small(step):
        return pltpu.make_async_remote_copy(
            src_ref=sums.at[step], dst_ref=misc_came.at[step],
            send_sem=misc_send.at[step], recv_sem=misc_recv.at[step],
            device_id=swaps[step], device_id_type=MESH,
        )

    taken = [0]

    def small_step():
        step = taken[0]
        if step == len(swaps):
            return
        small(step).wait()
        sums[step + 1] = sums[step] + misc_came[step]
        taken[0] += 1
        if step + 1 < len(swaps):
            small(step + 1).start()

    swap = pltpu.make_async_remote_copy(
        src_ref=far, dst_ref=came, send_sem=chip_send, recv_sem=chip_recv,
        device_id={"head": member ^ 2}, device_id_type=MESH,
    )
    def ring(which, data, out, cut, slots):
        rows = slice(*cut)
        sems = [v.at[which] for v in (send, recv, out_send, out_recv)]
        return Ring(n, data.at[rows], out.at[rows], slots, sems)

    rings = (
        (0, done, out_done, cuts[0], slot_a),
        (1, done, out_done, cuts[1], slot_b),
        (2, total, out_own, cuts[2], slot_c),
        (3, total, out_own, cuts[3], slot_d),
    )
    first, second = ([ring(*v) for v in pair if v[3][1] > v[3][0]] for pair in (rings[:2], rings[2:]))

    def each(rings, name):
        return [getattr(v, name) for v in rings]

    def now(steps):
        for step in steps:
            step()

    middle, last = (n - 1) // 2, n - 1
    sums[0] = misc[...]
    small(0).start()
    swap.start()
    now(each(first, "start"))
    steps_of(0, middle, *each(first, "reduce"))
    small_step()
    steps_of(middle, last, *each(first, "reduce"))
    now(each(first, "turn"))
    small_step()
    swap.wait()
    total[...] = (own[...].astype(f32) + came[...].astype(f32)).astype(bf16)
    now(each(second, "start"))
    together = each(first, "gather") + each(second, "reduce")
    steps_of(0, middle, *together)
    small_step()
    steps_of(middle, last, *together)
    now(each(second, "turn"))
    small_step()
    steps_of(0, middle, *each(second, "gather"))
    small_step()
    steps_of(middle, last, *each(second, "gather"))
    for _ in swaps:
        small_step()
    out_misc[...] = sums[len(swaps)]
    steps_of(0, last, *each(first + second, "sent"))


def mix_sum(done, own, far, misc, n):
    if n == 1:
        misc = misc + core_swap(misc)
        own = (own.astype(f32) + chip_swap(far).astype(f32)).astype(bf16)
        return done, own, misc + chip_swap(misc)
    rows, cols = own.shape
    done_rows = done.shape[0]
    swaps = 2 + n.bit_length() - 1

    def two(total):
        lines = total // (32 * n)
        cut = (lines + 1) // 2 * 32 * n
        return (0, cut), (cut, total)

    cuts = two(done_rows) + two(rows)

    def body(*refs):
        mix_sum_kernel(n, cuts, *refs)

    vmem = pl.BlockSpec(memory_space=pltpu.VMEM)
    return pl.pallas_call(
        body,
        in_specs=[vmem] * 4,
        out_specs=[vmem] * 3,
        out_shape=[
            jax.ShapeDtypeStruct((done_rows, cols), bf16),
            jax.ShapeDtypeStruct((rows, cols), bf16),
        ]
        + [jax.ShapeDtypeStruct(misc.shape, f32)],
        scratch_shapes=[
            pltpu.VMEM((rows, cols), bf16),
            pltpu.VMEM((rows, cols), bf16),
        ]
        + [
            pltpu.VMEM((2, n - 1, max(16, (stop - at) // (2 * n)), cols), bf16) for at, stop in cuts
        ]
        + [pltpu.SemaphoreType.DMA((4, 2, n - 1))] * 4
        + [pltpu.SemaphoreType.DMA] * 2
        + [
            pltpu.VMEM((swaps + 1,) + misc.shape, f32),
            pltpu.VMEM((swaps,) + misc.shape, f32),
            pltpu.SemaphoreType.DMA((swaps,)),
            pltpu.SemaphoreType.DMA((swaps,)),
        ],
        compiler_params=pltpu.CompilerParams(
            collective_id=0, has_side_effects=True, vmem_limit_bytes=VMEM_LIMIT
        ),
    )(done, own, far, misc)


def norm_scale(hidden):
    return lax.rsqrt(jnp.mean(hidden * hidden, axis=-1, keepdims=True) + epsilon)


def norm_low(hidden, gain):
    return (hidden * norm_scale(hidden) * gain).astype(bf16)


def norm_back(hidden, gain, grad_normed):
    scale = norm_scale(hidden)
    weighted = grad_normed * gain
    grad_hidden = scale * weighted - hidden * (scale * scale * scale) * jnp.mean(
        weighted * hidden, axis=-1, keepdims=True
    )
    return grad_hidden, jnp.sum(grad_normed * hidden * scale, axis=0)


def core_swap(value):
    return lax.ppermute(value, "head", [(i, i ^ 1) for i in range(4)])


def chip_swap(value):
    return lax.ppermute(value, "head", [(i, i ^ 2) for i in range(4)])


def dp_slice(own):
    parts = own.reshape((lax.axis_size("dp"), -1) + own.shape[1:])
    return lax.dynamic_index_in_dim(parts, lax.axis_index("dp"), 0, keepdims=False)


def dp_ring():
    n = lax.axis_size("dp")
    return list(range(0, n, 2)) + list(range(n - 1, 0, -2)) if n > 1 else [0]


def after(value, *others):
    return lax.optimization_barrier((value,) + others)[0]


def per_device(
    tokens, doc_starts, grad_out, norm_one, w_query, w_key, w_value, w_outgate, w_rank, w_decay,
    decay_bias, group_gain, w_out, norm_two, w_gate, w_up, w_down,
):
    shard_len, width = tokens.shape[1:]
    ndoc = doc_starts.shape[1]
    ff = w_gate.shape[2]
    ffp = -(-ff // 128) * 128
    rank = w_decay.shape[1]
    member = lax.axis_index("head")
    core = member % 2
    chip = member // 2
    meta = jnp.concatenate(
        [doc_starts[0], jnp.stack([chip * (2 * shard_len), core]).astype(jnp.int32)]
    )
    mixer = Mixer(meta, ndoc, 2 * shard_len)

    def mix_pack(layer):
        return jnp.concatenate(
            [w_query[layer], w_key[layer], w_value[layer], w_outgate[layer]], axis=1
        )

    gate_t, up_t, rank_t = (jnp.swapaxes(v, 1, 2) for v in (w_gate, w_up, w_rank))

    def ff_slice(layer, wait):
        part = jnp.concatenate([dp_slice(v[layer]) for v in (gate_t, up_t, w_down)], axis=0)
        return chip_swap(after(part, wait))

    def ff_gather(part):
        dp = lax.axis_size("dp")
        whole = lax.all_gather(part, "dp", axis=0, tiled=True)
        return jnp.swapaxes(whole.reshape(dp, 3, ff // dp, width), 0, 1).reshape(3 * ff, width)

    def with_partner(local):
        return jnp.concatenate([local, core_swap(local)], axis=0)

    def settle(terms):
        sent = core_swap(sum_of_dots(terms, shard_len, shard_len, bf16))
        return sum_of_dots(terms, 0, shard_len, f32) + sent.astype(f32)

    small = jnp.concatenate([w_decay.astype(f32), decay_bias[:, None, :]], axis=1)
    small = jnp.concatenate([small, chip_swap(small)], axis=2)
    mix_own = mix_pack(0)
    first_far = chip_swap(mix_own[:, : 2 * HK])
    ff_part = ff_slice(0, meta)
    ff_far = ff_gather(ff_part)
    mix_far = (first_far, chip_swap(after(mix_own[:, 2 * HK :], ff_part)))
    out_far = chip_swap(after(w_out[0], ff_part))
    next_part = ff_slice(1, mix_far[1])
    next_own = mix_pack(1)
    spare = -3 * ff % (32 * lax.axis_size("dp"))

    grad = grad_out[0].astype(f32)
    hidden = tokens[0].astype(f32)
    saved = []
    for layer in range(LAYERS):
        hidden_in = hidden
        a = with_partner(norm_low(hidden, norm_one[layer]))
        x = project(a, ((mix_own, None),) + tuple((v, None) for v in mix_far) + ((rank_t, layer),))
        wdec, bias = small[layer, :rank], small[layer, rank:]
        run, states, cum, final = mixer.states(x, wdec, bias)
        got = chip_swap(after(final, next_part, next_own) if layer == 0 else after(final, out_far))
        first = got[::-1] * chip.astype(bf16)
        gain = group_gain[layer][None]
        gated, mixed = mixer.mix(x, run, states, cum, first, gain)
        if layer + 1 < LAYERS:
            next_mix = (chip_swap(after(next_own, got)),)
            next_out = chip_swap(after(w_out[layer + 1], got))
            next_far = ff_gather(next_part)
        hidden_mid = hidden + settle(
            [(gated, 0, (w_out, layer), False), (gated, HV, (out_far, None), False)]
        )
        m_own = norm_low(hidden_mid, norm_two[layer])
        m = (m_own, core_swap(m_own))
        gate, up, product = ff_forward(m, (gate_t, layer), (up_t, layer), ff_far, ffp)
        if layer + 1 < LAYERS:
            product = after(product, next_mix[0])
        hidden = hidden_mid + settle(
            [(product, 0, (w_down, layer), False), (product, ffp, (ff_far, (2, ff)), False)]
        )
        saved.append(
            (hidden_in, hidden_mid, a, m, x, run, states, cum, first, mixed, gated, gate, up, product,
             mix_own, mix_far, out_far, ff_far)
        )
        if layer + 1 < LAYERS:
            mix_own, mix_far, out_far, ff_far = next_own, next_mix, next_out, next_far
    result = hidden.astype(bf16)[None]

    ff_grads, misc_grads = [None] * LAYERS, [None] * LAYERS
    for layer in reversed(range(LAYERS)):
        (
            hidden_in, hidden_mid, a, m, x, run, states, cum, first, mixed, gated, gate, up, product,
            mix_own, mix_far, out_far, ff_far,
        ) = saved[layer]
        gain = group_gain[layer][None]
        wdec, bias = small[layer, :rank], small[layer, rank:]
        if layer + 1 < LAYERS:
            g_own = grad.astype(bf16)
            g_y = chip_swap(g_own)
            m_y = chip_swap(after(m[0], dfar))
            mix_done = (own.astype(f32) + chip_swap(after(far, g_y)).astype(f32)).astype(bf16)
            mix_done = lax.psum(mix_done, "dp", axis_index_groups=[dp_ring()])
        else:
            g_own = grad_out[0]
            g_y = chip_swap(after(g_own, got))
            m_y = chip_swap(after(m[0], g_y))
        g = (g_own, core_swap(g_own))
        dboth, dfar = ff_backward(g, gate, up, (w_down, layer), ff_far, ffp)
        back_mid, gain_two = norm_back(
            hidden_mid,
            norm_two[layer],
            settle(
                [
                    (dboth, 0, (gate_t, layer), False),
                    (dboth, ff, (up_t, layer), False),
                    (dfar, 0, (ff_far, (0, 2 * ff)), False),
                ]
            ),
        )
        ff_grad = ff_weight_grads(
            m + (m_y, core_swap(m_y)), g + (g_y, core_swap(g_y)), dboth, product,
            (gate_t, layer), (up_t, layer), (w_down, layer), 0 if layer else spare,
        )
        grad = grad + back_mid
        g_mix = with_partner(grad.astype(bf16))
        if layer + 1 == LAYERS:
            g_mix = after(g_mix, ff_grad)
        g_wout = tn(g_mix, gated).astype(bf16)
        dmixed, doutgate, dstates, dcum, dfinal, dgain = mixer.back_states(
            x, run, mixed, g_mix, w_out[layer], out_far, gain
        )
        got = chip_swap(dfinal)
        dlast = got[::-1] * (1 - chip).astype(bf16)
        dx, dwdec, dbias = mixer.back(
            x, run, states, cum, first, dmixed, doutgate, dstates, dcum, dlast, wdec, bias
        )
        g_wmix = tn(a, dx[:, : 2 * HEAD_COLS]).astype(bf16)
        g_rank = tn(dx[:, 2 * HEAD_COLS :], a)
        far = jnp.concatenate([g_wmix[:, HEAD_COLS:], g_wout[:, HV:]], axis=1)
        own = jnp.concatenate([g_wmix[:, :HEAD_COLS], g_wout[:, :HV]], axis=1)
        far_terms, at = [], HEAD_COLS
        for part in mix_far:
            far_terms.append((dx, at, (part, None), True))
            at += part.shape[1]
        back_first, gain_one = norm_back(hidden_in, norm_one[layer], settle(
            [
                (dx, 0, (mix_own, None), True),
                *far_terms,
                (dx, 2 * HEAD_COLS, (rank_t, layer), False),
            ]
        ))
        grad = grad + back_first
        if layer > 0:
            ff_grads[layer] = lax.psum(ff_grad, "dp")
        else:
            ff_grads[1] = after(ff_grads[1], grad)
        heads = jnp.concatenate([dwdec, dbias], axis=0)
        places = lax.iota(jnp.int32, 4)[:, None, None]
        heads = jnp.where(places == member, heads[None, :, :HK], 0.0) + jnp.where(
            places == member ^ 2, heads[None, :, HK:], 0.0
        )
        misc_grads[layer] = jnp.concatenate(
            [g_rank.reshape(-1), gain_one, gain_two, dgain[0], heads.reshape(-1)]
        )

    misc = jnp.stack(misc_grads)
    length = misc.shape[1]
    misc = jnp.pad(misc.reshape(-1), (0, -misc.size % 1024)).reshape(-1, 128)
    ff_done, first_mix, misc = mix_sum(ff_grad, own, far, misc, lax.axis_size("dp"))
    mix_grads = [first_mix, after(mix_done, grad)]
    ff_grads[0] = ff_done
    misc = misc.reshape(-1)[: LAYERS * length].reshape(LAYERS, length)
    sizes = (rank * width, width, width, HV, 4 * (rank + 1) * HK)
    pieces, at = [], 0
    for size in sizes:
        pieces.append(misc[:, at : at + size])
        at += size
    heads = lax.dynamic_index_in_dim(
        pieces[4].reshape(LAYERS, 4, rank + 1, HK), member, axis=1, keepdims=False
    )

    def rows_of(grads, start, stop):
        return jnp.stack([g[start:stop].astype(f32) for g in grads])

    def turned(grads, start, stop):
        return jnp.stack([g[start:stop].T.astype(f32) for g in grads])

    def cols_of(grads, start, stop):
        return jnp.stack([g[:, start:stop].astype(f32) for g in grads])

    return (
        result,
        grad[None],
        pieces[1],
        cols_of(mix_grads, 0, HK),
        cols_of(mix_grads, HK, 2 * HK),
        cols_of(mix_grads, 2 * HK, 2 * HK + HV),
        cols_of(mix_grads, 2 * HK + HV, HEAD_COLS),
        jnp.swapaxes(pieces[0].reshape(LAYERS, rank, width), 1, 2),
        heads[:, :rank],
        heads[:, rank],
        pieces[3],
        jnp.stack([g[:, HEAD_COLS:].T.astype(f32) for g in mix_grads]),
        pieces[2],
        turned(ff_grads, 0, ff),
        turned(ff_grads, ff, 2 * ff),
        rows_of(ff_grads, 2 * ff, 3 * ff),
    )


def solution(mesh):
    cols = P(None, None, "head")
    rows = P(None, "head", None)
    place = P("dp", "head", None)
    return jax.shard_map(
        per_device,
        mesh=mesh,
        in_specs=(
            place, P("dp", None), place, P(), cols, cols, cols, cols, P(), cols,
            P(None, "head"), P(), rows, P(), cols, cols, rows,
        ),
        out_specs=(
            place, place, P(), cols, cols, cols, cols, P(), cols, P(None, "head"), P(), rows,
            P(), cols, cols, rows,
        ),
        check_vma=False,
    )
```

```python
import jax
import jax.numpy as jnp
from jax import lax
from jax.experimental import pallas as pl
from jax.experimental.pallas import tpu as pltpu
from jax.sharding import PartitionSpec as P

LAYERS = 2
HK = 128
HV = 256
HEAD_COLS = 2 * HK + 2 * HV
BLK = 128
MID = BLK // 2 - 1
SUB = 2
epsilon = 1e-06
highest = lax.Precision.HIGHEST
VMEM_LIMIT = 48 * 1024 * 1024

f32 = jnp.float32
bf16 = jnp.bfloat16


def nn(left, right):
    return lax.dot_general(left, right, (((1,), (0,)), ((), ())), preferred_element_type=f32)


def nt(left, right):
    return lax.dot_general(left, right, (((1,), (1,)), ((), ())), preferred_element_type=f32)


def tn(left, right):
    return lax.dot_general(left, right, (((0,), (0,)), ((), ())), preferred_element_type=f32)


def doc_count(meta, ndoc, place):
    total = (meta[0] <= place).astype(jnp.int32)
    for which in range(1, ndoc):
        total = total + (meta[which] <= place).astype(jnp.int32)
    return total


def block_masks(meta, ndoc, start):
    rows = lax.broadcasted_iota(jnp.int32, (BLK, BLK), 0) + start
    cols = lax.broadcasted_iota(jnp.int32, (BLK, BLK), 1) + start
    row_ids = doc_count(meta, ndoc, rows)
    col_ids = doc_count(meta, ndoc, cols)
    id_prev = doc_count(meta, ndoc, start - 1)
    id_last = doc_count(meta, ndoc, start + BLK - 1)
    allowed = (rows >= cols) & (row_ids == col_ids)
    carried = jnp.where(row_ids == id_prev, 1.0, 0.0)
    same = jnp.where(row_ids == id_last, 1.0, 0.0)
    keep = jnp.where(id_last == id_prev, 1.0, 0.0)
    return allowed, carried, same, keep


def split_dot(ones_mat, value, dot):
    high = value.astype(bf16)
    low = (value - high.astype(f32)).astype(bf16)
    return dot(ones_mat, high) + dot(ones_mat, low)


def tri_ones():
    rows = lax.broadcasted_iota(jnp.int32, (BLK, BLK), 0)
    cols = lax.broadcasted_iota(jnp.int32, (BLK, BLK), 1)
    return jnp.where(rows >= cols, 1.0, 0.0).astype(bf16)


def head_parts(x_ref, slot):
    at = slot * HEAD_COLS
    query = x_ref[:, at : at + HK] * (HK**-0.5)
    key = x_ref[:, at + HK : at + 2 * HK]
    value = x_ref[:, at + 2 * HK : at + 2 * HK + HV]
    outgate = x_ref[:, at + 2 * HK + HV : at + HEAD_COLS]
    return query, key, value, outgate


def decay_before(x_ref, wdec_ref, bias_ref):
    ranked = x_ref[:, 2 * HEAD_COLS :]
    return jnp.dot(ranked, wdec_ref[...], precision=highest, preferred_element_type=f32) + bias_ref[...]


def states_kernel(ndoc, block, meta, x_ref, wdec_ref, bias_ref, run_ref, state_ref, cum_ref, final_ref, state, cum):
    start = meta[ndoc] + block * BLK
    _, _, same, keep = block_masks(meta, ndoc, start)
    before = decay_before(x_ref, wdec_ref, bias_ref)
    decays = (jnp.minimum(before, 0.0) - jnp.log1p(jnp.exp(-jnp.abs(before)))) * (1.0 / 16.0)
    running = split_dot(tri_ones(), decays, nn)
    run_ref[...] = running
    ending = running[BLK - 1 :, :]
    factor = jnp.exp(ending) * keep
    cum_ref[0] = cum[...]
    cum[...] = cum[...] * factor
    for slot in range(2):
        lanes = slice(slot * HK, slot * HK + HK)
        _, key, value, _ = head_parts(x_ref, slot)
        moved = (key * jnp.exp(ending[:, lanes] - running[:, lanes]) * same).astype(bf16)
        old = state[slot]
        state_ref[0, slot] = old.astype(bf16)
        new = old * factor[:, lanes] + tn(value.astype(bf16), moved)
        state[slot] = new
        final_ref[slot] = new.astype(bf16)


def mix_kernel(ndoc, block, meta, x_ref, run_ref, state_ref, cum_ref, first_ref, gain_ref, gated_ref, mixed_ref):
    start = meta[ndoc] + block * BLK
    allowed, carried, _, _ = block_masks(meta, ndoc, start)
    gain = gain_ref[...]
    for slot in range(2):
        lanes = slice(slot * HK, slot * HK + HK)
        cols = slice(slot * HV, slot * HV + HV)
        query, key, value, outgate = head_parts(x_ref, slot)
        running = run_ref[:, lanes]
        middle = running[MID : MID + 1, :]
        rel_query = (query * jnp.exp(running - middle)).astype(bf16)
        rel_key = (key * jnp.exp(middle - running)).astype(bf16)
        scores = jnp.where(allowed, nt(rel_query, rel_key), 0.0).astype(bf16)
        far_query = (query * jnp.exp(running) * carried).astype(bf16)
        state = (state_ref[0, slot].astype(f32) + first_ref[slot].astype(f32) * cum_ref[0][:, lanes]).astype(bf16)
        mixed = nn(scores, value.astype(bf16)) + nt(far_query, state)
        scale = lax.rsqrt(jnp.maximum(jnp.mean(mixed * mixed, axis=-1, keepdims=True), 1.0))
        gated_ref[:, cols] = (mixed * scale * gain * outgate * jax.nn.sigmoid(outgate)).astype(bf16)
        mixed_ref[:, cols] = mixed.astype(bf16)


def back_states_kernel(
    ndoc, block, meta, x_ref, run_ref, mixed_ref, grad_ref, own_out_ref, far_out_ref, gain_ref,
    dmixed_ref, doutgate_ref, dstate_ref, cum_ref, final_ref, dgain_ref, state, cum,
):
    start = meta[ndoc] + block * BLK
    _, carried, _, keep = block_masks(meta, ndoc, start)
    gain = gain_ref[...]
    running = run_ref[...]
    factor = jnp.exp(running[BLK - 1 :, :]) * keep
    cum_ref[0] = cum[...]
    cum[...] = cum[...] * factor
    for slot in range(2):
        lanes = slice(slot * HK, slot * HK + HK)
        cols = slice(slot * HV, slot * HV + HV)
        query, _, _, outgate = head_parts(x_ref, slot)
        mixed = mixed_ref[:, cols].astype(f32)
        dgated = nt(grad_ref[...], (own_out_ref, far_out_ref)[slot][...])
        mean = jnp.mean(mixed * mixed, axis=-1, keepdims=True)
        scale = lax.rsqrt(jnp.maximum(mean, 1.0))
        sig = jax.nn.sigmoid(outgate)
        silu = outgate * sig
        dnormed = dgated * silu
        plain = mixed * scale
        doutgate_ref[:, cols] = (dgated * plain * gain * (sig + silu * (1.0 - sig))).astype(bf16)
        dgain_ref[...] += jnp.sum(dnormed * plain, axis=0, keepdims=True)
        weighted = dnormed * gain
        inner = jnp.where(mean > 1.0, jnp.mean(weighted * plain, axis=-1, keepdims=True), 0.0)
        dmixed = (scale * (weighted - plain * inner)).astype(bf16)
        dmixed_ref[:, cols] = dmixed
        far_query = (query * jnp.exp(running[:, lanes]) * carried).astype(bf16)
        old = state[slot]
        dstate_ref[0, slot] = old.astype(bf16)
        new = old * factor[:, lanes] + tn(dmixed, far_query)
        state[slot] = new
        final_ref[slot] = new.astype(bf16)


def back_kernel(
    ndoc, block, meta, x_ref, run_ref, state_ref, cum_ref, first_ref, dmixed_ref, doutgate_ref,
    dstate_ref, dcum_ref, dlast_ref, wdec_ref, bias_ref, dx_ref, dwdec_ref, dbias_ref,
):
    start = meta[ndoc] + block * BLK
    allowed, carried, same, keep = block_masks(meta, ndoc, start)
    last_row = lax.broadcasted_iota(jnp.int32, (BLK, HK), 0) == BLK - 1
    drunning = []
    for slot in range(2):
        lanes = slice(slot * HK, slot * HK + HK)
        cols = slice(slot * HV, slot * HV + HV)
        at = slot * HEAD_COLS
        query, key, value, _ = head_parts(x_ref, slot)
        running = run_ref[:, lanes]
        middle = running[MID : MID + 1, :]
        ending = running[BLK - 1 :, :]
        up = jnp.exp(running - middle)
        down = jnp.exp(middle - running)
        far = jnp.exp(running) * carried
        near = jnp.exp(ending - running) * same
        rel_query = (query * up).astype(bf16)
        rel_key = (key * down).astype(bf16)
        far_query = (query * far).astype(bf16)
        moved = (key * near).astype(bf16)
        value = value.astype(bf16)
        scores = jnp.where(allowed, nt(rel_query, rel_key), 0.0).astype(bf16)
        state = state_ref[0, slot].astype(f32) + first_ref[slot].astype(f32) * cum_ref[0][:, lanes]
        dstate = dstate_ref[0, slot].astype(f32) + dlast_ref[slot].astype(f32) * dcum_ref[0][:, lanes]
        state_low = state.astype(bf16)
        dstate_low = dstate.astype(bf16)
        dmixed = dmixed_ref[:, cols]
        dvalue = tn(scores, dmixed) + nt(moved, dstate_low)
        dscores = jnp.where(allowed, nt(dmixed, value), 0.0).astype(bf16)
        drel_query = nn(dscores, rel_key)
        drel_key = tn(dscores, rel_query)
        dfar = nn(dmixed, state_low)
        dmoved = nn(value, dstate_low)
        dquery = drel_query * up + dfar * far
        dkey = drel_key * down + dmoved * near
        moved_grad = dmoved * moved.astype(f32)
        dending = jnp.sum(moved_grad, axis=0, keepdims=True) + jnp.sum(
            state * dstate, axis=0, keepdims=True
        ) * (jnp.exp(ending) * keep)
        drun = (
            drel_query * rel_query.astype(f32)
            - drel_key * rel_key.astype(f32)
            + dfar * far_query.astype(f32)
            - moved_grad
        )
        drunning.append(drun + jnp.where(last_row, dending, 0.0))
        dx_ref[:, at : at + HK] = (dquery * (HK**-0.5)).astype(bf16)
        dx_ref[:, at + HK : at + 2 * HK] = dkey.astype(bf16)
        dx_ref[:, at + 2 * HK : at + 2 * HK + HV] = dvalue.astype(bf16)
        dx_ref[:, at + 2 * HK + HV : at + HEAD_COLS] = doutgate_ref[:, cols]
    drun_both = jnp.concatenate(drunning, axis=1)
    ddecay = split_dot(tri_ones(), drun_both, tn)
    before = decay_before(x_ref, wdec_ref, bias_ref)
    dbefore = ddecay * (1.0 / 16.0) * jax.nn.sigmoid(-before)
    dbias_ref[...] += jnp.sum(dbefore, axis=0, keepdims=True)
    ranked = x_ref[:, 2 * HEAD_COLS :]
    dlow = dbefore.astype(bf16)
    dwdec_ref[...] += tn(ranked.astype(bf16), dlow)
    dx_ref[:, 2 * HEAD_COLS :] = nt(dlow, wdec_ref[...].astype(bf16)).astype(bf16)


def kernel_params():
    return pltpu.CompilerParams(dimension_semantics=("arbitrary",), vmem_limit_bytes=VMEM_LIMIT)


def sub_blocks(kernel, ndoc, tokens, rows, blocks, reverse, starts):
    steps = tokens // (BLK * SUB)

    def body(meta, *refs):
        step = pl.program_id(0)

        @pl.when(step == 0)
        def _():
            for which, value in starts:
                refs[which][...] = jnp.full_like(refs[which], value)

        first = (steps - 1 - step if reverse else step) * SUB
        for sub in reversed(range(SUB)) if reverse else range(SUB):
            views = [
                ref.at[sub * BLK : (sub + 1) * BLK] if i in rows
                else ref.at[sub : sub + 1] if i in blocks
                else ref
                for i, ref in enumerate(refs)
            ]
            kernel(ndoc, first + sub, meta, *views)

    return body


class Mixer:
    def __init__(self, meta, ndoc, tokens):
        self.meta = meta
        self.ndoc = ndoc
        self.tokens = tokens
        self.nblk = tokens // BLK
        self.steps = self.nblk // SUB

    def rows(self, width, reverse=False):
        steps, core = self.steps, self.ndoc + 1

        def place(step, meta):
            time = steps - 1 - step if reverse else step
            return (lax.rem(time + meta[core] * (steps // 2), steps), 0)

        return pl.BlockSpec((BLK * SUB, width), place)

    def per_block(self, shape, reverse=False):
        steps = self.steps
        zeros = (0,) * len(shape)
        return pl.BlockSpec(
            (SUB,) + shape, lambda step, meta: ((steps - 1 - step if reverse else step),) + zeros
        )

    def whole(self, shape):
        zeros = (0,) * len(shape)
        return pl.BlockSpec(shape, lambda step, meta: zeros)

    def call(self, kernel, layout, in_specs, out_specs, out_shape, scratch, *args):
        return pl.pallas_call(
            sub_blocks(kernel, self.ndoc, self.tokens, *layout),
            grid_spec=pltpu.PrefetchScalarGridSpec(
                num_scalar_prefetch=1,
                grid=(self.steps,),
                in_specs=in_specs,
                out_specs=out_specs,
                scratch_shapes=scratch,
            ),
            out_shape=[jax.ShapeDtypeStruct(s, d) for s, d in out_shape],
            cost_estimate=NO_COST,
            compiler_params=kernel_params(),
        )(self.meta, *args)

    def state_scratch(self):
        return [pltpu.VMEM((2, HV, HK), f32), pltpu.VMEM((1, 2 * HK), f32)]

    def states(self, x, wdec, bias):
        n = self.nblk
        return self.call(
            states_kernel,
            ((0, 3), (4, 5), False, ((7, 0.0), (8, 1.0))),
            [self.rows(x.shape[1]), self.whole(wdec.shape), self.whole(bias.shape)],
            [
                self.rows(2 * HK),
                self.per_block((2, HV, HK)),
                self.per_block((1, 2 * HK)),
                self.whole((2, HV, HK)),
            ],
            [
                ((self.tokens, 2 * HK), f32),
                ((n, 2, HV, HK), bf16),
                ((n, 1, 2 * HK), f32),
                ((2, HV, HK), bf16),
            ],
            self.state_scratch(),
            x, wdec, bias,
        )

    def mix(self, x, run, states, cum, first, gain):
        return self.call(
            mix_kernel,
            ((0, 1, 6, 7), (2, 3), False, ()),
            [
                self.rows(x.shape[1]),
                self.rows(2 * HK),
                self.per_block((2, HV, HK)),
                self.per_block((1, 2 * HK)),
                self.whole((2, HV, HK)),
                self.whole(gain.shape),
            ],
            [self.rows(2 * HV), self.rows(2 * HV)],
            [((self.tokens, 2 * HV), bf16), ((self.tokens, 2 * HV), bf16)],
            [],
            x, run, states, cum, first, gain,
        )

    def back_states(self, x, run, mixed, grad, own_out, far_out, gain):
        n = self.nblk
        return self.call(
            back_states_kernel,
            ((0, 1, 2, 3, 7, 8), (9, 10), True, ((12, 0.0), (13, 0.0), (14, 1.0))),
            [
                self.rows(x.shape[1], True),
                self.rows(2 * HK, True),
                self.rows(2 * HV, True),
                self.rows(grad.shape[1], True),
                self.whole(own_out.shape),
                self.whole(far_out.shape),
                self.whole(gain.shape),
            ],
            [
                self.rows(2 * HV, True),
                self.rows(2 * HV, True),
                self.per_block((2, HV, HK), True),
                self.per_block((1, 2 * HK), True),
                self.whole((2, HV, HK)),
                self.whole((1, HV)),
            ],
            [
                ((self.tokens, 2 * HV), bf16),
                ((self.tokens, 2 * HV), bf16),
                ((n, 2, HV, HK), bf16),
                ((n, 1, 2 * HK), f32),
                ((2, HV, HK), bf16),
                ((1, HV), f32),
            ],
            self.state_scratch(),
            x, run, mixed, grad, own_out, far_out, gain,
        )

    def back(self, x, run, states, cum, first, dmixed, doutgate, dstates, dcum, dlast, wdec, bias):
        rank = wdec.shape[0]
        return self.call(
            back_kernel,
            ((0, 1, 5, 6, 12), (2, 3, 7, 8), False, ((13, 0.0), (14, 0.0))),
            [
                self.rows(x.shape[1]),
                self.rows(2 * HK),
                self.per_block((2, HV, HK)),
                self.per_block((1, 2 * HK)),
                self.whole((2, HV, HK)),
                self.rows(2 * HV),
                self.rows(2 * HV),
                self.per_block((2, HV, HK)),
                self.per_block((1, 2 * HK)),
                self.whole((2, HV, HK)),
                self.whole(wdec.shape),
                self.whole(bias.shape),
            ],
            [self.rows(x.shape[1]), self.whole((rank, 2 * HK)), self.whole((1, 2 * HK))],
            [
                ((self.tokens, x.shape[1]), bf16),
                ((rank, 2 * HK), f32),
                ((1, 2 * HK), f32),
            ],
            [],
            x, run, states, cum, first, dmixed, doutgate, dstates, dcum, dlast, wdec, bias,
        )


ROWS_BLK = 256


def matrix_spec(part):
    array, which = part
    if array.ndim == 3:
        return pl.BlockSpec((None,) + array.shape[1:], lambda i: (which, 0, 0))
    if which is None:
        return pl.BlockSpec(array.shape, lambda i: (0, 0))
    at, rows = which
    return pl.BlockSpec((rows, array.shape[1]), lambda i: (at, 0))


def matrix_shape(part):
    array, which = part
    if array.ndim == 3 or which is None:
        return array.shape[-2:]
    return which[1], array.shape[1]


def row_spec(array, first=0):
    return pl.BlockSpec((ROWS_BLK, array.shape[1]), lambda i: (i + first, 0))


NO_COST = pl.CostEstimate(flops=0, bytes_accessed=0, transcendentals=0)


def local_call(body, grid, in_specs, out_specs, out_shape, args, scratch=()):
    return pl.pallas_call(
        body,
        grid=(grid,),
        in_specs=in_specs,
        out_specs=out_specs,
        out_shape=out_shape,
        scratch_shapes=list(scratch),
        cost_estimate=NO_COST,
        compiler_params=pltpu.CompilerParams(
            dimension_semantics=("arbitrary",), vmem_limit_bytes=VMEM_LIMIT
        ),
    )(*args)


def sum_of_dots(terms, first_row, rows, out_type):
    lefts = []
    for left, _, _, _ in terms:
        if not any(left is seen for seen in lefts):
            lefts.append(left)
    which = [next(i for i, seen in enumerate(lefts) if seen is left) for left, _, _, _ in terms]
    rights = [right for _, _, right, _ in terms]
    width = matrix_shape(rights[0])[0 if terms[0][3] else 1]

    def body(*refs):
        left_refs, right_refs, out = refs[: len(lefts)], refs[len(lefts) : -1], refs[-1]
        total = None
        for (_, at, _, turned), index, right in zip(terms, which, right_refs):
            depth = right.shape[1] if turned else right.shape[0]
            part = (nt if turned else nn)(left_refs[index][:, at : at + depth], right[...])
            total = part if total is None else total + part
        out[...] = total.astype(out_type)

    return local_call(
        body,
        rows // ROWS_BLK,
        [row_spec(v, first_row // ROWS_BLK) for v in lefts] + [matrix_spec(v) for v in rights],
        pl.BlockSpec((ROWS_BLK, width), lambda i: (i, 0)),
        jax.ShapeDtypeStruct((rows, width), out_type),
        lefts + [v[0] for v in rights],
    )


def project(a, parts):
    widths = [matrix_shape(v)[1] for v in parts[:-1]] + [matrix_shape(parts[-1])[0]]

    def body(left, *refs):
        out = refs[-1]
        at = 0
        for right, width in zip(refs[:-1], widths):
            turned = at + width == out.shape[1]
            out[:, at : at + width] = (nt if turned else nn)(left[...], right[...])
            at += width

    return local_call(
        body,
        a.shape[0] // ROWS_BLK,
        [row_spec(a)] + [matrix_spec(v) for v in parts],
        pl.BlockSpec((ROWS_BLK, sum(widths)), lambda i: (i, 0)),
        jax.ShapeDtypeStruct((a.shape[0], sum(widths)), f32),
        [a] + [v[0] for v in parts],
    )


def piece_specs(pieces):
    per = pieces[0].shape[0] // ROWS_BLK

    def spec(which, piece):
        return pl.BlockSpec(
            (ROWS_BLK, piece.shape[1]), lambda i: (jnp.clip(i - which * per, 0, per - 1), 0)
        )

    return [spec(which, piece) for which, piece in enumerate(pieces)]


def two_pieces(body, near, far):
    step = pl.program_id(0)
    half = pl.num_programs(0) // 2
    pl.when(step < half)(lambda: body(near))
    pl.when(step >= half)(lambda: body(far))


def ff_forward(pieces, gate_w, up_w, far, ffp):
    ff = matrix_shape(gate_w)[0]
    rows = sum(v.shape[0] for v in pieces)

    def body(near_ref, part_ref, gate_w, up_w, far_gate, far_up, gate_ref, up_ref, product_ref):
        def work(m_ref):
            m = m_ref[...]
            for slot, (gate_t, up_t) in enumerate(((gate_w, up_w), (far_gate, far_up))):
                gate, up = nt(m, gate_t[...]), nt(m, up_t[...])
                at = slot * ffp
                gate_ref[:, at : at + ff] = gate.astype(bf16)
                up_ref[:, at : at + ff] = up.astype(bf16)
                product_ref[:, at : at + ff] = (gate * jax.nn.sigmoid(gate) * up).astype(bf16)

        two_pieces(work, near_ref, part_ref)

    parts = [gate_w, up_w, (far, (0, ff)), (far, (1, ff))]
    return local_call(
        body,
        rows // ROWS_BLK,
        piece_specs(pieces) + [matrix_spec(v) for v in parts],
        [pl.BlockSpec((ROWS_BLK, 2 * ffp), lambda i: (i, 0))] * 3,
        [jax.ShapeDtypeStruct((rows, 2 * ffp), bf16)] * 3,
        list(pieces) + [v[0] for v in parts],
    )


def gate_pair(gate, up, dproduct):
    sig = jax.nn.sigmoid(gate)
    silu = gate * sig
    dgate = dproduct * up * (sig + silu * (1.0 - sig))
    return jnp.concatenate([dgate.astype(bf16), (dproduct * silu).astype(bf16)], axis=1), silu


def ff_backward(pieces, gate, up, down_w, far, ffp):
    ff = matrix_shape(down_w)[0]

    def body(near_ref, part_ref, gate_ref, up_ref, down_ref, far_ref, own_out, far_out):
        def work(g_ref):
            g = g_ref[...]
            for slot, (weight, out) in enumerate(((down_ref, own_out), (far_ref, far_out))):
                cols = slice(slot * ffp, slot * ffp + ff)
                out[...] = gate_pair(
                    gate_ref[:, cols].astype(f32), up_ref[:, cols].astype(f32), nt(g, weight[...])
                )[0]

        two_pieces(work, near_ref, part_ref)

    rows = gate.shape[0]
    parts = [down_w, (far, (2, ff))]
    return local_call(
        body,
        rows // ROWS_BLK,
        piece_specs(pieces) + [row_spec(gate), row_spec(up)] + [matrix_spec(v) for v in parts],
        [pl.BlockSpec((ROWS_BLK, 2 * ff), lambda i: (i, 0))] * 2,
        [jax.ShapeDtypeStruct((rows, 2 * ff), bf16)] * 2,
        list(pieces) + [gate, up] + [v[0] for v in parts],
    )


def ff_weight_grads(m_pieces, g_pieces, dboth, product, gate_w, up_w, down_w, spare):
    ff = matrix_shape(down_w)[0]
    rows, width = m_pieces[0].shape

    def body(m0, m1, m2, m3, g0, g1, g2, g3, both_ref, product_ref, gate_t, up_t, down_ref, out, total):
        step = pl.program_id(0)

        def add(both, product, m, g):
            for at, left, right in ((0, both, m), (2 * ff, product, g)):
                part = tn(left, right)
                place = slice(at, at + left.shape[1])

                @pl.when(step == 0)
                def _():
                    total[place] = part

                @pl.when(step > 0)
                def _():
                    total[place] += part

        def near(m_ref, g_ref):
            add(both_ref[...], product_ref[:, :ff], m_ref[...], g_ref[...])

        def far(m_ref, g_ref):
            m, g = m_ref[...], g_ref[...]
            gate, up = nt(m, gate_t[...]), nt(m, up_t[...])
            both, silu = gate_pair(gate, up, nt(g, down_ref[...]))
            add(both, (silu * up).astype(bf16), m, g)

        for which, (work, m_ref, g_ref) in enumerate(
            ((near, m0, g0), (near, m1, g1), (far, m2, g2), (far, m3, g3))
        ):
            pl.when(step == which)(lambda work=work, m_ref=m_ref, g_ref=g_ref: work(m_ref, g_ref))

        @pl.when(step == 3)
        def _():
            out[: 3 * ff] = total[...].astype(bf16)
            if spare:
                out[3 * ff :] = jnp.zeros((spare, width), bf16)

    parts = [gate_w, up_w, down_w]
    once = pl.Buffered(1)

    def alone(spec):
        return pl.BlockSpec(spec.block_shape, spec.index_map, pipeline_mode=once)

    piece = pl.BlockSpec((rows, width), lambda i: (0, 0), pipeline_mode=once)
    return local_call(
        body,
        4,
        [piece] * 8
        + [pl.BlockSpec((rows, v.shape[1]), lambda i: (jnp.minimum(i, 1), 0)) for v in (dboth, product)]
        + [alone(matrix_spec(v)) for v in parts],
        pl.BlockSpec((3 * ff + spare, width), lambda i: (0, 0), pipeline_mode=once),
        jax.ShapeDtypeStruct((3 * ff + spare, width), bf16),
        list(m_pieces) + list(g_pieces) + [dboth, product] + [v[0] for v in parts],
        scratch=[pltpu.VMEM((3 * ff, width), f32)],
    )


def weight_outputs(mix_grads, ff_grads, ff):
    rows, cols = mix_grads[0].shape
    steps = 4
    high, flat = rows // steps, ff // steps
    widths = (HK, HK, HV, HV)

    def body(*refs):
        ins, outs = refs[: 4 * LAYERS], refs[4 * LAYERS :]

        def work(mix, *parts):
            at = 0
            for ref, width in zip(outs, widths):
                ref[0] = mix[:, at : at + width].astype(f32)
                at += width
            outs[4][0] = mix[:, at : at + HV].astype(f32).T
            for ref, part in zip(outs[5:], parts):
                ref[0] = part[...].astype(f32)

        for layer in range(LAYERS):
            mine = ins[4 * layer : 4 * layer + 4]
            pl.when(pl.program_id(0) == layer)(lambda mine=mine: work(*mine))

    def spec(layer, height, first):
        def place(now, step):
            held = jnp.where(now < layer, 0, steps - 1)
            return (first + jnp.where(now == layer, step, held), 0)

        return pl.BlockSpec((height, cols), place)

    in_specs, args = [], []
    for layer in range(LAYERS):
        in_specs += [spec(layer, high, 0)] + [spec(layer, flat, part * steps) for part in range(3)]
        args += [mix_grads[layer]] + [ff_grads[layer]] * 3
    out_specs = [pl.BlockSpec((1, high, width), lambda now, step: (now, step, 0)) for width in widths]
    out_specs += [pl.BlockSpec((1, HV, high), lambda now, step: (now, 0, step))]
    out_specs += [pl.BlockSpec((1, flat, cols), lambda now, step: (now, step, 0))] * 3
    shapes = [(LAYERS, rows, width) for width in widths] + [(LAYERS, HV, rows)] + [(LAYERS, ff, cols)] * 3
    return pl.pallas_call(
        body,
        grid=(LAYERS, steps),
        in_specs=in_specs,
        out_specs=out_specs,
        out_shape=[jax.ShapeDtypeStruct(v, f32) for v in shapes],
        cost_estimate=NO_COST,
        compiler_params=pltpu.CompilerParams(
            dimension_semantics=("arbitrary", "arbitrary"), vmem_limit_bytes=VMEM_LIMIT
        ),
    )(*args)


def ring_place(index, n):
    return jnp.where(index % 2 == 0, index // 2, n - 1 - index // 2)


def ring_index(place, n):
    return jnp.where(place < n // 2, 2 * place, 2 * (n - 1 - place) + 1)


MESH = pl.DeviceIdType.MESH


class Ring:
    def __init__(self, n, data, out, slots, sems):
        self.n, self.data, self.out, self.slots = n, data, out, slots
        self.send, self.recv, self.out_send, self.out_recv = sems
        self.me = ring_place(lax.axis_index("dp"), n)
        self.peers = [
            ring_index(lax.rem(self.me + 1, n), n),
            ring_index(lax.rem(self.me + n - 1, n), n),
        ]
        self.rows = data.shape[0] // (2 * n)

    def chunk(self, ref, way, back):
        which = lax.rem(self.me + 2 * self.n - (1, -1)[way] * back, self.n)
        return ref.at[pl.ds(pl.multiple_of((2 * which + way) * self.rows, 16), self.rows)]

    def partial(self, way, source, step):
        return pltpu.make_async_remote_copy(
            src_ref=source, dst_ref=self.slots.at[way, step],
            send_sem=self.send.at[way, step], recv_sem=self.recv.at[way, step],
            device_id={"dp": self.peers[way]}, device_id_type=MESH,
        )

    def final(self, way, step, back):
        part = self.chunk(self.out, way, back)
        return pltpu.make_async_remote_copy(
            src_ref=part, dst_ref=part,
            send_sem=self.out_send.at[way, step], recv_sem=self.out_recv.at[way, step],
            device_id={"dp": self.peers[way]}, device_id_type=MESH,
        )

    def start(self):
        for way in range(2):
            self.partial(way, self.chunk(self.data, way, 0), 0).start()

    def reduce(self, step):
        for way in range(2):
            slot = self.slots.at[way, step]
            self.partial(way, slot, step).wait_recv()
            part = self.chunk(self.data, way, step + 1)
            slot[...] = (slot[...].astype(f32) + part[...].astype(f32)).astype(bf16)

            @pl.when(step < self.n - 2)
            def _():
                self.partial(way, slot, step + 1).start()

    def turn(self):
        for way in range(2):
            self.chunk(self.out, way, -1)[...] = self.slots[way, self.n - 2]
            self.final(way, 0, -1).start()

    def gather(self, step):
        for way in range(2):
            self.final(way, step, step).wait_recv()

            @pl.when(step < self.n - 2)
            def _():
                self.final(way, step + 1, step).start()

    def sent(self, step):
        for way in range(2):
            self.partial(way, self.slots.at[way, step], step).wait_send()
            self.final(way, step, step - 1).wait_send()


def steps_of(lo, hi, *bodies):
    def body(step, carry):
        for each in bodies:
            each(step)
        return carry

    lax.fori_loop(lo, hi, body, 0)


def mix_sum_kernel(
    n, cuts, done, late, own, far, misc, out_done, out_late, out_own, out_misc, came, total,
    slot_a, slot_b, slot_c, slot_d, slot_e, slot_f,
    send, recv, out_send, out_recv, chip_send, chip_recv, sums, misc_came, misc_send, misc_recv,
):
    me = ring_place(lax.axis_index("dp"), n)
    member, row = lax.axis_index("head"), lax.axis_index("dp")
    swaps = [{"head": member ^ 1}, {"head": member ^ 2}]
    swaps += [{"dp": row ^ (1 << bit)} for bit in range(n.bit_length() - 1)]
    peers = swaps + [
        {"dp": ring_index(lax.rem(me + 1, n), n)},
        {"dp": ring_index(lax.rem(me + n - 1, n), n)},
    ]
    barrier = pltpu.get_barrier_semaphore()
    for peer in peers:
        pl.semaphore_signal(barrier, inc=1, device_id=peer, device_id_type=MESH)
    pl.semaphore_wait(barrier, len(peers))

    def small(step):
        return pltpu.make_async_remote_copy(
            src_ref=sums.at[step], dst_ref=misc_came.at[step],
            send_sem=misc_send.at[step], recv_sem=misc_recv.at[step],
            device_id=swaps[step], device_id_type=MESH,
        )

    taken = [0]

    def small_step():
        step = taken[0]
        if step == len(swaps):
            return
        small(step).wait()
        sums[step + 1] = sums[step] + misc_came[step]
        taken[0] += 1
        if step + 1 < len(swaps):
            small(step + 1).start()

    swap = pltpu.make_async_remote_copy(
        src_ref=far, dst_ref=came, send_sem=chip_send, recv_sem=chip_recv,
        device_id={"head": member ^ 2}, device_id_type=MESH,
    )
    def ring(which, data, out, cut, slots):
        rows = slice(*cut)
        sems = [v.at[which] for v in (send, recv, out_send, out_recv)]
        return Ring(n, data.at[rows], out.at[rows], slots, sems)

    rings = (
        (0, done, out_done, cuts[0], slot_a),
        (1, done, out_done, cuts[1], slot_b),
        (2, late, out_late, cuts[2], slot_c),
        (3, late, out_late, cuts[3], slot_d),
        (4, total, out_own, cuts[4], slot_e),
        (5, total, out_own, cuts[5], slot_f),
    )
    first, second = ([ring(*v) for v in pair if v[3][1] > v[3][0]] for pair in (rings[:4], rings[4:]))

    def each(rings, name):
        return [getattr(v, name) for v in rings]

    def now(steps):
        for step in steps:
            step()

    middle, last = (n - 1) // 2, n - 1
    sums[0] = misc[...]
    small(0).start()
    swap.start()
    now(each(first, "start"))
    steps_of(0, middle, *each(first, "reduce"))
    small_step()
    steps_of(middle, last, *each(first, "reduce"))
    now(each(first, "turn"))
    small_step()
    swap.wait()
    total[...] = (own[...].astype(f32) + came[...].astype(f32)).astype(bf16)
    now(each(second, "start"))
    together = each(first, "gather") + each(second, "reduce")
    steps_of(0, middle, *together)
    small_step()
    steps_of(middle, last, *together)
    now(each(second, "turn"))
    small_step()
    steps_of(0, middle, *each(second, "gather"))
    small_step()
    steps_of(middle, last, *each(second, "gather"))
    for _ in swaps:
        small_step()
    out_misc[...] = sums[len(swaps)]
    steps_of(0, last, *each(first + second, "sent"))


def mix_sum(done, late, own, far, misc, n):
    if n == 1:
        misc = misc + core_swap(misc)
        own = (own.astype(f32) + chip_swap(far).astype(f32)).astype(bf16)
        return done, late, own, misc + chip_swap(misc)
    rows, cols = own.shape
    done_rows = done.shape[0]
    swaps = 2 + n.bit_length() - 1

    def two(total):
        lines = total // (32 * n)
        cut = (lines + 1) // 2 * 32 * n
        return (0, cut), (cut, total)

    cuts = two(done_rows) + two(rows) + two(rows)

    def body(*refs):
        mix_sum_kernel(n, cuts, *refs)

    vmem = pl.BlockSpec(memory_space=pltpu.VMEM)
    return pl.pallas_call(
        body,
        in_specs=[vmem] * 5,
        out_specs=[vmem] * 4,
        out_shape=[
            jax.ShapeDtypeStruct((done_rows, cols), bf16),
            jax.ShapeDtypeStruct((rows, cols), bf16),
            jax.ShapeDtypeStruct((rows, cols), bf16),
        ]
        + [jax.ShapeDtypeStruct(misc.shape, f32)],
        scratch_shapes=[
            pltpu.VMEM((rows, cols), bf16),
            pltpu.VMEM((rows, cols), bf16),
        ]
        + [
            pltpu.VMEM((2, n - 1, max(16, (stop - at) // (2 * n)), cols), bf16) for at, stop in cuts
        ]
        + [pltpu.SemaphoreType.DMA((6, 2, n - 1))] * 4
        + [pltpu.SemaphoreType.DMA] * 2
        + [
            pltpu.VMEM((swaps + 1,) + misc.shape, f32),
            pltpu.VMEM((swaps,) + misc.shape, f32),
            pltpu.SemaphoreType.DMA((swaps,)),
            pltpu.SemaphoreType.DMA((swaps,)),
        ],
        compiler_params=pltpu.CompilerParams(
            collective_id=0, has_side_effects=True, vmem_limit_bytes=VMEM_LIMIT
        ),
    )(done, late, own, far, misc)


def norm_scale(hidden):
    return lax.rsqrt(jnp.mean(hidden * hidden, axis=-1, keepdims=True) + epsilon)


def norm_low(hidden, gain):
    return (hidden * norm_scale(hidden) * gain).astype(bf16)


def norm_back(hidden, gain, grad_normed):
    scale = norm_scale(hidden)
    weighted = grad_normed * gain
    grad_hidden = scale * weighted - hidden * (scale * scale * scale) * jnp.mean(
        weighted * hidden, axis=-1, keepdims=True
    )
    return grad_hidden, jnp.sum(grad_normed * hidden * scale, axis=0)


def core_swap(value):
    return lax.ppermute(value, "head", [(i, i ^ 1) for i in range(4)])


def chip_swap(value):
    return lax.ppermute(value, "head", [(i, i ^ 2) for i in range(4)])


def dp_slice(own):
    parts = own.reshape((lax.axis_size("dp"), -1) + own.shape[1:])
    return lax.dynamic_index_in_dim(parts, lax.axis_index("dp"), 0, keepdims=False)


def dp_ring():
    n = lax.axis_size("dp")
    return list(range(0, n, 2)) + list(range(n - 1, 0, -2)) if n > 1 else [0]


def after(value, *others):
    return lax.optimization_barrier((value,) + others)[0]


def per_device(
    tokens, doc_starts, grad_out, norm_one, w_query, w_key, w_value, w_outgate, w_rank, w_decay,
    decay_bias, group_gain, w_out, norm_two, w_gate, w_up, w_down,
):
    shard_len, width = tokens.shape[1:]
    ndoc = doc_starts.shape[1]
    ff = w_gate.shape[2]
    ffp = -(-ff // 128) * 128
    rank = w_decay.shape[1]
    member = lax.axis_index("head")
    core = member % 2
    chip = member // 2
    meta = jnp.concatenate(
        [doc_starts[0], jnp.stack([chip * (2 * shard_len), core]).astype(jnp.int32)]
    )
    mixer = Mixer(meta, ndoc, 2 * shard_len)

    def mix_pack(layer):
        return jnp.concatenate(
            [w_query[layer], w_key[layer], w_value[layer], w_outgate[layer]], axis=1
        )

    gate_t, up_t, rank_t = (jnp.swapaxes(v, 1, 2) for v in (w_gate, w_up, w_rank))

    def ff_slice(layer, wait):
        part = jnp.concatenate([dp_slice(v[layer]) for v in (gate_t, up_t, w_down)], axis=0)
        return chip_swap(after(part, wait))

    def ff_gather(part):
        dp = lax.axis_size("dp")
        whole = lax.all_gather(part, "dp", axis=0, tiled=True)
        return jnp.swapaxes(whole.reshape(dp, 3, ff // dp, width), 0, 1).reshape(3 * ff, width)

    def with_partner(local):
        return jnp.concatenate([local, core_swap(local)], axis=0)

    def settle(terms):
        sent = core_swap(sum_of_dots(terms, shard_len, shard_len, bf16))
        return sum_of_dots(terms, 0, shard_len, f32) + sent.astype(f32)

    small = jnp.concatenate([w_decay.astype(f32), decay_bias[:, None, :]], axis=1)
    small = jnp.concatenate([small, chip_swap(small)], axis=2)
    mix_own = mix_pack(0)
    first_far = chip_swap(mix_own[:, : 2 * HK])
    ff_part = ff_slice(0, meta)
    ff_far = ff_gather(ff_part)
    mix_far = (first_far, chip_swap(after(mix_own[:, 2 * HK :], ff_part)))
    out_far = chip_swap(after(w_out[0], ff_part))
    next_part = ff_slice(1, mix_far[1])
    next_own = mix_pack(1)
    spare = -3 * ff % (32 * lax.axis_size("dp"))

    grad = grad_out[0].astype(f32)
    hidden = tokens[0].astype(f32)
    saved = []
    for layer in range(LAYERS):
        hidden_in = hidden
        a = with_partner(norm_low(hidden, norm_one[layer]))
        x = project(a, ((mix_own, None),) + tuple((v, None) for v in mix_far) + ((rank_t, layer),))
        wdec, bias = small[layer, :rank], small[layer, rank:]
        run, states, cum, final = mixer.states(x, wdec, bias)
        got = chip_swap(after(final, next_part, next_own) if layer == 0 else after(final, out_far))
        first = got[::-1] * chip.astype(bf16)
        gain = group_gain[layer][None]
        gated, mixed = mixer.mix(x, run, states, cum, first, gain)
        if layer + 1 < LAYERS:
            next_mix = (chip_swap(after(next_own, got)),)
            next_out = chip_swap(after(w_out[layer + 1], got))
            next_far = ff_gather(next_part)
        hidden_mid = hidden + settle(
            [(gated, 0, (w_out, layer), False), (gated, HV, (out_far, None), False)]
        )
        m_own = norm_low(hidden_mid, norm_two[layer])
        m = (m_own, core_swap(m_own))
        gate, up, product = ff_forward(m, (gate_t, layer), (up_t, layer), ff_far, ffp)
        if layer + 1 < LAYERS:
            product = after(product, next_mix[0])
        hidden = hidden_mid + settle(
            [(product, 0, (w_down, layer), False), (product, ffp, (ff_far, (2, ff)), False)]
        )
        saved.append(
            (hidden_in, hidden_mid, a, m, x, run, states, cum, first, mixed, gated, gate, up, product,
             mix_own, mix_far, out_far, ff_far)
        )
        if layer + 1 < LAYERS:
            mix_own, mix_far, out_far, ff_far = next_own, next_mix, next_out, next_far
    result = hidden.astype(bf16)[None]

    ff_grads, misc_grads = [None] * LAYERS, [None] * LAYERS
    for layer in reversed(range(LAYERS)):
        (
            hidden_in, hidden_mid, a, m, x, run, states, cum, first, mixed, gated, gate, up, product,
            mix_own, mix_far, out_far, ff_far,
        ) = saved[layer]
        gain = group_gain[layer][None]
        wdec, bias = small[layer, :rank], small[layer, rank:]
        if layer + 1 < LAYERS:
            g_own = grad.astype(bf16)
            g_y = chip_swap(g_own)
            mix_late = (own, chip_swap(after(far, g_y)))
        else:
            g_own = grad_out[0]
            g_y = chip_swap(after(g_own, got))
            m_y = chip_swap(jnp.concatenate([v[3][0] for v in saved], axis=0))
            m_far = (m_y, core_swap(m_y))
        g = (g_own, core_swap(g_own))
        dboth, dfar = ff_backward(g, gate, up, (w_down, layer), ff_far, ffp)
        back_mid, gain_two = norm_back(
            hidden_mid,
            norm_two[layer],
            settle(
                [
                    (dboth, 0, (gate_t, layer), False),
                    (dboth, ff, (up_t, layer), False),
                    (dfar, 0, (ff_far, (0, 2 * ff)), False),
                ]
            ),
        )
        ff_grad = ff_weight_grads(
            m + tuple(v[layer * shard_len : (layer + 1) * shard_len] for v in m_far), g + (g_y, core_swap(g_y)), dboth, product,
            (gate_t, layer), (up_t, layer), (w_down, layer), 0 if layer else spare,
        )
        grad = grad + back_mid
        g_mix = with_partner(grad.astype(bf16))
        if layer + 1 == LAYERS:
            g_mix = after(g_mix, ff_grad)
        g_wout = tn(g_mix, gated).astype(bf16)
        dmixed, doutgate, dstates, dcum, dfinal, dgain = mixer.back_states(
            x, run, mixed, g_mix, w_out[layer], out_far, gain
        )
        got = chip_swap(dfinal)
        dlast = got[::-1] * (1 - chip).astype(bf16)
        dx, dwdec, dbias = mixer.back(
            x, run, states, cum, first, dmixed, doutgate, dstates, dcum, dlast, wdec, bias
        )
        g_wmix = tn(a, dx[:, : 2 * HEAD_COLS]).astype(bf16)
        g_rank = tn(dx[:, 2 * HEAD_COLS :], a)
        if layer + 1 < LAYERS:
            mix_late = (mix_late[0].astype(f32) + after(mix_late[1], dx).astype(f32)).astype(bf16)
        far = jnp.concatenate([g_wmix[:, HEAD_COLS:], g_wout[:, HV:]], axis=1)
        own = jnp.concatenate([g_wmix[:, :HEAD_COLS], g_wout[:, :HV]], axis=1)
        far_terms, at = [], HEAD_COLS
        for part in mix_far:
            far_terms.append((dx, at, (part, None), True))
            at += part.shape[1]
        back_first, gain_one = norm_back(hidden_in, norm_one[layer], settle(
            [
                (dx, 0, (mix_own, None), True),
                *far_terms,
                (dx, 2 * HEAD_COLS, (rank_t, layer), False),
            ]
        ))
        grad = grad + back_first
        if layer > 0:
            ff_grads[layer] = lax.psum(ff_grad, "dp")
        heads = jnp.concatenate([dwdec, dbias], axis=0)
        places = lax.iota(jnp.int32, 4)[:, None, None]
        heads = jnp.where(places == member, heads[None, :, :HK], 0.0) + jnp.where(
            places == member ^ 2, heads[None, :, HK:], 0.0
        )
        misc_grads[layer] = jnp.concatenate(
            [g_rank.reshape(-1), gain_one, gain_two, dgain[0], heads.reshape(-1)]
        )

    misc = jnp.stack(misc_grads)
    length = misc.shape[1]
    misc = jnp.pad(misc.reshape(-1), (0, -misc.size % 1024)).reshape(-1, 128)
    ff_done, late_mix, first_mix, misc = mix_sum(ff_grad, mix_late, own, far, misc, lax.axis_size("dp"))
    mix_grads = [first_mix, late_mix]
    ff_grads[0] = ff_done
    misc = misc.reshape(-1)[: LAYERS * length].reshape(LAYERS, length)
    sizes = (rank * width, width, width, HV, 4 * (rank + 1) * HK)
    pieces, at = [], 0
    for size in sizes:
        pieces.append(misc[:, at : at + size])
        at += size
    heads = lax.dynamic_index_in_dim(
        pieces[4].reshape(LAYERS, 4, rank + 1, HK), member, axis=1, keepdims=False
    )

    query, key, value, outgate, out, gate, up, down = weight_outputs(mix_grads, ff_grads, ff)
    return (
        result,
        grad[None],
        pieces[1],
        query,
        key,
        value,
        outgate,
        jnp.swapaxes(pieces[0].reshape(LAYERS, rank, width), 1, 2),
        heads[:, :rank],
        heads[:, rank],
        pieces[3],
        out,
        pieces[2],
        jnp.swapaxes(gate, 1, 2),
        jnp.swapaxes(up, 1, 2),
        down,
    )


def solution(mesh):
    cols = P(None, None, "head")
    rows = P(None, "head", None)
    place = P("dp", "head", None)
    return jax.shard_map(
        per_device,
        mesh=mesh,
        in_specs=(
            place, P("dp", None), place, P(), cols, cols, cols, cols, P(), cols,
            P(None, "head"), P(), rows, P(), cols, cols, rows,
        ),
        out_specs=(
            place, place, P(), cols, cols, cols, cols, P(), cols, P(None, "head"), P(), rows,
            P(), cols, cols, rows,
        ),
        check_vma=False,
    )
```

```python
import jax
import jax.numpy as jnp
from jax import lax
from jax.experimental import pallas as pl
from jax.experimental.pallas import tpu as pltpu
from jax.sharding import PartitionSpec as P

LAYERS = 2
HK = 128
HV = 256
HEAD_COLS = 2 * HK + 2 * HV
BLK = 128
MID = BLK // 2 - 1
SUB = 2
epsilon = 1e-06
highest = lax.Precision.HIGHEST
VMEM_LIMIT = 48 * 1024 * 1024

f32 = jnp.float32
bf16 = jnp.bfloat16


def nn(left, right):
    return lax.dot_general(left, right, (((1,), (0,)), ((), ())), preferred_element_type=f32)


def nt(left, right):
    return lax.dot_general(left, right, (((1,), (1,)), ((), ())), preferred_element_type=f32)


def tn(left, right):
    return lax.dot_general(left, right, (((0,), (0,)), ((), ())), preferred_element_type=f32)


def doc_count(meta, ndoc, place):
    total = (meta[0] <= place).astype(jnp.int32)
    for which in range(1, ndoc):
        total = total + (meta[which] <= place).astype(jnp.int32)
    return total


def block_masks(meta, ndoc, start):
    rows = lax.broadcasted_iota(jnp.int32, (BLK, BLK), 0) + start
    cols = lax.broadcasted_iota(jnp.int32, (BLK, BLK), 1) + start
    row_ids = doc_count(meta, ndoc, rows)
    col_ids = doc_count(meta, ndoc, cols)
    id_prev = doc_count(meta, ndoc, start - 1)
    id_last = doc_count(meta, ndoc, start + BLK - 1)
    allowed = (rows >= cols) & (row_ids == col_ids)
    carried = jnp.where(row_ids == id_prev, 1.0, 0.0)
    same = jnp.where(row_ids == id_last, 1.0, 0.0)
    keep = jnp.where(id_last == id_prev, 1.0, 0.0)
    return allowed, carried, same, keep


def split_dot(ones_mat, value, dot):
    high = value.astype(bf16)
    low = (value - high.astype(f32)).astype(bf16)
    return dot(ones_mat, high) + dot(ones_mat, low)


def tri_ones():
    rows = lax.broadcasted_iota(jnp.int32, (BLK, BLK), 0)
    cols = lax.broadcasted_iota(jnp.int32, (BLK, BLK), 1)
    return jnp.where(rows >= cols, 1.0, 0.0).astype(bf16)


def head_parts(x_ref, slot):
    at = slot * HEAD_COLS
    query = x_ref[:, at : at + HK] * (HK**-0.5)
    key = x_ref[:, at + HK : at + 2 * HK]
    value = x_ref[:, at + 2 * HK : at + 2 * HK + HV]
    outgate = x_ref[:, at + 2 * HK + HV : at + HEAD_COLS]
    return query, key, value, outgate


def decay_before(x_ref, wdec_ref, bias_ref):
    ranked = x_ref[:, 2 * HEAD_COLS :]
    return jnp.dot(ranked, wdec_ref[...], precision=highest, preferred_element_type=f32) + bias_ref[...]


def states_kernel(ndoc, block, meta, x_ref, wdec_ref, bias_ref, run_ref, state_ref, cum_ref, final_ref, state, cum):
    start = meta[ndoc] + block * BLK
    _, _, same, keep = block_masks(meta, ndoc, start)
    before = decay_before(x_ref, wdec_ref, bias_ref)
    decays = (jnp.minimum(before, 0.0) - jnp.log1p(jnp.exp(-jnp.abs(before)))) * (1.0 / 16.0)
    running = split_dot(tri_ones(), decays, nn)
    run_ref[...] = running
    ending = running[BLK - 1 :, :]
    factor = jnp.exp(ending) * keep
    cum_ref[0] = cum[...]
    cum[...] = cum[...] * factor
    for slot in range(2):
        lanes = slice(slot * HK, slot * HK + HK)
        _, key, value, _ = head_parts(x_ref, slot)
        moved = (key * jnp.exp(ending[:, lanes] - running[:, lanes]) * same).astype(bf16)
        old = state[slot]
        state_ref[0, slot] = old.astype(bf16)
        new = old * factor[:, lanes] + tn(value.astype(bf16), moved)
        state[slot] = new
        final_ref[slot] = new.astype(bf16)


def mix_kernel(ndoc, block, meta, x_ref, run_ref, state_ref, cum_ref, first_ref, gain_ref, gated_ref, mixed_ref):
    start = meta[ndoc] + block * BLK
    allowed, carried, _, _ = block_masks(meta, ndoc, start)
    gain = gain_ref[...]
    for slot in range(2):
        lanes = slice(slot * HK, slot * HK + HK)
        cols = slice(slot * HV, slot * HV + HV)
        query, key, value, outgate = head_parts(x_ref, slot)
        running = run_ref[:, lanes]
        middle = running[MID : MID + 1, :]
        rel_query = (query * jnp.exp(running - middle)).astype(bf16)
        rel_key = (key * jnp.exp(middle - running)).astype(bf16)
        scores = jnp.where(allowed, nt(rel_query, rel_key), 0.0).astype(bf16)
        far_query = (query * jnp.exp(running) * carried).astype(bf16)
        state = (state_ref[0, slot].astype(f32) + first_ref[slot].astype(f32) * cum_ref[0][:, lanes]).astype(bf16)
        mixed = nn(scores, value.astype(bf16)) + nt(far_query, state)
        scale = lax.rsqrt(jnp.maximum(jnp.mean(mixed * mixed, axis=-1, keepdims=True), 1.0))
        gated_ref[:, cols] = (mixed * scale * gain * outgate * jax.nn.sigmoid(outgate)).astype(bf16)
        mixed_ref[:, cols] = mixed.astype(bf16)


def back_states_kernel(
    ndoc, block, meta, x_ref, run_ref, mixed_ref, grad_ref, own_out_ref, far_out_ref, gain_ref,
    dmixed_ref, doutgate_ref, dstate_ref, cum_ref, final_ref, dgain_ref, state, cum,
):
    start = meta[ndoc] + block * BLK
    _, carried, _, keep = block_masks(meta, ndoc, start)
    gain = gain_ref[...]
    running = run_ref[...]
    factor = jnp.exp(running[BLK - 1 :, :]) * keep
    cum_ref[0] = cum[...]
    cum[...] = cum[...] * factor
    for slot in range(2):
        lanes = slice(slot * HK, slot * HK + HK)
        cols = slice(slot * HV, slot * HV + HV)
        query, _, _, outgate = head_parts(x_ref, slot)
        mixed = mixed_ref[:, cols].astype(f32)
        dgated = nt(grad_ref[...], (own_out_ref, far_out_ref)[slot][...])
        mean = jnp.mean(mixed * mixed, axis=-1, keepdims=True)
        scale = lax.rsqrt(jnp.maximum(mean, 1.0))
        sig = jax.nn.sigmoid(outgate)
        silu = outgate * sig
        dnormed = dgated * silu
        plain = mixed * scale
        doutgate_ref[:, cols] = (dgated * plain * gain * (sig + silu * (1.0 - sig))).astype(bf16)
        dgain_ref[...] += jnp.sum(dnormed * plain, axis=0, keepdims=True)
        weighted = dnormed * gain
        inner = jnp.where(mean > 1.0, jnp.mean(weighted * plain, axis=-1, keepdims=True), 0.0)
        dmixed = (scale * (weighted - plain * inner)).astype(bf16)
        dmixed_ref[:, cols] = dmixed
        far_query = (query * jnp.exp(running[:, lanes]) * carried).astype(bf16)
        old = state[slot]
        dstate_ref[0, slot] = old.astype(bf16)
        new = old * factor[:, lanes] + tn(dmixed, far_query)
        state[slot] = new
        final_ref[slot] = new.astype(bf16)


def back_kernel(
    ndoc, block, meta, x_ref, run_ref, state_ref, cum_ref, first_ref, dmixed_ref, doutgate_ref,
    dstate_ref, dcum_ref, dlast_ref, wdec_ref, bias_ref, dx_ref, dwdec_ref, dbias_ref,
):
    start = meta[ndoc] + block * BLK
    allowed, carried, same, keep = block_masks(meta, ndoc, start)
    last_row = lax.broadcasted_iota(jnp.int32, (BLK, HK), 0) == BLK - 1
    drunning = []
    for slot in range(2):
        lanes = slice(slot * HK, slot * HK + HK)
        cols = slice(slot * HV, slot * HV + HV)
        at = slot * HEAD_COLS
        query, key, value, _ = head_parts(x_ref, slot)
        running = run_ref[:, lanes]
        middle = running[MID : MID + 1, :]
        ending = running[BLK - 1 :, :]
        up = jnp.exp(running - middle)
        down = jnp.exp(middle - running)
        far = jnp.exp(running) * carried
        near = jnp.exp(ending - running) * same
        rel_query = (query * up).astype(bf16)
        rel_key = (key * down).astype(bf16)
        far_query = (query * far).astype(bf16)
        moved = (key * near).astype(bf16)
        value = value.astype(bf16)
        scores = jnp.where(allowed, nt(rel_query, rel_key), 0.0).astype(bf16)
        state = state_ref[0, slot].astype(f32) + first_ref[slot].astype(f32) * cum_ref[0][:, lanes]
        dstate = dstate_ref[0, slot].astype(f32) + dlast_ref[slot].astype(f32) * dcum_ref[0][:, lanes]
        state_low = state.astype(bf16)
        dstate_low = dstate.astype(bf16)
        dmixed = dmixed_ref[:, cols]
        dvalue = tn(scores, dmixed) + nt(moved, dstate_low)
        dscores = jnp.where(allowed, nt(dmixed, value), 0.0).astype(bf16)
        drel_query = nn(dscores, rel_key)
        drel_key = tn(dscores, rel_query)
        dfar = nn(dmixed, state_low)
        dmoved = nn(value, dstate_low)
        dquery = drel_query * up + dfar * far
        dkey = drel_key * down + dmoved * near
        moved_grad = dmoved * moved.astype(f32)
        dending = jnp.sum(moved_grad, axis=0, keepdims=True) + jnp.sum(
            state * dstate, axis=0, keepdims=True
        ) * (jnp.exp(ending) * keep)
        drun = (
            drel_query * rel_query.astype(f32)
            - drel_key * rel_key.astype(f32)
            + dfar * far_query.astype(f32)
            - moved_grad
        )
        drunning.append(drun + jnp.where(last_row, dending, 0.0))
        dx_ref[:, at : at + HK] = (dquery * (HK**-0.5)).astype(bf16)
        dx_ref[:, at + HK : at + 2 * HK] = dkey.astype(bf16)
        dx_ref[:, at + 2 * HK : at + 2 * HK + HV] = dvalue.astype(bf16)
        dx_ref[:, at + 2 * HK + HV : at + HEAD_COLS] = doutgate_ref[:, cols]
    drun_both = jnp.concatenate(drunning, axis=1)
    ddecay = split_dot(tri_ones(), drun_both, tn)
    before = decay_before(x_ref, wdec_ref, bias_ref)
    dbefore = ddecay * (1.0 / 16.0) * jax.nn.sigmoid(-before)
    dbias_ref[...] += jnp.sum(dbefore, axis=0, keepdims=True)
    ranked = x_ref[:, 2 * HEAD_COLS :]
    dlow = dbefore.astype(bf16)
    dwdec_ref[...] += tn(ranked.astype(bf16), dlow)
    dx_ref[:, 2 * HEAD_COLS :] = nt(dlow, wdec_ref[...].astype(bf16)).astype(bf16)


def kernel_params():
    return pltpu.CompilerParams(dimension_semantics=("arbitrary",), vmem_limit_bytes=VMEM_LIMIT)


def sub_blocks(kernel, ndoc, tokens, rows, blocks, reverse, starts):
    steps = tokens // (BLK * SUB)

    def body(meta, *refs):
        step = pl.program_id(0)

        @pl.when(step == 0)
        def _():
            for which, value in starts:
                refs[which][...] = jnp.full_like(refs[which], value)

        first = (steps - 1 - step if reverse else step) * SUB
        for sub in reversed(range(SUB)) if reverse else range(SUB):
            views = [
                ref.at[sub * BLK : (sub + 1) * BLK] if i in rows
                else ref.at[sub : sub + 1] if i in blocks
                else ref
                for i, ref in enumerate(refs)
            ]
            kernel(ndoc, first + sub, meta, *views)

    return body


class Mixer:
    def __init__(self, meta, ndoc, tokens):
        self.meta = meta
        self.ndoc = ndoc
        self.tokens = tokens
        self.nblk = tokens // BLK
        self.steps = self.nblk // SUB

    def rows(self, width, reverse=False):
        steps, core = self.steps, self.ndoc + 1

        def place(step, meta):
            time = steps - 1 - step if reverse else step
            return (lax.rem(time + meta[core] * (steps // 2), steps), 0)

        return pl.BlockSpec((BLK * SUB, width), place)

    def per_block(self, shape, reverse=False):
        steps = self.steps
        zeros = (0,) * len(shape)
        return pl.BlockSpec(
            (SUB,) + shape, lambda step, meta: ((steps - 1 - step if reverse else step),) + zeros
        )

    def whole(self, shape):
        zeros = (0,) * len(shape)
        return pl.BlockSpec(shape, lambda step, meta: zeros)

    def call(self, kernel, layout, in_specs, out_specs, out_shape, scratch, *args):
        return pl.pallas_call(
            sub_blocks(kernel, self.ndoc, self.tokens, *layout),
            grid_spec=pltpu.PrefetchScalarGridSpec(
                num_scalar_prefetch=1,
                grid=(self.steps,),
                in_specs=in_specs,
                out_specs=out_specs,
                scratch_shapes=scratch,
            ),
            out_shape=[jax.ShapeDtypeStruct(s, d) for s, d in out_shape],
            cost_estimate=NO_COST,
            compiler_params=kernel_params(),
        )(self.meta, *args)

    def state_scratch(self):
        return [pltpu.VMEM((2, HV, HK), f32), pltpu.VMEM((1, 2 * HK), f32)]

    def states(self, x, wdec, bias):
        n = self.nblk
        return self.call(
            states_kernel,
            ((0, 3), (4, 5), False, ((7, 0.0), (8, 1.0))),
            [self.rows(x.shape[1]), self.whole(wdec.shape), self.whole(bias.shape)],
            [
                self.rows(2 * HK),
                self.per_block((2, HV, HK)),
                self.per_block((1, 2 * HK)),
                self.whole((2, HV, HK)),
            ],
            [
                ((self.tokens, 2 * HK), f32),
                ((n, 2, HV, HK), bf16),
                ((n, 1, 2 * HK), f32),
                ((2, HV, HK), bf16),
            ],
            self.state_scratch(),
            x, wdec, bias,
        )

    def mix(self, x, run, states, cum, first, gain):
        return self.call(
            mix_kernel,
            ((0, 1, 6, 7), (2, 3), False, ()),
            [
                self.rows(x.shape[1]),
                self.rows(2 * HK),
                self.per_block((2, HV, HK)),
                self.per_block((1, 2 * HK)),
                self.whole((2, HV, HK)),
                self.whole(gain.shape),
            ],
            [self.rows(2 * HV), self.rows(2 * HV)],
            [((self.tokens, 2 * HV), bf16), ((self.tokens, 2 * HV), bf16)],
            [],
            x, run, states, cum, first, gain,
        )

    def back_states(self, x, run, mixed, grad, own_out, far_out, gain):
        n = self.nblk
        return self.call(
            back_states_kernel,
            ((0, 1, 2, 3, 7, 8), (9, 10), True, ((12, 0.0), (13, 0.0), (14, 1.0))),
            [
                self.rows(x.shape[1], True),
                self.rows(2 * HK, True),
                self.rows(2 * HV, True),
                self.rows(grad.shape[1], True),
                self.whole(own_out.shape),
                self.whole(far_out.shape),
                self.whole(gain.shape),
            ],
            [
                self.rows(2 * HV, True),
                self.rows(2 * HV, True),
                self.per_block((2, HV, HK), True),
                self.per_block((1, 2 * HK), True),
                self.whole((2, HV, HK)),
                self.whole((1, HV)),
            ],
            [
                ((self.tokens, 2 * HV), bf16),
                ((self.tokens, 2 * HV), bf16),
                ((n, 2, HV, HK), bf16),
                ((n, 1, 2 * HK), f32),
                ((2, HV, HK), bf16),
                ((1, HV), f32),
            ],
            self.state_scratch(),
            x, run, mixed, grad, own_out, far_out, gain,
        )

    def back(self, x, run, states, cum, first, dmixed, doutgate, dstates, dcum, dlast, wdec, bias):
        rank = wdec.shape[0]
        return self.call(
            back_kernel,
            ((0, 1, 5, 6, 12), (2, 3, 7, 8), False, ((13, 0.0), (14, 0.0))),
            [
                self.rows(x.shape[1]),
                self.rows(2 * HK),
                self.per_block((2, HV, HK)),
                self.per_block((1, 2 * HK)),
                self.whole((2, HV, HK)),
                self.rows(2 * HV),
                self.rows(2 * HV),
                self.per_block((2, HV, HK)),
                self.per_block((1, 2 * HK)),
                self.whole((2, HV, HK)),
                self.whole(wdec.shape),
                self.whole(bias.shape),
            ],
            [self.rows(x.shape[1]), self.whole((rank, 2 * HK)), self.whole((1, 2 * HK))],
            [
                ((self.tokens, x.shape[1]), bf16),
                ((rank, 2 * HK), f32),
                ((1, 2 * HK), f32),
            ],
            [],
            x, run, states, cum, first, dmixed, doutgate, dstates, dcum, dlast, wdec, bias,
        )


ROWS_BLK = 256


def matrix_spec(part):
    array, which = part
    if array.ndim == 3:
        return pl.BlockSpec((None,) + array.shape[1:], lambda i: (which, 0, 0))
    if which is None:
        return pl.BlockSpec(array.shape, lambda i: (0, 0))
    at, rows = which
    return pl.BlockSpec((rows, array.shape[1]), lambda i: (at, 0))


def matrix_shape(part):
    array, which = part
    if array.ndim == 3 or which is None:
        return array.shape[-2:]
    return which[1], array.shape[1]


def row_spec(array, first=0):
    return pl.BlockSpec((ROWS_BLK, array.shape[1]), lambda i: (i + first, 0))


NO_COST = pl.CostEstimate(flops=0, bytes_accessed=0, transcendentals=0)


def local_call(body, grid, in_specs, out_specs, out_shape, args, scratch=()):
    return pl.pallas_call(
        body,
        grid=(grid,),
        in_specs=in_specs,
        out_specs=out_specs,
        out_shape=out_shape,
        scratch_shapes=list(scratch),
        cost_estimate=NO_COST,
        compiler_params=pltpu.CompilerParams(
            dimension_semantics=("arbitrary",), vmem_limit_bytes=VMEM_LIMIT
        ),
    )(*args)


def sum_of_dots(terms, first_row, rows, out_type):
    lefts = []
    for left, _, _, _ in terms:
        if not any(left is seen for seen in lefts):
            lefts.append(left)
    which = [next(i for i, seen in enumerate(lefts) if seen is left) for left, _, _, _ in terms]
    rights = [right for _, _, right, _ in terms]
    width = matrix_shape(rights[0])[0 if terms[0][3] else 1]

    def body(*refs):
        left_refs, right_refs, out = refs[: len(lefts)], refs[len(lefts) : -1], refs[-1]
        total = None
        for (_, at, _, turned), index, right in zip(terms, which, right_refs):
            depth = right.shape[1] if turned else right.shape[0]
            part = (nt if turned else nn)(left_refs[index][:, at : at + depth], right[...])
            total = part if total is None else total + part
        out[...] = total.astype(out_type)

    return local_call(
        body,
        rows // ROWS_BLK,
        [row_spec(v, first_row // ROWS_BLK) for v in lefts] + [matrix_spec(v) for v in rights],
        pl.BlockSpec((ROWS_BLK, width), lambda i: (i, 0)),
        jax.ShapeDtypeStruct((rows, width), out_type),
        lefts + [v[0] for v in rights],
    )


def project(a, parts):
    widths = [matrix_shape(v)[1] for v in parts[:-1]] + [matrix_shape(parts[-1])[0]]

    def body(left, *refs):
        out = refs[-1]
        at = 0
        for right, width in zip(refs[:-1], widths):
            turned = at + width == out.shape[1]
            out[:, at : at + width] = (nt if turned else nn)(left[...], right[...])
            at += width

    return local_call(
        body,
        a.shape[0] // ROWS_BLK,
        [row_spec(a)] + [matrix_spec(v) for v in parts],
        pl.BlockSpec((ROWS_BLK, sum(widths)), lambda i: (i, 0)),
        jax.ShapeDtypeStruct((a.shape[0], sum(widths)), f32),
        [a] + [v[0] for v in parts],
    )


def piece_specs(pieces):
    per = pieces[0].shape[0] // ROWS_BLK

    def spec(which, piece):
        return pl.BlockSpec(
            (ROWS_BLK, piece.shape[1]), lambda i: (jnp.clip(i - which * per, 0, per - 1), 0)
        )

    return [spec(which, piece) for which, piece in enumerate(pieces)]


def two_pieces(body, near, far):
    step = pl.program_id(0)
    half = pl.num_programs(0) // 2
    pl.when(step < half)(lambda: body(near))
    pl.when(step >= half)(lambda: body(far))


def ff_forward(pieces, gate_w, up_w, far, ffp):
    ff = matrix_shape(gate_w)[0]
    rows = sum(v.shape[0] for v in pieces)

    def body(near_ref, part_ref, gate_w, up_w, far_gate, far_up, gate_ref, up_ref, product_ref):
        def work(m_ref):
            m = m_ref[...]
            for slot, (gate_t, up_t) in enumerate(((gate_w, up_w), (far_gate, far_up))):
                gate, up = nt(m, gate_t[...]), nt(m, up_t[...])
                at = slot * ffp
                gate_ref[:, at : at + ff] = gate.astype(bf16)
                up_ref[:, at : at + ff] = up.astype(bf16)
                product_ref[:, at : at + ff] = (gate * jax.nn.sigmoid(gate) * up).astype(bf16)

        two_pieces(work, near_ref, part_ref)

    parts = [gate_w, up_w, (far, (0, ff)), (far, (1, ff))]
    return local_call(
        body,
        rows // ROWS_BLK,
        piece_specs(pieces) + [matrix_spec(v) for v in parts],
        [pl.BlockSpec((ROWS_BLK, 2 * ffp), lambda i: (i, 0))] * 3,
        [jax.ShapeDtypeStruct((rows, 2 * ffp), bf16)] * 3,
        list(pieces) + [v[0] for v in parts],
    )


def gate_pair(gate, up, dproduct):
    sig = jax.nn.sigmoid(gate)
    silu = gate * sig
    dgate = dproduct * up * (sig + silu * (1.0 - sig))
    return jnp.concatenate([dgate.astype(bf16), (dproduct * silu).astype(bf16)], axis=1), silu


def ff_backward(pieces, gate, up, down_w, far, ffp):
    ff = matrix_shape(down_w)[0]

    def body(near_ref, part_ref, gate_ref, up_ref, down_ref, far_ref, own_out, far_out):
        def work(g_ref):
            g = g_ref[...]
            for slot, (weight, out) in enumerate(((down_ref, own_out), (far_ref, far_out))):
                cols = slice(slot * ffp, slot * ffp + ff)
                out[...] = gate_pair(
                    gate_ref[:, cols].astype(f32), up_ref[:, cols].astype(f32), nt(g, weight[...])
                )[0]

        two_pieces(work, near_ref, part_ref)

    rows = gate.shape[0]
    parts = [down_w, (far, (2, ff))]
    return local_call(
        body,
        rows // ROWS_BLK,
        piece_specs(pieces) + [row_spec(gate), row_spec(up)] + [matrix_spec(v) for v in parts],
        [pl.BlockSpec((ROWS_BLK, 2 * ff), lambda i: (i, 0))] * 2,
        [jax.ShapeDtypeStruct((rows, 2 * ff), bf16)] * 2,
        list(pieces) + [gate, up] + [v[0] for v in parts],
    )


def ff_weight_grads(m_pieces, g_pieces, dboth, product, gate_w, up_w, down_w, spare):
    ff = matrix_shape(down_w)[0]
    rows, width = m_pieces[0][0].shape

    def body(m0, m1, m2, m3, g0, g1, g2, g3, both_ref, product_ref, gate_t, up_t, down_ref, out, total):
        step = pl.program_id(0)

        def add(both, product, m, g):
            for at, left, right in ((0, both, m), (2 * ff, product, g)):
                part = tn(left, right)
                place = slice(at, at + left.shape[1])

                @pl.when(step == 0)
                def _():
                    total[place] = part

                @pl.when(step > 0)
                def _():
                    total[place] += part

        def near(m_ref, g_ref):
            add(both_ref[...], product_ref[:, :ff], m_ref[...], g_ref[...])

        def far(m_ref, g_ref):
            m, g = m_ref[...], g_ref[...]
            gate, up = nt(m, gate_t[...]), nt(m, up_t[...])
            both, silu = gate_pair(gate, up, nt(g, down_ref[...]))
            add(both, (silu * up).astype(bf16), m, g)

        for which, (work, m_ref, g_ref) in enumerate(
            ((near, m0, g0), (near, m1, g1), (far, m2, g2), (far, m3, g3))
        ):
            pl.when(step == which)(lambda work=work, m_ref=m_ref, g_ref=g_ref: work(m_ref, g_ref))

        @pl.when(step == 3)
        def _():
            out[: 3 * ff] = total[...].astype(bf16)
            if spare:
                out[3 * ff :] = jnp.zeros((spare, width), bf16)

    parts = [gate_w, up_w, down_w]
    once = pl.Buffered(1)

    def alone(spec):
        return pl.BlockSpec(spec.block_shape, spec.index_map, pipeline_mode=once)

    pieces = list(m_pieces) + list(g_pieces)
    return local_call(
        body,
        4,
        [
            pl.BlockSpec((rows, width), lambda i, at=at: (at, 0), pipeline_mode=once) for _, at in pieces
        ]
        + [pl.BlockSpec((rows, v.shape[1]), lambda i: (jnp.minimum(i, 1), 0)) for v in (dboth, product)]
        + [alone(matrix_spec(v)) for v in parts],
        pl.BlockSpec((3 * ff + spare, width), lambda i: (0, 0), pipeline_mode=once),
        jax.ShapeDtypeStruct((3 * ff + spare, width), bf16),
        [v for v, _ in pieces] + [dboth, product] + [v[0] for v in parts],
        scratch=[pltpu.VMEM((3 * ff, width), f32)],
    )


def weight_outputs(mix_grads, ff_grads, ff):
    rows, cols = mix_grads[0].shape
    steps = 4
    high, flat = rows // steps, ff // steps
    widths = (HK, HK, HV, HV)

    def body(*refs):
        ins, outs = refs[: 4 * LAYERS], refs[4 * LAYERS :]

        def work(mix, *parts):
            at = 0
            for ref, width in zip(outs, widths):
                ref[0] = mix[:, at : at + width].astype(f32)
                at += width
            outs[4][0] = mix[:, at : at + HV].astype(f32).T
            for ref, part in zip(outs[5:], parts):
                ref[0] = part[...].astype(f32)

        for layer in range(LAYERS):
            mine = ins[4 * layer : 4 * layer + 4]
            pl.when(pl.program_id(0) == layer)(lambda mine=mine: work(*mine))

    def spec(layer, height, first):
        def place(now, step):
            held = jnp.where(now < layer, 0, steps - 1)
            return (first + jnp.where(now == layer, step, held), 0)

        return pl.BlockSpec((height, cols), place)

    in_specs, args = [], []
    for layer in range(LAYERS):
        in_specs += [spec(layer, high, 0)] + [spec(layer, flat, part * steps) for part in range(3)]
        args += [mix_grads[layer]] + [ff_grads[layer]] * 3
    out_specs = [pl.BlockSpec((1, high, width), lambda now, step: (now, step, 0)) for width in widths]
    out_specs += [pl.BlockSpec((1, HV, high), lambda now, step: (now, 0, step))]
    out_specs += [pl.BlockSpec((1, flat, cols), lambda now, step: (now, step, 0))] * 3
    shapes = [(LAYERS, rows, width) for width in widths] + [(LAYERS, HV, rows)] + [(LAYERS, ff, cols)] * 3
    return pl.pallas_call(
        body,
        grid=(LAYERS, steps),
        in_specs=in_specs,
        out_specs=out_specs,
        out_shape=[jax.ShapeDtypeStruct(v, f32) for v in shapes],
        cost_estimate=NO_COST,
        compiler_params=pltpu.CompilerParams(
            dimension_semantics=("arbitrary", "arbitrary"), vmem_limit_bytes=VMEM_LIMIT
        ),
    )(*args)


def ring_place(index, n):
    return jnp.where(index % 2 == 0, index // 2, n - 1 - index // 2)


def ring_index(place, n):
    return jnp.where(place < n // 2, 2 * place, 2 * (n - 1 - place) + 1)


MESH = pl.DeviceIdType.MESH


class Ring:
    def __init__(self, n, data, out, slots, sems):
        self.n, self.data, self.out, self.slots = n, data, out, slots
        self.send, self.recv, self.out_send, self.out_recv = sems
        self.me = ring_place(lax.axis_index("dp"), n)
        self.peers = [
            ring_index(lax.rem(self.me + 1, n), n),
            ring_index(lax.rem(self.me + n - 1, n), n),
        ]
        self.rows = data.shape[0] // (2 * n)

    def chunk(self, ref, way, back):
        which = lax.rem(self.me + 2 * self.n - (1, -1)[way] * back, self.n)
        return ref.at[pl.ds(pl.multiple_of((2 * which + way) * self.rows, 16), self.rows)]

    def partial(self, way, source, step):
        return pltpu.make_async_remote_copy(
            src_ref=source, dst_ref=self.slots.at[way, step],
            send_sem=self.send.at[way, step], recv_sem=self.recv.at[way, step],
            device_id={"dp": self.peers[way]}, device_id_type=MESH,
        )

    def final(self, way, step, back):
        part = self.chunk(self.out, way, back)
        return pltpu.make_async_remote_copy(
            src_ref=part, dst_ref=part,
            send_sem=self.out_send.at[way, step], recv_sem=self.out_recv.at[way, step],
            device_id={"dp": self.peers[way]}, device_id_type=MESH,
        )

    def start(self):
        for way in range(2):
            self.partial(way, self.chunk(self.data, way, 0), 0).start()

    def reduce(self, step):
        for way in range(2):
            slot = self.slots.at[way, step]
            self.partial(way, slot, step).wait_recv()
            part = self.chunk(self.data, way, step + 1)
            slot[...] = (slot[...].astype(f32) + part[...].astype(f32)).astype(bf16)

            @pl.when(step < self.n - 2)
            def _():
                self.partial(way, slot, step + 1).start()

    def turn(self):
        for way in range(2):
            self.chunk(self.out, way, -1)[...] = self.slots[way, self.n - 2]
            self.final(way, 0, -1).start()

    def gather(self, step):
        for way in range(2):
            self.final(way, step, step).wait_recv()

            @pl.when(step < self.n - 2)
            def _():
                self.final(way, step + 1, step).start()

    def sent(self, step):
        for way in range(2):
            self.partial(way, self.slots.at[way, step], step).wait_send()
            self.final(way, step, step - 1).wait_send()


def steps_of(lo, hi, *bodies):
    def body(step, carry):
        for each in bodies:
            each(step)
        return carry

    lax.fori_loop(lo, hi, body, 0)


def mix_sum_kernel(
    n, cuts, done, late, own, far, misc, out_done, out_late, out_own, out_misc, came, total,
    slot_a, slot_b, slot_c, slot_d, slot_e, slot_f,
    send, recv, out_send, out_recv, chip_send, chip_recv, sums, misc_came, misc_send, misc_recv,
):
    me = ring_place(lax.axis_index("dp"), n)
    member, row = lax.axis_index("head"), lax.axis_index("dp")
    swaps = [{"head": member ^ 1}, {"head": member ^ 2}]
    swaps += [{"dp": row ^ (1 << bit)} for bit in range(n.bit_length() - 1)]
    peers = swaps + [
        {"dp": ring_index(lax.rem(me + 1, n), n)},
        {"dp": ring_index(lax.rem(me + n - 1, n), n)},
    ]
    barrier = pltpu.get_barrier_semaphore()
    for peer in peers:
        pl.semaphore_signal(barrier, inc=1, device_id=peer, device_id_type=MESH)
    pl.semaphore_wait(barrier, len(peers))

    def small(step):
        return pltpu.make_async_remote_copy(
            src_ref=sums.at[step], dst_ref=misc_came.at[step],
            send_sem=misc_send.at[step], recv_sem=misc_recv.at[step],
            device_id=swaps[step], device_id_type=MESH,
        )

    taken = [0]

    def small_step():
        step = taken[0]
        if step == len(swaps):
            return
        small(step).wait()
        sums[step + 1] = sums[step] + misc_came[step]
        taken[0] += 1
        if step + 1 < len(swaps):
            small(step + 1).start()

    swap = pltpu.make_async_remote_copy(
        src_ref=far, dst_ref=came, send_sem=chip_send, recv_sem=chip_recv,
        device_id={"head": member ^ 2}, device_id_type=MESH,
    )
    def ring(which, data, out, cut, slots):
        rows = slice(*cut)
        sems = [v.at[which] for v in (send, recv, out_send, out_recv)]
        return Ring(n, data.at[rows], out.at[rows], slots, sems)

    rings = (
        (0, done, out_done, cuts[0], slot_a),
        (1, done, out_done, cuts[1], slot_b),
        (2, late, out_late, cuts[2], slot_c),
        (3, late, out_late, cuts[3], slot_d),
        (4, total, out_own, cuts[4], slot_e),
        (5, total, out_own, cuts[5], slot_f),
    )
    first, second = ([ring(*v) for v in pair if v[3][1] > v[3][0]] for pair in (rings[:4], rings[4:]))

    def each(rings, name):
        return [getattr(v, name) for v in rings]

    def now(steps):
        for step in steps:
            step()

    middle, last = (n - 1) // 2, n - 1
    sums[0] = misc[...]
    small(0).start()
    swap.start()
    now(each(first, "start"))
    steps_of(0, middle, *each(first, "reduce"))
    small_step()
    steps_of(middle, last, *each(first, "reduce"))
    now(each(first, "turn"))
    small_step()
    swap.wait()
    total[...] = (own[...].astype(f32) + came[...].astype(f32)).astype(bf16)
    now(each(second, "start"))
    together = each(first, "gather") + each(second, "reduce")
    steps_of(0, middle, *together)
    small_step()
    steps_of(middle, last, *together)
    now(each(second, "turn"))
    small_step()
    steps_of(0, middle, *each(second, "gather"))
    small_step()
    steps_of(middle, last, *each(second, "gather"))
    for _ in swaps:
        small_step()
    out_misc[...] = sums[len(swaps)]
    steps_of(0, last, *each(first + second, "sent"))


def mix_sum(done, late, own, far, misc, n):
    if n == 1:
        misc = misc + core_swap(misc)
        own = (own.astype(f32) + chip_swap(far).astype(f32)).astype(bf16)
        return done, late, own, misc + chip_swap(misc)
    rows, cols = own.shape
    done_rows = done.shape[0]
    swaps = 2 + n.bit_length() - 1

    def two(total):
        lines = total // (32 * n)
        cut = (lines + 1) // 2 * 32 * n
        return (0, cut), (cut, total)

    cuts = two(done_rows) + two(rows) + two(rows)

    def body(*refs):
        mix_sum_kernel(n, cuts, *refs)

    vmem = pl.BlockSpec(memory_space=pltpu.VMEM)
    return pl.pallas_call(
        body,
        in_specs=[vmem] * 5,
        out_specs=[vmem] * 4,
        out_shape=[
            jax.ShapeDtypeStruct((done_rows, cols), bf16),
            jax.ShapeDtypeStruct((rows, cols), bf16),
            jax.ShapeDtypeStruct((rows, cols), bf16),
        ]
        + [jax.ShapeDtypeStruct(misc.shape, f32)],
        scratch_shapes=[
            pltpu.VMEM((rows, cols), bf16),
            pltpu.VMEM((rows, cols), bf16),
        ]
        + [
            pltpu.VMEM((2, n - 1, max(16, (stop - at) // (2 * n)), cols), bf16) for at, stop in cuts
        ]
        + [pltpu.SemaphoreType.DMA((6, 2, n - 1))] * 4
        + [pltpu.SemaphoreType.DMA] * 2
        + [
            pltpu.VMEM((swaps + 1,) + misc.shape, f32),
            pltpu.VMEM((swaps,) + misc.shape, f32),
            pltpu.SemaphoreType.DMA((swaps,)),
            pltpu.SemaphoreType.DMA((swaps,)),
        ],
        compiler_params=pltpu.CompilerParams(
            collective_id=0, has_side_effects=True, vmem_limit_bytes=VMEM_LIMIT
        ),
    )(done, late, own, far, misc)


def norm_scale(hidden):
    return lax.rsqrt(jnp.mean(hidden * hidden, axis=-1, keepdims=True) + epsilon)


def norm_low(hidden, gain):
    return (hidden * norm_scale(hidden) * gain).astype(bf16)


def norm_back(hidden, gain, grad_normed):
    scale = norm_scale(hidden)
    weighted = grad_normed * gain
    grad_hidden = scale * weighted - hidden * (scale * scale * scale) * jnp.mean(
        weighted * hidden, axis=-1, keepdims=True
    )
    return grad_hidden, jnp.sum(grad_normed * hidden * scale, axis=0)


def core_swap(value):
    return lax.ppermute(value, "head", [(i, i ^ 1) for i in range(4)])


def chip_swap(value):
    return lax.ppermute(value, "head", [(i, i ^ 2) for i in range(4)])


def dp_slices(arrays, layer):
    n = lax.axis_size("dp")
    height, width = arrays[0].shape[1] // n, arrays[0].shape[2]
    views = [v.reshape(v.shape[0], n, height, width) for v in arrays]

    def body(at, *refs):
        for which, ref in enumerate(refs[:-1]):
            refs[-1][which] = ref[...]

    return pl.pallas_call(
        body,
        grid_spec=pltpu.PrefetchScalarGridSpec(
            num_scalar_prefetch=1,
            grid=(1,),
            in_specs=[pl.BlockSpec((None, None, height, width), lambda i, at: (layer, at[0], 0, 0))] * len(views),
            out_specs=pl.BlockSpec((len(views), height, width), lambda i, at: (0, 0, 0)),
        ),
        out_shape=jax.ShapeDtypeStruct((len(views), height, width), bf16),
        cost_estimate=NO_COST,
        compiler_params=kernel_params(),
    )(lax.axis_index("dp").astype(jnp.int32).reshape(1), *views)


def dp_ring():
    n = lax.axis_size("dp")
    return list(range(0, n, 2)) + list(range(n - 1, 0, -2)) if n > 1 else [0]


def after(value, *others):
    return lax.optimization_barrier((value,) + others)[0]


def per_device(
    tokens, doc_starts, grad_out, norm_one, w_query, w_key, w_value, w_outgate, w_rank, w_decay,
    decay_bias, group_gain, w_out, norm_two, w_gate, w_up, w_down,
):
    shard_len, width = tokens.shape[1:]
    ndoc = doc_starts.shape[1]
    ff = w_gate.shape[2]
    ffp = -(-ff // 128) * 128
    rank = w_decay.shape[1]
    member = lax.axis_index("head")
    core = member % 2
    chip = member // 2
    meta = jnp.concatenate(
        [doc_starts[0], jnp.stack([chip * (2 * shard_len), core]).astype(jnp.int32)]
    )
    mixer = Mixer(meta, ndoc, 2 * shard_len)

    def mix_pack(layer):
        return jnp.concatenate(
            [w_query[layer], w_key[layer], w_value[layer], w_outgate[layer]], axis=1
        )

    gate_t, up_t, rank_t = (jnp.swapaxes(v, 1, 2) for v in (w_gate, w_up, w_rank))

    def ff_slice(layer, wait):
        return chip_swap(after(dp_slices((gate_t, up_t, w_down), layer), wait))

    def ff_gather(part):
        dp = lax.axis_size("dp")
        whole = lax.all_gather(part, "dp", axis=0, tiled=True)
        return jnp.swapaxes(whole.reshape(dp, 3, ff // dp, width), 0, 1).reshape(3 * ff, width)

    def with_partner(local):
        return jnp.concatenate([local, core_swap(local)], axis=0)

    def settle(terms):
        sent = core_swap(sum_of_dots(terms, shard_len, shard_len, bf16))
        return sum_of_dots(terms, 0, shard_len, f32) + sent.astype(f32)

    small = jnp.concatenate([w_decay.astype(f32), decay_bias[:, None, :]], axis=1)
    small = jnp.concatenate([small, chip_swap(small)], axis=2)
    ff_part = ff_slice(0, meta)
    ff_far = ff_gather(ff_part)
    mix_own = mix_pack(0)
    mix_far = chip_swap(after(mix_own, ff_part))
    out_far = chip_swap(after(w_out[0], mix_far))
    next_own = mix_pack(1)
    spare = -3 * ff % (32 * lax.axis_size("dp"))

    grad = grad_out[0].astype(f32)
    hidden = tokens[0].astype(f32)
    saved = []
    for layer in range(LAYERS):
        hidden_in = hidden
        a = with_partner(norm_low(hidden, norm_one[layer]))
        x = project(a, ((mix_own, None), (mix_far, None), (rank_t, layer)))
        if layer == 0:
            next_part = ff_slice(1, x)
        wdec, bias = small[layer, :rank], small[layer, rank:]
        run, states, cum, final = mixer.states(x, wdec, bias)
        got = chip_swap(after(final, next_part, next_own) if layer == 0 else after(final, out_far))
        first = got[::-1] * chip.astype(bf16)
        gain = group_gain[layer][None]
        gated, mixed = mixer.mix(x, run, states, cum, first, gain)
        if layer + 1 < LAYERS:
            next_mix = chip_swap(after(next_own, got))
            next_out = chip_swap(after(w_out[layer + 1], got))
            next_far = ff_gather(next_part)
        if layer > 0:
            gated = after(gated, ff_far)
        hidden_mid = hidden + settle(
            [(gated, 0, (w_out, layer), False), (gated, HV, (out_far, None), False)]
        )
        m_own = norm_low(hidden_mid, norm_two[layer])
        m = (m_own, core_swap(m_own))
        gate, up, product = ff_forward(m, (gate_t, layer), (up_t, layer), ff_far, ffp)
        if layer + 1 < LAYERS:
            product = after(product, next_mix)
        hidden = hidden_mid + settle(
            [(product, 0, (w_down, layer), False), (product, ffp, (ff_far, (2, ff)), False)]
        )
        saved.append(
            (hidden_in, hidden_mid, a, m, x, run, states, cum, first, mixed, gated, gate, up, product,
             mix_own, mix_far, out_far, ff_far)
        )
        if layer + 1 < LAYERS:
            mix_own, mix_far, out_far, ff_far = next_own, next_mix, next_out, next_far
    result = hidden.astype(bf16)[None]

    ff_grads, misc_grads = [None] * LAYERS, [None] * LAYERS
    for layer in reversed(range(LAYERS)):
        (
            hidden_in, hidden_mid, a, m, x, run, states, cum, first, mixed, gated, gate, up, product,
            mix_own, mix_far, out_far, ff_far,
        ) = saved[layer]
        gain = group_gain[layer][None]
        wdec, bias = small[layer, :rank], small[layer, rank:]
        if layer + 1 < LAYERS:
            g_own = grad.astype(bf16)
            g_y = chip_swap(g_own)
            g_far = [(g_y, 0), (core_swap(g_y), 0)]
            mix_late = (own, chip_swap(after(far, g_y)))
        else:
            g_own = grad_out[0]
            came = chip_swap(jnp.concatenate([v[3][0] for v in saved] + [g_own], axis=0))
            came = (came, core_swap(came))
            g_far = [(v, LAYERS) for v in came]
        g = (g_own, core_swap(g_own))
        dboth, dfar = ff_backward(g, gate, up, (w_down, layer), ff_far, ffp)
        back_mid, gain_two = norm_back(
            hidden_mid,
            norm_two[layer],
            settle(
                [
                    (dboth, 0, (gate_t, layer), False),
                    (dboth, ff, (up_t, layer), False),
                    (dfar, 0, (ff_far, (0, 2 * ff)), False),
                ]
            ),
        )
        ff_grad = ff_weight_grads(
            [(v, 0) for v in m] + [(v, layer) for v in came], [(v, 0) for v in g] + g_far, dboth, product,
            (gate_t, layer), (up_t, layer), (w_down, layer), 0 if layer else spare,
        )
        grad = grad + back_mid
        g_mix = with_partner(grad.astype(bf16))
        if layer + 1 == LAYERS:
            g_mix = after(g_mix, ff_grad)
        g_wout = tn(g_mix, gated).astype(bf16)
        dmixed, doutgate, dstates, dcum, dfinal, dgain = mixer.back_states(
            x, run, mixed, g_mix, w_out[layer], out_far, gain
        )
        got = chip_swap(dfinal)
        dlast = got[::-1] * (1 - chip).astype(bf16)
        dx, dwdec, dbias = mixer.back(
            x, run, states, cum, first, dmixed, doutgate, dstates, dcum, dlast, wdec, bias
        )
        g_wmix = tn(a, dx[:, : 2 * HEAD_COLS]).astype(bf16)
        g_rank = tn(dx[:, 2 * HEAD_COLS :], a)
        if layer + 1 < LAYERS:
            mix_late = (mix_late[0].astype(f32) + after(mix_late[1], dx).astype(f32)).astype(bf16)
        far = jnp.concatenate([g_wmix[:, HEAD_COLS:], g_wout[:, HV:]], axis=1)
        own = jnp.concatenate([g_wmix[:, :HEAD_COLS], g_wout[:, :HV]], axis=1)
        back_first, gain_one = norm_back(hidden_in, norm_one[layer], settle(
            [
                (dx, 0, (mix_own, None), True),
                (dx, HEAD_COLS, (mix_far, None), True),
                (dx, 2 * HEAD_COLS, (rank_t, layer), False),
            ]
        ))
        grad = grad + back_first
        if layer > 0:
            ff_grads[layer] = lax.psum(ff_grad, "dp")
        heads = jnp.concatenate([dwdec, dbias], axis=0)
        places = lax.iota(jnp.int32, 4)[:, None, None]
        heads = jnp.where(places == member, heads[None, :, :HK], 0.0) + jnp.where(
            places == member ^ 2, heads[None, :, HK:], 0.0
        )
        misc_grads[layer] = jnp.concatenate(
            [g_rank.reshape(-1), gain_one, gain_two, dgain[0], heads.reshape(-1)]
        )

    misc = jnp.stack(misc_grads)
    length = misc.shape[1]
    misc = jnp.pad(misc.reshape(-1), (0, -misc.size % 1024)).reshape(-1, 128)
    ff_done, late_mix, first_mix, misc = mix_sum(ff_grad, mix_late, own, far, misc, lax.axis_size("dp"))
    mix_grads = [first_mix, late_mix]
    ff_grads[0] = ff_done
    misc = misc.reshape(-1)[: LAYERS * length].reshape(LAYERS, length)
    sizes = (rank * width, width, width, HV, 4 * (rank + 1) * HK)
    pieces, at = [], 0
    for size in sizes:
        pieces.append(misc[:, at : at + size])
        at += size
    heads = lax.dynamic_index_in_dim(
        pieces[4].reshape(LAYERS, 4, rank + 1, HK), member, axis=1, keepdims=False
    )

    query, key, value, outgate, out, gate, up, down = weight_outputs(mix_grads, ff_grads, ff)
    return (
        result,
        grad[None],
        pieces[1],
        query,
        key,
        value,
        outgate,
        jnp.swapaxes(pieces[0].reshape(LAYERS, rank, width), 1, 2),
        heads[:, :rank],
        heads[:, rank],
        pieces[3],
        out,
        pieces[2],
        jnp.swapaxes(gate, 1, 2),
        jnp.swapaxes(up, 1, 2),
        down,
    )


def solution(mesh):
    cols = P(None, None, "head")
    rows = P(None, "head", None)
    place = P("dp", "head", None)
    return jax.shard_map(
        per_device,
        mesh=mesh,
        in_specs=(
            place, P("dp", None), place, P(), cols, cols, cols, cols, P(), cols,
            P(None, "head"), P(), rows, P(), cols, cols, rows,
        ),
        out_specs=(
            place, place, P(), cols, cols, cols, cols, P(), cols, P(None, "head"), P(), rows,
            P(), cols, cols, rows,
        ),
        check_vma=False,
    )
```

```python
import jax
import jax.numpy as jnp
from jax import lax
from jax.experimental import pallas as pl
from jax.experimental.pallas import tpu as pltpu
from jax.sharding import PartitionSpec as P

LAYERS = 2
HK = 128
HV = 256
HEAD_COLS = 2 * HK + 2 * HV
BLK = 128
MID = BLK // 2 - 1
SUB = 2
epsilon = 1e-06
highest = lax.Precision.HIGHEST
VMEM_LIMIT = 48 * 1024 * 1024

f32 = jnp.float32
bf16 = jnp.bfloat16


def nn(left, right):
    return lax.dot_general(left, right, (((1,), (0,)), ((), ())), preferred_element_type=f32)


def nt(left, right):
    return lax.dot_general(left, right, (((1,), (1,)), ((), ())), preferred_element_type=f32)


def tn(left, right):
    return lax.dot_general(left, right, (((0,), (0,)), ((), ())), preferred_element_type=f32)


def doc_count(meta, ndoc, place):
    total = (meta[0] <= place).astype(jnp.int32)
    for which in range(1, ndoc):
        total = total + (meta[which] <= place).astype(jnp.int32)
    return total


def block_masks(meta, ndoc, start):
    rows = lax.broadcasted_iota(jnp.int32, (BLK, BLK), 0) + start
    cols = lax.broadcasted_iota(jnp.int32, (BLK, BLK), 1) + start
    row_ids = doc_count(meta, ndoc, rows)
    col_ids = doc_count(meta, ndoc, cols)
    id_prev = doc_count(meta, ndoc, start - 1)
    id_last = doc_count(meta, ndoc, start + BLK - 1)
    allowed = (rows >= cols) & (row_ids == col_ids)
    carried = jnp.where(row_ids == id_prev, 1.0, 0.0)
    same = jnp.where(row_ids == id_last, 1.0, 0.0)
    keep = jnp.where(id_last == id_prev, 1.0, 0.0)
    return allowed, carried, same, keep


def split_dot(ones_mat, value, dot):
    high = value.astype(bf16)
    low = (value - high.astype(f32)).astype(bf16)
    return dot(ones_mat, high) + dot(ones_mat, low)


def tri_ones():
    rows = lax.broadcasted_iota(jnp.int32, (BLK, BLK), 0)
    cols = lax.broadcasted_iota(jnp.int32, (BLK, BLK), 1)
    return jnp.where(rows >= cols, 1.0, 0.0).astype(bf16)


def head_parts(x_ref, slot):
    at = slot * HEAD_COLS
    query = x_ref[:, at : at + HK] * (HK**-0.5)
    key = x_ref[:, at + HK : at + 2 * HK]
    value = x_ref[:, at + 2 * HK : at + 2 * HK + HV]
    outgate = x_ref[:, at + 2 * HK + HV : at + HEAD_COLS]
    return query, key, value, outgate


def decay_before(x_ref, wdec_ref, bias_ref):
    ranked = x_ref[:, 2 * HEAD_COLS :]
    return jnp.dot(ranked, wdec_ref[...], precision=highest, preferred_element_type=f32) + bias_ref[...]


def states_kernel(ndoc, block, meta, x_ref, wdec_ref, bias_ref, run_ref, state_ref, cum_ref, final_ref, state, cum):
    start = meta[ndoc] + block * BLK
    _, _, same, keep = block_masks(meta, ndoc, start)
    before = decay_before(x_ref, wdec_ref, bias_ref)
    decays = (jnp.minimum(before, 0.0) - jnp.log1p(jnp.exp(-jnp.abs(before)))) * (1.0 / 16.0)
    running = split_dot(tri_ones(), decays, nn)
    run_ref[...] = running
    ending = running[BLK - 1 :, :]
    factor = jnp.exp(ending) * keep
    cum_ref[0] = cum[...]
    cum[...] = cum[...] * factor
    for slot in range(2):
        lanes = slice(slot * HK, slot * HK + HK)
        _, key, value, _ = head_parts(x_ref, slot)
        moved = (key * jnp.exp(ending[:, lanes] - running[:, lanes]) * same).astype(bf16)
        old = state[slot]
        state_ref[0, slot] = old.astype(bf16)
        new = old * factor[:, lanes] + tn(value.astype(bf16), moved)
        state[slot] = new
        final_ref[slot] = new.astype(bf16)


def mix_kernel(ndoc, block, meta, x_ref, run_ref, state_ref, cum_ref, first_ref, gain_ref, gated_ref, mixed_ref):
    start = meta[ndoc] + block * BLK
    allowed, carried, _, _ = block_masks(meta, ndoc, start)
    gain = gain_ref[...]
    for slot in range(2):
        lanes = slice(slot * HK, slot * HK + HK)
        cols = slice(slot * HV, slot * HV + HV)
        query, key, value, outgate = head_parts(x_ref, slot)
        running = run_ref[:, lanes]
        middle = running[MID : MID + 1, :]
        rel_query = (query * jnp.exp(running - middle)).astype(bf16)
        rel_key = (key * jnp.exp(middle - running)).astype(bf16)
        scores = jnp.where(allowed, nt(rel_query, rel_key), 0.0).astype(bf16)
        far_query = (query * jnp.exp(running) * carried).astype(bf16)
        state = (state_ref[0, slot].astype(f32) + first_ref[slot].astype(f32) * cum_ref[0][:, lanes]).astype(bf16)
        mixed = nn(scores, value.astype(bf16)) + nt(far_query, state)
        scale = lax.rsqrt(jnp.maximum(jnp.mean(mixed * mixed, axis=-1, keepdims=True), 1.0))
        gated_ref[:, cols] = (mixed * scale * gain * outgate * jax.nn.sigmoid(outgate)).astype(bf16)
        mixed_ref[:, cols] = mixed.astype(bf16)


def back_states_kernel(
    ndoc, block, meta, x_ref, run_ref, mixed_ref, grad_ref, own_out_ref, far_out_ref, gain_ref,
    dmixed_ref, doutgate_ref, dstate_ref, cum_ref, final_ref, dgain_ref, state, cum,
):
    start = meta[ndoc] + block * BLK
    _, carried, _, keep = block_masks(meta, ndoc, start)
    gain = gain_ref[...]
    running = run_ref[...]
    factor = jnp.exp(running[BLK - 1 :, :]) * keep
    cum_ref[0] = cum[...]
    cum[...] = cum[...] * factor
    for slot in range(2):
        lanes = slice(slot * HK, slot * HK + HK)
        cols = slice(slot * HV, slot * HV + HV)
        query, _, _, outgate = head_parts(x_ref, slot)
        mixed = mixed_ref[:, cols].astype(f32)
        dgated = nt(grad_ref[...], (own_out_ref, far_out_ref)[slot][...])
        mean = jnp.mean(mixed * mixed, axis=-1, keepdims=True)
        scale = lax.rsqrt(jnp.maximum(mean, 1.0))
        sig = jax.nn.sigmoid(outgate)
        silu = outgate * sig
        dnormed = dgated * silu
        plain = mixed * scale
        doutgate_ref[:, cols] = (dgated * plain * gain * (sig + silu * (1.0 - sig))).astype(bf16)
        dgain_ref[...] += jnp.sum(dnormed * plain, axis=0, keepdims=True)
        weighted = dnormed * gain
        inner = jnp.where(mean > 1.0, jnp.mean(weighted * plain, axis=-1, keepdims=True), 0.0)
        dmixed = (scale * (weighted - plain * inner)).astype(bf16)
        dmixed_ref[:, cols] = dmixed
        far_query = (query * jnp.exp(running[:, lanes]) * carried).astype(bf16)
        old = state[slot]
        dstate_ref[0, slot] = old.astype(bf16)
        new = old * factor[:, lanes] + tn(dmixed, far_query)
        state[slot] = new
        final_ref[slot] = new.astype(bf16)


def back_kernel(
    ndoc, block, meta, x_ref, run_ref, state_ref, cum_ref, first_ref, dmixed_ref, doutgate_ref,
    dstate_ref, dcum_ref, dlast_ref, wdec_ref, bias_ref, dx_ref, dwdec_ref, dbias_ref,
):
    start = meta[ndoc] + block * BLK
    allowed, carried, same, keep = block_masks(meta, ndoc, start)
    last_row = lax.broadcasted_iota(jnp.int32, (BLK, HK), 0) == BLK - 1
    drunning = []
    for slot in range(2):
        lanes = slice(slot * HK, slot * HK + HK)
        cols = slice(slot * HV, slot * HV + HV)
        at = slot * HEAD_COLS
        query, key, value, _ = head_parts(x_ref, slot)
        running = run_ref[:, lanes]
        middle = running[MID : MID + 1, :]
        ending = running[BLK - 1 :, :]
        up = jnp.exp(running - middle)
        down = jnp.exp(middle - running)
        far = jnp.exp(running) * carried
        near = jnp.exp(ending - running) * same
        rel_query = (query * up).astype(bf16)
        rel_key = (key * down).astype(bf16)
        far_query = (query * far).astype(bf16)
        moved = (key * near).astype(bf16)
        value = value.astype(bf16)
        scores = jnp.where(allowed, nt(rel_query, rel_key), 0.0).astype(bf16)
        state = state_ref[0, slot].astype(f32) + first_ref[slot].astype(f32) * cum_ref[0][:, lanes]
        dstate = dstate_ref[0, slot].astype(f32) + dlast_ref[slot].astype(f32) * dcum_ref[0][:, lanes]
        state_low = state.astype(bf16)
        dstate_low = dstate.astype(bf16)
        dmixed = dmixed_ref[:, cols]
        dvalue = tn(scores, dmixed) + nt(moved, dstate_low)
        dscores = jnp.where(allowed, nt(dmixed, value), 0.0).astype(bf16)
        drel_query = nn(dscores, rel_key)
        drel_key = tn(dscores, rel_query)
        dfar = nn(dmixed, state_low)
        dmoved = nn(value, dstate_low)
        dquery = drel_query * up + dfar * far
        dkey = drel_key * down + dmoved * near
        moved_grad = dmoved * moved.astype(f32)
        dending = jnp.sum(moved_grad, axis=0, keepdims=True) + jnp.sum(
            state * dstate, axis=0, keepdims=True
        ) * (jnp.exp(ending) * keep)
        drun = (
            drel_query * rel_query.astype(f32)
            - drel_key * rel_key.astype(f32)
            + dfar * far_query.astype(f32)
            - moved_grad
        )
        drunning.append(drun + jnp.where(last_row, dending, 0.0))
        dx_ref[:, at : at + HK] = (dquery * (HK**-0.5)).astype(bf16)
        dx_ref[:, at + HK : at + 2 * HK] = dkey.astype(bf16)
        dx_ref[:, at + 2 * HK : at + 2 * HK + HV] = dvalue.astype(bf16)
        dx_ref[:, at + 2 * HK + HV : at + HEAD_COLS] = doutgate_ref[:, cols]
    drun_both = jnp.concatenate(drunning, axis=1)
    ddecay = split_dot(tri_ones(), drun_both, tn)
    before = decay_before(x_ref, wdec_ref, bias_ref)
    dbefore = ddecay * (1.0 / 16.0) * jax.nn.sigmoid(-before)
    dbias_ref[...] += jnp.sum(dbefore, axis=0, keepdims=True)
    ranked = x_ref[:, 2 * HEAD_COLS :]
    dlow = dbefore.astype(bf16)
    dwdec_ref[...] += tn(ranked.astype(bf16), dlow)
    dx_ref[:, 2 * HEAD_COLS :] = nt(dlow, wdec_ref[...].astype(bf16)).astype(bf16)


def kernel_params():
    return pltpu.CompilerParams(dimension_semantics=("arbitrary",), vmem_limit_bytes=VMEM_LIMIT)


def sub_blocks(kernel, ndoc, tokens, rows, blocks, reverse, starts):
    steps = tokens // (BLK * SUB)

    def body(meta, *refs):
        step = pl.program_id(0)

        @pl.when(step == 0)
        def _():
            for which, value in starts:
                refs[which][...] = jnp.full_like(refs[which], value)

        first = (steps - 1 - step if reverse else step) * SUB
        for sub in reversed(range(SUB)) if reverse else range(SUB):
            views = [
                ref.at[sub * BLK : (sub + 1) * BLK] if i in rows
                else ref.at[sub : sub + 1] if i in blocks
                else ref
                for i, ref in enumerate(refs)
            ]
            kernel(ndoc, first + sub, meta, *views)

    return body


class Mixer:
    def __init__(self, meta, ndoc, tokens):
        self.meta = meta
        self.ndoc = ndoc
        self.tokens = tokens
        self.nblk = tokens // BLK
        self.steps = self.nblk // SUB

    def rows(self, width, reverse=False):
        steps, core = self.steps, self.ndoc + 1

        def place(step, meta):
            time = steps - 1 - step if reverse else step
            return (lax.rem(time + meta[core] * (steps // 2), steps), 0)

        return pl.BlockSpec((BLK * SUB, width), place)

    def per_block(self, shape, reverse=False):
        steps = self.steps
        zeros = (0,) * len(shape)
        return pl.BlockSpec(
            (SUB,) + shape, lambda step, meta: ((steps - 1 - step if reverse else step),) + zeros
        )

    def whole(self, shape):
        zeros = (0,) * len(shape)
        return pl.BlockSpec(shape, lambda step, meta: zeros)

    def call(self, kernel, layout, in_specs, out_specs, out_shape, scratch, *args):
        return pl.pallas_call(
            sub_blocks(kernel, self.ndoc, self.tokens, *layout),
            grid_spec=pltpu.PrefetchScalarGridSpec(
                num_scalar_prefetch=1,
                grid=(self.steps,),
                in_specs=in_specs,
                out_specs=out_specs,
                scratch_shapes=scratch,
            ),
            out_shape=[jax.ShapeDtypeStruct(s, d) for s, d in out_shape],
            cost_estimate=NO_COST,
            compiler_params=kernel_params(),
        )(self.meta, *args)

    def state_scratch(self):
        return [pltpu.VMEM((2, HV, HK), f32), pltpu.VMEM((1, 2 * HK), f32)]

    def states(self, x, wdec, bias):
        n = self.nblk
        return self.call(
            states_kernel,
            ((0, 3), (4, 5), False, ((7, 0.0), (8, 1.0))),
            [self.rows(x.shape[1]), self.whole(wdec.shape), self.whole(bias.shape)],
            [
                self.rows(2 * HK),
                self.per_block((2, HV, HK)),
                self.per_block((1, 2 * HK)),
                self.whole((2, HV, HK)),
            ],
            [
                ((self.tokens, 2 * HK), f32),
                ((n, 2, HV, HK), bf16),
                ((n, 1, 2 * HK), f32),
                ((2, HV, HK), bf16),
            ],
            self.state_scratch(),
            x, wdec, bias,
        )

    def mix(self, x, run, states, cum, first, gain):
        return self.call(
            mix_kernel,
            ((0, 1, 6, 7), (2, 3), False, ()),
            [
                self.rows(x.shape[1]),
                self.rows(2 * HK),
                self.per_block((2, HV, HK)),
                self.per_block((1, 2 * HK)),
                self.whole((2, HV, HK)),
                self.whole(gain.shape),
            ],
            [self.rows(2 * HV), self.rows(2 * HV)],
            [((self.tokens, 2 * HV), bf16), ((self.tokens, 2 * HV), bf16)],
            [],
            x, run, states, cum, first, gain,
        )

    def back_states(self, x, run, mixed, grad, own_out, far_out, gain):
        n = self.nblk
        return self.call(
            back_states_kernel,
            ((0, 1, 2, 3, 7, 8), (9, 10), True, ((12, 0.0), (13, 0.0), (14, 1.0))),
            [
                self.rows(x.shape[1], True),
                self.rows(2 * HK, True),
                self.rows(2 * HV, True),
                self.rows(grad.shape[1], True),
                self.whole(own_out.shape),
                self.whole(far_out.shape),
                self.whole(gain.shape),
            ],
            [
                self.rows(2 * HV, True),
                self.rows(2 * HV, True),
                self.per_block((2, HV, HK), True),
                self.per_block((1, 2 * HK), True),
                self.whole((2, HV, HK)),
                self.whole((1, HV)),
            ],
            [
                ((self.tokens, 2 * HV), bf16),
                ((self.tokens, 2 * HV), bf16),
                ((n, 2, HV, HK), bf16),
                ((n, 1, 2 * HK), f32),
                ((2, HV, HK), bf16),
                ((1, HV), f32),
            ],
            self.state_scratch(),
            x, run, mixed, grad, own_out, far_out, gain,
        )

    def back(self, x, run, states, cum, first, dmixed, doutgate, dstates, dcum, dlast, wdec, bias):
        rank = wdec.shape[0]
        return self.call(
            back_kernel,
            ((0, 1, 5, 6, 12), (2, 3, 7, 8), False, ((13, 0.0), (14, 0.0))),
            [
                self.rows(x.shape[1]),
                self.rows(2 * HK),
                self.per_block((2, HV, HK)),
                self.per_block((1, 2 * HK)),
                self.whole((2, HV, HK)),
                self.rows(2 * HV),
                self.rows(2 * HV),
                self.per_block((2, HV, HK)),
                self.per_block((1, 2 * HK)),
                self.whole((2, HV, HK)),
                self.whole(wdec.shape),
                self.whole(bias.shape),
            ],
            [self.rows(x.shape[1]), self.whole((rank, 2 * HK)), self.whole((1, 2 * HK))],
            [
                ((self.tokens, x.shape[1]), bf16),
                ((rank, 2 * HK), f32),
                ((1, 2 * HK), f32),
            ],
            [],
            x, run, states, cum, first, dmixed, doutgate, dstates, dcum, dlast, wdec, bias,
        )


ROWS_BLK = 256


def matrix_spec(part):
    array, which = part
    if array.ndim == 3:
        return pl.BlockSpec((None,) + array.shape[1:], lambda i: (which, 0, 0))
    if which is None:
        return pl.BlockSpec(array.shape, lambda i: (0, 0))
    at, rows = which
    return pl.BlockSpec((rows, array.shape[1]), lambda i: (at, 0))


def matrix_shape(part):
    array, which = part
    if array.ndim == 3 or which is None:
        return array.shape[-2:]
    return which[1], array.shape[1]


def row_spec(array, first=0):
    return pl.BlockSpec((ROWS_BLK, array.shape[1]), lambda i: (i + first, 0))


NO_COST = pl.CostEstimate(flops=0, bytes_accessed=0, transcendentals=0)


def local_call(body, grid, in_specs, out_specs, out_shape, args, scratch=()):
    return pl.pallas_call(
        body,
        grid=(grid,),
        in_specs=in_specs,
        out_specs=out_specs,
        out_shape=out_shape,
        scratch_shapes=list(scratch),
        cost_estimate=NO_COST,
        compiler_params=pltpu.CompilerParams(
            dimension_semantics=("arbitrary",), vmem_limit_bytes=VMEM_LIMIT
        ),
    )(*args)


def sum_of_dots(terms, first_row, rows, out_type):
    lefts = []
    for left, _, _, _ in terms:
        if not any(left is seen for seen in lefts):
            lefts.append(left)
    which = [next(i for i, seen in enumerate(lefts) if seen is left) for left, _, _, _ in terms]
    rights = [right for _, _, right, _ in terms]
    width = matrix_shape(rights[0])[0 if terms[0][3] else 1]

    def body(*refs):
        left_refs, right_refs, out = refs[: len(lefts)], refs[len(lefts) : -1], refs[-1]
        total = None
        for (_, at, _, turned), index, right in zip(terms, which, right_refs):
            depth = right.shape[1] if turned else right.shape[0]
            part = (nt if turned else nn)(left_refs[index][:, at : at + depth], right[...])
            total = part if total is None else total + part
        out[...] = total.astype(out_type)

    return local_call(
        body,
        rows // ROWS_BLK,
        [row_spec(v, first_row // ROWS_BLK) for v in lefts] + [matrix_spec(v) for v in rights],
        pl.BlockSpec((ROWS_BLK, width), lambda i: (i, 0)),
        jax.ShapeDtypeStruct((rows, width), out_type),
        lefts + [v[0] for v in rights],
    )


def project(a, parts):
    widths = [matrix_shape(v)[1] for v in parts[:-1]] + [matrix_shape(parts[-1])[0]]

    def body(left, *refs):
        out = refs[-1]
        at = 0
        for right, width in zip(refs[:-1], widths):
            turned = at + width == out.shape[1]
            out[:, at : at + width] = (nt if turned else nn)(left[...], right[...])
            at += width

    return local_call(
        body,
        a.shape[0] // ROWS_BLK,
        [row_spec(a)] + [matrix_spec(v) for v in parts],
        pl.BlockSpec((ROWS_BLK, sum(widths)), lambda i: (i, 0)),
        jax.ShapeDtypeStruct((a.shape[0], sum(widths)), f32),
        [a] + [v[0] for v in parts],
    )


def piece_specs(pieces):
    per = pieces[0].shape[0] // ROWS_BLK

    def spec(which, piece):
        return pl.BlockSpec(
            (ROWS_BLK, piece.shape[1]), lambda i: (jnp.clip(i - which * per, 0, per - 1), 0)
        )

    return [spec(which, piece) for which, piece in enumerate(pieces)]


def two_pieces(body, near, far):
    step = pl.program_id(0)
    half = pl.num_programs(0) // 2
    pl.when(step < half)(lambda: body(near))
    pl.when(step >= half)(lambda: body(far))


def ff_forward(pieces, gate_w, up_w, far, ffp):
    ff = matrix_shape(gate_w)[0]
    rows = sum(v.shape[0] for v in pieces)

    def body(near_ref, part_ref, gate_w, up_w, far_gate, far_up, gate_ref, up_ref, product_ref):
        def work(m_ref):
            m = m_ref[...]
            for slot, (gate_t, up_t) in enumerate(((gate_w, up_w), (far_gate, far_up))):
                gate, up = nt(m, gate_t[...]), nt(m, up_t[...])
                at = slot * ffp
                gate_ref[:, at : at + ff] = gate.astype(bf16)
                up_ref[:, at : at + ff] = up.astype(bf16)
                product_ref[:, at : at + ff] = (gate * jax.nn.sigmoid(gate) * up).astype(bf16)

        two_pieces(work, near_ref, part_ref)

    parts = [gate_w, up_w, (far, (0, ff)), (far, (1, ff))]
    return local_call(
        body,
        rows // ROWS_BLK,
        piece_specs(pieces) + [matrix_spec(v) for v in parts],
        [pl.BlockSpec((ROWS_BLK, 2 * ffp), lambda i: (i, 0))] * 3,
        [jax.ShapeDtypeStruct((rows, 2 * ffp), bf16)] * 3,
        list(pieces) + [v[0] for v in parts],
    )


def gate_pair(gate, up, dproduct):
    sig = jax.nn.sigmoid(gate)
    silu = gate * sig
    dgate = dproduct * up * (sig + silu * (1.0 - sig))
    return jnp.concatenate([dgate.astype(bf16), (dproduct * silu).astype(bf16)], axis=1), silu


def ff_backward(pieces, gate, up, down_w, far, ffp):
    ff = matrix_shape(down_w)[0]

    def body(near_ref, part_ref, gate_ref, up_ref, down_ref, far_ref, own_out, far_out):
        def work(g_ref):
            g = g_ref[...]
            for slot, (weight, out) in enumerate(((down_ref, own_out), (far_ref, far_out))):
                cols = slice(slot * ffp, slot * ffp + ff)
                out[...] = gate_pair(
                    gate_ref[:, cols].astype(f32), up_ref[:, cols].astype(f32), nt(g, weight[...])
                )[0]

        two_pieces(work, near_ref, part_ref)

    rows = gate.shape[0]
    parts = [down_w, (far, (2, ff))]
    return local_call(
        body,
        rows // ROWS_BLK,
        piece_specs(pieces) + [row_spec(gate), row_spec(up)] + [matrix_spec(v) for v in parts],
        [pl.BlockSpec((ROWS_BLK, 2 * ff), lambda i: (i, 0))] * 2,
        [jax.ShapeDtypeStruct((rows, 2 * ff), bf16)] * 2,
        list(pieces) + [gate, up] + [v[0] for v in parts],
    )


def ff_weight_grads(m_pieces, g_pieces, dboth, product, gate_w, up_w, down_w, spare):
    ff = matrix_shape(down_w)[0]
    rows, width = m_pieces[0][0].shape

    def body(m0, m1, m2, m3, g0, g1, g2, g3, both_ref, product_ref, gate_t, up_t, down_ref, out, total):
        step = pl.program_id(0)

        def add(both, product, m, g):
            for at, left, right in ((0, both, m), (2 * ff, product, g)):
                part = tn(left, right)
                place = slice(at, at + left.shape[1])

                @pl.when(step == 0)
                def _():
                    total[place] = part

                @pl.when(step > 0)
                def _():
                    total[place] += part

        def near(m_ref, g_ref):
            add(both_ref[...], product_ref[:, :ff], m_ref[...], g_ref[...])

        def far(m_ref, g_ref):
            m, g = m_ref[...], g_ref[...]
            gate, up = nt(m, gate_t[...]), nt(m, up_t[...])
            both, silu = gate_pair(gate, up, nt(g, down_ref[...]))
            add(both, (silu * up).astype(bf16), m, g)

        for which, (work, m_ref, g_ref) in enumerate(
            ((near, m0, g0), (near, m1, g1), (far, m2, g2), (far, m3, g3))
        ):
            pl.when(step == which)(lambda work=work, m_ref=m_ref, g_ref=g_ref: work(m_ref, g_ref))

        @pl.when(step == 3)
        def _():
            out[: 3 * ff] = total[...].astype(bf16)
            if spare:
                out[3 * ff :] = jnp.zeros((spare, width), bf16)

    parts = [gate_w, up_w, down_w]
    once = pl.Buffered(1)

    def alone(spec):
        return pl.BlockSpec(spec.block_shape, spec.index_map, pipeline_mode=once)

    pieces = list(m_pieces) + list(g_pieces)
    return local_call(
        body,
        4,
        [
            pl.BlockSpec((rows, width), lambda i, at=at: (at, 0), pipeline_mode=once) for _, at in pieces
        ]
        + [pl.BlockSpec((rows, v.shape[1]), lambda i: (jnp.minimum(i, 1), 0)) for v in (dboth, product)]
        + [alone(matrix_spec(v)) for v in parts],
        pl.BlockSpec((3 * ff + spare, width), lambda i: (0, 0), pipeline_mode=once),
        jax.ShapeDtypeStruct((3 * ff + spare, width), bf16),
        [v for v, _ in pieces] + [dboth, product] + [v[0] for v in parts],
        scratch=[pltpu.VMEM((3 * ff, width), f32)],
    )


def weight_outputs(mix_grads, ff_grads, ff):
    rows, cols = mix_grads[0].shape
    steps = 4
    high, flat = rows // steps, ff // steps
    widths = (HK, HK, HV, HV)

    def body(*refs):
        ins, outs = refs[: 4 * LAYERS], refs[4 * LAYERS :]

        def work(mix, *parts):
            at = 0
            for ref, width in zip(outs, widths):
                ref[0] = mix[:, at : at + width].astype(f32)
                at += width
            outs[4][0] = mix[:, at : at + HV].astype(f32).T
            for ref, part in zip(outs[5:], parts):
                ref[0] = part[...].astype(f32)

        for layer in range(LAYERS):
            mine = ins[4 * layer : 4 * layer + 4]
            pl.when(pl.program_id(0) == layer)(lambda mine=mine: work(*mine))

    def spec(layer, height, first):
        def place(now, step):
            held = jnp.where(now < layer, 0, steps - 1)
            return (first + jnp.where(now == layer, step, held), 0)

        return pl.BlockSpec((height, cols), place)

    in_specs, args = [], []
    for layer in range(LAYERS):
        in_specs += [spec(layer, high, 0)] + [spec(layer, flat, part * steps) for part in range(3)]
        args += [mix_grads[layer]] + [ff_grads[layer]] * 3
    out_specs = [pl.BlockSpec((1, high, width), lambda now, step: (now, step, 0)) for width in widths]
    out_specs += [pl.BlockSpec((1, HV, high), lambda now, step: (now, 0, step))]
    out_specs += [pl.BlockSpec((1, flat, cols), lambda now, step: (now, step, 0))] * 3
    shapes = [(LAYERS, rows, width) for width in widths] + [(LAYERS, HV, rows)] + [(LAYERS, ff, cols)] * 3
    return pl.pallas_call(
        body,
        grid=(LAYERS, steps),
        in_specs=in_specs,
        out_specs=out_specs,
        out_shape=[jax.ShapeDtypeStruct(v, f32) for v in shapes],
        cost_estimate=NO_COST,
        compiler_params=pltpu.CompilerParams(
            dimension_semantics=("arbitrary", "arbitrary"), vmem_limit_bytes=VMEM_LIMIT
        ),
    )(*args)


def ring_place(index, n):
    return jnp.where(index % 2 == 0, index // 2, n - 1 - index // 2)


def ring_index(place, n):
    return jnp.where(place < n // 2, 2 * place, 2 * (n - 1 - place) + 1)


MESH = pl.DeviceIdType.MESH


class Ring:
    def __init__(self, n, data, out, slots, sems):
        self.n, self.data, self.out, self.slots = n, data, out, slots
        self.send, self.recv, self.out_send, self.out_recv = sems
        self.me = ring_place(lax.axis_index("dp"), n)
        self.peers = [
            ring_index(lax.rem(self.me + 1, n), n),
            ring_index(lax.rem(self.me + n - 1, n), n),
        ]
        self.rows = data.shape[0] // (2 * n)

    def chunk(self, ref, way, back):
        which = lax.rem(self.me + 2 * self.n - (1, -1)[way] * back, self.n)
        return ref.at[pl.ds(pl.multiple_of((2 * which + way) * self.rows, 16), self.rows)]

    def partial(self, way, source, step):
        return pltpu.make_async_remote_copy(
            src_ref=source, dst_ref=self.slots.at[way, step],
            send_sem=self.send.at[way, step], recv_sem=self.recv.at[way, step],
            device_id={"dp": self.peers[way]}, device_id_type=MESH,
        )

    def final(self, way, step, back):
        part = self.chunk(self.out, way, back)
        return pltpu.make_async_remote_copy(
            src_ref=part, dst_ref=part,
            send_sem=self.out_send.at[way, step], recv_sem=self.out_recv.at[way, step],
            device_id={"dp": self.peers[way]}, device_id_type=MESH,
        )

    def start(self):
        for way in range(2):
            self.partial(way, self.chunk(self.data, way, 0), 0).start()

    def reduce(self, step):
        for way in range(2):
            slot = self.slots.at[way, step]
            self.partial(way, slot, step).wait_recv()
            part = self.chunk(self.data, way, step + 1)
            slot[...] = (slot[...].astype(f32) + part[...].astype(f32)).astype(bf16)

            @pl.when(step < self.n - 2)
            def _():
                self.partial(way, slot, step + 1).start()

    def turn(self):
        for way in range(2):
            self.chunk(self.out, way, -1)[...] = self.slots[way, self.n - 2]
            self.final(way, 0, -1).start()

    def gather(self, step):
        for way in range(2):
            self.final(way, step, step).wait_recv()

            @pl.when(step < self.n - 2)
            def _():
                self.final(way, step + 1, step).start()

    def sent(self, step):
        for way in range(2):
            self.partial(way, self.slots.at[way, step], step).wait_send()
            self.final(way, step, step - 1).wait_send()


def steps_of(lo, hi, *bodies):
    def body(step, carry):
        for each in bodies:
            each(step)
        return carry

    lax.fori_loop(lo, hi, body, 0)


def mix_sum_kernel(
    n, cuts, done, late, own, far, misc, out_done, out_late, out_own, out_misc, came, total,
    slot_a, slot_b, slot_c, slot_d, slot_e, slot_f,
    send, recv, out_send, out_recv, chip_send, chip_recv, sums, misc_came, misc_send, misc_recv,
):
    me = ring_place(lax.axis_index("dp"), n)
    member, row = lax.axis_index("head"), lax.axis_index("dp")
    swaps = [{"head": member ^ 1}, {"head": member ^ 2}]
    swaps += [{"dp": row ^ (1 << bit)} for bit in range(n.bit_length() - 1)]
    peers = swaps + [
        {"dp": ring_index(lax.rem(me + 1, n), n)},
        {"dp": ring_index(lax.rem(me + n - 1, n), n)},
    ]
    barrier = pltpu.get_barrier_semaphore()
    for peer in peers:
        pl.semaphore_signal(barrier, inc=1, device_id=peer, device_id_type=MESH)
    pl.semaphore_wait(barrier, len(peers))

    def small(step):
        return pltpu.make_async_remote_copy(
            src_ref=sums.at[step], dst_ref=misc_came.at[step],
            send_sem=misc_send.at[step], recv_sem=misc_recv.at[step],
            device_id=swaps[step], device_id_type=MESH,
        )

    taken = [0]

    def small_step():
        step = taken[0]
        if step == len(swaps):
            return
        small(step).wait()
        sums[step + 1] = sums[step] + misc_came[step]
        taken[0] += 1
        if step + 1 < len(swaps):
            small(step + 1).start()

    swap = pltpu.make_async_remote_copy(
        src_ref=far, dst_ref=came, send_sem=chip_send, recv_sem=chip_recv,
        device_id={"head": member ^ 2}, device_id_type=MESH,
    )
    def ring(which, data, out, cut, slots):
        rows = slice(*cut)
        sems = [v.at[which] for v in (send, recv, out_send, out_recv)]
        return Ring(n, data.at[rows], out.at[rows], slots, sems)

    rings = (
        (0, done, out_done, cuts[0], slot_a),
        (1, done, out_done, cuts[1], slot_b),
        (2, late, out_late, cuts[2], slot_c),
        (3, late, out_late, cuts[3], slot_d),
        (4, total, out_own, cuts[4], slot_e),
        (5, total, out_own, cuts[5], slot_f),
    )
    first, second = ([ring(*v) for v in pair if v[3][1] > v[3][0]] for pair in (rings[:4], rings[4:]))

    def each(rings, name):
        return [getattr(v, name) for v in rings]

    def now(steps):
        for step in steps:
            step()

    middle, last = (n - 1) // 2, n - 1
    sums[0] = misc[...]
    small(0).start()
    swap.start()
    now(each(first, "start"))
    steps_of(0, middle, *each(first, "reduce"))
    small_step()
    steps_of(middle, last, *each(first, "reduce"))
    now(each(first, "turn"))
    small_step()
    swap.wait()
    total[...] = (own[...].astype(f32) + came[...].astype(f32)).astype(bf16)
    now(each(second, "start"))
    together = each(first, "gather") + each(second, "reduce")
    steps_of(0, middle, *together)
    small_step()
    steps_of(middle, last, *together)
    now(each(second, "turn"))
    small_step()
    steps_of(0, middle, *each(second, "gather"))
    small_step()
    steps_of(middle, last, *each(second, "gather"))
    for _ in swaps:
        small_step()
    out_misc[...] = sums[len(swaps)]
    steps_of(0, last, *each(first + second, "sent"))


def mix_sum(done, late, own, far, misc, n):
    if n == 1:
        misc = misc + core_swap(misc)
        own = (own.astype(f32) + chip_swap(far).astype(f32)).astype(bf16)
        return done, late, own, misc + chip_swap(misc)
    rows, cols = own.shape
    done_rows = done.shape[0]
    swaps = 2 + n.bit_length() - 1

    def two(total):
        lines = total // (32 * n)
        cut = (lines + 1) // 2 * 32 * n
        return (0, cut), (cut, total)

    cuts = two(done_rows) + two(rows) + two(rows)

    def body(*refs):
        mix_sum_kernel(n, cuts, *refs)

    vmem = pl.BlockSpec(memory_space=pltpu.VMEM)
    return pl.pallas_call(
        body,
        in_specs=[vmem] * 5,
        out_specs=[vmem] * 4,
        out_shape=[
            jax.ShapeDtypeStruct((done_rows, cols), bf16),
            jax.ShapeDtypeStruct((rows, cols), bf16),
            jax.ShapeDtypeStruct((rows, cols), bf16),
        ]
        + [jax.ShapeDtypeStruct(misc.shape, f32)],
        scratch_shapes=[
            pltpu.VMEM((rows, cols), bf16),
            pltpu.VMEM((rows, cols), bf16),
        ]
        + [
            pltpu.VMEM((2, n - 1, max(16, (stop - at) // (2 * n)), cols), bf16) for at, stop in cuts
        ]
        + [pltpu.SemaphoreType.DMA((6, 2, n - 1))] * 4
        + [pltpu.SemaphoreType.DMA] * 2
        + [
            pltpu.VMEM((swaps + 1,) + misc.shape, f32),
            pltpu.VMEM((swaps,) + misc.shape, f32),
            pltpu.SemaphoreType.DMA((swaps,)),
            pltpu.SemaphoreType.DMA((swaps,)),
        ],
        compiler_params=pltpu.CompilerParams(
            collective_id=0, has_side_effects=True, vmem_limit_bytes=VMEM_LIMIT
        ),
    )(done, late, own, far, misc)


def norm_scale(hidden):
    return lax.rsqrt(jnp.mean(hidden * hidden, axis=-1, keepdims=True) + epsilon)


def norm_low(hidden, gain):
    return (hidden * norm_scale(hidden) * gain).astype(bf16)


def norm_back(hidden, gain, grad_normed):
    scale = norm_scale(hidden)
    weighted = grad_normed * gain
    grad_hidden = scale * weighted - hidden * (scale * scale * scale) * jnp.mean(
        weighted * hidden, axis=-1, keepdims=True
    )
    return grad_hidden, jnp.sum(grad_normed * hidden * scale, axis=0)


def core_swap(value):
    return lax.ppermute(value, "head", [(i, i ^ 1) for i in range(4)])


def chip_swap(value):
    return lax.ppermute(value, "head", [(i, i ^ 2) for i in range(4)])


def dp_slices(arrays, layer):
    n = lax.axis_size("dp")
    height, width = arrays[0].shape[1] // n, arrays[0].shape[2]
    views = [v.reshape(v.shape[0], n, height, width) for v in arrays]

    def body(at, *refs):
        for which, ref in enumerate(refs[:-1]):
            refs[-1][which] = ref[...]

    return pl.pallas_call(
        body,
        grid_spec=pltpu.PrefetchScalarGridSpec(
            num_scalar_prefetch=1,
            grid=(1,),
            in_specs=[pl.BlockSpec((None, None, height, width), lambda i, at: (layer, at[0], 0, 0))] * len(views),
            out_specs=pl.BlockSpec((len(views), height, width), lambda i, at: (0, 0, 0)),
        ),
        out_shape=jax.ShapeDtypeStruct((len(views), height, width), bf16),
        cost_estimate=NO_COST,
        compiler_params=kernel_params(),
    )(lax.axis_index("dp").astype(jnp.int32).reshape(1), *views)


def dp_ring():
    n = lax.axis_size("dp")
    return list(range(0, n, 2)) + list(range(n - 1, 0, -2)) if n > 1 else [0]


def after(value, *others):
    return lax.optimization_barrier((value,) + others)[0]


def per_device(
    tokens, doc_starts, grad_out, norm_one, w_query, w_key, w_value, w_outgate, w_rank, w_decay,
    decay_bias, group_gain, w_out, norm_two, w_gate, w_up, w_down,
):
    shard_len, width = tokens.shape[1:]
    ndoc = doc_starts.shape[1]
    ff = w_gate.shape[2]
    ffp = -(-ff // 128) * 128
    rank = w_decay.shape[1]
    member = lax.axis_index("head")
    core = member % 2
    chip = member // 2
    meta = jnp.concatenate(
        [doc_starts[0], jnp.stack([chip * (2 * shard_len), core]).astype(jnp.int32)]
    )
    mixer = Mixer(meta, ndoc, 2 * shard_len)

    def mix_pack(layer):
        return jnp.concatenate(
            [w_query[layer], w_key[layer], w_value[layer], w_outgate[layer]], axis=1
        )

    gate_t, up_t, rank_t = (jnp.swapaxes(v, 1, 2) for v in (w_gate, w_up, w_rank))

    def ff_slice(layer, wait):
        return chip_swap(after(dp_slices((gate_t, up_t, w_down), layer), wait))

    def ff_gather(part):
        dp = lax.axis_size("dp")
        whole = lax.all_gather(part, "dp", axis=0, tiled=True)
        return jnp.swapaxes(whole.reshape(dp, 3, ff // dp, width), 0, 1).reshape(3 * ff, width)

    def with_partner(local):
        return jnp.concatenate([local, core_swap(local)], axis=0)

    def settle(terms):
        sent = core_swap(sum_of_dots(terms, shard_len, shard_len, bf16))
        return sum_of_dots(terms, 0, shard_len, f32) + sent.astype(f32)

    small = jnp.concatenate([w_decay.astype(f32), decay_bias[:, None, :]], axis=1)
    small = jnp.concatenate([small, chip_swap(small)], axis=2)
    ff_part = ff_slice(0, meta)
    ff_far = ff_gather(ff_part)
    mix_own = mix_pack(0)
    mix_far = chip_swap(after(mix_own, ff_part))
    out_far = chip_swap(after(w_out[0], mix_far))
    next_part = ff_slice(1, ff_part)
    next_own = mix_pack(1)
    spare = -3 * ff % (32 * lax.axis_size("dp"))

    grad = grad_out[0].astype(f32)
    hidden = tokens[0].astype(f32)
    saved = []
    for layer in range(LAYERS):
        hidden_in = hidden
        a = with_partner(norm_low(hidden, norm_one[layer]))
        x = project(a, ((mix_own, None), (mix_far, None), (rank_t, layer)))
        wdec, bias = small[layer, :rank], small[layer, rank:]
        run, states, cum, final = mixer.states(x, wdec, bias)
        got = chip_swap(final if layer == 0 else after(final, out_far))
        first = got[::-1] * chip.astype(bf16)
        gain = group_gain[layer][None]
        gated, mixed = mixer.mix(x, run, states, cum, first, gain)
        if layer + 1 < LAYERS:
            next_mix = chip_swap(after(next_own, got))
            next_out = chip_swap(after(w_out[layer + 1], got))
            next_far = ff_gather(next_part)
        if layer > 0:
            gated = after(gated, ff_far)
        hidden_mid = hidden + settle(
            [(gated, 0, (w_out, layer), False), (gated, HV, (out_far, None), False)]
        )
        m_own = norm_low(hidden_mid, norm_two[layer])
        m = (m_own, core_swap(m_own))
        gate, up, product = ff_forward(m, (gate_t, layer), (up_t, layer), ff_far, ffp)
        if layer + 1 < LAYERS:
            product = after(product, next_mix)
        hidden = hidden_mid + settle(
            [(product, 0, (w_down, layer), False), (product, ffp, (ff_far, (2, ff)), False)]
        )
        saved.append(
            (hidden_in, hidden_mid, a, m, x, run, states, cum, first, mixed, gated, gate, up, product,
             mix_own, mix_far, out_far, ff_far)
        )
        if layer + 1 < LAYERS:
            mix_own, mix_far, out_far, ff_far = next_own, next_mix, next_out, next_far
    result = hidden.astype(bf16)[None]

    ff_grads, misc_grads = [None] * LAYERS, [None] * LAYERS
    for layer in reversed(range(LAYERS)):
        (
            hidden_in, hidden_mid, a, m, x, run, states, cum, first, mixed, gated, gate, up, product,
            mix_own, mix_far, out_far, ff_far,
        ) = saved[layer]
        gain = group_gain[layer][None]
        wdec, bias = small[layer, :rank], small[layer, rank:]
        if layer + 1 < LAYERS:
            g_own = grad.astype(bf16)
            g_y = chip_swap(g_own)
            g_far = [(g_y, 0), (core_swap(g_y), 0)]
            mix_late = (own, chip_swap(after(far, g_y)))
        else:
            g_own = grad_out[0]
            g_y = chip_swap(after(g_own, got))
            g_far = [(g_y, 0), (core_swap(g_y), 0)]
            came = chip_swap(jnp.concatenate([v[3][0] for v in saved], axis=0))
            came = (came, core_swap(came))
        g = (g_own, core_swap(g_own))
        dboth, dfar = ff_backward(g, gate, up, (w_down, layer), ff_far, ffp)
        back_mid, gain_two = norm_back(
            hidden_mid,
            norm_two[layer],
            settle(
                [
                    (dboth, 0, (gate_t, layer), False),
                    (dboth, ff, (up_t, layer), False),
                    (dfar, 0, (ff_far, (0, 2 * ff)), False),
                ]
            ),
        )
        ff_grad = ff_weight_grads(
            [(v, 0) for v in m] + [(v, layer) for v in came], [(v, 0) for v in g] + g_far, dboth, product,
            (gate_t, layer), (up_t, layer), (w_down, layer), 0 if layer else spare,
        )
        grad = grad + back_mid
        g_mix = with_partner(grad.astype(bf16))
        g_wout = tn(g_mix, gated).astype(bf16)
        dmixed, doutgate, dstates, dcum, dfinal, dgain = mixer.back_states(
            x, run, mixed, g_mix, w_out[layer], out_far, gain
        )
        got = chip_swap(dfinal)
        dlast = got[::-1] * (1 - chip).astype(bf16)
        if layer + 1 == LAYERS:
            dlast = after(dlast, ff_grad)
        dx, dwdec, dbias = mixer.back(
            x, run, states, cum, first, dmixed, doutgate, dstates, dcum, dlast, wdec, bias
        )
        g_wmix = tn(a, dx[:, : 2 * HEAD_COLS]).astype(bf16)
        g_rank = tn(dx[:, 2 * HEAD_COLS :], a)
        if layer + 1 < LAYERS:
            mix_late = (mix_late[0].astype(f32) + after(mix_late[1], dx).astype(f32)).astype(bf16)
        far = jnp.concatenate([g_wmix[:, HEAD_COLS:], g_wout[:, HV:]], axis=1)
        own = jnp.concatenate([g_wmix[:, :HEAD_COLS], g_wout[:, :HV]], axis=1)
        back_first, gain_one = norm_back(hidden_in, norm_one[layer], settle(
            [
                (dx, 0, (mix_own, None), True),
                (dx, HEAD_COLS, (mix_far, None), True),
                (dx, 2 * HEAD_COLS, (rank_t, layer), False),
            ]
        ))
        grad = grad + back_first
        if layer > 0:
            ff_grads[layer] = lax.psum(ff_grad, "dp")
        heads = jnp.concatenate([dwdec, dbias], axis=0)
        places = lax.iota(jnp.int32, 4)[:, None, None]
        heads = jnp.where(places == member, heads[None, :, :HK], 0.0) + jnp.where(
            places == member ^ 2, heads[None, :, HK:], 0.0
        )
        misc_grads[layer] = jnp.concatenate(
            [g_rank.reshape(-1), gain_one, gain_two, dgain[0], heads.reshape(-1)]
        )

    misc = jnp.stack(misc_grads)
    length = misc.shape[1]
    misc = jnp.pad(misc.reshape(-1), (0, -misc.size % 1024)).reshape(-1, 128)
    ff_done, late_mix, first_mix, misc = mix_sum(ff_grad, mix_late, own, far, misc, lax.axis_size("dp"))
    mix_grads = [first_mix, late_mix]
    ff_grads[0] = ff_done
    misc = misc.reshape(-1)[: LAYERS * length].reshape(LAYERS, length)
    sizes = (rank * width, width, width, HV, 4 * (rank + 1) * HK)
    pieces, at = [], 0
    for size in sizes:
        pieces.append(misc[:, at : at + size])
        at += size
    heads = lax.dynamic_index_in_dim(
        pieces[4].reshape(LAYERS, 4, rank + 1, HK), member, axis=1, keepdims=False
    )

    query, key, value, outgate, out, gate, up, down = weight_outputs(mix_grads, ff_grads, ff)
    return (
        result,
        grad[None],
        pieces[1],
        query,
        key,
        value,
        outgate,
        jnp.swapaxes(pieces[0].reshape(LAYERS, rank, width), 1, 2),
        heads[:, :rank],
        heads[:, rank],
        pieces[3],
        out,
        pieces[2],
        jnp.swapaxes(gate, 1, 2),
        jnp.swapaxes(up, 1, 2),
        down,
    )


def solution(mesh):
    cols = P(None, None, "head")
    rows = P(None, "head", None)
    place = P("dp", "head", None)
    return jax.shard_map(
        per_device,
        mesh=mesh,
        in_specs=(
            place, P("dp", None), place, P(), cols, cols, cols, cols, P(), cols,
            P(None, "head"), P(), rows, P(), cols, cols, rows,
        ),
        out_specs=(
            place, place, P(), cols, cols, cols, cols, P(), cols, P(None, "head"), P(), rows,
            P(), cols, cols, rows,
        ),
        check_vma=False,
    )
```

```python
import jax
import jax.numpy as jnp
from jax import lax
from jax.experimental import pallas as pl
from jax.experimental.pallas import tpu as pltpu
from jax.sharding import PartitionSpec as P

LAYERS = 2
HK = 128
HV = 256
HEAD_COLS = 2 * HK + 2 * HV
BLK = 128
MID = BLK // 2 - 1
SUB = 2
epsilon = 1e-06
highest = lax.Precision.HIGHEST
VMEM_LIMIT = 48 * 1024 * 1024

f32 = jnp.float32
bf16 = jnp.bfloat16


def nn(left, right):
    return lax.dot_general(left, right, (((1,), (0,)), ((), ())), preferred_element_type=f32)


def nt(left, right):
    return lax.dot_general(left, right, (((1,), (1,)), ((), ())), preferred_element_type=f32)


def tn(left, right):
    return lax.dot_general(left, right, (((0,), (0,)), ((), ())), preferred_element_type=f32)


def doc_count(meta, ndoc, place):
    total = (meta[0] <= place).astype(jnp.int32)
    for which in range(1, ndoc):
        total = total + (meta[which] <= place).astype(jnp.int32)
    return total


def block_masks(meta, ndoc, start):
    rows = lax.broadcasted_iota(jnp.int32, (BLK, BLK), 0) + start
    cols = lax.broadcasted_iota(jnp.int32, (BLK, BLK), 1) + start
    row_ids = doc_count(meta, ndoc, rows)
    col_ids = doc_count(meta, ndoc, cols)
    id_prev = doc_count(meta, ndoc, start - 1)
    id_last = doc_count(meta, ndoc, start + BLK - 1)
    allowed = (rows >= cols) & (row_ids == col_ids)
    carried = jnp.where(row_ids == id_prev, 1.0, 0.0)
    same = jnp.where(row_ids == id_last, 1.0, 0.0)
    keep = jnp.where(id_last == id_prev, 1.0, 0.0)
    return allowed, carried, same, keep


def split_dot(ones_mat, value, dot):
    high = value.astype(bf16)
    low = (value - high.astype(f32)).astype(bf16)
    return dot(ones_mat, high) + dot(ones_mat, low)


def tri_ones():
    rows = lax.broadcasted_iota(jnp.int32, (BLK, BLK), 0)
    cols = lax.broadcasted_iota(jnp.int32, (BLK, BLK), 1)
    return jnp.where(rows >= cols, 1.0, 0.0).astype(bf16)


def head_parts(x_ref, slot):
    at = slot * HEAD_COLS
    query = x_ref[:, at : at + HK] * (HK**-0.5)
    key = x_ref[:, at + HK : at + 2 * HK]
    value = x_ref[:, at + 2 * HK : at + 2 * HK + HV]
    outgate = x_ref[:, at + 2 * HK + HV : at + HEAD_COLS]
    return query, key, value, outgate


def decay_before(x_ref, wdec_ref, bias_ref):
    ranked = x_ref[:, 2 * HEAD_COLS :]
    return jnp.dot(ranked, wdec_ref[...], precision=highest, preferred_element_type=f32) + bias_ref[...]


def states_kernel(ndoc, block, meta, x_ref, wdec_ref, bias_ref, run_ref, state_ref, cum_ref, final_ref, state, cum):
    start = meta[ndoc] + block * BLK
    _, _, same, keep = block_masks(meta, ndoc, start)
    before = decay_before(x_ref, wdec_ref, bias_ref)
    decays = (jnp.minimum(before, 0.0) - jnp.log1p(jnp.exp(-jnp.abs(before)))) * (1.0 / 16.0)
    running = split_dot(tri_ones(), decays, nn)
    run_ref[...] = running
    ending = running[BLK - 1 :, :]
    factor = jnp.exp(ending) * keep
    cum_ref[0] = cum[...]
    cum[...] = cum[...] * factor
    for slot in range(2):
        lanes = slice(slot * HK, slot * HK + HK)
        _, key, value, _ = head_parts(x_ref, slot)
        moved = (key * jnp.exp(ending[:, lanes] - running[:, lanes]) * same).astype(bf16)
        old = state[slot]
        state_ref[0, slot] = old.astype(bf16)
        new = old * factor[:, lanes] + tn(value.astype(bf16), moved)
        state[slot] = new
        final_ref[slot] = new.astype(bf16)


def mix_kernel(ndoc, block, meta, x_ref, run_ref, state_ref, cum_ref, first_ref, gain_ref, gated_ref, mixed_ref):
    start = meta[ndoc] + block * BLK
    allowed, carried, _, _ = block_masks(meta, ndoc, start)
    gain = gain_ref[...]
    for slot in range(2):
        lanes = slice(slot * HK, slot * HK + HK)
        cols = slice(slot * HV, slot * HV + HV)
        query, key, value, outgate = head_parts(x_ref, slot)
        running = run_ref[:, lanes]
        middle = running[MID : MID + 1, :]
        rel_query = (query * jnp.exp(running - middle)).astype(bf16)
        rel_key = (key * jnp.exp(middle - running)).astype(bf16)
        scores = jnp.where(allowed, nt(rel_query, rel_key), 0.0).astype(bf16)
        far_query = (query * jnp.exp(running) * carried).astype(bf16)
        state = (state_ref[0, slot].astype(f32) + first_ref[slot].astype(f32) * cum_ref[0][:, lanes]).astype(bf16)
        mixed = nn(scores, value.astype(bf16)) + nt(far_query, state)
        scale = lax.rsqrt(jnp.maximum(jnp.mean(mixed * mixed, axis=-1, keepdims=True), 1.0))
        gated_ref[:, cols] = (mixed * scale * gain * outgate * jax.nn.sigmoid(outgate)).astype(bf16)
        mixed_ref[:, cols] = mixed.astype(bf16)


def back_states_kernel(
    ndoc, block, meta, x_ref, run_ref, mixed_ref, grad_ref, own_out_ref, far_out_ref, gain_ref,
    dmixed_ref, doutgate_ref, dstate_ref, cum_ref, final_ref, dgain_ref, state, cum,
):
    start = meta[ndoc] + block * BLK
    _, carried, _, keep = block_masks(meta, ndoc, start)
    gain = gain_ref[...]
    running = run_ref[...]
    factor = jnp.exp(running[BLK - 1 :, :]) * keep
    cum_ref[0] = cum[...]
    cum[...] = cum[...] * factor
    for slot in range(2):
        lanes = slice(slot * HK, slot * HK + HK)
        cols = slice(slot * HV, slot * HV + HV)
        query, _, _, outgate = head_parts(x_ref, slot)
        mixed = mixed_ref[:, cols].astype(f32)
        dgated = nt(grad_ref[...], (own_out_ref, far_out_ref)[slot][...])
        mean = jnp.mean(mixed * mixed, axis=-1, keepdims=True)
        scale = lax.rsqrt(jnp.maximum(mean, 1.0))
        sig = jax.nn.sigmoid(outgate)
        silu = outgate * sig
        dnormed = dgated * silu
        plain = mixed * scale
        doutgate_ref[:, cols] = (dgated * plain * gain * (sig + silu * (1.0 - sig))).astype(bf16)
        dgain_ref[...] += jnp.sum(dnormed * plain, axis=0, keepdims=True)
        weighted = dnormed * gain
        inner = jnp.where(mean > 1.0, jnp.mean(weighted * plain, axis=-1, keepdims=True), 0.0)
        dmixed = (scale * (weighted - plain * inner)).astype(bf16)
        dmixed_ref[:, cols] = dmixed
        far_query = (query * jnp.exp(running[:, lanes]) * carried).astype(bf16)
        old = state[slot]
        dstate_ref[0, slot] = old.astype(bf16)
        new = old * factor[:, lanes] + tn(dmixed, far_query)
        state[slot] = new
        final_ref[slot] = new.astype(bf16)


def back_kernel(
    ndoc, block, meta, x_ref, run_ref, state_ref, cum_ref, first_ref, dmixed_ref, doutgate_ref,
    dstate_ref, dcum_ref, dlast_ref, wdec_ref, bias_ref, dx_ref, dwdec_ref, dbias_ref,
):
    start = meta[ndoc] + block * BLK
    allowed, carried, same, keep = block_masks(meta, ndoc, start)
    last_row = lax.broadcasted_iota(jnp.int32, (BLK, HK), 0) == BLK - 1
    drunning = []
    for slot in range(2):
        lanes = slice(slot * HK, slot * HK + HK)
        cols = slice(slot * HV, slot * HV + HV)
        at = slot * HEAD_COLS
        query, key, value, _ = head_parts(x_ref, slot)
        running = run_ref[:, lanes]
        middle = running[MID : MID + 1, :]
        ending = running[BLK - 1 :, :]
        up = jnp.exp(running - middle)
        down = jnp.exp(middle - running)
        far = jnp.exp(running) * carried
        near = jnp.exp(ending - running) * same
        rel_query = (query * up).astype(bf16)
        rel_key = (key * down).astype(bf16)
        far_query = (query * far).astype(bf16)
        moved = (key * near).astype(bf16)
        value = value.astype(bf16)
        scores = jnp.where(allowed, nt(rel_query, rel_key), 0.0).astype(bf16)
        state = state_ref[0, slot].astype(f32) + first_ref[slot].astype(f32) * cum_ref[0][:, lanes]
        dstate = dstate_ref[0, slot].astype(f32) + dlast_ref[slot].astype(f32) * dcum_ref[0][:, lanes]
        state_low = state.astype(bf16)
        dstate_low = dstate.astype(bf16)
        dmixed = dmixed_ref[:, cols]
        dvalue = tn(scores, dmixed) + nt(moved, dstate_low)
        dscores = jnp.where(allowed, nt(dmixed, value), 0.0).astype(bf16)
        drel_query = nn(dscores, rel_key)
        drel_key = tn(dscores, rel_query)
        dfar = nn(dmixed, state_low)
        dmoved = nn(value, dstate_low)
        dquery = drel_query * up + dfar * far
        dkey = drel_key * down + dmoved * near
        moved_grad = dmoved * moved.astype(f32)
        dending = jnp.sum(moved_grad, axis=0, keepdims=True) + jnp.sum(
            state * dstate, axis=0, keepdims=True
        ) * (jnp.exp(ending) * keep)
        drun = (
            drel_query * rel_query.astype(f32)
            - drel_key * rel_key.astype(f32)
            + dfar * far_query.astype(f32)
            - moved_grad
        )
        drunning.append(drun + jnp.where(last_row, dending, 0.0))
        dx_ref[:, at : at + HK] = (dquery * (HK**-0.5)).astype(bf16)
        dx_ref[:, at + HK : at + 2 * HK] = dkey.astype(bf16)
        dx_ref[:, at + 2 * HK : at + 2 * HK + HV] = dvalue.astype(bf16)
        dx_ref[:, at + 2 * HK + HV : at + HEAD_COLS] = doutgate_ref[:, cols]
    drun_both = jnp.concatenate(drunning, axis=1)
    ddecay = split_dot(tri_ones(), drun_both, tn)
    before = decay_before(x_ref, wdec_ref, bias_ref)
    dbefore = ddecay * (1.0 / 16.0) * jax.nn.sigmoid(-before)
    dbias_ref[...] += jnp.sum(dbefore, axis=0, keepdims=True)
    ranked = x_ref[:, 2 * HEAD_COLS :]
    dlow = dbefore.astype(bf16)
    dwdec_ref[...] += tn(ranked.astype(bf16), dlow)
    dx_ref[:, 2 * HEAD_COLS :] = nt(dlow, wdec_ref[...].astype(bf16)).astype(bf16)


def kernel_params():
    return pltpu.CompilerParams(dimension_semantics=("arbitrary",), vmem_limit_bytes=VMEM_LIMIT)


def sub_blocks(kernel, ndoc, tokens, rows, blocks, reverse, starts):
    steps = tokens // (BLK * SUB)

    def body(meta, *refs):
        step = pl.program_id(0)

        @pl.when(step == 0)
        def _():
            for which, value in starts:
                refs[which][...] = jnp.full_like(refs[which], value)

        first = (steps - 1 - step if reverse else step) * SUB
        for sub in reversed(range(SUB)) if reverse else range(SUB):
            views = [
                ref.at[sub * BLK : (sub + 1) * BLK] if i in rows
                else ref.at[sub : sub + 1] if i in blocks
                else ref
                for i, ref in enumerate(refs)
            ]
            kernel(ndoc, first + sub, meta, *views)

    return body


class Mixer:
    def __init__(self, meta, ndoc, tokens):
        self.meta = meta
        self.ndoc = ndoc
        self.tokens = tokens
        self.nblk = tokens // BLK
        self.steps = self.nblk // SUB

    def rows(self, width, reverse=False):
        steps, core = self.steps, self.ndoc + 1

        def place(step, meta):
            time = steps - 1 - step if reverse else step
            return (lax.rem(time + meta[core] * (steps // 2), steps), 0)

        return pl.BlockSpec((BLK * SUB, width), place)

    def per_block(self, shape, reverse=False):
        steps = self.steps
        zeros = (0,) * len(shape)
        return pl.BlockSpec(
            (SUB,) + shape, lambda step, meta: ((steps - 1 - step if reverse else step),) + zeros
        )

    def whole(self, shape):
        zeros = (0,) * len(shape)
        return pl.BlockSpec(shape, lambda step, meta: zeros)

    def call(self, kernel, layout, in_specs, out_specs, out_shape, scratch, *args):
        return pl.pallas_call(
            sub_blocks(kernel, self.ndoc, self.tokens, *layout),
            grid_spec=pltpu.PrefetchScalarGridSpec(
                num_scalar_prefetch=1,
                grid=(self.steps,),
                in_specs=in_specs,
                out_specs=out_specs,
                scratch_shapes=scratch,
            ),
            out_shape=[jax.ShapeDtypeStruct(s, d) for s, d in out_shape],
            cost_estimate=NO_COST,
            compiler_params=kernel_params(),
        )(self.meta, *args)

    def state_scratch(self):
        return [pltpu.VMEM((2, HV, HK), f32), pltpu.VMEM((1, 2 * HK), f32)]

    def states(self, x, wdec, bias):
        n = self.nblk
        return self.call(
            states_kernel,
            ((0, 3), (4, 5), False, ((7, 0.0), (8, 1.0))),
            [self.rows(x.shape[1]), self.whole(wdec.shape), self.whole(bias.shape)],
            [
                self.rows(2 * HK),
                self.per_block((2, HV, HK)),
                self.per_block((1, 2 * HK)),
                self.whole((2, HV, HK)),
            ],
            [
                ((self.tokens, 2 * HK), f32),
                ((n, 2, HV, HK), bf16),
                ((n, 1, 2 * HK), f32),
                ((2, HV, HK), bf16),
            ],
            self.state_scratch(),
            x, wdec, bias,
        )

    def mix(self, x, run, states, cum, first, gain):
        return self.call(
            mix_kernel,
            ((0, 1, 6, 7), (2, 3), False, ()),
            [
                self.rows(x.shape[1]),
                self.rows(2 * HK),
                self.per_block((2, HV, HK)),
                self.per_block((1, 2 * HK)),
                self.whole((2, HV, HK)),
                self.whole(gain.shape),
            ],
            [self.rows(2 * HV), self.rows(2 * HV)],
            [((self.tokens, 2 * HV), bf16), ((self.tokens, 2 * HV), bf16)],
            [],
            x, run, states, cum, first, gain,
        )

    def back_states(self, x, run, mixed, grad, own_out, far_out, gain):
        n = self.nblk
        return self.call(
            back_states_kernel,
            ((0, 1, 2, 3, 7, 8), (9, 10), True, ((12, 0.0), (13, 0.0), (14, 1.0))),
            [
                self.rows(x.shape[1], True),
                self.rows(2 * HK, True),
                self.rows(2 * HV, True),
                self.rows(grad.shape[1], True),
                self.whole(own_out.shape),
                self.whole(far_out.shape),
                self.whole(gain.shape),
            ],
            [
                self.rows(2 * HV, True),
                self.rows(2 * HV, True),
                self.per_block((2, HV, HK), True),
                self.per_block((1, 2 * HK), True),
                self.whole((2, HV, HK)),
                self.whole((1, HV)),
            ],
            [
                ((self.tokens, 2 * HV), bf16),
                ((self.tokens, 2 * HV), bf16),
                ((n, 2, HV, HK), bf16),
                ((n, 1, 2 * HK), f32),
                ((2, HV, HK), bf16),
                ((1, HV), f32),
            ],
            self.state_scratch(),
            x, run, mixed, grad, own_out, far_out, gain,
        )

    def back(self, x, run, states, cum, first, dmixed, doutgate, dstates, dcum, dlast, wdec, bias):
        rank = wdec.shape[0]
        return self.call(
            back_kernel,
            ((0, 1, 5, 6, 12), (2, 3, 7, 8), False, ((13, 0.0), (14, 0.0))),
            [
                self.rows(x.shape[1]),
                self.rows(2 * HK),
                self.per_block((2, HV, HK)),
                self.per_block((1, 2 * HK)),
                self.whole((2, HV, HK)),
                self.rows(2 * HV),
                self.rows(2 * HV),
                self.per_block((2, HV, HK)),
                self.per_block((1, 2 * HK)),
                self.whole((2, HV, HK)),
                self.whole(wdec.shape),
                self.whole(bias.shape),
            ],
            [self.rows(x.shape[1]), self.whole((rank, 2 * HK)), self.whole((1, 2 * HK))],
            [
                ((self.tokens, x.shape[1]), bf16),
                ((rank, 2 * HK), f32),
                ((1, 2 * HK), f32),
            ],
            [],
            x, run, states, cum, first, dmixed, doutgate, dstates, dcum, dlast, wdec, bias,
        )


ROWS_BLK = 256


def matrix_spec(part):
    array, which = part
    if array.ndim == 3:
        return pl.BlockSpec((None,) + array.shape[1:], lambda i: (which, 0, 0))
    if which is None:
        return pl.BlockSpec(array.shape, lambda i: (0, 0))
    at, rows = which
    return pl.BlockSpec((rows, array.shape[1]), lambda i: (at, 0))


def matrix_shape(part):
    array, which = part
    if array.ndim == 3 or which is None:
        return array.shape[-2:]
    return which[1], array.shape[1]


def row_spec(array, first=0):
    return pl.BlockSpec((ROWS_BLK, array.shape[1]), lambda i: (i + first, 0))


NO_COST = pl.CostEstimate(flops=0, bytes_accessed=0, transcendentals=0)


def local_call(body, grid, in_specs, out_specs, out_shape, args, scratch=()):
    return pl.pallas_call(
        body,
        grid=(grid,),
        in_specs=in_specs,
        out_specs=out_specs,
        out_shape=out_shape,
        scratch_shapes=list(scratch),
        cost_estimate=NO_COST,
        compiler_params=pltpu.CompilerParams(
            dimension_semantics=("arbitrary",), vmem_limit_bytes=VMEM_LIMIT
        ),
    )(*args)


def sum_of_dots(terms, first_row, rows, out_type):
    lefts = []
    for left, _, _, _ in terms:
        if not any(left is seen for seen in lefts):
            lefts.append(left)
    which = [next(i for i, seen in enumerate(lefts) if seen is left) for left, _, _, _ in terms]
    rights = [right for _, _, right, _ in terms]
    width = matrix_shape(rights[0])[0 if terms[0][3] else 1]

    def body(*refs):
        left_refs, right_refs, out = refs[: len(lefts)], refs[len(lefts) : -1], refs[-1]
        total = None
        for (_, at, _, turned), index, right in zip(terms, which, right_refs):
            depth = right.shape[1] if turned else right.shape[0]
            part = (nt if turned else nn)(left_refs[index][:, at : at + depth], right[...])
            total = part if total is None else total + part
        out[...] = total.astype(out_type)

    return local_call(
        body,
        rows // ROWS_BLK,
        [row_spec(v, first_row // ROWS_BLK) for v in lefts] + [matrix_spec(v) for v in rights],
        pl.BlockSpec((ROWS_BLK, width), lambda i: (i, 0)),
        jax.ShapeDtypeStruct((rows, width), out_type),
        lefts + [v[0] for v in rights],
    )


def project(a, parts):
    widths = [matrix_shape(v)[1] for v in parts[:-1]] + [matrix_shape(parts[-1])[0]]

    def body(left, *refs):
        out = refs[-1]
        at = 0
        for right, width in zip(refs[:-1], widths):
            turned = at + width == out.shape[1]
            out[:, at : at + width] = (nt if turned else nn)(left[...], right[...])
            at += width

    return local_call(
        body,
        a.shape[0] // ROWS_BLK,
        [row_spec(a)] + [matrix_spec(v) for v in parts],
        pl.BlockSpec((ROWS_BLK, sum(widths)), lambda i: (i, 0)),
        jax.ShapeDtypeStruct((a.shape[0], sum(widths)), f32),
        [a] + [v[0] for v in parts],
    )


def piece_specs(pieces):
    per = pieces[0].shape[0] // ROWS_BLK

    def spec(which, piece):
        return pl.BlockSpec(
            (ROWS_BLK, piece.shape[1]), lambda i: (jnp.clip(i - which * per, 0, per - 1), 0)
        )

    return [spec(which, piece) for which, piece in enumerate(pieces)]


def two_pieces(body, near, far):
    step = pl.program_id(0)
    half = pl.num_programs(0) // 2
    pl.when(step < half)(lambda: body(near))
    pl.when(step >= half)(lambda: body(far))


def ff_forward(pieces, gate_w, up_w, far, ffp):
    ff = matrix_shape(gate_w)[0]
    rows = sum(v.shape[0] for v in pieces)

    def body(near_ref, part_ref, gate_w, up_w, far_gate, far_up, gate_ref, up_ref, product_ref):
        def work(m_ref):
            m = m_ref[...]
            for slot, (gate_t, up_t) in enumerate(((gate_w, up_w), (far_gate, far_up))):
                gate, up = nt(m, gate_t[...]), nt(m, up_t[...])
                at = slot * ffp
                gate_ref[:, at : at + ff] = gate.astype(bf16)
                up_ref[:, at : at + ff] = up.astype(bf16)
                product_ref[:, at : at + ff] = (gate * jax.nn.sigmoid(gate) * up).astype(bf16)

        two_pieces(work, near_ref, part_ref)

    parts = [gate_w, up_w, (far, (0, ff)), (far, (1, ff))]
    return local_call(
        body,
        rows // ROWS_BLK,
        piece_specs(pieces) + [matrix_spec(v) for v in parts],
        [pl.BlockSpec((ROWS_BLK, 2 * ffp), lambda i: (i, 0))] * 3,
        [jax.ShapeDtypeStruct((rows, 2 * ffp), bf16)] * 3,
        list(pieces) + [v[0] for v in parts],
    )


def gate_pair(gate, up, dproduct):
    sig = jax.nn.sigmoid(gate)
    silu = gate * sig
    dgate = dproduct * up * (sig + silu * (1.0 - sig))
    return jnp.concatenate([dgate.astype(bf16), (dproduct * silu).astype(bf16)], axis=1), silu


def ff_backward(pieces, gate, up, down_w, far, ffp):
    ff = matrix_shape(down_w)[0]

    def body(near_ref, part_ref, gate_ref, up_ref, down_ref, far_ref, own_out, far_out):
        def work(g_ref):
            g = g_ref[...]
            for slot, (weight, out) in enumerate(((down_ref, own_out), (far_ref, far_out))):
                cols = slice(slot * ffp, slot * ffp + ff)
                out[...] = gate_pair(
                    gate_ref[:, cols].astype(f32), up_ref[:, cols].astype(f32), nt(g, weight[...])
                )[0]

        two_pieces(work, near_ref, part_ref)

    rows = gate.shape[0]
    parts = [down_w, (far, (2, ff))]
    return local_call(
        body,
        rows // ROWS_BLK,
        piece_specs(pieces) + [row_spec(gate), row_spec(up)] + [matrix_spec(v) for v in parts],
        [pl.BlockSpec((ROWS_BLK, 2 * ff), lambda i: (i, 0))] * 2,
        [jax.ShapeDtypeStruct((rows, 2 * ff), bf16)] * 2,
        list(pieces) + [gate, up] + [v[0] for v in parts],
    )


def ff_weight_grads(m_pieces, g_pieces, dboth, product, gate_w, up_w, down_w, spare):
    ff = matrix_shape(down_w)[0]
    rows, width = m_pieces[0][0].shape

    def body(m0, m1, m2, m3, g0, g1, g2, g3, both_ref, product_ref, gate_t, up_t, down_ref, out, total):
        step = pl.program_id(0)

        def add(both, product, m, g):
            for at, left, right in ((0, both, m), (2 * ff, product, g)):
                part = tn(left, right)
                place = slice(at, at + left.shape[1])

                @pl.when(step == 0)
                def _():
                    total[place] = part

                @pl.when(step > 0)
                def _():
                    total[place] += part

        def near(m_ref, g_ref):
            add(both_ref[...], product_ref[:, :ff], m_ref[...], g_ref[...])

        def far(m_ref, g_ref):
            m, g = m_ref[...], g_ref[...]
            gate, up = nt(m, gate_t[...]), nt(m, up_t[...])
            both, silu = gate_pair(gate, up, nt(g, down_ref[...]))
            add(both, (silu * up).astype(bf16), m, g)

        for which, (work, m_ref, g_ref) in enumerate(
            ((near, m0, g0), (near, m1, g1), (far, m2, g2), (far, m3, g3))
        ):
            pl.when(step == which)(lambda work=work, m_ref=m_ref, g_ref=g_ref: work(m_ref, g_ref))

        @pl.when(step == 3)
        def _():
            out[: 3 * ff] = total[...].astype(bf16)
            if spare:
                out[3 * ff :] = jnp.zeros((spare, width), bf16)

    parts = [gate_w, up_w, down_w]
    once = pl.Buffered(1)

    def alone(spec):
        return pl.BlockSpec(spec.block_shape, spec.index_map, pipeline_mode=once)

    pieces = list(m_pieces) + list(g_pieces)
    return local_call(
        body,
        4,
        [
            pl.BlockSpec((rows, width), lambda i, at=at: (at, 0), pipeline_mode=once) for _, at in pieces
        ]
        + [pl.BlockSpec((rows, v.shape[1]), lambda i: (jnp.minimum(i, 1), 0)) for v in (dboth, product)]
        + [alone(matrix_spec(v)) for v in parts],
        pl.BlockSpec((3 * ff + spare, width), lambda i: (0, 0), pipeline_mode=once),
        jax.ShapeDtypeStruct((3 * ff + spare, width), bf16),
        [v for v, _ in pieces] + [dboth, product] + [v[0] for v in parts],
        scratch=[pltpu.VMEM((3 * ff, width), f32)],
    )


def weight_outputs(mix_grads, ff_grads, ff):
    rows, cols = mix_grads[0].shape
    steps = 4
    high, flat = rows // steps, ff // steps
    widths = (HK, HK, HV, HV)

    def body(*refs):
        ins, outs = refs[: 4 * LAYERS], refs[4 * LAYERS :]

        def work(mix, *parts):
            at = 0
            for ref, width in zip(outs, widths):
                ref[0] = mix[:, at : at + width].astype(f32)
                at += width
            outs[4][0] = mix[:, at : at + HV].astype(f32).T
            for ref, part in zip(outs[5:], parts):
                ref[0] = part[...].astype(f32)

        for layer in range(LAYERS):
            mine = ins[4 * layer : 4 * layer + 4]
            pl.when(pl.program_id(0) == layer)(lambda mine=mine: work(*mine))

    def spec(layer, height, first):
        def place(now, step):
            held = jnp.where(now < layer, 0, steps - 1)
            return (first + jnp.where(now == layer, step, held), 0)

        return pl.BlockSpec((height, cols), place)

    in_specs, args = [], []
    for layer in range(LAYERS):
        in_specs += [spec(layer, high, 0)] + [spec(layer, flat, part * steps) for part in range(3)]
        args += [mix_grads[layer]] + [ff_grads[layer]] * 3
    out_specs = [pl.BlockSpec((1, high, width), lambda now, step: (now, step, 0)) for width in widths]
    out_specs += [pl.BlockSpec((1, HV, high), lambda now, step: (now, 0, step))]
    out_specs += [pl.BlockSpec((1, flat, cols), lambda now, step: (now, step, 0))] * 3
    shapes = [(LAYERS, rows, width) for width in widths] + [(LAYERS, HV, rows)] + [(LAYERS, ff, cols)] * 3
    return pl.pallas_call(
        body,
        grid=(LAYERS, steps),
        in_specs=in_specs,
        out_specs=out_specs,
        out_shape=[jax.ShapeDtypeStruct(v, f32) for v in shapes],
        cost_estimate=NO_COST,
        compiler_params=pltpu.CompilerParams(
            dimension_semantics=("arbitrary", "arbitrary"), vmem_limit_bytes=VMEM_LIMIT
        ),
    )(*args)


def ring_place(index, n):
    return jnp.where(index % 2 == 0, index // 2, n - 1 - index // 2)


def ring_index(place, n):
    return jnp.where(place < n // 2, 2 * place, 2 * (n - 1 - place) + 1)


MESH = pl.DeviceIdType.MESH


class Ring:
    def __init__(self, n, data, out, slots, sems):
        self.n, self.data, self.out, self.slots = n, data, out, slots
        self.send, self.recv, self.out_send, self.out_recv = sems
        self.me = ring_place(lax.axis_index("dp"), n)
        self.peers = [
            ring_index(lax.rem(self.me + 1, n), n),
            ring_index(lax.rem(self.me + n - 1, n), n),
        ]
        self.rows = data.shape[0] // (2 * n)

    def chunk(self, ref, way, back):
        which = lax.rem(self.me + 2 * self.n - (1, -1)[way] * back, self.n)
        return ref.at[pl.ds(pl.multiple_of((2 * which + way) * self.rows, 16), self.rows)]

    def partial(self, way, source, step):
        return pltpu.make_async_remote_copy(
            src_ref=source, dst_ref=self.slots.at[way, step],
            send_sem=self.send.at[way, step], recv_sem=self.recv.at[way, step],
            device_id={"dp": self.peers[way]}, device_id_type=MESH,
        )

    def final(self, way, step, back):
        part = self.chunk(self.out, way, back)
        return pltpu.make_async_remote_copy(
            src_ref=part, dst_ref=part,
            send_sem=self.out_send.at[way, step], recv_sem=self.out_recv.at[way, step],
            device_id={"dp": self.peers[way]}, device_id_type=MESH,
        )

    def start(self):
        for way in range(2):
            self.partial(way, self.chunk(self.data, way, 0), 0).start()

    def reduce(self, step):
        for way in range(2):
            slot = self.slots.at[way, step]
            self.partial(way, slot, step).wait_recv()
            part = self.chunk(self.data, way, step + 1)
            slot[...] = (slot[...].astype(f32) + part[...].astype(f32)).astype(bf16)

            @pl.when(step < self.n - 2)
            def _():
                self.partial(way, slot, step + 1).start()

    def turn(self):
        for way in range(2):
            self.chunk(self.out, way, -1)[...] = self.slots[way, self.n - 2]
            self.final(way, 0, -1).start()

    def gather(self, step):
        for way in range(2):
            self.final(way, step, step).wait_recv()

            @pl.when(step < self.n - 2)
            def _():
                self.final(way, step + 1, step).start()

    def sent(self, step):
        for way in range(2):
            self.partial(way, self.slots.at[way, step], step).wait_send()
            self.final(way, step, step - 1).wait_send()


def steps_of(lo, hi, *bodies):
    def body(step, carry):
        for each in bodies:
            each(step)
        return carry

    lax.fori_loop(lo, hi, body, 0)


def mix_sum_kernel(
    n, cuts, done, late, own, far, misc, out_done, out_late, out_own, out_misc, came, total,
    slot_a, slot_b, slot_c, slot_d, slot_e, slot_f,
    send, recv, out_send, out_recv, chip_send, chip_recv, sums, misc_came, misc_send, misc_recv,
):
    me = ring_place(lax.axis_index("dp"), n)
    member, row = lax.axis_index("head"), lax.axis_index("dp")
    swaps = [{"head": member ^ 1}, {"head": member ^ 2}]
    swaps += [{"dp": row ^ (1 << bit)} for bit in range(n.bit_length() - 1)]
    peers = swaps + [
        {"dp": ring_index(lax.rem(me + 1, n), n)},
        {"dp": ring_index(lax.rem(me + n - 1, n), n)},
    ]
    barrier = pltpu.get_barrier_semaphore()
    for peer in peers:
        pl.semaphore_signal(barrier, inc=1, device_id=peer, device_id_type=MESH)
    pl.semaphore_wait(barrier, len(peers))

    def small(step):
        return pltpu.make_async_remote_copy(
            src_ref=sums.at[step], dst_ref=misc_came.at[step],
            send_sem=misc_send.at[step], recv_sem=misc_recv.at[step],
            device_id=swaps[step], device_id_type=MESH,
        )

    taken = [0]

    def small_step():
        step = taken[0]
        if step == len(swaps):
            return
        small(step).wait()
        sums[step + 1] = sums[step] + misc_came[step]
        taken[0] += 1
        if step + 1 < len(swaps):
            small(step + 1).start()

    swap = pltpu.make_async_remote_copy(
        src_ref=far, dst_ref=came, send_sem=chip_send, recv_sem=chip_recv,
        device_id={"head": member ^ 2}, device_id_type=MESH,
    )
    def ring(which, data, out, cut, slots):
        rows = slice(*cut)
        sems = [v.at[which] for v in (send, recv, out_send, out_recv)]
        return Ring(n, data.at[rows], out.at[rows], slots, sems)

    rings = (
        (0, done, out_done, cuts[0], slot_a),
        (1, done, out_done, cuts[1], slot_b),
        (2, late, out_late, cuts[2], slot_c),
        (3, late, out_late, cuts[3], slot_d),
        (4, total, out_own, cuts[4], slot_e),
        (5, total, out_own, cuts[5], slot_f),
    )
    first, second = ([ring(*v) for v in pair if v[3][1] > v[3][0]] for pair in (rings[:4], rings[4:]))

    def each(rings, name):
        return [getattr(v, name) for v in rings]

    def now(steps):
        for step in steps:
            step()

    middle, last = (n - 1) // 2, n - 1
    sums[0] = misc[...]
    small(0).start()
    swap.start()
    now(each(first, "start"))
    steps_of(0, middle, *each(first, "reduce"))
    small_step()
    steps_of(middle, last, *each(first, "reduce"))
    now(each(first, "turn"))
    small_step()
    swap.wait()
    total[...] = (own[...].astype(f32) + came[...].astype(f32)).astype(bf16)
    now(each(second, "start"))
    together = each(first, "gather") + each(second, "reduce")
    steps_of(0, middle, *together)
    small_step()
    steps_of(middle, last, *together)
    now(each(second, "turn"))
    small_step()
    steps_of(0, middle, *each(second, "gather"))
    small_step()
    steps_of(middle, last, *each(second, "gather"))
    for _ in swaps:
        small_step()
    out_misc[...] = sums[len(swaps)]
    steps_of(0, last, *each(first + second, "sent"))


def mix_sum(done, late, own, far, misc, n):
    if n == 1:
        misc = misc + core_swap(misc)
        own = (own.astype(f32) + chip_swap(far).astype(f32)).astype(bf16)
        return done, late, own, misc + chip_swap(misc)
    rows, cols = own.shape
    done_rows = done.shape[0]
    swaps = 2 + n.bit_length() - 1

    def two(total):
        lines = total // (32 * n)
        cut = (lines + 1) // 2 * 32 * n
        return (0, cut), (cut, total)

    cuts = two(done_rows) + two(rows) + two(rows)

    def body(*refs):
        mix_sum_kernel(n, cuts, *refs)

    vmem = pl.BlockSpec(memory_space=pltpu.VMEM)
    return pl.pallas_call(
        body,
        in_specs=[vmem] * 5,
        out_specs=[vmem] * 4,
        out_shape=[
            jax.ShapeDtypeStruct((done_rows, cols), bf16),
            jax.ShapeDtypeStruct((rows, cols), bf16),
            jax.ShapeDtypeStruct((rows, cols), bf16),
        ]
        + [jax.ShapeDtypeStruct(misc.shape, f32)],
        scratch_shapes=[
            pltpu.VMEM((rows, cols), bf16),
            pltpu.VMEM((rows, cols), bf16),
        ]
        + [
            pltpu.VMEM((2, n - 1, max(16, (stop - at) // (2 * n)), cols), bf16) for at, stop in cuts
        ]
        + [pltpu.SemaphoreType.DMA((6, 2, n - 1))] * 4
        + [pltpu.SemaphoreType.DMA] * 2
        + [
            pltpu.VMEM((swaps + 1,) + misc.shape, f32),
            pltpu.VMEM((swaps,) + misc.shape, f32),
            pltpu.SemaphoreType.DMA((swaps,)),
            pltpu.SemaphoreType.DMA((swaps,)),
        ],
        compiler_params=pltpu.CompilerParams(
            collective_id=0, has_side_effects=True, vmem_limit_bytes=VMEM_LIMIT
        ),
    )(done, late, own, far, misc)


def norm_scale(hidden):
    return lax.rsqrt(jnp.mean(hidden * hidden, axis=-1, keepdims=True) + epsilon)


def norm_low(hidden, gain):
    return (hidden * norm_scale(hidden) * gain).astype(bf16)


def norm_back(hidden, gain, grad_normed):
    scale = norm_scale(hidden)
    weighted = grad_normed * gain
    grad_hidden = scale * weighted - hidden * (scale * scale * scale) * jnp.mean(
        weighted * hidden, axis=-1, keepdims=True
    )
    return grad_hidden, jnp.sum(grad_normed * hidden * scale, axis=0)


def core_swap(value):
    return lax.ppermute(value, "head", [(i, i ^ 1) for i in range(4)])


def chip_swap(value):
    return lax.ppermute(value, "head", [(i, i ^ 2) for i in range(4)])


def dp_slices(arrays, layer):
    n = lax.axis_size("dp")
    height, width = arrays[0].shape[1] // n, arrays[0].shape[2]
    views = [v.reshape(v.shape[0], n, height, width) for v in arrays]

    def body(at, *refs):
        for which, ref in enumerate(refs[:-1]):
            refs[-1][which] = ref[...]

    return pl.pallas_call(
        body,
        grid_spec=pltpu.PrefetchScalarGridSpec(
            num_scalar_prefetch=1,
            grid=(1,),
            in_specs=[pl.BlockSpec((None, None, height, width), lambda i, at: (layer, at[0], 0, 0))] * len(views),
            out_specs=pl.BlockSpec((len(views), height, width), lambda i, at: (0, 0, 0)),
        ),
        out_shape=jax.ShapeDtypeStruct((len(views), height, width), bf16),
        cost_estimate=NO_COST,
        compiler_params=kernel_params(),
    )(lax.axis_index("dp").astype(jnp.int32).reshape(1), *views)


def dp_ring():
    n = lax.axis_size("dp")
    return list(range(0, n, 2)) + list(range(n - 1, 0, -2)) if n > 1 else [0]


def after(value, *others):
    return lax.optimization_barrier((value,) + others)[0]


def per_device(
    tokens, doc_starts, grad_out, norm_one, w_query, w_key, w_value, w_outgate, w_rank, w_decay,
    decay_bias, group_gain, w_out, norm_two, w_gate, w_up, w_down,
):
    shard_len, width = tokens.shape[1:]
    ndoc = doc_starts.shape[1]
    ff = w_gate.shape[2]
    ffp = -(-ff // 128) * 128
    rank = w_decay.shape[1]
    member = lax.axis_index("head")
    core = member % 2
    chip = member // 2
    meta = jnp.concatenate(
        [doc_starts[0], jnp.stack([chip * (2 * shard_len), core]).astype(jnp.int32)]
    )
    mixer = Mixer(meta, ndoc, 2 * shard_len)

    def mix_pack(layer):
        return jnp.concatenate(
            [w_query[layer], w_key[layer], w_value[layer], w_outgate[layer]], axis=1
        )

    gate_t, up_t, rank_t = (jnp.swapaxes(v, 1, 2) for v in (w_gate, w_up, w_rank))

    def ff_slice(layer, wait):
        return chip_swap(after(dp_slices((gate_t, up_t, w_down), layer), wait))

    def ff_gather(part):
        dp = lax.axis_size("dp")
        whole = lax.all_gather(part, "dp", axis=0, tiled=True)
        return jnp.swapaxes(whole.reshape(dp, 3, ff // dp, width), 0, 1).reshape(3 * ff, width)

    def with_partner(local):
        return jnp.concatenate([local, core_swap(local)], axis=0)

    def settle(terms):
        sent = core_swap(sum_of_dots(terms, shard_len, shard_len, bf16))
        return sum_of_dots(terms, 0, shard_len, f32) + sent.astype(f32)

    small = jnp.concatenate([w_decay.astype(f32), decay_bias[:, None, :]], axis=1)
    small = jnp.concatenate([small, chip_swap(small)], axis=2)
    mix_own = mix_pack(0)
    first_far = chip_swap(mix_own[:, : 2 * HK])
    ff_part = ff_slice(0, meta)
    ff_far = ff_gather(ff_part)
    mix_far = (first_far, chip_swap(after(mix_own[:, 2 * HK :], ff_part)))
    out_far = chip_swap(after(w_out[0], ff_part))
    next_part = ff_slice(1, mix_far[1])
    next_own = mix_pack(1)
    spare = -3 * ff % (32 * lax.axis_size("dp"))

    grad = grad_out[0].astype(f32)
    hidden = tokens[0].astype(f32)
    saved = []
    for layer in range(LAYERS):
        hidden_in = hidden
        a = with_partner(norm_low(hidden, norm_one[layer]))
        x = project(a, ((mix_own, None),) + tuple((v, None) for v in mix_far) + ((rank_t, layer),))
        wdec, bias = small[layer, :rank], small[layer, rank:]
        run, states, cum, final = mixer.states(x, wdec, bias)
        got = chip_swap(after(final, next_part, next_own) if layer == 0 else after(final, out_far))
        first = got[::-1] * chip.astype(bf16)
        gain = group_gain[layer][None]
        gated, mixed = mixer.mix(x, run, states, cum, first, gain)
        if layer + 1 < LAYERS:
            next_mix = (chip_swap(after(next_own, got)),)
            next_out = chip_swap(after(w_out[layer + 1], got))
            next_far = ff_gather(next_part)
        hidden_mid = hidden + settle(
            [(gated, 0, (w_out, layer), False), (gated, HV, (out_far, None), False)]
        )
        m_own = norm_low(hidden_mid, norm_two[layer])
        m = (m_own, core_swap(m_own))
        gate, up, product = ff_forward(m, (gate_t, layer), (up_t, layer), ff_far, ffp)
        if layer + 1 < LAYERS:
            product = after(product, next_mix[0])
        hidden = hidden_mid + settle(
            [(product, 0, (w_down, layer), False), (product, ffp, (ff_far, (2, ff)), False)]
        )
        saved.append(
            (hidden_in, hidden_mid, a, m, x, run, states, cum, first, mixed, gated, gate, up, product,
             mix_own, mix_far, out_far, ff_far)
        )
        if layer + 1 < LAYERS:
            mix_own, mix_far, out_far, ff_far = next_own, next_mix, next_out, next_far
    result = hidden.astype(bf16)[None]

    ff_grads, misc_grads = [None] * LAYERS, [None] * LAYERS
    for layer in reversed(range(LAYERS)):
        (
            hidden_in, hidden_mid, a, m, x, run, states, cum, first, mixed, gated, gate, up, product,
            mix_own, mix_far, out_far, ff_far,
        ) = saved[layer]
        gain = group_gain[layer][None]
        wdec, bias = small[layer, :rank], small[layer, rank:]
        if layer + 1 < LAYERS:
            g_own = grad.astype(bf16)
            g_y = chip_swap(jnp.concatenate([g_own, m[0]], axis=0))
            came = (g_y, core_swap(g_y))
            g_far, m_far = [(v, 0) for v in came], [(v, 1) for v in came]
            mix_late = (own, chip_swap(after(far, g_y)))
        else:
            g_own = grad_out[0]
            g_y = chip_swap(after(g_own, got))
            m_y = chip_swap(m[0])
            m_far, g_far = ([(v, 0), (core_swap(v), 0)] for v in (m_y, g_y))
        g = (g_own, core_swap(g_own))
        dboth, dfar = ff_backward(g, gate, up, (w_down, layer), ff_far, ffp)
        back_mid, gain_two = norm_back(
            hidden_mid,
            norm_two[layer],
            settle(
                [
                    (dboth, 0, (gate_t, layer), False),
                    (dboth, ff, (up_t, layer), False),
                    (dfar, 0, (ff_far, (0, 2 * ff)), False),
                ]
            ),
        )
        ff_grad = ff_weight_grads(
            [(v, 0) for v in m] + m_far, [(v, 0) for v in g] + g_far, dboth, product,
            (gate_t, layer), (up_t, layer), (w_down, layer), 0 if layer else spare,
        )
        grad = grad + back_mid
        g_mix = with_partner(grad.astype(bf16))
        if layer + 1 == LAYERS:
            g_mix = after(g_mix, ff_grad)
        g_wout = tn(g_mix, gated).astype(bf16)
        dmixed, doutgate, dstates, dcum, dfinal, dgain = mixer.back_states(
            x, run, mixed, g_mix, w_out[layer], out_far, gain
        )
        got = chip_swap(dfinal)
        dlast = got[::-1] * (1 - chip).astype(bf16)
        dx, dwdec, dbias = mixer.back(
            x, run, states, cum, first, dmixed, doutgate, dstates, dcum, dlast, wdec, bias
        )
        g_wmix = tn(a, dx[:, : 2 * HEAD_COLS]).astype(bf16)
        g_rank = tn(dx[:, 2 * HEAD_COLS :], a)
        if layer + 1 < LAYERS:
            mix_late = (mix_late[0].astype(f32) + after(mix_late[1], dx).astype(f32)).astype(bf16)
        far = jnp.concatenate([g_wmix[:, HEAD_COLS:], g_wout[:, HV:]], axis=1)
        own = jnp.concatenate([g_wmix[:, :HEAD_COLS], g_wout[:, :HV]], axis=1)
        far_terms, at = [], HEAD_COLS
        for part in mix_far:
            far_terms.append((dx, at, (part, None), True))
            at += part.shape[1]
        back_first, gain_one = norm_back(hidden_in, norm_one[layer], settle(
            [
                (dx, 0, (mix_own, None), True),
                *far_terms,
                (dx, 2 * HEAD_COLS, (rank_t, layer), False),
            ]
        ))
        grad = grad + back_first
        if layer > 0:
            ff_grads[layer] = lax.psum(ff_grad, "dp")
        heads = jnp.concatenate([dwdec, dbias], axis=0)
        places = lax.iota(jnp.int32, 4)[:, None, None]
        heads = jnp.where(places == member, heads[None, :, :HK], 0.0) + jnp.where(
            places == member ^ 2, heads[None, :, HK:], 0.0
        )
        misc_grads[layer] = jnp.concatenate(
            [g_rank.reshape(-1), gain_one, gain_two, dgain[0], heads.reshape(-1)]
        )

    misc = jnp.stack(misc_grads)
    length = misc.shape[1]
    misc = jnp.pad(misc.reshape(-1), (0, -misc.size % 1024)).reshape(-1, 128)
    ff_done, late_mix, first_mix, misc = mix_sum(ff_grad, mix_late, own, far, misc, lax.axis_size("dp"))
    mix_grads = [first_mix, late_mix]
    ff_grads[0] = ff_done
    misc = misc.reshape(-1)[: LAYERS * length].reshape(LAYERS, length)
    sizes = (rank * width, width, width, HV, 4 * (rank + 1) * HK)
    pieces, at = [], 0
    for size in sizes:
        pieces.append(misc[:, at : at + size])
        at += size
    heads = lax.dynamic_index_in_dim(
        pieces[4].reshape(LAYERS, 4, rank + 1, HK), member, axis=1, keepdims=False
    )

    query, key, value, outgate, out, gate, up, down = weight_outputs(mix_grads, ff_grads, ff)
    return (
        result,
        grad[None],
        pieces[1],
        query,
        key,
        value,
        outgate,
        jnp.swapaxes(pieces[0].reshape(LAYERS, rank, width), 1, 2),
        heads[:, :rank],
        heads[:, rank],
        pieces[3],
        out,
        pieces[2],
        jnp.swapaxes(gate, 1, 2),
        jnp.swapaxes(up, 1, 2),
        down,
    )


def solution(mesh):
    cols = P(None, None, "head")
    rows = P(None, "head", None)
    place = P("dp", "head", None)
    return jax.shard_map(
        per_device,
        mesh=mesh,
        in_specs=(
            place, P("dp", None), place, P(), cols, cols, cols, cols, P(), cols,
            P(None, "head"), P(), rows, P(), cols, cols, rows,
        ),
        out_specs=(
            place, place, P(), cols, cols, cols, cols, P(), cols, P(None, "head"), P(), rows,
            P(), cols, cols, rows,
        ),
        check_vma=False,
    )
```
